32 devices in a mesh: gx: 2 (over y), gy: 4 (over z), gz: 4 (over x, core).
Axes of the slice: x: 2, y: 2, z: 4, core: 2. Of those that a mesh axis runs over, the one named last changes fastest.
Arguments:
- state: float32 [1024, 5, 4096], P(('gx', 'gy', 'gz')), may hold values from -1 to 5.75, as said below
- send_slots: int32 [3, 32, 8], P(None, ('gx', 'gy', 'gz')), may hold values from 0 to 32, as said below
- recv_slots: int32 [3, 32, 8], P(None, ('gx', 'gy', 'gz')), may hold values from 0 to 32, as said below
- owner_slot: int32 [256], replicated, may hold values from 0 to 31, as said below
Outputs:
- new_state: float32 [1024, 5, 4096], P(('gx', 'gy', 'gz'))
The draws below stay inside these ranges and needn't reach their ends.
Inputs may be any that keep to these rules, and one draw needn't show every extreme that they name: `state`: in every slot that holds a block at the start, density lies in 1 to 2, each velocity component in -0.5 to 0.5 and pressure in 1 to 2; slots holding no block carry values that no output reads. `send_slots`: at each level and device, the entries under 32 come first, are distinct, and name slots that hold a block at the start of that level; the rest equal 32. At most 8 are named, and at each level one device names exactly 8. `recv_slots`: at each level and device, the entries under 32 come first, are as many as the partner names in send_slots at that level, are distinct, and name slots that hold no block once the device's own sent slots are emptied; the rest equal 32. After the three levels, each device holds exactly the 8 blocks of its box (the blocks of the second step's rule), block b in slot owner_slot[b]; its other slots hold no block.
All inputs are finite; a program needn't handle non-finite values.
Results may differ from the reference program's by a relative error of at most 0.0003.
Values sent between devices are 32-bit elements; how exact they have to be, the bound alone decides.
No kernel may reach another device: no remote copies, remote signals or barrier semaphores. Data moves between devices by JAX's collectives and lax.ppermute only.
A program may use at most 64 MiB of HBM per device.

```python
import jax
import jax.numpy as jnp
from jax import lax

BLK = 16
RX = 1
RY = 1
RZ = 8
OCC = 8
MOVE = 8
SLOTS = 32
CELLS = 4096
BX = 2
BY = 4
BZ = 32
NBLK = 256
HALF_X = 16
HALF_Y = 8
HALF_Z = 2
DEVICES = 32


def migration_plan(key):
    base = jax.random.fold_in(key, 7)
    perm_keys = jax.random.split(jax.random.fold_in(base, 1), DEVICES)
    perms = jax.vmap(lambda sub: jax.random.permutation(sub, SLOTS))(perm_keys).astype(jnp.int32)
    position = jnp.argsort(perms, axis=1)
    filled = position < OCC
    slot_index = jnp.arange(SLOTS, dtype=jnp.int32)
    move_index = jnp.arange(MOVE, dtype=jnp.int32)
    devices = jnp.arange(DEVICES, dtype=jnp.int32)
    halves = (HALF_X, HALF_Y, HALF_Z)
    send_lists = [None, None, None]
    recv_lists = [None, None, None]
    for section_level in (2, 1, 0):
        level_key = jax.random.fold_in(base, 10 + section_level)
        count_key = jax.random.fold_in(level_key, 0)
        recv_key = jax.random.fold_in(level_key, 2)
        send_key = jax.random.fold_in(level_key, 3)
        partner = jnp.bitwise_xor(devices, halves[section_level])
        fill_count = jnp.sum(filled.astype(jnp.int32), axis=1)
        counts = jax.random.randint(count_key, (DEVICES,), 0, MOVE, dtype=jnp.int32)
        counts = jnp.minimum(counts, fill_count[partner])
        busiest = partner[jnp.argmax(fill_count)]
        counts = jnp.where(devices == busiest, MOVE, counts)
        taken = counts[partner]
        scores = jax.random.randint(recv_key, (DEVICES, SLOTS), 0, 2 ** 20, dtype=jnp.int32) * SLOTS + slot_index
        order = jnp.argsort(jnp.where(filled, scores, scores + 2 ** 27), axis=1, stable=True)[:, :MOVE].astype(jnp.int32)
        recv_list = jnp.where(move_index[None, :] < taken[:, None], order, SLOTS)
        cleared = jnp.any(recv_list[:, :, None] == slot_index[None, None, :], axis=1)
        filled = jnp.logical_and(filled, jnp.logical_not(cleared))
        scores_two = jax.random.randint(send_key, (DEVICES, SLOTS), 0, 2 ** 20, dtype=jnp.int32) * SLOTS + slot_index
        order_two = jnp.argsort(jnp.where(filled, scores_two + 2 ** 27, scores_two), axis=1, stable=True)[:, :MOVE].astype(jnp.int32)
        send_list = jnp.where(move_index[None, :] < counts[:, None], order_two, SLOTS)
        placed = jnp.any(send_list[:, :, None] == slot_index[None, None, :], axis=1)
        filled = jnp.logical_or(filled, placed)
        send_lists[section_level] = send_list
        recv_lists[section_level] = recv_list
    grid_y = BY // RY
    grid_z = BZ // RZ
    blocks = jnp.arange(NBLK, dtype=jnp.int32)
    block_x = blocks // (BY * BZ)
    block_y = blocks // BZ % BY
    block_z = blocks % BZ
    owner_dev = (block_x // RX * grid_y + block_y // RY) * grid_z + block_z // RZ
    within = (block_x % RX * RY + block_y % RY) * RZ + block_z % RZ
    owner = perms[owner_dev, within]
    return (jnp.stack(send_lists).astype(jnp.int32), jnp.stack(recv_lists).astype(jnp.int32), owner.astype(jnp.int32))


def draw_send_slots(key, part):
    return migration_plan(key)[0]


def draw_recv_slots(key, part):
    return migration_plan(key)[1]


def draw_owner_slot(key, part):
    return migration_plan(key)[2]


def draw_state(key, part):
    keys = jax.random.split(jax.random.fold_in(key, 3), 5)
    shape = (DEVICES * SLOTS, CELLS)
    uniforms = [jax.random.uniform(sub, shape, jnp.float32) for sub in keys]
    density = 1.0 + uniforms[0]
    velocity = [sample - 0.5 for sample in uniforms[1:4]]
    pressure = 1.0 + uniforms[4]
    energy = pressure / 0.4 + 0.5 * density * (velocity[0] * velocity[0] + velocity[1] * velocity[1] + velocity[2] * velocity[2])
    return jnp.stack([density, density * velocity[0], density * velocity[1], density * velocity[2], energy], axis=1).astype(jnp.float32)


def setup_inputs(seed: int = 0) -> dict:
    seeds = jax.random.split(jax.random.key(seed), 5)
    state = draw_state(jax.random.fold_in(seeds[4], 71), 0)
    send_slots = draw_send_slots(jax.random.fold_in(seeds[4], 71), 0)
    recv_slots = draw_recv_slots(jax.random.fold_in(seeds[4], 71), 0)
    owner_slot = draw_owner_slot(jax.random.fold_in(seeds[4], 71), 0)
    return {"state": state, "send_slots": send_slots, "recv_slots": recv_slots, "owner_slot": owner_slot}


gamma_ratio = 1.4
time_step = 0.05

def minmod(lower, upper):
    return 0.5 * (jnp.sign(lower) + jnp.sign(upper)) * jnp.minimum(jnp.abs(lower), jnp.abs(upper))

def primitives(conserved):
    density = conserved[0]
    inverse = 1.0 / density
    vel_x = conserved[1] * inverse
    vel_y = conserved[2] * inverse
    vel_z = conserved[3] * inverse
    pressure = (gamma_ratio - 1.0) * (conserved[4] - 0.5 * (conserved[1] * vel_x + conserved[2] * vel_y + conserved[3] * vel_z))
    return jnp.stack([density, vel_x, vel_y, vel_z, pressure])

def side_terms(primitive, normal):
    density = primitive[0]
    velocity = (primitive[1], primitive[2], primitive[3])
    pressure = primitive[4]
    normal_vel = velocity[normal]
    energy = pressure / (gamma_ratio - 1.0) + 0.5 * density * (velocity[0] * velocity[0] + velocity[1] * velocity[1] + velocity[2] * velocity[2])
    conserved = jnp.stack([density, density * velocity[0], density * velocity[1], density * velocity[2], energy])
    momenta = []
    for component in range(3):
        term = density * velocity[component] * normal_vel
        if component == normal:
            term = term + pressure
        momenta.append(term)
    fluxes = jnp.stack([density * normal_vel] + momenta + [(energy + pressure) * normal_vel])
    speeds = jnp.abs(normal_vel) + jnp.sqrt(gamma_ratio * pressure / density)
    return (conserved, fluxes, speeds)

def face_fluxes(primitive, along, normal):
    length = primitive.shape[along]
    jumps = lax.slice_in_dim(primitive, 1, length, axis=along) - lax.slice_in_dim(primitive, 0, length - 1, axis=along)
    slopes = minmod(lax.slice_in_dim(jumps, 0, length - 2, axis=along), lax.slice_in_dim(jumps, 1, length - 1, axis=along))
    left_state = lax.slice_in_dim(primitive, 1, length - 2, axis=along) + 0.5 * lax.slice_in_dim(slopes, 0, length - 3, axis=along)
    right_state = lax.slice_in_dim(primitive, 2, length - 1, axis=along) - 0.5 * lax.slice_in_dim(slopes, 1, length - 2, axis=along)
    left_cons, left_flux, left_speed = side_terms(left_state, normal)
    right_cons, right_flux, right_speed = side_terms(right_state, normal)
    speeds = jnp.maximum(left_speed, right_speed)
    return 0.5 * (left_flux + right_flux) - 0.5 * speeds * (right_cons - left_cons)

def advance(padded):
    center = padded[:, 2:-2, 2:-2, 2:-2]
    summed = None
    for normal in range(3):
        along = normal + 1
        window = padded
        for other in (1, 2, 3):
            if other != along:
                window = lax.slice_in_dim(window, 2, window.shape[other] - 2, axis=other)
        fluxes = face_fluxes(primitives(window), along, normal)
        count = fluxes.shape[along]
        difference = lax.slice_in_dim(fluxes, 1, count, axis=along) - lax.slice_in_dim(fluxes, 0, count - 1, axis=along)
        summed = difference if summed is None else summed + difference
    return center - time_step * summed

def reference(state, send_slots, recv_slots, owner_slot):
    grid_x = BX // RX
    grid_y = BY // RY
    grid_z = BZ // RZ
    devices = jnp.arange(DEVICES, dtype=jnp.int32)
    anchor = jnp.arange(DEVICES * SLOTS, dtype=jnp.int32).reshape(DEVICES, SLOTS)
    halves = (HALF_X, HALF_Y, HALF_Z)
    row_index = devices[:, None]
    for section_level in range(3):
        partner = jnp.bitwise_xor(devices, halves[section_level])
        moved = jnp.take_along_axis(anchor, jnp.minimum(send_slots[section_level], SLOTS - 1), axis=1)
        anchor = anchor.at[row_index, recv_slots[section_level]].set(moved[partner], mode='drop')
    blocks = jnp.arange(NBLK, dtype=jnp.int32)
    block_x = blocks // (BY * BZ)
    block_y = blocks // BZ % BY
    block_z = blocks % BZ
    owner_dev = (block_x // RX * grid_y + block_y // RY) * grid_z + block_z // RZ
    source = anchor[owner_dev, owner_slot]
    block_data = jnp.take(state, source, axis=0)
    field_grid = block_data.reshape(BX, BY, BZ, 5, BLK, BLK, BLK).transpose(3, 0, 4, 1, 5, 2, 6).reshape(5, BX * BLK, BY * BLK, BZ * BLK)
    extent_x = RX * BLK
    extent_y = RY * BLK
    extent_z = RZ * BLK

    def window_of(field, device):
        index_x = device // (grid_y * grid_z)
        index_y = device // grid_z % grid_y
        index_z = device % grid_z
        rows_x = (index_x * extent_x - 2 + jnp.arange(extent_x + 4, dtype=jnp.int32)) % (BX * BLK)
        rows_y = (index_y * extent_y - 2 + jnp.arange(extent_y + 4, dtype=jnp.int32)) % (BY * BLK)
        rows_z = (index_z * extent_z - 2 + jnp.arange(extent_z + 4, dtype=jnp.int32)) % (BZ * BLK)
        piece = jnp.take(field, rows_x, axis=1)
        piece = jnp.take(piece, rows_y, axis=2)
        return jnp.take(piece, rows_z, axis=3)

    def sweep(field):
        boxes = lax.map(lambda device: advance(window_of(field, device)), devices)
        boxes = boxes.reshape(grid_x, grid_y, grid_z, 5, extent_x, extent_y, extent_z)
        return boxes.transpose(3, 0, 4, 1, 5, 2, 6).reshape(5, BX * BLK, BY * BLK, BZ * BLK)
    section_one = sweep(field_grid)
    section_two = 0.5 * field_grid + 0.5 * sweep(section_one)
    result = section_two.reshape(5, BX, BLK, BY, BLK, BZ, BLK).transpose(1, 3, 5, 0, 2, 4, 6).reshape(NBLK, 5, CELLS)
    return jnp.zeros_like(state).at[owner_dev * SLOTS + owner_slot].set(result)
```

```python
import functools

import jax
import jax.numpy as jnp
from jax import lax
from jax.experimental import pallas as pl
from jax.experimental.pallas import tpu as pltpu
from jax.sharding import PartitionSpec as P

gamma_ratio = 1.4
time_step = 0.05
LANES = 128
SUB = 8
PIECES = 4
NF = 5
AXES = ("gx", "gy", "gz")

VMEM = pltpu.VMEM
SMEM = pltpu.SMEM


def whole(space):
    return pl.BlockSpec(memory_space=space)


def params():
    return pltpu.CompilerParams(vmem_limit_bytes=24 * 1024 * 1024)


def cost(flops, moved):
    return pl.CostEstimate(flops=flops, bytes_accessed=moved, transcendentals=0)


def row_pack(source, slot, target, index, piece, per_piece):
    for i in range(per_piece):
        lo = (piece * per_piece + i) * LANES
        target[index, i * NF : (i + 1) * NF, :] = source[slot, :, lo : lo + LANES]


def first_kernel(send, state, *refs, pieces, per_piece, moves, slots):
    outs, (held, sems) = refs[:pieces], refs[pieces:]

    def copy(k):
        slot = jnp.minimum(send[0, 0, k], slots - 1)
        return pltpu.make_async_copy(state.at[slot], held.at[k], sems.at[k])

    for k in range(moves):
        copy(k).start()
    for k in range(moves):
        copy(k).wait()

    def body(k, carry):
        for piece in range(pieces):
            row_pack(held, k, outs[piece], k, piece, per_piece)
        return carry

    lax.fori_loop(0, moves, body, 0)


def rows_kernel(send, recv, own, state, *refs, pieces, per_piece, moves, slots, occ, group):
    outs, tags = refs[:pieces], refs[pieces]

    @pl.when(pl.program_id(0) == 0)
    def _():
        def find(slot, levels):
            tag = slot
            for level in range(levels):
                for j in range(moves):
                    tag = jnp.where(recv[level, 0, j] == slot, slots + level * moves + j, tag)
            return tag

        def one(k, carry):
            for level in (1, 2):
                slot = jnp.minimum(send[level, 0, k], slots - 1)
                tags[(level - 1) * moves + k] = find(slot, level)
            return carry

        lax.fori_loop(0, moves, one, 0)

        def last(b, carry):
            tags[2 * moves + b] = find(own[b], 3)
            return carry

        lax.fori_loop(0, occ, last, 0)

    def body(s, carry):
        for piece in range(pieces):
            row_pack(state, s, outs[piece], s, piece, per_piece)
        return carry

    lax.fori_loop(0, group, body, 0)


def pick(tag, sources, slots, moves, put):
    for number, ref in enumerate(sources):
        base = 0 if number == 0 else slots + (number - 1) * moves
        count = slots if number == 0 else moves

        @pl.when(jnp.logical_and(tag >= base, tag < base + count))
        def _(ref=ref, base=base):
            put(ref, tag - base)


def select_kernel(tags, *refs, sources, level, slots, moves, passed):
    given = refs[:sources]
    out = refs[sources + passed]

    def body(k, carry):
        def put(ref, index):
            out[k] = ref[index]

        pick(tags[(level - 1) * moves + k], given, slots, moves, put)
        return carry

    lax.fori_loop(0, moves, body, 0)


def primitives(cons):
    density = cons[0]
    inverse = 1.0 / density
    vel = [cons[1] * inverse, cons[2] * inverse, cons[3] * inverse]
    kinetic = cons[1] * vel[0] + cons[2] * vel[1] + cons[3] * vel[2]
    pressure = (gamma_ratio - 1.0) * (cons[4] - 0.5 * kinetic)
    return [density, vel[0], vel[1], vel[2], pressure]


def half_minmod(lower, upper):
    both = jnp.maximum(0.0, jnp.minimum(lower, upper)) + jnp.minimum(
        0.0, jnp.maximum(lower, upper)
    )
    return 0.5 * both


def half_slopes(before, here, after):
    return [half_minmod(h - b, a - h) for b, h, a in zip(before, here, after)]


def plus(a, b):
    return [x + y for x, y in zip(a, b)]


def minus(a, b):
    return [x - y for x, y in zip(a, b)]


def side_terms(prim, normal):
    density, vel, pressure = prim[0], prim[1:4], prim[4]
    along = vel[normal]
    mom = [density * v for v in vel]
    kinetic = mom[0] * vel[0] + mom[1] * vel[1] + mom[2] * vel[2]
    energy = pressure * (1.0 / (gamma_ratio - 1.0)) + 0.5 * kinetic
    flux = [m * along for m in mom]
    flux[normal] = flux[normal] + pressure
    scaled = gamma_ratio * pressure
    speed = jnp.abs(along) + scaled * lax.rsqrt(scaled * density)
    return [density] + mom + [energy], [mom[normal]] + flux + [(energy + pressure) * along], speed


def twice_flux(left, right, normal):
    left_cons, left_flux, left_speed = side_terms(left, normal)
    right_cons, right_flux, right_speed = side_terms(right, normal)
    speed = jnp.maximum(left_speed, right_speed)
    return [
        (fl + fr) - speed * (ur - ul)
        for fl, fr, ul, ur in zip(left_flux, right_flux, left_cons, right_cons)
    ]


def lane_of():
    return lax.broadcasted_iota(jnp.int32, (SUB, LANES), 1)


def sub_of():
    return lax.broadcasted_iota(jnp.int32, (SUB, LANES), 0)


def lane_roll(value, amount):
    if isinstance(amount, int):
        amount = amount % LANES
        if amount == 0:
            return value
    return pltpu.roll(value, amount, 1)


def pack_y(field, low, high, edge):
    halves = edge * edge // LANES
    width = 2 * edge
    fit = LANES // width
    lane = lane_of()
    for q in range(edge // fit):
        for f in range(NF):
            lo = None
            for k in range(fit):
                x = q * fit + k
                below = lane_roll(field[f, x * halves], width * k)
                above = lane_roll(field[f, x * halves + halves - 1], width * (k + 1))
                if lo is None:
                    lo, hi = below, above
                else:
                    mine = lane >= width * k
                    lo = jnp.where(mine, below, lo)
                    hi = jnp.where(mine, above, hi)
            low[f, q] = lo
            high[f, q] = hi


def assemble_kernel(tags, *refs, pieces, per_piece, slots, moves, occ, edge):
    count = 4 * pieces
    given, (field, prim, x_lo, x_hi, y_lo, y_hi, z_lo, z_hi) = refs[:count], refs[count : count + 8]
    held = refs[count + 8]
    rows = NF * per_piece
    for piece in range(pieces):
        sources = given[piece * 4 : piece * 4 + 4]

        def body(b, carry, sources=sources):
            def put(ref, index):
                held[pl.ds(pl.multiple_of(b * rows, SUB), rows), :] = ref[index]

            pick(tags[2 * moves + b], sources, slots, moves, put)
            return carry

        lax.fori_loop(0, occ, body, 0)
        for i in range(per_piece):
            row = piece * per_piece + i
            cons = [held[pl.ds(i * NF + f, occ, stride=rows), :] for f in range(NF)]
            for f, (c, w) in enumerate(zip(cons, primitives(cons))):
                field[f, row] = c
                prim[f, row] = w
    send_faces(prim, x_lo, x_hi, y_lo, y_hi, z_lo, z_hi, edge)


def send_faces(prim, x_lo, x_hi, y_lo, y_hi, z_lo, z_hi, edge):
    rows = prim.shape[1]
    wide = x_lo.shape[1]
    for f in range(NF):
        for i in range(wide):
            x_lo[f, i] = prim[f, i]
            x_hi[f, i] = prim[f, rows - wide + i]
        for r in range(rows):
            z_lo[f, r : r + 1, :] = prim[f, r, 0:1, :]
            z_hi[f, r : r + 1, :] = prim[f, r, SUB - 1 : SUB, :]
    pack_y(prim, y_lo, y_hi, edge)


def section(prim, x_prev, x_next, y_lo, y_hi, y_prev, y_next, z_lo, z_hi, z_prev, z_next,
            wide, x_flux, x_left, y_below, y_flux, y_right, z_below, z_flux, z_right, edge, finish):
    rows = prim.shape[1]
    halves = rows // edge
    pad = 2 * halves
    width = 2 * edge
    fit = LANES // width
    fields = range(NF)
    for f in fields:
        for i in range(pad):
            wide[f, i] = x_prev[f, i]
            wide[f, pad + rows + i] = x_next[f, i]

        def copy(r, carry, f=f):
            wide[f, pad + r] = prim[f, r]
            return carry

        lax.fori_loop(0, rows, copy, 0, unroll=8)

    def ghost_y(q, carry):
        low = [y_lo[f, q] for f in fields]
        high = [y_hi[f, q] for f in fields]
        prev = [y_prev[f, q] for f in fields]
        after = [y_next[f, q] for f in fields]
        below = [lane_roll(v, -edge) for v in prev]
        second = [lane_roll(v, -edge) for v in low]
        left = plus(below, half_slopes(prev, below, low))
        right = minus(low, half_slopes(below, low, second))
        flux = twice_flux(left, right, 1)
        last = [lane_roll(v, -edge) for v in high]
        beyond = [lane_roll(v, -edge) for v in after]
        ghost = minus(after, half_slopes(last, after, beyond))
        for f in fields:
            y_below[f, q] = below[f]
            y_flux[f, q] = flux[f]
            y_right[f, q] = ghost[f]
        return carry

    lax.fori_loop(0, edge // fit, ghost_y, 0)

    def ghost_z(a, carry):
        at = pl.ds(pl.multiple_of(a * SUB, SUB), SUB)
        low = [z_lo[f, at, :] for f in fields]
        high = [z_hi[f, at, :] for f in fields]
        prev = [z_prev[f, at, :] for f in fields]
        after = [z_next[f, at, :] for f in fields]
        below = [lane_roll(v, -(edge - 1)) for v in prev]
        before = [lane_roll(v, -(edge - 2)) for v in prev]
        second = [lane_roll(v, -1) for v in low]
        left = plus(below, half_slopes(before, below, low))
        right = minus(low, half_slopes(below, low, second))
        flux = twice_flux(left, right, 2)
        last = [lane_roll(v, -(edge - 1)) for v in high]
        beyond = [lane_roll(v, -1) for v in after]
        ghost = minus(after, half_slopes(last, after, beyond))
        for f in fields:
            z_below[f, at, :] = below[f]
            z_flux[f, at, :] = flux[f]
            z_right[f, at, :] = ghost[f]
        return carry

    lax.fori_loop(0, rows // SUB, ghost_z, 0)

    for h in range(halves):
        cells = [[wide[f, i * halves + h] for f in fields] for i in range(4)]
        left = plus(cells[1], half_slopes(*cells[0:3]))
        shift = half_slopes(*cells[1:4])
        flux = twice_flux(left, minus(cells[2], shift), 0)
        keep = plus(cells[2], shift)
        for f in fields:
            x_flux[f, h] = flux[f]
            x_left[f, h] = keep[f]

    lane = lane_of()
    sub = sub_of()
    z_of = lax.rem(lane, edge)
    top_lanes = lane >= LANES - edge
    low_lanes = lane < edge
    first_z = z_of == 0
    last_z = z_of == edge - 1
    last_sub = sub == SUB - 1
    first_sub = sub == 0

    def y_up(values, insert):
        rolled = [lane_roll(v, -edge) for v in values]
        follow = rolled[1:] + [insert]
        return [jnp.where(top_lanes, n, r) for r, n in zip(rolled, follow)]

    def y_down(values, insert):
        rolled = [lane_roll(v, edge) for v in values]
        lead = [insert] + rolled[:-1]
        return [jnp.where(low_lanes, n, r) for r, n in zip(rolled, lead)]

    def z_up(value, insert):
        across = pltpu.roll(lane_roll(value, edge - 1), SUB - 1, 0)
        across = jnp.where(last_sub, insert, across)
        return jnp.where(last_z, across, lane_roll(value, -1))

    def z_down(value, insert):
        across = pltpu.roll(lane_roll(value, -(edge - 1)), 1, 0)
        across = jnp.where(first_sub, insert, across)
        return jnp.where(first_z, across, lane_roll(value, 1))

    def body(x, carry):
        q = x // fit
        k = x - q * fit
        to_low = lax.rem(LANES - width * k, LANES)
        to_top = lax.rem(2 * LANES - edge - width * k, LANES)
        here = [[wide[f, pad + x * halves + h] for f in fields] for h in range(halves)]
        total = []
        for h in range(halves):
            one = [wide[f, pad + (x + 1) * halves + h] for f in fields]
            two = [wide[f, pad + (x + 2) * halves + h] for f in fields]
            shift = half_slopes(here[h], one, two)
            flux = twice_flux([x_left[f, h] for f in fields], minus(one, shift), 0)
            keep = plus(one, shift)
            total.append([flux[f] - x_flux[f, h] for f in fields])
            for f in fields:
                x_flux[f, h] = flux[f]
                x_left[f, h] = keep[f]

        left = [[None] * NF for _ in range(halves)]
        right = [[None] * NF for _ in range(halves)]
        for f in fields:
            mine = [here[h][f] for h in range(halves)]
            up = y_up(mine, lane_roll(y_next[f, q], to_top))
            down = y_down(mine, lane_roll(y_below[f, q], to_low))
            shift = [half_minmod(m - d, u - m) for m, d, u in zip(mine, down, up)]
            above = y_up(
                [m - s for m, s in zip(mine, shift)], lane_roll(y_right[f, q], to_top)
            )
            for h in range(halves):
                left[h][f] = mine[h] + shift[h]
                right[h][f] = above[h]
        fluxes = [twice_flux(left[h], right[h], 1) for h in range(halves)]
        for f in fields:
            mine = [fluxes[h][f] for h in range(halves)]
            down = y_down(mine, lane_roll(y_flux[f, q], to_low))
            for h in range(halves):
                total[h][f] = total[h][f] + (mine[h] - down[h])

        for h in range(halves):
            row = pl.ds(x * halves + h, 1)

            def insert(ref, f, row=row):
                return jnp.broadcast_to(ref[f, row, :], (SUB, LANES))

            def insert_up(ref, f, insert=insert):
                return lane_roll(insert(ref, f), edge - 1)

            left_z, right_z = [], []
            for f in fields:
                mine = here[h][f]
                up = z_up(mine, insert_up(z_next, f))
                down = z_down(mine, insert(z_below, f))
                shift = half_minmod(mine - down, up - mine)
                left_z.append(mine + shift)
                right_z.append(z_up(mine - shift, insert_up(z_right, f)))
            flux = twice_flux(left_z, right_z, 2)
            for f in fields:
                down = z_down(flux[f], insert(z_flux, f))
                total[h][f] = total[h][f] + (flux[f] - down)
            finish(x, h, total[h])
        return carry

    lax.fori_loop(0, edge, body, 0)


def section_scratch(rows, edge):
    halves = rows // edge
    fit = LANES // (2 * edge)
    packed = (NF, edge // fit, SUB, LANES)
    return [
        VMEM((NF, rows + 4 * halves, SUB, LANES), jnp.float32),
        VMEM((NF, halves, SUB, LANES), jnp.float32),
        VMEM((NF, halves, SUB, LANES), jnp.float32),
    ] + [VMEM(packed, jnp.float32)] * 3 + [VMEM((NF, rows, LANES), jnp.float32)] * 3


def first_section_kernel(field, prim, *refs, edge):
    faces = refs[:10]
    one, one_prim, x_lo, x_hi, y_lo, y_hi, z_lo, z_hi = refs[10:18]
    scratch = refs[18:]
    halves = prim.shape[1] // edge

    def finish(x, h, total):
        row = x * halves + h
        cons = [field[f, row] - (0.5 * time_step) * total[f] for f in range(NF)]
        for f, (c, w) in enumerate(zip(cons, primitives(cons))):
            one[f, row] = c
            one_prim[f, row] = w

    section(prim, *faces, *scratch, edge, finish)
    send_faces(one_prim, x_lo, x_hi, y_lo, y_hi, z_lo, z_hi, edge)


def second_section_kernel(own, field, one, prim, *refs, edge):
    faces = refs[:10]
    _, out = refs[10:12]
    scratch = refs[12:21]
    result, blocks, sems = refs[21:]
    rows = prim.shape[1]
    halves = rows // edge

    def finish(x, h, total):
        row = x * halves + h
        for f in range(NF):
            advanced = one[f, row] - (0.5 * time_step) * total[f]
            final = 0.5 * field[f, row] + 0.5 * advanced
            result[pl.ds(pl.multiple_of((f * rows + row) * SUB, SUB), SUB), :] = final

    section(prim, *faces, *scratch, edge, finish)

    def copy(b):
        return pltpu.make_async_copy(blocks.at[b], out.at[own[b]], sems.at[b])

    for b in range(SUB):
        for r in range(rows):
            blocks[b, :, r * LANES : (r + 1) * LANES] = result[
                pl.ds(r * SUB + b, NF, stride=rows * SUB), :
            ]
        copy(b).start()
    for b in range(SUB):
        copy(b).wait()


def shards(state, send_slots, recv_slots, owner_slot):
    slots, _, cells = state.shape
    moves = send_slots.shape[2]
    size_x, size_y, size_z = (lax.axis_size(axis) for axis in AXES)
    occ = owner_slot.shape[0] // (size_x * size_y * size_z)
    edge = round(cells ** (1 / 3))
    rows = cells // LANES
    halves = rows // edge
    per_piece = rows // PIECES
    piece_rows = NF * per_piece
    f32 = jnp.float32

    bit_z = size_z.bit_length() - 2
    bit_y = bit_z + size_y.bit_length() - 1
    bit_x = bit_y + size_x.bit_length() - 1
    pair_bits = (bit_x, bit_y, bit_z)

    def swapped(value, level):
        mask = 2 ** pair_bits[level]
        pairs = [(source, source ^ mask) for source in range(lax.axis_size(AXES))]
        return lax.ppermute(value, AXES, pairs)

    device = lax.axis_index(AXES)
    own = lax.dynamic_slice(owner_slot, (device * occ,), (occ,))
    message = jax.ShapeDtypeStruct((moves, piece_rows, LANES), f32)

    sent = pl.pallas_call(
        functools.partial(
            first_kernel, pieces=PIECES, per_piece=per_piece, moves=moves, slots=slots
        ),
        out_shape=[message] * PIECES,
        in_specs=[whole(SMEM), whole(pl.ANY)],
        out_specs=[whole(VMEM)] * PIECES,
        scratch_shapes=[VMEM((moves, NF, cells), f32), pltpu.SemaphoreType.DMA((moves,))],
        compiler_params=params(),
        name="pack_first",
    )(send_slots, state)
    sent = list(sent)

    group = SUB
    kept = pl.pallas_call(
        functools.partial(
            rows_kernel, pieces=PIECES, per_piece=per_piece, moves=moves, slots=slots,
            occ=occ, group=group,
        ),
        grid=(slots // group,),
        out_shape=[jax.ShapeDtypeStruct((slots, piece_rows, LANES), f32)] * PIECES
        + [jax.ShapeDtypeStruct((2 * moves + occ,), jnp.int32)],
        in_specs=[whole(SMEM)] * 3 + [pl.BlockSpec((group, NF, cells), lambda i: (i, 0, 0))],
        out_specs=[pl.BlockSpec((group, piece_rows, LANES), lambda i: (i, 0, 0))] * PIECES
        + [whole(SMEM)],
        compiler_params=params(),
        cost_estimate=cost(0, 8 * 1024 * 1024),
        name="state_rows",
    )(send_slots, recv_slots, own, state)
    kept, tags = kept[:PIECES], kept[PIECES]

    def select(level, sources, through):
        passed = len(through)
        out = pl.pallas_call(
            functools.partial(
                select_kernel, sources=len(sources), level=level, slots=slots, moves=moves,
                passed=passed,
            ),
            out_shape=[message] * (1 + passed),
            in_specs=[whole(SMEM)] + [whole(VMEM)] * len(sources) + [whole(pl.ANY)] * passed,
            out_specs=[whole(VMEM)] + [whole(pl.ANY)] * passed,
            input_output_aliases={1 + len(sources) + i: 1 + i for i in range(passed)},
            compiler_params=params(),
            name="pick_level_%d" % level,
        )(tags, *sources, *through)
        return out[0], list(out[1:])

    got = [[None] * PIECES for _ in range(3)]
    got[0][0] = swapped(sent[0], 0)
    for p in range(PIECES):
        through = sent[p + 1 : p + 2]
        second, through = select(1, [kept[p], got[0][p]], through)
        if through:
            got[0][p + 1] = swapped(through[0], 0)
        got[1][p] = swapped(second, 1)
    for p in range(PIECES):
        third, _ = select(2, [kept[p], got[0][p], got[1][p]], [])
        got[2][p] = swapped(third, 2)

    grid = jax.ShapeDtypeStruct((NF, rows, SUB, LANES), f32)
    face_x = jax.ShapeDtypeStruct((NF, 2 * halves, SUB, LANES), f32)
    face_y = jax.ShapeDtypeStruct((NF, edge * 2 * edge // LANES, SUB, LANES), f32)
    face_z = jax.ShapeDtypeStruct((NF, rows, LANES), f32)
    produced = [grid, grid, face_x, face_x, face_y, face_y, face_z, face_z]

    sources = [a for p in range(PIECES) for a in (kept[p], got[0][p], got[1][p], got[2][p])]
    made = pl.pallas_call(
        functools.partial(
            assemble_kernel, pieces=PIECES, per_piece=per_piece, slots=slots, moves=moves,
            occ=occ, edge=edge,
        ),
        out_shape=produced,
        in_specs=[whole(SMEM)] + [whole(VMEM)] * len(sources),
        out_specs=[whole(VMEM)] * len(produced),
        scratch_shapes=[VMEM((occ * piece_rows, LANES), f32)],
        compiler_params=params(),
        name="assemble",
    )(tags, *sources)

    def ring(value, axis, step):
        size = lax.axis_size(axis)
        return lax.ppermute(value, axis, [(i, (i + step) % size) for i in range(size)])

    def exchanged(x_lo, x_hi, y_lo, y_hi, z_lo, z_hi):
        if size_x == 2:
            x_prev, x_next = ring(jnp.stack([x_hi, x_lo]), "gx", 1)
        else:
            x_prev, x_next = ring(x_hi, "gx", 1), ring(x_lo, "gx", -1)
        y_prev, y_next = ring(y_hi, "gy", 1), ring(y_lo, "gy", -1)
        z_prev, z_next = ring(z_hi, "gz", 1), ring(z_lo, "gz", -1)
        return (x_prev, x_next, y_lo, y_hi, y_prev, y_next, z_lo, z_hi, z_prev, z_next)

    field, prim = made[0], made[1]
    faces = exchanged(*made[2:])
    scratch = section_scratch(rows, edge)
    made = pl.pallas_call(
        functools.partial(first_section_kernel, edge=edge),
        out_shape=produced,
        in_specs=[whole(VMEM)] * 12,
        out_specs=[whole(VMEM)] * len(produced),
        scratch_shapes=scratch,
        compiler_params=params(),
        name="section_one",
    )(field, prim, *faces)
    one, one_prim = made[0], made[1]
    faces = exchanged(*made[2:])
    return pl.pallas_call(
        functools.partial(second_section_kernel, edge=edge),
        out_shape=jax.ShapeDtypeStruct(state.shape, f32),
        in_specs=[whole(SMEM)] + [whole(VMEM)] * 13 + [whole(pl.ANY)],
        out_specs=whole(pl.ANY),
        scratch_shapes=scratch
        + [
            VMEM((NF * rows * SUB, LANES), f32),
            VMEM((SUB, NF, cells), f32),
            pltpu.SemaphoreType.DMA((SUB,)),
        ],
        input_output_aliases={14: 0},
        compiler_params=params(),
        name="section_two",
    )(own, field, one, one_prim, *faces, jnp.zeros_like(state))


def solution(mesh):
    placed = (
        P(AXES, None, None),
        P(None, AXES, None),
        P(None, AXES, None),
        P(),
    )
    return jax.shard_map(
        shards,
        mesh=mesh,
        in_specs=placed,
        out_specs=P(AXES, None, None),
        check_vma=False,
    )
```

```python
import functools

import jax
import jax.numpy as jnp
from jax import lax
from jax.experimental import pallas as pl
from jax.experimental.pallas import tpu as pltpu
from jax.sharding import PartitionSpec as P

gamma_ratio = 1.4
time_step = 0.05
LANES = 128
SUB = 8
NF = 5
FIELDS = range(NF)
AXES = ("gx", "gy", "gz")

VMEM = pltpu.VMEM
SMEM = pltpu.SMEM
HBM = pltpu.HBM
f32 = jnp.float32


def whole(space):
    return pl.BlockSpec(memory_space=space)


def params():
    return pltpu.CompilerParams(vmem_limit_bytes=16 * 1024 * 1024)


def cost(flops, moved):
    return pl.CostEstimate(flops=flops, bytes_accessed=moved, transcendentals=0)


def split_units(units):
    first, last = units // 10, 3 * units // 20
    middle = units - first - last
    sizes = [first] + [middle // 3 + (i < middle % 3) for i in range(3)] + [last]
    starts = [sum(sizes[:i]) for i in range(len(sizes) + 1)]
    return list(zip(starts[:-1], starts[1:]))


def from_state(state, tag, unit, slots, rows):
    slab, field = unit // NF, unit % NF
    groups = slots // SUB
    base = (tag // SUB) * (rows * SUB) + lax.rem(tag, SUB)
    start = base + (field * groups * rows + slab * SUB) * SUB
    return state[pl.ds(start, SUB, stride=SUB), :]


def pick(tag, unit, local, state, arrived, slots, rows, moves):
    value = from_state(state, jnp.minimum(tag, slots - 1), unit, slots, rows)
    for level, ref in enumerate(arrived):
        base = slots + level * moves
        index = jnp.clip(tag - base, 0, moves - 1)
        value = jnp.where(tag >= base, ref[index, local * SUB : (local + 1) * SUB, :], value)
    return value


def first_kernel(send, state, *outs, pieces, slots, rows, moves):
    for k in range(moves):
        slot = jnp.minimum(send[0, 0, k], slots - 1)
        for (begin, end), out in zip(pieces, outs):
            for unit in range(begin, end):
                at = (unit - begin) * SUB
                out[k, at : at + SUB, :] = from_state(state, slot, unit, slots, rows)


def tags_kernel(send, recv, own, tags, *, slots, moves, occ):
    def find(slot, levels):
        tag = slot
        for level in range(levels):
            for j in range(moves):
                tag = jnp.where(recv[level, 0, j] == slot, slots + level * moves + j, tag)
        return tag

    def one(k, carry):
        for level in (1, 2):
            slot = jnp.minimum(send[level, 0, k], slots - 1)
            tags[(level - 1) * moves + k] = find(slot, level)
        return carry

    lax.fori_loop(0, moves, one, 0)

    def last(b, carry):
        tags[2 * moves + b] = find(own[b], 3)
        return carry

    lax.fori_loop(0, occ, last, 0)


def pick_kernel(tags, state, *refs, plan, given, passed, slots, rows, moves):
    arrived = refs[:given]
    outs = refs[given + passed :]
    for (level, begin, end, which), out in zip(plan, outs):
        sources = [arrived[i] for i in which]
        for k in range(moves):
            tag = tags[(level - 1) * moves + k]
            for unit in range(begin, end):
                local = unit - begin
                out[k, local * SUB : (local + 1) * SUB, :] = pick(
                    tag, unit, local, state, sources, slots, rows, moves
                )


def primitives(cons):
    density = cons[0]
    inverse = 1.0 / density
    vel = [cons[1] * inverse, cons[2] * inverse, cons[3] * inverse]
    kinetic = cons[1] * vel[0] + cons[2] * vel[1] + cons[3] * vel[2]
    pressure = (gamma_ratio - 1.0) * (cons[4] - 0.5 * kinetic)
    return [density, vel[0], vel[1], vel[2], pressure]


def half_minmod(lower, upper):
    both = jnp.maximum(0.0, jnp.minimum(lower, upper)) + jnp.minimum(
        0.0, jnp.maximum(lower, upper)
    )
    return 0.5 * both


def half_slopes(before, here, after):
    return [half_minmod(h - b, a - h) for b, h, a in zip(before, here, after)]


def plus(a, b):
    return [x + y for x, y in zip(a, b)]


def minus(a, b):
    return [x - y for x, y in zip(a, b)]


def side_terms(prim, normal):
    density, vel, pressure = prim[0], prim[1:4], prim[4]
    along = vel[normal]
    mom = [density * v for v in vel]
    kinetic = mom[0] * vel[0] + mom[1] * vel[1] + mom[2] * vel[2]
    energy = pressure * (1.0 / (gamma_ratio - 1.0)) + 0.5 * kinetic
    flux = [m * along for m in mom]
    flux[normal] = flux[normal] + pressure
    scaled = gamma_ratio * pressure
    speed = jnp.abs(along) + scaled * lax.rsqrt(scaled * density)
    return [density] + mom + [energy], [mom[normal]] + flux + [(energy + pressure) * along], speed


def twice_flux(left, right, normal):
    left_cons, left_flux, left_speed = side_terms(left, normal)
    right_cons, right_flux, right_speed = side_terms(right, normal)
    speed = jnp.maximum(left_speed, right_speed)
    return [
        (fl + fr) - speed * (ur - ul)
        for fl, fr, ul, ur in zip(left_flux, right_flux, left_cons, right_cons)
    ]


def lane_of():
    return lax.broadcasted_iota(jnp.int32, (SUB, LANES), 1)


def sub_of():
    return lax.broadcasted_iota(jnp.int32, (SUB, LANES), 0)


def lane_roll(value, amount):
    amount = amount % LANES
    return value if amount == 0 else pltpu.roll(value, amount, 1)


class Shape:
    def __init__(self, rows, edge):
        self.rows, self.edge = rows, edge
        self.halves = rows // edge
        self.width = 2 * edge
        self.fit = LANES // self.width
        self.slabs = rows // SUB
        self.pad = 2 * self.halves

    def at(self, f, row):
        start = (f * self.rows + row) * SUB
        return pl.ds(start if isinstance(start, int) else pl.multiple_of(start, SUB), SUB)

    def across(self, f, slab, sub):
        return pl.ds((f * self.rows + slab * SUB) * SUB + sub, SUB, stride=SUB)

    def grid(self):
        return jax.ShapeDtypeStruct((NF * self.rows * SUB, LANES), f32)

    def faces(self):
        x = jax.ShapeDtypeStruct((NF, self.pad, SUB, LANES), f32)
        y = jax.ShapeDtypeStruct((NF, self.edge // self.fit, SUB, LANES), f32)
        z = jax.ShapeDtypeStruct((NF, self.rows, LANES), f32)
        return [x, x, y, y, z, z]


def send_slab(shape, prim, y_lo, y_hi, z_lo, z_hi, slab):
    lane = lane_of()
    halves = shape.halves
    for f in FIELDS:
        lo = hi = None
        for k in range(shape.fit):
            row = slab * SUB + k * halves
            below = lane_roll(prim[shape.at(f, row), :], shape.width * k)
            above = lane_roll(prim[shape.at(f, row + halves - 1), :], shape.width * (k + 1))
            if lo is None:
                lo, hi = below, above
            else:
                mine = lane >= shape.width * k
                lo = jnp.where(mine, below, lo)
                hi = jnp.where(mine, above, hi)
        y_lo[f, slab] = lo
        y_hi[f, slab] = hi
        to = pl.ds(slab * SUB, SUB) if isinstance(slab, int) else pl.ds(
            pl.multiple_of(slab * SUB, SUB), SUB
        )
        z_lo[f, to, :] = prim[shape.across(f, slab, 0), :]
        z_hi[f, to, :] = prim[shape.across(f, slab, SUB - 1), :]


def send_x(shape, prim, x_lo, x_hi):
    for f in FIELDS:
        for i in range(shape.pad):
            x_lo[f, i] = prim[shape.at(f, i), :]
            x_hi[f, i] = prim[shape.at(f, shape.rows - shape.pad + i), :]


def assemble_kernel(tags, state, *refs, pieces, slots, moves, occ, shape):
    count = 3 * len(pieces)
    given = refs[:count]
    field, prim, x_lo, x_hi, y_lo, y_hi, z_lo, z_hi, held = refs[count:]
    rows = shape.rows
    units = NF * shape.slabs
    for b in range(occ):
        tag = tags[2 * moves + b]
        for number, (begin, end) in enumerate(pieces):
            sources = given[3 * number : 3 * number + 3]
            for unit in range(begin, end):
                at = (b * units + unit) * SUB
                held[at : at + SUB, :] = pick(
                    tag, unit, unit - begin, state, sources, slots, rows, moves
                )
    for slab in range(shape.slabs):
        for i in range(SUB):
            row = slab * SUB + i
            cons = [
                held[pl.ds((slab * NF + f) * SUB + i, occ, stride=units * SUB), :] for f in FIELDS
            ]
            for f, (c, w) in enumerate(zip(cons, primitives(cons))):
                field[shape.at(f, row), :] = c
                prim[shape.at(f, row), :] = w
        send_slab(shape, prim, y_lo, y_hi, z_lo, z_hi, slab)
    send_x(shape, prim, x_lo, x_hi)


def sweep_z_kernel(prim, z_lo, z_hi, z_prev, z_next, total, below_z, flux_z, over_z, right_z, *, shape):
    edge, rows = shape.edge, shape.rows

    def ghost(a, carry):
        at = pl.ds(pl.multiple_of(a * SUB, SUB), SUB)
        low = [z_lo[f, at, :] for f in FIELDS]
        high = [z_hi[f, at, :] for f in FIELDS]
        prev = [z_prev[f, at, :] for f in FIELDS]
        after = [z_next[f, at, :] for f in FIELDS]
        below = [lane_roll(v, -(edge - 1)) for v in prev]
        before = [lane_roll(v, -(edge - 2)) for v in prev]
        second = [lane_roll(v, -1) for v in low]
        left = plus(below, half_slopes(before, below, low))
        right = minus(low, half_slopes(below, low, second))
        flux = twice_flux(left, right, 2)
        last = [lane_roll(v, -(edge - 1)) for v in high]
        beyond = [lane_roll(v, -1) for v in after]
        over = minus(after, half_slopes(last, after, beyond))
        for f in FIELDS:
            below_z[f, at, :] = below[f]
            flux_z[f, at, :] = flux[f]
            over_z[f, at, :] = lane_roll(after[f], edge - 1)
            right_z[f, at, :] = lane_roll(over[f], edge - 1)
        return carry

    lax.fori_loop(0, shape.slabs, ghost, 0)
    z_of = lax.rem(lane_of(), edge)
    sub = sub_of()
    first_z, last_z = z_of == 0, z_of == edge - 1
    first_sub, last_sub = sub == 0, sub == SUB - 1

    def up(value, insert):
        across = pltpu.roll(lane_roll(value, edge - 1), SUB - 1, 0)
        across = jnp.where(last_sub, insert, across)
        return jnp.where(last_z, across, lane_roll(value, -1))

    def down(value, insert):
        across = pltpu.roll(lane_roll(value, -(edge - 1)), 1, 0)
        across = jnp.where(first_sub, insert, across)
        return jnp.where(first_z, across, lane_roll(value, 1))

    def body(row, carry):
        def insert(ref, f):
            return jnp.broadcast_to(ref[f, pl.ds(row, 1), :], (SUB, LANES))

        left, right = [], []
        for f in FIELDS:
            mine = prim[shape.at(f, row), :]
            shift = half_minmod(
                mine - down(mine, insert(below_z, f)), up(mine, insert(over_z, f)) - mine
            )
            left.append(mine + shift)
            right.append(up(mine - shift, insert(right_z, f)))
        flux = twice_flux(left, right, 2)
        for f in FIELDS:
            total[shape.at(f, row), :] = flux[f] - down(flux[f], insert(flux_z, f))
        return carry

    lax.fori_loop(0, rows, body, 0, unroll=2)


def sweep_x_kernel(prim, x_prev, x_next, sofar, total, wide, *, shape):
    rows, halves, pad = shape.rows, shape.halves, shape.pad
    for f in FIELDS:
        for i in range(pad):
            wide[f, i] = x_prev[f, i]
            wide[f, pad + rows + i] = x_next[f, i]

        def copy(r, carry, f=f):
            wide[f, pad + r] = prim[shape.at(f, r), :]
            return carry

        lax.fori_loop(0, rows, copy, 0, unroll=8)

    for h in range(halves):
        cells = [[wide[f, i * halves + h] for f in FIELDS] for i in range(4)]
        left = plus(cells[1], half_slopes(*cells[0:3]))
        shift = half_slopes(*cells[1:4])
        flux = twice_flux(left, minus(cells[2], shift), 0)
        keep = plus(cells[2], shift)

        def body(x, carry, h=h):
            below, left = carry
            here, one, two = (
                [wide[f, pad + (x + i) * halves + h] for f in FIELDS] for i in range(3)
            )
            shift = half_slopes(here, one, two)
            flux = twice_flux(left, minus(one, shift), 0)
            row = x * halves + h
            for f in FIELDS:
                at = shape.at(f, row)
                total[at, :] = sofar[at, :] + (flux[f] - below[f])
            return flux, plus(one, shift)

        lax.fori_loop(0, shape.edge, body, (flux, keep), unroll=4)


def sweep_y(prim, y_lo, y_hi, y_prev, y_next, sofar, ghost_prim, ghost_flux, shape, finish, after_slab):
    edge, halves, fit, width = shape.edge, shape.halves, shape.fit, shape.width
    lane = lane_of()
    upper = lax.rem(lane, width) >= edge

    def ghost(q, carry):
        low = [y_lo[f, q] for f in FIELDS]
        high = [y_hi[f, q] for f in FIELDS]
        below = [y_prev[f, q] for f in FIELDS]
        after = [y_next[f, q] for f in FIELDS]
        before = [lane_roll(v, edge) for v in below]
        first = [lane_roll(v, edge) for v in low]
        left = plus(below, half_slopes(before, below, first))
        right = minus(first, half_slopes(below, first, low))
        flux = twice_flux(left, right, 1)
        last = [lane_roll(v, -edge) for v in high]
        beyond = [lane_roll(v, -edge) for v in after]
        over = minus(after, half_slopes(last, after, beyond))
        for f in FIELDS:
            ghost_prim[f, q] = jnp.where(upper, below[f], after[f])
            ghost_flux[f, q] = jnp.where(upper, flux[f], over[f])
        return carry

    lax.fori_loop(0, edge // fit, ghost, 0)
    top_lanes = lane >= LANES - edge
    low_lanes = lane < edge

    def up(values, insert):
        rolled = [lane_roll(v, -edge) for v in values]
        follow = rolled[1:] + [insert]
        return [jnp.where(top_lanes, n, r) for r, n in zip(rolled, follow)]

    def down(values, insert):
        rolled = [lane_roll(v, edge) for v in values]
        lead = [insert] + rolled[:-1]
        return [jnp.where(low_lanes, n, r) for r, n in zip(rolled, lead)]

    def body(q, carry):
        for k in range(fit):
            turn = -(width * k + edge)
            base = (q * fit + k) * halves
            left = [[None] * NF for _ in range(halves)]
            right = [[None] * NF for _ in range(halves)]
            for f in FIELDS:
                mine = [prim[shape.at(f, base + h), :] for h in range(halves)]
                ghost = lane_roll(ghost_prim[f, q], turn)
                over, under = up(mine, ghost), down(mine, ghost)
                shift = [half_minmod(m - d, u - m) for m, d, u in zip(mine, under, over)]
                above = up(minus(mine, shift), lane_roll(ghost_flux[f, q], turn))
                for h in range(halves):
                    left[h][f] = mine[h] + shift[h]
                    right[h][f] = above[h]
            fluxes = [twice_flux(left[h], right[h], 1) for h in range(halves)]
            total = [[None] * NF for _ in range(halves)]
            for f in FIELDS:
                mine = [fluxes[h][f] for h in range(halves)]
                under = down(mine, lane_roll(ghost_flux[f, q], turn))
                for h in range(halves):
                    total[h][f] = sofar[shape.at(f, base + h), :] + (mine[h] - under[h])
            for h in range(halves):
                finish(base + h, total[h])
        after_slab(q)
        return carry

    lax.fori_loop(0, edge // fit, body, 0)


def sweep_y_one_kernel(field, prim, y_lo, y_hi, y_prev, y_next, sofar, *refs, shape):
    one, one_prim, x_lo, x_hi, out_y_lo, out_y_hi, z_lo, z_hi = refs[:8]

    def finish(row, total):
        cons = [field[shape.at(f, row), :] - (0.5 * time_step) * total[f] for f in FIELDS]
        for f, (c, w) in enumerate(zip(cons, primitives(cons))):
            one[shape.at(f, row), :] = c
            one_prim[shape.at(f, row), :] = w

    def after_slab(q):
        send_slab(shape, one_prim, out_y_lo, out_y_hi, z_lo, z_hi, q)

    sweep_y(prim, y_lo, y_hi, y_prev, y_next, sofar, *refs[8:], shape, finish, after_slab)
    send_x(shape, one_prim, x_lo, x_hi)


def sweep_y_two_kernel(own, field, one, prim, y_lo, y_hi, y_prev, y_next, sofar, out,
                       ghost_prim, ghost_flux, result, canvas, sems, *, shape, occ, groups):
    rows = shape.rows
    span = SUB * SUB

    def clear(i, carry):
        canvas[pl.ds(pl.multiple_of(i * SUB, SUB), SUB), :] = jnp.zeros((SUB, LANES), f32)
        return carry

    lax.fori_loop(0, NF * groups * rows, clear, 0, unroll=16)

    def finish(row, total):
        for f in FIELDS:
            at = shape.at(f, row)
            advanced = one[at, :] - (0.5 * time_step) * total[f]
            result[at, :] = 0.5 * field[at, :] + 0.5 * advanced

    def copy(part):
        begin = part * span if isinstance(part, int) else pl.multiple_of(part * span, span)
        return [
            pltpu.make_async_copy(
                canvas.at[pl.ds(i * rows * SUB + begin, span), :],
                out.at[pl.ds(i * rows * SUB + begin, span), :],
                sems.at[part, i],
            )
            for i in range(NF * groups)
        ]

    def after_slab(q):
        for b in range(occ):
            slot = own[b]
            base = (slot // SUB) * (rows * SUB) + lax.rem(slot, SUB) + q * span
            for f in FIELDS:
                canvas[pl.ds(base + f * groups * rows * SUB, SUB, stride=SUB), :] = result[
                    shape.across(f, q, b), :
                ]
        for c in copy(q):
            c.start()

    sweep_y(prim, y_lo, y_hi, y_prev, y_next, sofar, ghost_prim, ghost_flux, shape, finish, after_slab)
    for part in range(shape.slabs):
        for c in copy(part):
            c.wait()


def shards(state, send_slots, recv_slots, owner_slot):
    slots, _, cells = state.shape
    moves = send_slots.shape[2]
    size_x, size_y, size_z = (lax.axis_size(axis) for axis in AXES)
    occ = owner_slot.shape[0] // (size_x * size_y * size_z)
    edge = round(cells ** (1 / 3))
    rows = cells // LANES
    groups = slots // SUB
    shape = Shape(rows, edge)
    pieces = split_units(NF * shape.slabs)
    count = len(pieces)

    bit_z = size_z.bit_length() - 2
    bit_y = bit_z + size_y.bit_length() - 1
    bit_x = bit_y + size_x.bit_length() - 1
    pair_bits = (bit_x, bit_y, bit_z)

    def swapped(value, level):
        mask = 2 ** pair_bits[level]
        pairs = [(source, source ^ mask) for source in range(lax.axis_size(AXES))]
        return lax.ppermute(value, AXES, pairs)

    rows_of_state = (
        state.reshape(groups, SUB, NF, rows, LANES)
        .transpose(2, 0, 3, 1, 4)
        .reshape(NF * groups * rows * SUB, LANES)
    )
    device = lax.axis_index(AXES)
    own = lax.dynamic_slice(owner_slot, (device * occ,), (occ,))
    sizes = dict(slots=slots, moves=moves)

    def message(p):
        begin, end = pieces[p]
        return jax.ShapeDtypeStruct((moves, (end - begin) * SUB, LANES), f32)

    sent = pl.pallas_call(
        functools.partial(first_kernel, pieces=pieces, rows=rows, **sizes),
        out_shape=[message(p) for p in range(count)],
        in_specs=[whole(SMEM), whole(VMEM)],
        out_specs=[whole(VMEM)] * count,
        compiler_params=params(),
        name="pack_first",
    )(send_slots, rows_of_state)

    tags = pl.pallas_call(
        functools.partial(tags_kernel, occ=occ, **sizes),
        out_shape=jax.ShapeDtypeStruct((2 * moves + occ,), jnp.int32),
        in_specs=[whole(SMEM)] * 3,
        out_specs=whole(SMEM),
        compiler_params=params(),
        name="block_tags",
    )(send_slots, recv_slots, own)

    got = [[None] * count for _ in range(3)]

    def make(wanted, through):
        arrays, plan, shapes = [], [], []
        for level, p in wanted:
            which = []
            for earlier in range(level):
                which.append(len(arrays))
                arrays.append(got[earlier][p])
            plan.append((level, *pieces[p], tuple(which)))
            shapes.append(message(p))
        given, passed, made = len(arrays), len(through), len(wanted)
        outs = pl.pallas_call(
            functools.partial(
                pick_kernel, plan=tuple(plan), given=given, passed=passed, rows=rows, **sizes
            ),
            out_shape=shapes + [jax.ShapeDtypeStruct(t.shape, f32) for t in through],
            in_specs=[whole(SMEM)] + [whole(VMEM)] * (1 + given) + [whole(pl.ANY)] * passed,
            out_specs=[whole(VMEM)] * made + [whole(pl.ANY)] * passed,
            input_output_aliases={2 + given + i: made + i for i in range(passed)},
            compiler_params=params(),
            name="pick_" + "_".join("%d%d" % w for w in wanted),
        )(tags, rows_of_state, *arrays, *through)
        return outs[:made], outs[made:]

    ahead = 2
    for p in range(ahead):
        got[0][p] = swapped(sent[p], 0)
    for step in range(count + ahead):
        wanted = []
        if step < count:
            wanted.append((1, step))
        if step >= ahead:
            wanted.append((2, step - ahead))
        through = sent[step + ahead : step + ahead + 1]
        made, passed = make(wanted, list(through))
        for (level, p), value in zip(wanted, made):
            got[level][p] = swapped(value, level)
        if passed:
            got[0][step + ahead] = swapped(passed[0], 0)

    grid = shape.grid()
    produced = [grid, grid] + shape.faces()
    sources = [got[level][p] for p in range(count) for level in range(3)]
    made = pl.pallas_call(
        functools.partial(assemble_kernel, pieces=pieces, occ=occ, shape=shape, **sizes),
        out_shape=produced,
        in_specs=[whole(SMEM)] + [whole(VMEM)] * (1 + len(sources)),
        out_specs=[whole(VMEM)] * len(produced),
        scratch_shapes=[VMEM((occ * NF * rows, LANES), f32)],
        compiler_params=params(),
        name="assemble",
    )(tags, rows_of_state, *sources)

    def ring(value, axis, step):
        size = lax.axis_size(axis)
        return lax.ppermute(value, axis, [(i, (i + step) % size) for i in range(size)])

    def flux_sums(prim, x_lo, x_hi, y_lo, y_hi, z_lo, z_hi):
        y_prev, y_next = ring(y_hi, "gy", 1), ring(y_lo, "gy", -1)
        z_prev, z_next = ring(z_hi, "gz", 1), ring(z_lo, "gz", -1)
        if size_x == 2:
            x_prev, x_next = ring(jnp.stack([x_hi, x_lo]), "gx", 1)
        else:
            x_prev, x_next = ring(x_hi, "gx", 1), ring(x_lo, "gx", -1)
        ghost = VMEM((NF, rows, LANES), f32)
        total = pl.pallas_call(
            functools.partial(sweep_z_kernel, shape=shape),
            out_shape=grid,
            in_specs=[whole(VMEM)] * 5,
            out_specs=whole(VMEM),
            scratch_shapes=[ghost] * 4,
            compiler_params=params(),
            name="sweep_z",
        )(prim, z_lo, z_hi, z_prev, z_next)
        total = pl.pallas_call(
            functools.partial(sweep_x_kernel, shape=shape),
            out_shape=grid,
            in_specs=[whole(VMEM)] * 4,
            out_specs=whole(VMEM),
            scratch_shapes=[VMEM((NF, rows + 2 * shape.pad, SUB, LANES), f32)],
            input_output_aliases={3: 0},
            compiler_params=params(),
            name="sweep_x",
        )(prim, x_prev, x_next, total)
        return y_lo, y_hi, y_prev, y_next, total

    packed = VMEM(shape.faces()[2].shape, f32)
    field, prim = made[0], made[1]
    sums = flux_sums(prim, *made[2:])
    made = pl.pallas_call(
        functools.partial(sweep_y_one_kernel, shape=shape),
        out_shape=produced,
        in_specs=[whole(VMEM)] * 7,
        out_specs=[whole(VMEM)] * len(produced),
        scratch_shapes=[packed] * 2,
        compiler_params=params(),
        name="sweep_y_one",
    )(field, prim, *sums)
    one, one_prim = made[0], made[1]
    sums = flux_sums(one_prim, *made[2:])
    state_rows = NF * groups * rows * SUB
    out = pl.pallas_call(
        functools.partial(sweep_y_two_kernel, shape=shape, occ=occ, groups=groups),
        out_shape=jax.ShapeDtypeStruct((state_rows, LANES), f32),
        in_specs=[whole(SMEM)] + [whole(VMEM)] * 8,
        out_specs=whole(HBM),
        scratch_shapes=[packed] * 2
        + [
            VMEM(grid.shape, f32),
            VMEM((state_rows, LANES), f32),
            pltpu.SemaphoreType.DMA((shape.slabs, NF * groups)),
        ],
        compiler_params=params(),
        name="sweep_y_two",
    )(own, field, one, one_prim, *sums)
    return (
        out.reshape(NF, groups, rows, SUB, LANES)
        .transpose(1, 3, 0, 2, 4)
        .reshape(slots, NF, cells)
    )


def solution(mesh):
    placed = (
        P(AXES, None, None),
        P(None, AXES, None),
        P(None, AXES, None),
        P(),
    )
    return jax.shard_map(
        shards,
        mesh=mesh,
        in_specs=placed,
        out_specs=P(AXES, None, None),
        check_vma=False,
    )
```

```python
import functools

import jax
import jax.numpy as jnp
from jax import lax
from jax.experimental import pallas as pl
from jax.experimental.pallas import tpu as pltpu
from jax.sharding import PartitionSpec as P

gamma_ratio = 1.4
time_step = 0.05
LANES = 128
SUB = 8
NF = 5
FIELDS = range(NF)
AXES = ("gx", "gy", "gz")

VMEM = pltpu.VMEM
SMEM = pltpu.SMEM
HBM = pltpu.HBM
f32 = jnp.float32


def whole(space):
    return pl.BlockSpec(memory_space=space)


def params():
    return pltpu.CompilerParams(vmem_limit_bytes=16 * 1024 * 1024)


def cost(flops, moved):
    return pl.CostEstimate(flops=flops, bytes_accessed=moved, transcendentals=0)


def split_units(units):
    shares = (2, 4, 5, 6)
    sizes = [units * share // 20 for share in shares]
    sizes.append(units - sum(sizes))
    starts = [sum(sizes[:i]) for i in range(len(sizes) + 1)]
    return list(zip(starts[:-1], starts[1:]))


def from_state(state, tag, unit, slots, rows):
    slab, field = unit // NF, unit % NF
    groups = slots // SUB
    base = (tag // SUB) * (rows * SUB) + lax.rem(tag, SUB)
    start = base + (field * groups * rows + slab * SUB) * SUB
    return state[pl.ds(start, SUB, stride=SUB), :]


def pick(tag, unit, local, state, arrived, slots, rows, moves):
    value = from_state(state, jnp.minimum(tag, slots - 1), unit, slots, rows)
    for level, ref in enumerate(arrived):
        base = slots + level * moves
        index = jnp.clip(tag - base, 0, moves - 1)
        value = jnp.where(tag >= base, ref[index, local * SUB : (local + 1) * SUB, :], value)
    return value


def pack_pieces(send, state, outs, pieces, slots, rows, moves):
    for k in range(moves):
        slot = jnp.minimum(send[0, 0, k], slots - 1)
        for (begin, end), out in zip(pieces, outs):
            for unit in range(begin, end):
                at = (unit - begin) * SUB
                out[k, at : at + SUB, :] = from_state(state, slot, unit, slots, rows)


def first_kernel(send_hbm, state_hbm, out, send, held, sems, *, piece, slots, rows, moves):
    span = SUB * SUB
    groups = slots // SUB
    copies = [pltpu.make_async_copy(send_hbm, send, sems.at[0])]
    for unit in range(*piece):
        slab, field = unit // NF, unit % NF
        for g in range(groups):
            at = ((field * groups + g) * rows + slab * SUB) * SUB
            to = ((unit - piece[0]) * groups + g) * span
            copies.append(
                pltpu.make_async_copy(
                    state_hbm.at[pl.ds(at, span), :],
                    held.at[pl.ds(to, span), :],
                    sems.at[len(copies)],
                )
            )
    for c in copies:
        c.start()
    for c in copies:
        c.wait()
    for k in range(moves):
        slot = jnp.minimum(send[0, 0, k], slots - 1)
        base = (slot // SUB) * span + lax.rem(slot, SUB)
        for i in range(piece[1] - piece[0]):
            out[k, i * SUB : (i + 1) * SUB, :] = held[
                pl.ds(base + i * groups * span, SUB, stride=SUB), :
            ]


def load_kernel(send, recv, own, state_hbm, *refs, pieces, slots, rows, moves, occ):
    state, tags = refs[:2]
    outs = refs[2 : 2 + len(pieces)]
    where, sem = refs[2 + len(pieces) :]
    copy = pltpu.make_async_copy(state_hbm, state, sem)
    copy.start()
    for slot in range(slots):
        where[slot] = slot
    for level in range(3):
        if level:
            for k in range(moves):
                slot = jnp.minimum(send[level, 0, k], slots - 1)
                tags[(level - 1) * moves + k] = where[slot]
        for k in range(moves):
            where[recv[level, 0, k]] = slots + level * moves + k
    for b in range(occ):
        tags[2 * moves + b] = where[own[b]]
    copy.wait()
    pack_pieces(send, state, outs, pieces, slots, rows, moves)


def pick_kernel(tags, state, *refs, plan, given, passed, slots, rows, moves):
    arrived = refs[:given]
    outs = refs[given + passed :]
    for (level, begin, end, which), out in zip(plan, outs):
        sources = [arrived[i] for i in which]
        for k in range(moves):
            tag = tags[(level - 1) * moves + k]
            for unit in range(begin, end):
                local = unit - begin
                out[k, local * SUB : (local + 1) * SUB, :] = pick(
                    tag, unit, local, state, sources, slots, rows, moves
                )


def primitives(cons):
    density = cons[0]
    inverse = 1.0 / density
    vel = [cons[1] * inverse, cons[2] * inverse, cons[3] * inverse]
    kinetic = cons[1] * vel[0] + cons[2] * vel[1] + cons[3] * vel[2]
    pressure = (gamma_ratio - 1.0) * (cons[4] - 0.5 * kinetic)
    return [density, vel[0], vel[1], vel[2], pressure]


def half_minmod(lower, upper):
    both = jnp.maximum(0.0, jnp.minimum(lower, upper)) + jnp.minimum(
        0.0, jnp.maximum(lower, upper)
    )
    return 0.5 * both


def half_slopes(before, here, after):
    return [half_minmod(h - b, a - h) for b, h, a in zip(before, here, after)]


def plus(a, b):
    return [x + y for x, y in zip(a, b)]


def minus(a, b):
    return [x - y for x, y in zip(a, b)]


def side_terms(prim, normal):
    density, vel, pressure = prim[0], prim[1:4], prim[4]
    along = vel[normal]
    mom = [density * v for v in vel]
    kinetic = mom[0] * vel[0] + mom[1] * vel[1] + mom[2] * vel[2]
    energy = pressure * (1.0 / (gamma_ratio - 1.0)) + 0.5 * kinetic
    flux = [m * along for m in mom]
    flux[normal] = flux[normal] + pressure
    scaled = gamma_ratio * pressure
    speed = jnp.abs(along) + scaled * lax.rsqrt(scaled * density)
    return [density] + mom + [energy], [mom[normal]] + flux + [(energy + pressure) * along], speed


def twice_flux(left, right, normal):
    left_cons, left_flux, left_speed = side_terms(left, normal)
    right_cons, right_flux, right_speed = side_terms(right, normal)
    speed = jnp.maximum(left_speed, right_speed)
    return [
        (fl + fr) - speed * (ur - ul)
        for fl, fr, ul, ur in zip(left_flux, right_flux, left_cons, right_cons)
    ]


def lane_of():
    return lax.broadcasted_iota(jnp.int32, (SUB, LANES), 1)


def sub_of():
    return lax.broadcasted_iota(jnp.int32, (SUB, LANES), 0)


def lane_roll(value, amount):
    amount = amount % LANES
    return value if amount == 0 else pltpu.roll(value, amount, 1)


class Shape:
    def __init__(self, rows, edge):
        self.rows, self.edge = rows, edge
        self.halves = rows // edge
        self.width = 2 * edge
        self.fit = LANES // self.width
        self.slabs = rows // SUB
        self.pad = 2 * self.halves

    def at(self, f, row):
        start = SUB + (f * self.rows + row) * SUB
        return pl.ds(start if isinstance(start, int) else pl.multiple_of(start, SUB), SUB)

    def across(self, f, slab, sub):
        return pl.ds(SUB + (f * self.rows + slab * SUB) * SUB + sub, SUB, stride=SUB)

    def beside(self, f, row, step):
        return pl.ds(SUB + (f * self.rows + row) * SUB + step, SUB)

    def grid(self):
        return jax.ShapeDtypeStruct(((NF * self.rows + 2) * SUB, LANES), f32)

    def faces(self):
        x = jax.ShapeDtypeStruct((NF, self.pad, SUB, LANES), f32)
        y = jax.ShapeDtypeStruct((NF, self.edge // self.fit, SUB, LANES), f32)
        z = jax.ShapeDtypeStruct((NF, self.rows, LANES), f32)
        return [x, x, y, y, z, z]


def send_slab(shape, prim, y_lo, y_hi, z_lo, z_hi, slab):
    lane = lane_of()
    halves = shape.halves
    for f in FIELDS:
        lo = hi = None
        for k in range(shape.fit):
            row = slab * SUB + k * halves
            below = lane_roll(prim[shape.at(f, row), :], shape.width * k)
            above = lane_roll(prim[shape.at(f, row + halves - 1), :], shape.width * (k + 1))
            if lo is None:
                lo, hi = below, above
            else:
                mine = lane >= shape.width * k
                lo = jnp.where(mine, below, lo)
                hi = jnp.where(mine, above, hi)
        y_lo[f, slab] = lo
        y_hi[f, slab] = hi
        to = pl.ds(slab * SUB, SUB) if isinstance(slab, int) else pl.ds(
            pl.multiple_of(slab * SUB, SUB), SUB
        )
        z_lo[f, to, :] = prim[shape.across(f, slab, 0), :]
        z_hi[f, to, :] = prim[shape.across(f, slab, SUB - 1), :]


def send_x(shape, prim, x_lo, x_hi):
    for f in FIELDS:
        for i in range(shape.pad):
            x_lo[f, i] = prim[shape.at(f, i), :]
            x_hi[f, i] = prim[shape.at(f, shape.rows - shape.pad + i), :]


def assemble_kernel(tags, state, *refs, pieces, slabs, slots, moves, occ, shape, first):
    given = refs[: 3 * len(pieces)]
    rest = refs[len(given) + (0 if first else 7) :]
    field, prim, y_lo, y_hi, z_lo, z_hi, other = rest[:7]
    held = rest[7]
    units = NF * shape.slabs
    begin_unit, end_unit = slabs[0] * NF, slabs[1] * NF
    for b in range(occ):
        tag = tags[2 * moves + b]
        for number, (begin, end) in enumerate(pieces):
            sources = given[3 * number : 3 * number + 3]
            for unit in range(max(begin, begin_unit), min(end, end_unit)):
                at = (b * units + unit) * SUB
                held[at : at + SUB, :] = pick(
                    tag, unit, unit - begin, state, sources, slots, shape.rows, moves
                )
    for slab in range(*slabs):
        for i in range(SUB):
            row = slab * SUB + i
            cons = [
                held[pl.ds((slab * NF + f) * SUB + i, occ, stride=units * SUB), :] for f in FIELDS
            ]
            for f, (c, w) in enumerate(zip(cons, primitives(cons))):
                field[shape.at(f, row), :] = c
                prim[shape.at(f, row), :] = w
        send_slab(shape, prim, y_lo, y_hi, z_lo, z_hi, slab)
    if first:

        def clear(i, carry):
            other[pl.ds(pl.multiple_of(i * SUB, SUB), SUB), :] = jnp.zeros((SUB, LANES), f32)
            return carry

        lax.fori_loop(0, other.shape[0] // SUB, clear, 0, unroll=16)
        for f in FIELDS:
            for i in range(shape.pad):
                rest[8][f, i] = prim[shape.at(f, i), :]
    else:
        for f in FIELDS:
            for i in range(shape.pad):
                rest[8][f, i] = prim[shape.at(f, shape.rows - shape.pad + i), :]


def sweep_z_kernel(prim, z_lo, z_hi, z_prev, z_next, total, flux_z, right_z, left, right, flux, *, shape):
    edge, rows = shape.edge, shape.rows

    def ghost(a, carry):
        at = pl.ds(pl.multiple_of(a * SUB, SUB), SUB)
        low = [z_lo[f, at, :] for f in FIELDS]
        high = [z_hi[f, at, :] for f in FIELDS]
        prev = [z_prev[f, at, :] for f in FIELDS]
        after = [z_next[f, at, :] for f in FIELDS]
        below = [lane_roll(v, -(edge - 1)) for v in prev]
        before = [lane_roll(v, -(edge - 2)) for v in prev]
        second = [lane_roll(v, -1) for v in low]
        lefts = plus(below, half_slopes(before, below, low))
        rights = minus(low, half_slopes(below, low, second))
        fluxes = twice_flux(lefts, rights, 2)
        last = [lane_roll(v, -(edge - 1)) for v in high]
        beyond = [lane_roll(v, -1) for v in after]
        over = minus(after, half_slopes(last, after, beyond))
        for f in FIELDS:
            flux_z[f, at, :] = lane_roll(fluxes[f], edge - 1)
            right_z[f, at, :] = over[f]
        return carry

    lax.fori_loop(0, shape.slabs, ghost, 0)
    lane = lane_of()
    z_of = lax.rem(lane, edge)
    sub = sub_of()
    first_z, last_z = z_of == 0, z_of == edge - 1
    first_sub, last_sub = sub == 0, sub == SUB - 1
    higher = lane - z_of + lax.rem(z_of + 1, edge)
    lower = lane - z_of + lax.rem(z_of + edge - 1, edge)

    def insert(ref, f, row):
        return jnp.broadcast_to(ref[f, pl.ds(row, 1), :], (SUB, LANES))

    def up(ref, value, f, row, ghosts):
        across = ref[shape.beside(f, row, 1), :]
        across = jnp.where(last_sub, insert(ghosts, f, row), across)
        return jnp.take_along_axis(jnp.where(first_z, across, value), higher, axis=1)

    def down(ref, value, f, row, ghosts):
        across = ref[shape.beside(f, row, -1), :]
        across = jnp.where(first_sub, insert(ghosts, f, row), across)
        return jnp.take_along_axis(jnp.where(last_z, across, value), lower, axis=1)

    def slopes(slab, carry):
        for i in range(SUB):
            row = slab * SUB + i
            for f in FIELDS:
                at = shape.at(f, row)
                mine = prim[at, :]
                shift = half_minmod(
                    mine - down(prim, mine, f, row, z_prev), up(prim, mine, f, row, z_next) - mine
                )
                left[at, :] = mine + shift
                right[at, :] = mine - shift
        return carry

    def fluxes(slab, carry):
        for i in range(SUB):
            row = slab * SUB + i
            lefts = [left[shape.at(f, row), :] for f in FIELDS]
            rights = [up(right, right[shape.at(f, row), :], f, row, right_z) for f in FIELDS]
            for f, value in enumerate(twice_flux(lefts, rights, 2)):
                flux[shape.at(f, row), :] = value
        return carry

    def differences(slab, carry):
        for i in range(SUB):
            row = slab * SUB + i
            for f in FIELDS:
                at = shape.at(f, row)
                mine = flux[at, :]
                total[at, :] = mine - down(flux, mine, f, row, flux_z)
        return carry

    lax.fori_loop(0, shape.slabs, slopes, 0)
    lax.fori_loop(0, shape.slabs, fluxes, 0)
    lax.fori_loop(0, shape.slabs, differences, 0)


def sweep_x_kernel(prim, x_prev, x_next, sofar, total, wide, *, shape):
    rows, halves, pad = shape.rows, shape.halves, shape.pad
    for f in FIELDS:
        for i in range(pad):
            wide[f, i] = x_prev[f, i]
            wide[f, pad + rows + i] = x_next[f, i]

        def copy(r, carry, f=f):
            wide[f, pad + r] = prim[shape.at(f, r), :]
            return carry

        lax.fori_loop(0, rows, copy, 0, unroll=8)

    for h in range(halves):
        cells = [[wide[f, i * halves + h] for f in FIELDS] for i in range(4)]
        left = plus(cells[1], half_slopes(*cells[0:3]))
        shift = half_slopes(*cells[1:4])
        flux = twice_flux(left, minus(cells[2], shift), 0)
        keep = plus(cells[2], shift)

        def body(x, carry, h=h):
            below, left = carry
            here, one, two = (
                [wide[f, pad + (x + i) * halves + h] for f in FIELDS] for i in range(3)
            )
            shift = half_slopes(here, one, two)
            flux = twice_flux(left, minus(one, shift), 0)
            row = x * halves + h
            for f in FIELDS:
                at = shape.at(f, row)
                total[at, :] = sofar[at, :] + (flux[f] - below[f])
            return flux, plus(one, shift)

        lax.fori_loop(0, shape.edge, body, (flux, keep), unroll=4)


def sweep_y(prim, y_lo, y_hi, y_prev, y_next, sofar, ghost_prim, ghost_flux, left, right, flux,
            shape, finish, after_slab):
    edge, halves, fit, width = shape.edge, shape.halves, shape.fit, shape.width
    lane = lane_of()
    upper = lax.rem(lane, width) >= edge

    def ghost(q, carry):
        low = [y_lo[f, q] for f in FIELDS]
        high = [y_hi[f, q] for f in FIELDS]
        below = [y_prev[f, q] for f in FIELDS]
        after = [y_next[f, q] for f in FIELDS]
        before = [lane_roll(v, edge) for v in below]
        first = [lane_roll(v, edge) for v in low]
        lefts = plus(below, half_slopes(before, below, first))
        rights = minus(first, half_slopes(below, first, low))
        fluxes = twice_flux(lefts, rights, 1)
        last = [lane_roll(v, -edge) for v in high]
        beyond = [lane_roll(v, -edge) for v in after]
        over = minus(after, half_slopes(last, after, beyond))
        for f in FIELDS:
            ghost_prim[f, q] = jnp.where(upper, below[f], after[f])
            ghost_flux[f, q] = jnp.where(upper, fluxes[f], over[f])
        return carry

    lax.fori_loop(0, edge // fit, ghost, 0)
    top_lanes = lane >= LANES - edge
    low_lanes = lane < edge

    def up(values, insert):
        rolled = [lane_roll(v, -edge) for v in values]
        follow = rolled[1:] + [insert]
        return [jnp.where(top_lanes, n, r) for r, n in zip(rolled, follow)]

    def down(values, insert):
        rolled = [lane_roll(v, edge) for v in values]
        lead = [insert] + rolled[:-1]
        return [jnp.where(low_lanes, n, r) for r, n in zip(rolled, lead)]

    def each(q):
        for k in range(fit):
            yield -(width * k + edge), (q * fit + k) * halves

    def slopes(q, carry):
        for turn, base in each(q):
            for f in FIELDS:
                mine = [prim[shape.at(f, base + h), :] for h in range(halves)]
                ghost = lane_roll(ghost_prim[f, q], turn)
                over, under = up(mine, ghost), down(mine, ghost)
                for h in range(halves):
                    shift = half_minmod(mine[h] - under[h], over[h] - mine[h])
                    left[shape.at(f, base + h), :] = mine[h] + shift
                    right[shape.at(f, base + h), :] = mine[h] - shift
        return carry

    def fluxes(q, carry):
        for turn, base in each(q):
            rights = []
            for f in FIELDS:
                mine = [right[shape.at(f, base + h), :] for h in range(halves)]
                rights.append(up(mine, lane_roll(ghost_flux[f, q], turn)))
            for h in range(halves):
                lefts = [left[shape.at(f, base + h), :] for f in FIELDS]
                result = twice_flux(lefts, [rights[f][h] for f in FIELDS], 1)
                for f in FIELDS:
                    flux[shape.at(f, base + h), :] = result[f]
        return carry

    def differences(q, carry):
        for turn, base in each(q):
            total = [[None] * NF for _ in range(halves)]
            for f in FIELDS:
                mine = [flux[shape.at(f, base + h), :] for h in range(halves)]
                under = down(mine, lane_roll(ghost_flux[f, q], turn))
                for h in range(halves):
                    total[h][f] = sofar[shape.at(f, base + h), :] + (mine[h] - under[h])
            for h in range(halves):
                finish(base + h, total[h])
        after_slab(q)
        return carry

    lax.fori_loop(0, edge // fit, slopes, 0)
    lax.fori_loop(0, edge // fit, fluxes, 0)
    lax.fori_loop(0, edge // fit, differences, 0)


def sweep_y_one_kernel(field, prim, y_lo, y_hi, y_prev, y_next, sofar, *refs, shape):
    one, one_prim, x_lo, x_hi, out_y_lo, out_y_hi, z_lo, z_hi = refs[:8]

    def finish(row, total):
        cons = [field[shape.at(f, row), :] - (0.5 * time_step) * total[f] for f in FIELDS]
        for f, (c, w) in enumerate(zip(cons, primitives(cons))):
            one[shape.at(f, row), :] = c
            one_prim[shape.at(f, row), :] = w

    def after_slab(q):
        send_slab(shape, one_prim, out_y_lo, out_y_hi, z_lo, z_hi, q)

    sweep_y(prim, y_lo, y_hi, y_prev, y_next, sofar, *refs[8:], shape, finish, after_slab)
    send_x(shape, one_prim, x_lo, x_hi)


def sweep_y_two_kernel(own, field, one, prim, y_lo, y_hi, y_prev, y_next, sofar, zeros, out,
                       canvas, *refs, shape, occ, groups):
    scratch, (result, sems) = refs[:5], refs[5:]
    rows = shape.rows
    span = SUB * SUB

    def finish(row, total):
        for f in FIELDS:
            at = shape.at(f, row)
            advanced = one[at, :] - (0.5 * time_step) * total[f]
            result[at, :] = 0.5 * field[at, :] + 0.5 * advanced

    def copy(part):
        begin = part * span if isinstance(part, int) else pl.multiple_of(part * span, span)
        return [
            pltpu.make_async_copy(
                canvas.at[pl.ds(i * rows * SUB + begin, span), :],
                out.at[pl.ds(i * rows * SUB + begin, span), :],
                sems.at[part, i],
            )
            for i in range(NF * groups)
        ]

    def after_slab(q):
        for b in range(occ):
            slot = own[b]
            base = (slot // SUB) * (rows * SUB) + lax.rem(slot, SUB) + q * span
            for f in FIELDS:
                canvas[pl.ds(base + f * groups * rows * SUB, SUB, stride=SUB), :] = result[
                    shape.across(f, q, b), :
                ]
        for c in copy(q):
            c.start()

    sweep_y(prim, y_lo, y_hi, y_prev, y_next, sofar, *scratch, shape, finish, after_slab)
    for part in range(shape.slabs):
        for c in copy(part):
            c.wait()


def shards(state, send_slots, recv_slots, owner_slot):
    slots, _, cells = state.shape
    moves = send_slots.shape[2]
    size_x, size_y, size_z = (lax.axis_size(axis) for axis in AXES)
    occ = owner_slot.shape[0] // (size_x * size_y * size_z)
    edge = round(cells ** (1 / 3))
    rows = cells // LANES
    groups = slots // SUB
    shape = Shape(rows, edge)
    pieces = split_units(NF * shape.slabs)
    count = len(pieces)

    bit_z = size_z.bit_length() - 2
    bit_y = bit_z + size_y.bit_length() - 1
    bit_x = bit_y + size_x.bit_length() - 1
    pair_bits = (bit_x, bit_y, bit_z)

    def swapped(value, level):
        mask = 2 ** pair_bits[level]
        pairs = [(source, source ^ mask) for source in range(lax.axis_size(AXES))]
        return lax.ppermute(value, AXES, pairs)

    rows_of_state = (
        state.reshape(groups, SUB, NF, rows, LANES)
        .transpose(2, 0, 3, 1, 4)
        .reshape(NF * groups * rows * SUB, LANES)
    )
    rows_of_state = pltpu.with_memory_space_constraint(rows_of_state, HBM)
    send_there = pltpu.with_memory_space_constraint(send_slots, HBM)
    device = lax.axis_index(AXES)
    own = lax.dynamic_slice(owner_slot, (device * occ,), (occ,))
    sizes = dict(slots=slots, moves=moves)

    def message(p):
        begin, end = pieces[p]
        return jax.ShapeDtypeStruct((moves, (end - begin) * SUB, LANES), f32)

    state_rows = NF * groups * rows * SUB
    head = pieces[0]
    sent = [None] * count
    sent[0] = pl.pallas_call(
        functools.partial(first_kernel, piece=head, rows=rows, **sizes),
        out_shape=message(0),
        in_specs=[whole(HBM)] * 2,
        out_specs=whole(VMEM),
        scratch_shapes=[
            SMEM(send_slots.shape, jnp.int32),
            VMEM(((head[1] - head[0]) * groups * SUB * SUB, LANES), f32),
            pltpu.SemaphoreType.DMA((1 + (head[1] - head[0]) * groups,)),
        ],
        compiler_params=params(),
        name="pack_first",
    )(send_there, rows_of_state)
    rows_of_state, tags, *sent[1:] = pl.pallas_call(
        functools.partial(load_kernel, pieces=pieces[1:], rows=rows, occ=occ, **sizes),
        out_shape=[
            jax.ShapeDtypeStruct((state_rows, LANES), f32),
            jax.ShapeDtypeStruct((2 * moves + occ,), jnp.int32),
        ]
        + [message(p) for p in range(1, count)],
        in_specs=[whole(SMEM)] * 3 + [whole(HBM)],
        out_specs=[whole(VMEM), whole(SMEM)] + [whole(VMEM)] * (count - 1),
        scratch_shapes=[SMEM((slots + SUB,), jnp.int32), pltpu.SemaphoreType.DMA],
        compiler_params=params(),
        name="load_state",
    )(send_slots, recv_slots, own, rows_of_state)

    got = [[None] * count for _ in range(3)]

    def make(wanted, through):
        arrays, plan, shapes = [], [], []
        for level, p in wanted:
            which = []
            for earlier in range(level):
                which.append(len(arrays))
                arrays.append(got[earlier][p])
            plan.append((level, *pieces[p], tuple(which)))
            shapes.append(message(p))
        given, passed, made = len(arrays), len(through), len(wanted)
        outs = pl.pallas_call(
            functools.partial(
                pick_kernel, plan=tuple(plan), given=given, passed=passed, rows=rows, **sizes
            ),
            out_shape=shapes + [jax.ShapeDtypeStruct(t.shape, f32) for t in through],
            in_specs=[whole(SMEM)] + [whole(VMEM)] * (1 + given) + [whole(pl.ANY)] * passed,
            out_specs=[whole(VMEM)] * made + [whole(pl.ANY)] * passed,
            input_output_aliases={2 + given + i: made + i for i in range(passed)},
            compiler_params=params(),
            name="pick_" + "_".join("%d%d" % w for w in wanted),
        )(tags, rows_of_state, *arrays, *through)
        return outs[:made], outs[made:]

    steps = [
        ([(1, 0)], [2], []),
        ([(1, 1), (2, 0)], [3], []),
        ([(1, 2)], [4], []),
        ([(1, 3), (2, 1)], [], [0]),
        ([(1, 4), (2, 2)], [], []),
        ([(2, 3)], [], [1]),
        ([(2, 4)], [], [2]),
    ]
    got[0][0] = swapped(sent[0], 0)
    got[0][1] = swapped(sent[1], 0)
    for wanted, leaving, awaited in steps:
        through = [sent[p] for p in leaving] + [got[2][p] for p in awaited]
        made, passed = make(wanted, through)
        for (level, p), value in zip(wanted, made):
            got[level][p] = swapped(value, level)
        for p, value in zip(leaving, passed):
            got[0][p] = swapped(value, 0)
        for p, value in zip(awaited, passed[len(leaving) :]):
            got[2][p] = value

    grid = shape.grid()
    face_x, _, face_y, _, face_z, _ = shape.faces()
    part = [grid, grid, face_y, face_y, face_z, face_z]
    canvas = jax.ShapeDtypeStruct((state_rows, LANES), f32)
    full = pieces[-1][0] // NF

    def assemble(slabs, before):
        first = not before
        use = [p for p in range(count) if pieces[p][0] < slabs[1] * NF and pieces[p][1] > slabs[0] * NF]
        sources = [got[level][p] for p in use for level in range(3)]
        shapes = part + [canvas if first else face_x, face_x]
        fixed = 2 + len(sources)

        def kernel(tags, state, *refs):
            lead = refs[: len(sources) + len(before)]
            outs = refs[len(lead) : len(lead) + 8]
            assemble_kernel(
                tags, state, *lead, *outs[:7], refs[-1], outs[7],
                pieces=[pieces[p] for p in use], slabs=slabs, occ=occ, shape=shape, first=first,
                **sizes,
            )

        return pl.pallas_call(
            kernel,
            out_shape=shapes,
            in_specs=[whole(SMEM)] + [whole(VMEM)] * (1 + len(sources)) + [whole(VMEM)] * len(before),
            out_specs=[whole(VMEM)] * len(shapes),
            scratch_shapes=[VMEM((occ * NF * rows, LANES), f32)],
            input_output_aliases={fixed + i: i for i in range(len(before))},
            compiler_params=params(),
            name="assemble_%d" % slabs[0],
        )(tags, rows_of_state, *sources, *before)

    *made, blank, x_lo = assemble((0, full), [])
    *made, x_lo, x_hi = assemble((full, shape.slabs), [*made, x_lo])
    made = made[:2] + [x_lo, x_hi] + made[2:]

    def ring(value, axis, step):
        size = lax.axis_size(axis)
        return lax.ppermute(value, axis, [(i, (i + step) % size) for i in range(size)])

    def flux_sums(prim, x_lo, x_hi, y_lo, y_hi, z_lo, z_hi):
        y_prev, y_next = ring(y_hi, "gy", 1), ring(y_lo, "gy", -1)
        z_prev, z_next = ring(z_hi, "gz", 1), ring(z_lo, "gz", -1)
        if size_x == 2:
            x_prev, x_next = ring(jnp.stack([x_hi, x_lo]), "gx", 1)
        else:
            x_prev, x_next = ring(x_hi, "gx", 1), ring(x_lo, "gx", -1)
        ghost = VMEM((NF, rows, LANES), f32)
        work = [VMEM(grid.shape, f32)] * 3
        total = pl.pallas_call(
            functools.partial(sweep_z_kernel, shape=shape),
            out_shape=grid,
            in_specs=[whole(VMEM)] * 5,
            out_specs=whole(VMEM),
            scratch_shapes=[ghost] * 2 + work,
            compiler_params=params(),
            name="sweep_z",
        )(prim, z_lo, z_hi, z_prev, z_next)
        total = pl.pallas_call(
            functools.partial(sweep_x_kernel, shape=shape),
            out_shape=grid,
            in_specs=[whole(VMEM)] * 4,
            out_specs=whole(VMEM),
            scratch_shapes=[VMEM((NF, rows + 2 * shape.pad, SUB, LANES), f32)],
            input_output_aliases={3: 0},
            compiler_params=params(),
            name="sweep_x",
        )(prim, x_prev, x_next, total)
        return y_lo, y_hi, y_prev, y_next, total

    produced = [grid, grid] + shape.faces()
    scratch = [VMEM(face_y.shape, f32)] * 2 + [VMEM(grid.shape, f32)] * 3
    field, prim = made[0], made[1]
    sums = flux_sums(prim, *made[2:])
    made = pl.pallas_call(
        functools.partial(sweep_y_one_kernel, shape=shape),
        out_shape=produced,
        in_specs=[whole(VMEM)] * 7,
        out_specs=[whole(VMEM)] * len(produced),
        scratch_shapes=scratch,
        compiler_params=params(),
        name="sweep_y_one",
    )(field, prim, *sums)
    one, one_prim = made[0], made[1]
    sums = flux_sums(one_prim, *made[2:])
    out, _ = pl.pallas_call(
        functools.partial(sweep_y_two_kernel, shape=shape, occ=occ, groups=groups),
        out_shape=[canvas, canvas],
        in_specs=[whole(SMEM)] + [whole(VMEM)] * 9,
        out_specs=[whole(HBM), whole(VMEM)],
        scratch_shapes=scratch
        + [
            VMEM(grid.shape, f32),
            pltpu.SemaphoreType.DMA((shape.slabs, NF * groups)),
        ],
        input_output_aliases={9: 1},
        compiler_params=params(),
        name="sweep_y_two",
    )(own, field, one, one_prim, *sums, blank)
    return (
        out.reshape(NF, groups, rows, SUB, LANES)
        .transpose(1, 3, 0, 2, 4)
        .reshape(slots, NF, cells)
    )


def solution(mesh):
    placed = (
        P(AXES, None, None),
        P(None, AXES, None),
        P(None, AXES, None),
        P(),
    )
    return jax.shard_map(
        shards,
        mesh=mesh,
        in_specs=placed,
        out_specs=P(AXES, None, None),
        check_vma=False,
    )
```

```python
import functools

import jax
import jax.numpy as jnp
from jax import lax
from jax.experimental import pallas as pl
from jax.experimental.pallas import tpu as pltpu
from jax.sharding import PartitionSpec as P

gamma_ratio = 1.4
time_step = 0.05
LANES = 128
SUB = 8
NF = 5
FIELDS = range(NF)
AXES = ("gx", "gy", "gz")

VMEM = pltpu.VMEM
SMEM = pltpu.SMEM
HBM = pltpu.HBM
f32 = jnp.float32


def whole(space):
    return pl.BlockSpec(memory_space=space)


def params():
    return pltpu.CompilerParams(vmem_limit_bytes=16 * 1024 * 1024)


def cost(flops, moved):
    return pl.CostEstimate(flops=flops, bytes_accessed=moved, transcendentals=0)


def split_units(units, shares):
    ends = [units * sum(shares[: i + 1]) // sum(shares) for i in range(len(shares))]
    return list(zip([0] + ends[:-1], ends))


def from_state(state, tag, unit, slots, rows):
    slab, field = unit // NF, unit % NF
    groups = slots // SUB
    base = (tag // SUB) * (rows * SUB) + lax.rem(tag, SUB)
    start = base + (field * groups * rows + slab * SUB) * SUB
    return state[pl.ds(start, SUB, stride=SUB), :]


def pick(tag, unit, state, arrived, slots, rows, moves):
    value = from_state(state, jnp.minimum(tag, slots - 1), unit, slots, rows)
    for level, held in enumerate(arrived):
        base = slots + level * moves
        index = jnp.clip(tag - base, 0, moves - 1)
        for (begin, end), ref in held:
            if begin <= unit < end:
                at = (unit - begin) * SUB
                value = jnp.where(tag >= base, ref[index, at : at + SUB, :], value)
    return value


def first_kernel(send_hbm, state_hbm, out, send, held, sems, *, piece, slots, rows, moves):
    span = SUB * SUB
    groups = slots // SUB
    copies = [pltpu.make_async_copy(send_hbm, send, sems.at[0])]
    for unit in range(*piece):
        slab, field = unit // NF, unit % NF
        for g in range(groups):
            at = ((field * groups + g) * rows + slab * SUB) * SUB
            to = ((unit - piece[0]) * groups + g) * span
            copies.append(
                pltpu.make_async_copy(
                    state_hbm.at[pl.ds(at, span), :],
                    held.at[pl.ds(to, span), :],
                    sems.at[len(copies)],
                )
            )
    for c in copies:
        c.start()
    for c in copies:
        c.wait()
    for k in range(moves):
        slot = jnp.minimum(send[0, 0, k], slots - 1)
        base = (slot // SUB) * span + lax.rem(slot, SUB)
        for i in range(piece[1] - piece[0]):
            out[k, i * SUB : (i + 1) * SUB, :] = held[
                pl.ds(base + i * groups * span, SUB, stride=SUB), :
            ]


def load_kernel(send, recv, own, state_hbm, *refs, pieces, slots, rows, moves, occ):
    state, tags = refs[:2]
    outs = refs[2 : 2 + len(pieces)]
    where, sems = refs[2 + len(pieces) :]
    span = slots * rows
    copies = [
        pltpu.make_async_copy(
            state_hbm.at[pl.ds(f * span, span), :], state.at[pl.ds(f * span, span), :], sems.at[f]
        )
        for f in FIELDS
    ]
    for c in copies:
        c.start()
    for slot in range(slots):
        where[slot] = slot
    for level in range(3):
        if level:
            for k in range(moves):
                slot = jnp.minimum(send[level, 0, k], slots - 1)
                tags[(level - 1) * moves + k] = where[slot]
        for k in range(moves):
            where[recv[level, 0, k]] = slots + level * moves + k
    for b in range(occ):
        tags[2 * moves + b] = where[own[b]]
    for f in FIELDS:
        copies[f].wait()
        for k in range(moves):
            slot = jnp.minimum(send[0, 0, k], slots - 1)
            for (begin, end), out in zip(pieces, outs):
                for unit in range(begin, end):
                    if unit % NF == f:
                        at = (unit - begin) * SUB
                        out[k, at : at + SUB, :] = from_state(state, slot, unit, slots, rows)


def group_levels(refs, held):
    levels = [[], [], []]
    for ref, (level, piece) in zip(refs, held):
        levels[level].append((piece, ref))
    return levels


def pick_kernel(tags, state, *refs, plan, held, passed, slots, rows, moves):
    given = len(held)
    arrived = group_levels(refs[:given], held)
    outs = refs[given + passed :]
    for (level, (begin, end)), out in zip(plan, outs):
        for k in range(moves):
            tag = tags[(level - 1) * moves + k]
            for unit in range(begin, end):
                at = (unit - begin) * SUB
                out[k, at : at + SUB, :] = pick(
                    tag, unit, state, arrived[:level], slots, rows, moves
                )


def primitives(cons):
    density = cons[0]
    inverse = 1.0 / density
    vel = [cons[1] * inverse, cons[2] * inverse, cons[3] * inverse]
    kinetic = cons[1] * vel[0] + cons[2] * vel[1] + cons[3] * vel[2]
    pressure = (gamma_ratio - 1.0) * (cons[4] - 0.5 * kinetic)
    return [density, vel[0], vel[1], vel[2], pressure]


def half_minmod(lower, upper):
    both = jnp.maximum(0.0, jnp.minimum(lower, upper)) + jnp.minimum(
        0.0, jnp.maximum(lower, upper)
    )
    return 0.5 * both


def half_slopes(before, here, after):
    return [half_minmod(h - b, a - h) for b, h, a in zip(before, here, after)]


def plus(a, b):
    return [x + y for x, y in zip(a, b)]


def minus(a, b):
    return [x - y for x, y in zip(a, b)]


def side_terms(prim, normal):
    density, vel, pressure = prim[0], prim[1:4], prim[4]
    along = vel[normal]
    mom = [density * v for v in vel]
    kinetic = mom[0] * vel[0] + mom[1] * vel[1] + mom[2] * vel[2]
    energy = pressure * (1.0 / (gamma_ratio - 1.0)) + 0.5 * kinetic
    flux = [m * along for m in mom]
    flux[normal] = flux[normal] + pressure
    scaled = gamma_ratio * pressure
    speed = jnp.abs(along) + scaled * lax.rsqrt(scaled * density)
    return [density] + mom + [energy], [mom[normal]] + flux + [(energy + pressure) * along], speed


def twice_flux(left, right, normal):
    left_cons, left_flux, left_speed = side_terms(left, normal)
    right_cons, right_flux, right_speed = side_terms(right, normal)
    speed = jnp.maximum(left_speed, right_speed)
    return [
        (fl + fr) - speed * (ur - ul)
        for fl, fr, ul, ur in zip(left_flux, right_flux, left_cons, right_cons)
    ]


def lane_of():
    return lax.broadcasted_iota(jnp.int32, (SUB, LANES), 1)


def sub_of():
    return lax.broadcasted_iota(jnp.int32, (SUB, LANES), 0)


def lane_roll(value, amount):
    amount = amount % LANES
    return value if amount == 0 else pltpu.roll(value, amount, 1)


class Shape:
    def __init__(self, rows, edge):
        self.rows, self.edge = rows, edge
        self.halves = rows // edge
        self.width = 2 * edge
        self.fit = LANES // self.width
        self.slabs = rows // SUB
        self.pad = 2 * self.halves

    def at(self, f, row):
        start = SUB + (f * self.rows + row) * SUB
        return pl.ds(start if isinstance(start, int) else pl.multiple_of(start, SUB), SUB)

    def across(self, f, slab, sub):
        return pl.ds(SUB + (f * self.rows + slab * SUB) * SUB + sub, SUB, stride=SUB)

    def beside(self, f, row, step):
        return pl.ds(SUB + (f * self.rows + row) * SUB + step, SUB)

    def grid(self):
        return jax.ShapeDtypeStruct(((NF * self.rows + 2) * SUB, LANES), f32)

    def faces(self):
        x = jax.ShapeDtypeStruct((2, NF, self.pad, SUB, LANES), f32)
        y = jax.ShapeDtypeStruct((NF, self.edge // self.fit, SUB, LANES), f32)
        z = jax.ShapeDtypeStruct((NF, self.rows, LANES), f32)
        return [x, y, y, z, z]


def send_slab(shape, prim, y_lo, y_hi, z_lo, z_hi, slab):
    lane = lane_of()
    halves = shape.halves
    for f in FIELDS:
        lo = hi = None
        for k in range(shape.fit):
            row = slab * SUB + k * halves
            below = lane_roll(prim[shape.at(f, row), :], shape.width * k)
            above = lane_roll(prim[shape.at(f, row + halves - 1), :], shape.width * (k + 1))
            if lo is None:
                lo, hi = below, above
            else:
                mine = lane >= shape.width * k
                lo = jnp.where(mine, below, lo)
                hi = jnp.where(mine, above, hi)
        y_lo[f, slab] = lo
        y_hi[f, slab] = hi
        to = pl.ds(slab * SUB, SUB) if isinstance(slab, int) else pl.ds(
            pl.multiple_of(slab * SUB, SUB), SUB
        )
        z_lo[f, to, :] = prim[shape.across(f, slab, 0), :]
        z_hi[f, to, :] = prim[shape.across(f, slab, SUB - 1), :]


def send_x(shape, prim, faces, low=True, high=True):
    for f in FIELDS:
        for i in range(shape.pad):
            if high:
                faces[0, f, i] = prim[shape.at(f, shape.rows - shape.pad + i), :]
            if low:
                faces[1, f, i] = prim[shape.at(f, i), :]


def assemble_kernel(tags, state, *refs, held, slabs, slots, moves, occ, shape, first):
    given = len(held)
    arrived = group_levels(refs[:given], held)
    outs = refs[given + (0 if first else 7) :]
    field, prim, y_lo, y_hi, z_lo, z_hi, x_faces = outs[:7]
    blocks = outs[-1]
    units = NF * shape.slabs
    for b in range(occ):
        tag = tags[2 * moves + b]
        for unit in range(slabs[0] * NF, slabs[1] * NF):
            at = (b * units + unit) * SUB
            blocks[at : at + SUB, :] = pick(tag, unit, state, arrived, slots, shape.rows, moves)
    for slab in range(*slabs):
        for i in range(SUB):
            row = slab * SUB + i
            cons = [
                blocks[pl.ds((slab * NF + f) * SUB + i, occ, stride=units * SUB), :] for f in FIELDS
            ]
            for f, (c, w) in enumerate(zip(cons, primitives(cons))):
                field[shape.at(f, row), :] = c
                prim[shape.at(f, row), :] = w
        send_slab(shape, prim, y_lo, y_hi, z_lo, z_hi, slab)
    if first:
        canvas = outs[7]

        def clear(i, carry):
            canvas[pl.ds(pl.multiple_of(i * SUB, SUB), SUB), :] = jnp.zeros((SUB, LANES), f32)
            return carry

        lax.fori_loop(0, canvas.shape[0] // SUB, clear, 0, unroll=16)
    send_x(shape, prim, x_faces, low=first, high=not first)


def sweep_z_kernel(prim, z_lo, z_hi, z_prev, z_next, total, flux_z, right_z, left, right, flux, *, shape):
    edge, rows = shape.edge, shape.rows

    def ghost(a, carry):
        at = pl.ds(pl.multiple_of(a * SUB, SUB), SUB)
        low = [z_lo[f, at, :] for f in FIELDS]
        high = [z_hi[f, at, :] for f in FIELDS]
        prev = [z_prev[f, at, :] for f in FIELDS]
        after = [z_next[f, at, :] for f in FIELDS]
        below = [lane_roll(v, -(edge - 1)) for v in prev]
        before = [lane_roll(v, -(edge - 2)) for v in prev]
        second = [lane_roll(v, -1) for v in low]
        lefts = plus(below, half_slopes(before, below, low))
        rights = minus(low, half_slopes(below, low, second))
        fluxes = twice_flux(lefts, rights, 2)
        last = [lane_roll(v, -(edge - 1)) for v in high]
        beyond = [lane_roll(v, -1) for v in after]
        over = minus(after, half_slopes(last, after, beyond))
        for f in FIELDS:
            flux_z[f, at, :] = lane_roll(fluxes[f], edge - 1)
            right_z[f, at, :] = over[f]
        return carry

    lax.fori_loop(0, shape.slabs, ghost, 0)
    lane = lane_of()
    z_of = lax.rem(lane, edge)
    sub = sub_of()
    first_z, last_z = z_of == 0, z_of == edge - 1
    first_sub, last_sub = sub == 0, sub == SUB - 1
    higher = lane - z_of + lax.rem(z_of + 1, edge)
    lower = lane - z_of + lax.rem(z_of + edge - 1, edge)

    def insert(ref, f, row):
        return jnp.broadcast_to(ref[f, pl.ds(row, 1), :], (SUB, LANES))

    def up(ref, value, f, row, ghosts):
        across = ref[shape.beside(f, row, 1), :]
        across = jnp.where(last_sub, insert(ghosts, f, row), across)
        return jnp.take_along_axis(jnp.where(first_z, across, value), higher, axis=1)

    def down(ref, value, f, row, ghosts):
        across = ref[shape.beside(f, row, -1), :]
        across = jnp.where(first_sub, insert(ghosts, f, row), across)
        return jnp.take_along_axis(jnp.where(last_z, across, value), lower, axis=1)

    def slopes(slab, carry):
        for i in range(SUB):
            row = slab * SUB + i
            for f in FIELDS:
                at = shape.at(f, row)
                mine = prim[at, :]
                shift = half_minmod(
                    mine - down(prim, mine, f, row, z_prev), up(prim, mine, f, row, z_next) - mine
                )
                left[at, :] = mine + shift
                right[at, :] = mine - shift
        return carry

    def fluxes(slab, carry):
        for i in range(SUB):
            row = slab * SUB + i
            lefts = [left[shape.at(f, row), :] for f in FIELDS]
            rights = [up(right, right[shape.at(f, row), :], f, row, right_z) for f in FIELDS]
            for f, value in enumerate(twice_flux(lefts, rights, 2)):
                flux[shape.at(f, row), :] = value
        return carry

    def differences(slab, carry):
        for i in range(SUB):
            row = slab * SUB + i
            for f in FIELDS:
                at = shape.at(f, row)
                mine = flux[at, :]
                total[at, :] = mine - down(flux, mine, f, row, flux_z)
        return carry

    lax.fori_loop(0, shape.slabs, slopes, 0)
    lax.fori_loop(0, shape.slabs, fluxes, 0)
    lax.fori_loop(0, shape.slabs, differences, 0)


def sweep_x_kernel(prim, x_faces, sofar, total, wide, *, shape):
    rows, halves, pad = shape.rows, shape.halves, shape.pad
    for f in FIELDS:
        for i in range(pad):
            wide[f, i] = x_faces[0, f, i]
            wide[f, pad + rows + i] = x_faces[1, f, i]

        def copy(r, carry, f=f):
            wide[f, pad + r] = prim[shape.at(f, r), :]
            return carry

        lax.fori_loop(0, rows, copy, 0, unroll=8)

    for h in range(halves):
        cells = [[wide[f, i * halves + h] for f in FIELDS] for i in range(4)]
        left = plus(cells[1], half_slopes(*cells[0:3]))
        shift = half_slopes(*cells[1:4])
        flux = twice_flux(left, minus(cells[2], shift), 0)
        keep = plus(cells[2], shift)

        def body(x, carry, h=h):
            below, left = carry
            here, one, two = (
                [wide[f, pad + (x + i) * halves + h] for f in FIELDS] for i in range(3)
            )
            shift = half_slopes(here, one, two)
            flux = twice_flux(left, minus(one, shift), 0)
            row = x * halves + h
            for f in FIELDS:
                at = shape.at(f, row)
                total[at, :] = sofar[at, :] + (flux[f] - below[f])
            return flux, plus(one, shift)

        lax.fori_loop(0, shape.edge, body, (flux, keep), unroll=4)


def sweep_y(prim, y_lo, y_hi, y_prev, y_next, sofar, ghost_prim, ghost_flux, left, right, flux, turned,
            shape, finish, after_slab):
    edge, halves, fit, width = shape.edge, shape.halves, shape.fit, shape.width
    lane = lane_of()
    upper = lax.rem(lane, width) >= edge

    def ghost(q, carry):
        low = [y_lo[f, q] for f in FIELDS]
        high = [y_hi[f, q] for f in FIELDS]
        below = [y_prev[f, q] for f in FIELDS]
        after = [y_next[f, q] for f in FIELDS]
        before = [lane_roll(v, edge) for v in below]
        first = [lane_roll(v, edge) for v in low]
        lefts = plus(below, half_slopes(before, below, first))
        rights = minus(first, half_slopes(below, first, low))
        fluxes = twice_flux(lefts, rights, 1)
        last = [lane_roll(v, -edge) for v in high]
        beyond = [lane_roll(v, -edge) for v in after]
        over = minus(after, half_slopes(last, after, beyond))
        for f in FIELDS:
            ghost_prim[f, q] = jnp.where(upper, below[f], after[f])
            ghost_flux[f, q] = jnp.where(upper, fluxes[f], over[f])
        return carry

    lax.fori_loop(0, edge // fit, ghost, 0)
    top_lanes = lane >= LANES - edge
    low_lanes = lane < edge

    def up(values, insert):
        rolled = [lane_roll(v, -edge) for v in values]
        follow = rolled[1:] + [insert]
        return [jnp.where(top_lanes, n, r) for r, n in zip(rolled, follow)]

    def down(values, insert):
        rolled = [lane_roll(v, edge) for v in values]
        lead = [insert] + rolled[:-1]
        return [jnp.where(low_lanes, n, r) for r, n in zip(rolled, lead)]

    def each(q):
        for k in range(fit):
            yield -(width * k + edge), (q * fit + k) * halves

    def slopes(q, carry):
        for turn, base in each(q):
            for f in FIELDS:
                mine = [prim[shape.at(f, base + h), :] for h in range(halves)]
                ghost = lane_roll(ghost_prim[f, q], turn)
                over, under = up(mine, ghost), down(mine, ghost)
                for h in range(halves):
                    shift = half_minmod(mine[h] - under[h], over[h] - mine[h])
                    left[shape.at(f, base + h), :] = mine[h] + shift
                    right[shape.at(f, base + h), :] = mine[h] - shift
        return carry

    def fluxes(q, carry):
        for turn, base in each(q):
            rights = []
            for f in FIELDS:
                mine = [right[shape.at(f, base + h), :] for h in range(halves)]
                ghost = lane_roll(ghost_flux[f, q], turn)
                turned[shape.at(f, base), :] = ghost
                rights.append(up(mine, ghost))
            for h in range(halves):
                lefts = [left[shape.at(f, base + h), :] for f in FIELDS]
                result = twice_flux(lefts, [rights[f][h] for f in FIELDS], 1)
                for f in FIELDS:
                    flux[shape.at(f, base + h), :] = result[f]
        return carry

    def differences(q, carry):
        for turn, base in each(q):
            total = [[None] * NF for _ in range(halves)]
            for f in FIELDS:
                mine = [flux[shape.at(f, base + h), :] for h in range(halves)]
                under = down(mine, turned[shape.at(f, base), :])
                for h in range(halves):
                    total[h][f] = sofar[shape.at(f, base + h), :] + (mine[h] - under[h])
            for h in range(halves):
                finish(base + h, total[h])
        after_slab(q)
        return carry

    lax.fori_loop(0, edge // fit, slopes, 0)
    lax.fori_loop(0, edge // fit, fluxes, 0)
    lax.fori_loop(0, edge // fit, differences, 0)


def sweep_y_one_kernel(field, prim, y_lo, y_hi, y_prev, y_next, sofar, *refs, shape):
    one, one_prim, x_faces, out_y_lo, out_y_hi, z_lo, z_hi = refs[:7]

    def finish(row, total):
        cons = [field[shape.at(f, row), :] - (0.5 * time_step) * total[f] for f in FIELDS]
        for f, (c, w) in enumerate(zip(cons, primitives(cons))):
            one[shape.at(f, row), :] = c
            one_prim[shape.at(f, row), :] = w

    def after_slab(q):
        send_slab(shape, one_prim, out_y_lo, out_y_hi, z_lo, z_hi, q)

    sweep_y(prim, y_lo, y_hi, y_prev, y_next, sofar, *refs[7:], shape, finish, after_slab)
    send_x(shape, one_prim, x_faces)


def sweep_y_two_kernel(own, field, one, prim, y_lo, y_hi, y_prev, y_next, sofar, zeros, out,
                       canvas, *refs, shape, occ, groups):
    scratch, (result, sems) = refs[:6], refs[6:]
    rows = shape.rows
    span = SUB * SUB

    def finish(row, total):
        for f in FIELDS:
            at = shape.at(f, row)
            advanced = one[at, :] - (0.5 * time_step) * total[f]
            result[at, :] = 0.5 * field[at, :] + 0.5 * advanced

    def copy(part):
        begin = part * span if isinstance(part, int) else pl.multiple_of(part * span, span)
        return [
            pltpu.make_async_copy(
                canvas.at[pl.ds(i * rows * SUB + begin, span), :],
                out.at[pl.ds(i * rows * SUB + begin, span), :],
                sems.at[part, i],
            )
            for i in range(NF * groups)
        ]

    def after_slab(q):
        for b in range(occ):
            slot = own[b]
            base = (slot // SUB) * (rows * SUB) + lax.rem(slot, SUB) + q * span
            for f in FIELDS:
                canvas[pl.ds(base + f * groups * rows * SUB, SUB, stride=SUB), :] = result[
                    shape.across(f, q, b), :
                ]
        for c in copy(q):
            c.start()

    sweep_y(prim, y_lo, y_hi, y_prev, y_next, sofar, *scratch, shape, finish, after_slab)
    for part in range(shape.slabs):
        for c in copy(part):
            c.wait()


def shards(state, send_slots, recv_slots, owner_slot):
    slots, _, cells = state.shape
    moves = send_slots.shape[2]
    size_x, size_y, size_z = (lax.axis_size(axis) for axis in AXES)
    occ = owner_slot.shape[0] // (size_x * size_y * size_z)
    edge = round(cells ** (1 / 3))
    rows = cells // LANES
    groups = slots // SUB
    shape = Shape(rows, edge)
    units = NF * shape.slabs
    pieces = split_units(units, (2, 4, 6, 5, 3))
    firsts = split_units(units, (2, 4, 6, 8))

    bit_z = size_z.bit_length() - 2
    bit_y = bit_z + size_y.bit_length() - 1
    bit_x = bit_y + size_x.bit_length() - 1
    pair_bits = (bit_x, bit_y, bit_z)

    def swapped(value, level):
        mask = 2 ** pair_bits[level]
        pairs = [(source, source ^ mask) for source in range(lax.axis_size(AXES))]
        return lax.ppermute(value, AXES, pairs)

    rows_of_state = (
        state.reshape(groups, SUB, NF, rows, LANES)
        .transpose(2, 0, 3, 1, 4)
        .reshape(NF * groups * rows * SUB, LANES)
    )
    rows_of_state = pltpu.with_memory_space_constraint(rows_of_state, HBM)
    send_there = pltpu.with_memory_space_constraint(send_slots, HBM)
    device = lax.axis_index(AXES)
    own = lax.dynamic_slice(owner_slot, (device * occ,), (occ,))
    sizes = dict(slots=slots, moves=moves)

    def message(piece):
        begin, end = piece
        return jax.ShapeDtypeStruct((moves, (end - begin) * SUB, LANES), f32)

    state_rows = NF * groups * rows * SUB
    head = firsts[0]
    sent = [None] * len(firsts)
    sent[0] = pl.pallas_call(
        functools.partial(first_kernel, piece=head, rows=rows, **sizes),
        out_shape=message(head),
        in_specs=[whole(HBM)] * 2,
        out_specs=whole(VMEM),
        scratch_shapes=[
            SMEM(send_slots.shape, jnp.int32),
            VMEM(((head[1] - head[0]) * groups * SUB * SUB, LANES), f32),
            pltpu.SemaphoreType.DMA((1 + (head[1] - head[0]) * groups,)),
        ],
        compiler_params=params(),
        name="pack_first",
    )(send_there, rows_of_state)
    rows_of_state, tags, *sent[1:] = pl.pallas_call(
        functools.partial(load_kernel, pieces=firsts[1:], rows=rows, occ=occ, **sizes),
        out_shape=[
            jax.ShapeDtypeStruct((state_rows, LANES), f32),
            jax.ShapeDtypeStruct((2 * moves + occ,), jnp.int32),
        ]
        + [message(piece) for piece in firsts[1:]],
        in_specs=[whole(SMEM)] * 3 + [whole(HBM)],
        out_specs=[whole(VMEM), whole(SMEM)] + [whole(VMEM)] * len(firsts[1:]),
        scratch_shapes=[SMEM((slots + SUB,), jnp.int32), pltpu.SemaphoreType.DMA((NF,))],
        compiler_params=params(),
        name="load_state",
    )(send_slots, recv_slots, own, rows_of_state)

    cuts = (firsts, pieces, pieces)
    got = [[None] * len(cut) for cut in cuts]

    def holding(levels, begin, end):
        found = [
            ((level, piece), got[level][p])
            for level in levels
            for p, piece in enumerate(cuts[level])
            if piece[0] < end and piece[1] > begin
        ]
        return found

    def make(wanted, through):
        found = {}
        for level, p in wanted:
            for key, value in holding(range(level), *pieces[p]):
                found[key] = value
        plan = tuple((level, pieces[p]) for level, p in wanted)
        given, passed, made = len(found), len(through), len(wanted)
        outs = pl.pallas_call(
            functools.partial(
                pick_kernel, plan=plan, held=tuple(found), passed=passed, rows=rows, **sizes
            ),
            out_shape=[message(piece) for _, piece in plan]
            + [jax.ShapeDtypeStruct(t.shape, f32) for t in through],
            in_specs=[whole(SMEM)] + [whole(VMEM)] * (1 + given) + [whole(pl.ANY)] * passed,
            out_specs=[whole(VMEM)] * made + [whole(pl.ANY)] * passed,
            input_output_aliases={2 + given + i: made + i for i in range(passed)},
            compiler_params=params(),
            cost_estimate=cost(10**9, 10**9),
            name="pick_" + "_".join("%d%d" % w for w in wanted),
        )(tags, rows_of_state, *found.values(), *through)
        return outs[:made], outs[made:]

    steps = [
        ([(1, 0)], [2], []),
        ([(1, 1), (2, 0)], [3], []),
        ([(1, 2)], [], []),
        ([(1, 3), (1, 4), (2, 1)], [], [0]),
        ([(2, 2)], [], []),
        ([(2, 3)], [], [1]),
        ([(2, 4)], [], [2]),
    ]
    got[0][0] = swapped(sent[0], 0)
    got[0][1] = swapped(sent[1], 0)
    for wanted, leaving, awaited in steps:
        through = [sent[p] for p in leaving] + [got[2][p] for p in awaited]
        made, passed = make(wanted, through)
        for p, value in zip(leaving, passed):
            got[0][p] = swapped(value, 0)
        for (level, p), value in reversed(list(zip(wanted, made))):
            got[level][p] = swapped(value, level)
        for p, value in zip(awaited, passed[len(leaving) :]):
            got[2][p] = value

    grid = shape.grid()
    face_x, face_y, _, face_z, _ = shape.faces()
    part = [grid, grid, face_y, face_y, face_z, face_z, face_x]
    canvas = jax.ShapeDtypeStruct((state_rows, LANES), f32)
    full = pieces[-1][0] // NF

    def assemble(slabs, before):
        first = not before
        found = dict(holding(range(3), slabs[0] * NF, slabs[1] * NF))
        shapes = part + [canvas] * first
        fixed = 2 + len(found)
        return pl.pallas_call(
            functools.partial(
                assemble_kernel, held=tuple(found), slabs=slabs, occ=occ, shape=shape,
                first=first, **sizes,
            ),
            out_shape=shapes,
            in_specs=[whole(SMEM)] + [whole(VMEM)] * (1 + len(found) + len(before)),
            out_specs=[whole(VMEM)] * len(shapes),
            scratch_shapes=[VMEM((occ * NF * rows, LANES), f32)],
            input_output_aliases={fixed + i: i for i in range(len(before))},
            compiler_params=params(),
            name="assemble_%d" % slabs[0],
        )(tags, rows_of_state, *found.values(), *before)

    *made, blank = assemble((0, full), [])
    *made, x_faces = assemble((full, shape.slabs), made)
    made = made[:2] + [x_faces] + made[2:]

    def ring(value, axis, step):
        size = lax.axis_size(axis)
        return lax.ppermute(value, axis, [(i, (i + step) % size) for i in range(size)])

    def flux_sums(prim, x_faces, y_lo, y_hi, z_lo, z_hi):
        if size_x == 2:
            x_faces = ring(x_faces, "gx", 1)
        else:
            x_faces = jnp.stack([ring(x_faces[0], "gx", 1), ring(x_faces[1], "gx", -1)])
        y_prev, y_next = ring(y_hi, "gy", 1), ring(y_lo, "gy", -1)
        z_prev, z_next = ring(z_hi, "gz", 1), ring(z_lo, "gz", -1)
        ghost = VMEM((NF, rows, LANES), f32)
        work = [VMEM(grid.shape, f32)] * 3
        total = pl.pallas_call(
            functools.partial(sweep_z_kernel, shape=shape),
            out_shape=grid,
            in_specs=[whole(VMEM)] * 5,
            out_specs=whole(VMEM),
            scratch_shapes=[ghost] * 2 + work,
            compiler_params=params(),
            name="sweep_z",
        )(prim, z_lo, z_hi, z_prev, z_next)
        total = pl.pallas_call(
            functools.partial(sweep_x_kernel, shape=shape),
            out_shape=grid,
            in_specs=[whole(VMEM)] * 3,
            out_specs=whole(VMEM),
            scratch_shapes=[VMEM((NF, rows + 2 * shape.pad, SUB, LANES), f32)],
            input_output_aliases={2: 0},
            compiler_params=params(),
            name="sweep_x",
        )(prim, x_faces, total)
        return y_lo, y_hi, y_prev, y_next, total

    produced = [grid, grid] + shape.faces()
    scratch = [VMEM(face_y.shape, f32)] * 2 + [VMEM(grid.shape, f32)] * 4
    field, prim = made[0], made[1]
    sums = flux_sums(prim, *made[2:])
    made = pl.pallas_call(
        functools.partial(sweep_y_one_kernel, shape=shape),
        out_shape=produced,
        in_specs=[whole(VMEM)] * 7,
        out_specs=[whole(VMEM)] * len(produced),
        scratch_shapes=scratch,
        compiler_params=params(),
        name="sweep_y_one",
    )(field, prim, *sums)
    one, one_prim = made[0], made[1]
    sums = flux_sums(one_prim, *made[2:])
    out, _ = pl.pallas_call(
        functools.partial(sweep_y_two_kernel, shape=shape, occ=occ, groups=groups),
        out_shape=[canvas, canvas],
        in_specs=[whole(SMEM)] + [whole(VMEM)] * 9,
        out_specs=[whole(HBM), whole(VMEM)],
        scratch_shapes=scratch
        + [
            VMEM(grid.shape, f32),
            pltpu.SemaphoreType.DMA((shape.slabs, NF * groups)),
        ],
        input_output_aliases={9: 1},
        compiler_params=params(),
        name="sweep_y_two",
    )(own, field, one, one_prim, *sums, blank)
    return (
        out.reshape(NF, groups, rows, SUB, LANES)
        .transpose(1, 3, 0, 2, 4)
        .reshape(slots, NF, cells)
    )


def solution(mesh):
    placed = (
        P(AXES, None, None),
        P(None, AXES, None),
        P(None, AXES, None),
        P(),
    )
    return jax.shard_map(
        shards,
        mesh=mesh,
        in_specs=placed,
        out_specs=P(AXES, None, None),
        check_vma=False,
    )
```

```python
import functools

import jax
import jax.numpy as jnp
from jax import lax
from jax.experimental import pallas as pl
from jax.experimental.pallas import tpu as pltpu
from jax.sharding import PartitionSpec as P

gamma_ratio = 1.4
time_step = 0.05
LANES = 128
SUB = 8
NF = 5
FIELDS = range(NF)
AXES = ("gx", "gy", "gz")

VMEM = pltpu.VMEM
SMEM = pltpu.SMEM
HBM = pltpu.HBM
f32 = jnp.float32


def whole(space):
    return pl.BlockSpec(memory_space=space)


def params():
    return pltpu.CompilerParams(vmem_limit_bytes=16 * 1024 * 1024)


def cost(flops, moved):
    return pl.CostEstimate(flops=flops, bytes_accessed=moved, transcendentals=0)


def split_units(units, shares):
    ends = [units * sum(shares[: i + 1]) // sum(shares) for i in range(len(shares))]
    return list(zip([0] + ends[:-1], ends))


def from_state(state, tag, unit, slots, rows):
    slab, field = unit // NF, unit % NF
    groups = slots // SUB
    base = (tag // SUB) * (rows * SUB) + lax.rem(tag, SUB)
    start = base + (field * groups * rows + slab * SUB) * SUB
    return state[pl.ds(start, SUB, stride=SUB), :]


def pick(tag, unit, state, arrived, slots, rows, moves):
    value = from_state(state, jnp.minimum(tag, slots - 1), unit, slots, rows)
    for level, held in enumerate(arrived):
        base = slots + level * moves
        index = jnp.clip(tag - base, 0, moves - 1)
        for (begin, end), ref in held:
            if begin <= unit < end:
                at = (unit - begin) * SUB
                value = jnp.where(tag >= base, ref[index, at : at + SUB, :], value)
    return value


def first_kernel(send_hbm, state_hbm, out, send, held, sems, *, piece, slots, rows, moves):
    span = SUB * SUB
    groups = slots // SUB
    copies = [pltpu.make_async_copy(send_hbm, send, sems.at[0])]
    for unit in range(*piece):
        slab, field = unit // NF, unit % NF
        for g in range(groups):
            at = ((field * groups + g) * rows + slab * SUB) * SUB
            to = ((unit - piece[0]) * groups + g) * span
            copies.append(
                pltpu.make_async_copy(
                    state_hbm.at[pl.ds(at, span), :],
                    held.at[pl.ds(to, span), :],
                    sems.at[len(copies)],
                )
            )
    for c in copies:
        c.start()
    for c in copies:
        c.wait()
    for k in range(moves):
        slot = jnp.minimum(send[0, 0, k], slots - 1)
        base = (slot // SUB) * span + lax.rem(slot, SUB)
        for i in range(piece[1] - piece[0]):
            out[k, i * SUB : (i + 1) * SUB, :] = held[
                pl.ds(base + i * groups * span, SUB, stride=SUB), :
            ]


def rest_kernel(send, recv, own, state, tags, token, *refs, pieces, slots, rows, moves, occ):
    outs, where = refs[:-1], refs[-1]
    token[...] = jnp.zeros_like(token)
    for slot in range(slots):
        where[slot] = slot
    for level in range(3):
        if level:
            for k in range(moves):
                slot = jnp.minimum(send[level, 0, k], slots - 1)
                tags[(level - 1) * moves + k] = where[slot]
        for k in range(moves):
            where[recv[level, 0, k]] = slots + level * moves + k
    for b in range(occ):
        tags[2 * moves + b] = where[own[b]]
    for k in range(moves):
        slot = jnp.minimum(send[0, 0, k], slots - 1)
        for (begin, end), out in zip(pieces, outs):
            for unit in range(begin, end):
                at = (unit - begin) * SUB
                out[k, at : at + SUB, :] = from_state(state, slot, unit, slots, rows)


def group_levels(refs, held):
    levels = [[], [], []]
    for ref, (level, piece) in zip(refs, held):
        levels[level].append((piece, ref))
    return levels


def pick_kernel(tags, state, *refs, plan, held, passed, slots, rows, moves):
    given = len(held)
    arrived = group_levels(refs[:given], held)
    outs = refs[given + passed :]
    for (level, (begin, end)), out in zip(plan, outs):
        for k in range(moves):
            tag = tags[(level - 1) * moves + k]
            for unit in range(begin, end):
                at = (unit - begin) * SUB
                out[k, at : at + SUB, :] = pick(
                    tag, unit, state, arrived[:level], slots, rows, moves
                )


def primitives(cons):
    density = cons[0]
    inverse = 1.0 / density
    vel = [cons[1] * inverse, cons[2] * inverse, cons[3] * inverse]
    kinetic = cons[1] * vel[0] + cons[2] * vel[1] + cons[3] * vel[2]
    pressure = (gamma_ratio - 1.0) * (cons[4] - 0.5 * kinetic)
    return [density, vel[0], vel[1], vel[2], pressure]


def half_minmod(lower, upper):
    both = jnp.maximum(0.0, jnp.minimum(lower, upper)) + jnp.minimum(
        0.0, jnp.maximum(lower, upper)
    )
    return 0.5 * both


def half_slopes(before, here, after):
    return [half_minmod(h - b, a - h) for b, h, a in zip(before, here, after)]


def plus(a, b):
    return [x + y for x, y in zip(a, b)]


def minus(a, b):
    return [x - y for x, y in zip(a, b)]


def side_terms(prim, normal):
    density, vel, pressure = prim[0], prim[1:4], prim[4]
    along = vel[normal]
    mom = [density * v for v in vel]
    kinetic = mom[0] * vel[0] + mom[1] * vel[1] + mom[2] * vel[2]
    energy = pressure * (1.0 / (gamma_ratio - 1.0)) + 0.5 * kinetic
    flux = [m * along for m in mom]
    flux[normal] = flux[normal] + pressure
    scaled = gamma_ratio * pressure
    speed = jnp.abs(along) + scaled * lax.rsqrt(scaled * density)
    return [density] + mom + [energy], [mom[normal]] + flux + [(energy + pressure) * along], speed


def twice_flux(left, right, normal):
    left_cons, left_flux, left_speed = side_terms(left, normal)
    right_cons, right_flux, right_speed = side_terms(right, normal)
    speed = jnp.maximum(left_speed, right_speed)
    return [
        (fl + fr) - speed * (ur - ul)
        for fl, fr, ul, ur in zip(left_flux, right_flux, left_cons, right_cons)
    ]


def lane_of():
    return lax.broadcasted_iota(jnp.int32, (SUB, LANES), 1)


def sub_of():
    return lax.broadcasted_iota(jnp.int32, (SUB, LANES), 0)


def lane_roll(value, amount):
    amount = amount % LANES
    return value if amount == 0 else pltpu.roll(value, amount, 1)


class Shape:
    def __init__(self, rows, edge):
        self.rows, self.edge = rows, edge
        self.halves = rows // edge
        self.width = 2 * edge
        self.fit = LANES // self.width
        self.slabs = rows // SUB
        self.pad = 2 * self.halves

    def at(self, f, row):
        start = SUB + (f * self.rows + row) * SUB
        return pl.ds(start if isinstance(start, int) else pl.multiple_of(start, SUB), SUB)

    def across(self, f, slab, sub):
        return pl.ds(SUB + (f * self.rows + slab * SUB) * SUB + sub, SUB, stride=SUB)

    def beside(self, f, row, step):
        return pl.ds(SUB + (f * self.rows + row) * SUB + step, SUB)

    def grid(self):
        return jax.ShapeDtypeStruct(((NF * self.rows + 2) * SUB, LANES), f32)

    def faces(self):
        x = jax.ShapeDtypeStruct((2, NF, self.pad, SUB, LANES), f32)
        y = jax.ShapeDtypeStruct((NF, self.edge // self.fit, SUB, LANES), f32)
        z = jax.ShapeDtypeStruct((NF, self.rows, LANES), f32)
        return [x, y, y, z, z]


def send_slab(shape, prim, y_lo, y_hi, z_lo, z_hi, slab):
    lane = lane_of()
    halves = shape.halves
    for f in FIELDS:
        lo = hi = None
        for k in range(shape.fit):
            row = slab * SUB + k * halves
            below = lane_roll(prim[shape.at(f, row), :], shape.width * k)
            above = lane_roll(prim[shape.at(f, row + halves - 1), :], shape.width * (k + 1))
            if lo is None:
                lo, hi = below, above
            else:
                mine = lane >= shape.width * k
                lo = jnp.where(mine, below, lo)
                hi = jnp.where(mine, above, hi)
        y_lo[f, slab] = lo
        y_hi[f, slab] = hi
        to = pl.ds(slab * SUB, SUB) if isinstance(slab, int) else pl.ds(
            pl.multiple_of(slab * SUB, SUB), SUB
        )
        z_lo[f, to, :] = prim[shape.across(f, slab, 0), :]
        z_hi[f, to, :] = prim[shape.across(f, slab, SUB - 1), :]


def send_x(shape, prim, faces, low=True, high=True):
    for f in FIELDS:
        for i in range(shape.pad):
            if high:
                faces[0, f, i] = prim[shape.at(f, shape.rows - shape.pad + i), :]
            if low:
                faces[1, f, i] = prim[shape.at(f, i), :]


def assemble_kernel(tags, state, *refs, held, slabs, slots, moves, occ, shape, first):
    given = len(held)
    arrived = group_levels(refs[:given], held)
    outs = refs[given + (0 if first else 7) :]
    field, prim, y_lo, y_hi, z_lo, z_hi, x_faces = outs[:7]
    blocks = outs[-1]
    units = NF * shape.slabs
    for b in range(occ):
        tag = tags[2 * moves + b]
        for unit in range(slabs[0] * NF, slabs[1] * NF):
            at = (b * units + unit) * SUB
            blocks[at : at + SUB, :] = pick(tag, unit, state, arrived, slots, shape.rows, moves)
    for slab in range(*slabs):
        for i in range(SUB):
            row = slab * SUB + i
            cons = [
                blocks[pl.ds((slab * NF + f) * SUB + i, occ, stride=units * SUB), :] for f in FIELDS
            ]
            for f, (c, w) in enumerate(zip(cons, primitives(cons))):
                field[shape.at(f, row), :] = c
                prim[shape.at(f, row), :] = w
        send_slab(shape, prim, y_lo, y_hi, z_lo, z_hi, slab)
    if first:
        canvas = outs[7]

        def clear(i, carry):
            for c in range(canvas.shape[0]):
                canvas[c, pl.ds(pl.multiple_of(i * SUB, SUB), SUB), :] = jnp.zeros((SUB, LANES), f32)
            return carry

        lax.fori_loop(0, canvas.shape[1] // SUB, clear, 0)
    send_x(shape, prim, x_faces, low=first, high=not first)


def sweep_z_kernel(prim, z_lo, z_hi, z_prev, z_next, total, flux_z, right_z, left, right, flux, *, shape):
    edge, rows = shape.edge, shape.rows

    def ghost(a, carry):
        at = pl.ds(pl.multiple_of(a * SUB, SUB), SUB)
        low = [z_lo[f, at, :] for f in FIELDS]
        high = [z_hi[f, at, :] for f in FIELDS]
        prev = [z_prev[f, at, :] for f in FIELDS]
        after = [z_next[f, at, :] for f in FIELDS]
        below = [lane_roll(v, -(edge - 1)) for v in prev]
        before = [lane_roll(v, -(edge - 2)) for v in prev]
        second = [lane_roll(v, -1) for v in low]
        lefts = plus(below, half_slopes(before, below, low))
        rights = minus(low, half_slopes(below, low, second))
        fluxes = twice_flux(lefts, rights, 2)
        last = [lane_roll(v, -(edge - 1)) for v in high]
        beyond = [lane_roll(v, -1) for v in after]
        over = minus(after, half_slopes(last, after, beyond))
        for f in FIELDS:
            flux_z[f, at, :] = lane_roll(fluxes[f], edge - 1)
            right_z[f, at, :] = over[f]
        return carry

    lax.fori_loop(0, shape.slabs, ghost, 0)
    lane = lane_of()
    z_of = lax.rem(lane, edge)
    sub = sub_of()
    first_z, last_z = z_of == 0, z_of == edge - 1
    first_sub, last_sub = sub == 0, sub == SUB - 1
    higher = lane - z_of + lax.rem(z_of + 1, edge)
    lower = lane - z_of + lax.rem(z_of + edge - 1, edge)

    def insert(ref, f, row):
        return jnp.broadcast_to(ref[f, pl.ds(row, 1), :], (SUB, LANES))

    def up(ref, value, f, row, ghosts):
        across = ref[shape.beside(f, row, 1), :]
        across = jnp.where(last_sub, insert(ghosts, f, row), across)
        return jnp.take_along_axis(jnp.where(first_z, across, value), higher, axis=1)

    def down(ref, value, f, row, ghosts):
        across = ref[shape.beside(f, row, -1), :]
        across = jnp.where(first_sub, insert(ghosts, f, row), across)
        return jnp.take_along_axis(jnp.where(last_z, across, value), lower, axis=1)

    def slopes(slab, carry):
        for i in range(SUB):
            row = slab * SUB + i
            for f in FIELDS:
                at = shape.at(f, row)
                mine = prim[at, :]
                shift = half_minmod(
                    mine - down(prim, mine, f, row, z_prev), up(prim, mine, f, row, z_next) - mine
                )
                left[at, :] = mine + shift
                right[at, :] = mine - shift
        return carry

    def fluxes(slab, carry):
        for i in range(SUB):
            row = slab * SUB + i
            lefts = [left[shape.at(f, row), :] for f in FIELDS]
            rights = [up(right, right[shape.at(f, row), :], f, row, right_z) for f in FIELDS]
            for f, value in enumerate(twice_flux(lefts, rights, 2)):
                flux[shape.at(f, row), :] = value
        return carry

    def differences(slab, carry):
        for i in range(SUB):
            row = slab * SUB + i
            for f in FIELDS:
                at = shape.at(f, row)
                mine = flux[at, :]
                total[at, :] = mine - down(flux, mine, f, row, flux_z)
        return carry

    lax.fori_loop(0, shape.slabs, slopes, 0)
    lax.fori_loop(0, shape.slabs, fluxes, 0)
    lax.fori_loop(0, shape.slabs, differences, 0)


def sweep_x_kernel(prim, x_faces, sofar, total, wide, *, shape):
    rows, halves, pad = shape.rows, shape.halves, shape.pad
    for f in FIELDS:
        for i in range(pad):
            wide[f, i] = x_faces[0, f, i]
            wide[f, pad + rows + i] = x_faces[1, f, i]

        def copy(r, carry, f=f):
            wide[f, pad + r] = prim[shape.at(f, r), :]
            return carry

        lax.fori_loop(0, rows, copy, 0, unroll=8)

    for h in range(halves):
        cells = [[wide[f, i * halves + h] for f in FIELDS] for i in range(4)]
        left = plus(cells[1], half_slopes(*cells[0:3]))
        shift = half_slopes(*cells[1:4])
        flux = twice_flux(left, minus(cells[2], shift), 0)
        keep = plus(cells[2], shift)

        def body(x, carry, h=h):
            below, left = carry
            here, one, two = (
                [wide[f, pad + (x + i) * halves + h] for f in FIELDS] for i in range(3)
            )
            shift = half_slopes(here, one, two)
            flux = twice_flux(left, minus(one, shift), 0)
            row = x * halves + h
            for f in FIELDS:
                at = shape.at(f, row)
                total[at, :] = sofar[at, :] + (flux[f] - below[f])
            return flux, plus(one, shift)

        lax.fori_loop(0, shape.edge, body, (flux, keep), unroll=4)


def sweep_y(prim, y_lo, y_hi, y_prev, y_next, sofar, ghost_prim, ghost_flux, left, right, flux, turned,
            shape, finish, after_slab):
    edge, halves, fit, width = shape.edge, shape.halves, shape.fit, shape.width
    lane = lane_of()
    upper = lax.rem(lane, width) >= edge

    def ghost(q, carry):
        low = [y_lo[f, q] for f in FIELDS]
        high = [y_hi[f, q] for f in FIELDS]
        below = [y_prev[f, q] for f in FIELDS]
        after = [y_next[f, q] for f in FIELDS]
        before = [lane_roll(v, edge) for v in below]
        first = [lane_roll(v, edge) for v in low]
        lefts = plus(below, half_slopes(before, below, first))
        rights = minus(first, half_slopes(below, first, low))
        fluxes = twice_flux(lefts, rights, 1)
        last = [lane_roll(v, -edge) for v in high]
        beyond = [lane_roll(v, -edge) for v in after]
        over = minus(after, half_slopes(last, after, beyond))
        for f in FIELDS:
            ghost_prim[f, q] = jnp.where(upper, below[f], after[f])
            ghost_flux[f, q] = jnp.where(upper, fluxes[f], over[f])
        return carry

    lax.fori_loop(0, edge // fit, ghost, 0)
    top_lanes = lane >= LANES - edge
    low_lanes = lane < edge

    def up(values, insert):
        rolled = [lane_roll(v, -edge) for v in values]
        follow = rolled[1:] + [insert]
        return [jnp.where(top_lanes, n, r) for r, n in zip(rolled, follow)]

    def down(values, insert):
        rolled = [lane_roll(v, edge) for v in values]
        lead = [insert] + rolled[:-1]
        return [jnp.where(low_lanes, n, r) for r, n in zip(rolled, lead)]

    def each(q):
        for k in range(fit):
            yield -(width * k + edge), (q * fit + k) * halves

    def slopes(q, carry):
        for turn, base in each(q):
            for f in FIELDS:
                mine = [prim[shape.at(f, base + h), :] for h in range(halves)]
                ghost = lane_roll(ghost_prim[f, q], turn)
                over, under = up(mine, ghost), down(mine, ghost)
                for h in range(halves):
                    shift = half_minmod(mine[h] - under[h], over[h] - mine[h])
                    left[shape.at(f, base + h), :] = mine[h] + shift
                    right[shape.at(f, base + h), :] = mine[h] - shift
        return carry

    def fluxes(q, carry):
        for turn, base in each(q):
            rights = []
            for f in FIELDS:
                mine = [right[shape.at(f, base + h), :] for h in range(halves)]
                ghost = lane_roll(ghost_flux[f, q], turn)
                turned[shape.at(f, base), :] = ghost
                rights.append(up(mine, ghost))
            for h in range(halves):
                lefts = [left[shape.at(f, base + h), :] for f in FIELDS]
                result = twice_flux(lefts, [rights[f][h] for f in FIELDS], 1)
                for f in FIELDS:
                    flux[shape.at(f, base + h), :] = result[f]
        return carry

    def differences(q, carry):
        for turn, base in each(q):
            total = [[None] * NF for _ in range(halves)]
            for f in FIELDS:
                mine = [flux[shape.at(f, base + h), :] for h in range(halves)]
                under = down(mine, turned[shape.at(f, base), :])
                for h in range(halves):
                    total[h][f] = sofar[shape.at(f, base + h), :] + (mine[h] - under[h])
            for h in range(halves):
                finish(base + h, total[h])
        after_slab(q)
        return carry

    lax.fori_loop(0, edge // fit, slopes, 0)
    lax.fori_loop(0, edge // fit, fluxes, 0)
    lax.fori_loop(0, edge // fit, differences, 0)


def sweep_y_one_kernel(field, prim, y_lo, y_hi, y_prev, y_next, sofar, *refs, shape):
    one, one_prim, x_faces, out_y_lo, out_y_hi, z_lo, z_hi = refs[:7]

    def finish(row, total):
        cons = [field[shape.at(f, row), :] - (0.5 * time_step) * total[f] for f in FIELDS]
        for f, (c, w) in enumerate(zip(cons, primitives(cons))):
            one[shape.at(f, row), :] = c
            one_prim[shape.at(f, row), :] = w

    def after_slab(q):
        send_slab(shape, one_prim, out_y_lo, out_y_hi, z_lo, z_hi, q)

    sweep_y(prim, y_lo, y_hi, y_prev, y_next, sofar, *refs[7:], shape, finish, after_slab)
    send_x(shape, one_prim, x_faces)


def sweep_y_two_kernel(own, field, one, prim, y_lo, y_hi, y_prev, y_next, sofar, zeros, out,
                       canvas, *refs, shape, occ, groups):
    scratch, (result, sems) = refs[:6], refs[6:]
    rows = shape.rows
    span = SUB * SUB

    def finish(row, total):
        for f in FIELDS:
            at = shape.at(f, row)
            advanced = one[at, :] - (0.5 * time_step) * total[f]
            result[at, :] = 0.5 * field[at, :] + 0.5 * advanced

    def copy(part):
        begin = part * span if isinstance(part, int) else pl.multiple_of(part * span, span)
        at = pl.ds(begin, span)
        return pltpu.make_async_copy(canvas.at[:, at, :], out.at[:, at, :], sems.at[part])

    def after_slab(q):
        for b in range(occ):
            slot = own[b]
            to = pl.ds(q * span + lax.rem(slot, SUB), SUB, stride=SUB)
            for f in FIELDS:
                canvas[f * groups + slot // SUB, to, :] = result[shape.across(f, q, b), :]
        copy(q).start()

    sweep_y(prim, y_lo, y_hi, y_prev, y_next, sofar, *scratch, shape, finish, after_slab)
    for part in range(shape.slabs):
        copy(part).wait()


def shards(state, send_slots, recv_slots, owner_slot):
    slots, _, cells = state.shape
    moves = send_slots.shape[2]
    size_x, size_y, size_z = (lax.axis_size(axis) for axis in AXES)
    occ = owner_slot.shape[0] // (size_x * size_y * size_z)
    edge = round(cells ** (1 / 3))
    rows = cells // LANES
    groups = slots // SUB
    shape = Shape(rows, edge)
    units = NF * shape.slabs
    pieces = split_units(units, (4, 5, 5, 4, 2))
    firsts = split_units(units, (4, 5, 5, 6))

    bit_z = size_z.bit_length() - 2
    bit_y = bit_z + size_y.bit_length() - 1
    bit_x = bit_y + size_x.bit_length() - 1
    pair_bits = (bit_x, bit_y, bit_z)

    def swapped(value, level):
        mask = 2 ** pair_bits[level]
        pairs = [(source, source ^ mask) for source in range(lax.axis_size(AXES))]
        return lax.ppermute(value, AXES, pairs)

    rows_of_state = (
        state.reshape(groups, SUB, NF, rows, LANES)
        .transpose(2, 0, 3, 1, 4)
        .reshape(NF * groups * rows * SUB, LANES)
    )
    state_there = pltpu.with_memory_space_constraint(rows_of_state, HBM)
    send_there = pltpu.with_memory_space_constraint(send_slots, HBM)
    device = lax.axis_index(AXES)
    own = lax.dynamic_slice(owner_slot, (device * occ,), (occ,))
    sizes = dict(slots=slots, moves=moves)

    def message(piece):
        begin, end = piece
        return jax.ShapeDtypeStruct((moves, (end - begin) * SUB, LANES), f32)

    head = firsts[0]
    sent = [None] * len(firsts)
    sent[0] = pl.pallas_call(
        functools.partial(first_kernel, piece=head, rows=rows, **sizes),
        out_shape=message(head),
        in_specs=[whole(HBM)] * 2,
        out_specs=whole(VMEM),
        scratch_shapes=[
            SMEM(send_slots.shape, jnp.int32),
            VMEM(((head[1] - head[0]) * groups * SUB * SUB, LANES), f32),
            pltpu.SemaphoreType.DMA((1 + (head[1] - head[0]) * groups,)),
        ],
        compiler_params=params(),
        name="pack_first",
    )(send_there, state_there)
    tags, token, *sent[1:] = pl.pallas_call(
        functools.partial(rest_kernel, pieces=firsts[1:], rows=rows, occ=occ, **sizes),
        out_shape=[
            jax.ShapeDtypeStruct((2 * moves + occ,), jnp.int32),
            jax.ShapeDtypeStruct((SUB, LANES), f32),
        ]
        + [message(piece) for piece in firsts[1:]],
        in_specs=[whole(SMEM)] * 3 + [whole(VMEM)],
        out_specs=[whole(SMEM)] + [whole(VMEM)] * len(firsts),
        scratch_shapes=[SMEM((slots + SUB,), jnp.int32)],
        compiler_params=params(),
        name="pack_rest",
    )(send_slots, recv_slots, own, rows_of_state)

    cuts = (firsts, pieces, pieces)
    got = [[None] * len(cut) for cut in cuts]

    def holding(levels, begin, end):
        found = [
            ((level, piece), got[level][p])
            for level in levels
            for p, piece in enumerate(cuts[level])
            if piece[0] < end and piece[1] > begin
        ]
        return found

    def make(wanted, through):
        found = {}
        for level, p in wanted:
            for key, value in holding(range(level), *pieces[p]):
                found[key] = value
        plan = tuple((level, pieces[p]) for level, p in wanted)
        given, passed, made = len(found), len(through), len(wanted)
        outs = pl.pallas_call(
            functools.partial(
                pick_kernel, plan=plan, held=tuple(found), passed=passed, rows=rows, **sizes
            ),
            out_shape=[message(piece) for _, piece in plan]
            + [jax.ShapeDtypeStruct(t.shape, f32) for t in through],
            in_specs=[whole(SMEM)] + [whole(VMEM)] * (1 + given) + [whole(pl.ANY)] * passed,
            out_specs=[whole(VMEM)] * made + [whole(pl.ANY)] * passed,
            input_output_aliases={2 + given + i: made + i for i in range(passed)},
            compiler_params=params(),
            cost_estimate=cost(10**9, 10**9),
            name="pick_" + "_".join("%d%d" % w for w in wanted),
        )(tags, rows_of_state, *found.values(), *through)
        return outs[:made], outs[made:]

    steps = [
        ([(1, 0)], [2], []),
        ([(1, 1)], [3], []),
        ([(1, 2), (2, 0)], [], []),
        ([(1, 3), (2, 1)], [], []),
        ([(1, 4), (2, 2)], [], [0]),
        ([(2, 3)], [], [1]),
        ([(2, 4)], [], [2]),
    ]
    got[0][0] = swapped(sent[0], 0)
    got[0][1] = swapped(sent[1], 0)
    for wanted, leaving, awaited in steps:
        through = [token] + [sent[p] for p in leaving] + [got[2][p] for p in awaited]
        made, (token, *passed) = make(wanted, through)
        for p, value in zip(leaving, passed):
            got[0][p] = swapped(value, 0)
        for (level, p), value in reversed(list(zip(wanted, made))):
            got[level][p] = swapped(value, level)
        for p, value in zip(awaited, passed[len(leaving) :]):
            got[2][p] = value

    grid = shape.grid()
    face_x, face_y, _, face_z, _ = shape.faces()
    part = [grid, grid, face_y, face_y, face_z, face_z, face_x]
    canvas = jax.ShapeDtypeStruct((NF * groups, rows * SUB, LANES), f32)
    full = pieces[-1][0] // NF

    def assemble(slabs, before):
        first = not before
        found = dict(holding(range(3), slabs[0] * NF, slabs[1] * NF))
        shapes = part + [canvas] * first
        fixed = 2 + len(found)
        return pl.pallas_call(
            functools.partial(
                assemble_kernel, held=tuple(found), slabs=slabs, occ=occ, shape=shape,
                first=first, **sizes,
            ),
            out_shape=shapes,
            in_specs=[whole(SMEM)] + [whole(VMEM)] * (1 + len(found) + len(before)),
            out_specs=[whole(VMEM)] * len(shapes),
            scratch_shapes=[VMEM((occ * NF * rows, LANES), f32)],
            input_output_aliases={fixed + i: i for i in range(len(before))},
            compiler_params=params(),
            name="assemble_%d" % slabs[0],
        )(tags, rows_of_state, *found.values(), *before)

    *made, blank = assemble((0, full), [])
    *made, x_faces = assemble((full, shape.slabs), made)
    made = made[:2] + [x_faces] + made[2:]

    def ring(value, axis, step):
        size = lax.axis_size(axis)
        return lax.ppermute(value, axis, [(i, (i + step) % size) for i in range(size)])

    def flux_sums(prim, x_faces, y_lo, y_hi, z_lo, z_hi):
        if size_x == 2:
            x_faces = ring(x_faces, "gx", 1)
        else:
            x_faces = jnp.stack([ring(x_faces[0], "gx", 1), ring(x_faces[1], "gx", -1)])
        y_prev, y_next = ring(y_hi, "gy", 1), ring(y_lo, "gy", -1)
        z_prev, z_next = ring(z_hi, "gz", 1), ring(z_lo, "gz", -1)
        ghost = VMEM((NF, rows, LANES), f32)
        work = [VMEM(grid.shape, f32)] * 3
        total = pl.pallas_call(
            functools.partial(sweep_z_kernel, shape=shape),
            out_shape=grid,
            in_specs=[whole(VMEM)] * 5,
            out_specs=whole(VMEM),
            scratch_shapes=[ghost] * 2 + work,
            compiler_params=params(),
            name="sweep_z",
        )(prim, z_lo, z_hi, z_prev, z_next)
        total = pl.pallas_call(
            functools.partial(sweep_x_kernel, shape=shape),
            out_shape=grid,
            in_specs=[whole(VMEM)] * 3,
            out_specs=whole(VMEM),
            scratch_shapes=[VMEM((NF, rows + 2 * shape.pad, SUB, LANES), f32)],
            input_output_aliases={2: 0},
            compiler_params=params(),
            name="sweep_x",
        )(prim, x_faces, total)
        return y_lo, y_hi, y_prev, y_next, total

    produced = [grid, grid] + shape.faces()
    scratch = [VMEM(face_y.shape, f32)] * 2 + [VMEM(grid.shape, f32)] * 4
    field, prim = made[0], made[1]
    sums = flux_sums(prim, *made[2:])
    made = pl.pallas_call(
        functools.partial(sweep_y_one_kernel, shape=shape),
        out_shape=produced,
        in_specs=[whole(VMEM)] * 7,
        out_specs=[whole(VMEM)] * len(produced),
        scratch_shapes=scratch,
        compiler_params=params(),
        name="sweep_y_one",
    )(field, prim, *sums)
    one, one_prim = made[0], made[1]
    sums = flux_sums(one_prim, *made[2:])
    out, _ = pl.pallas_call(
        functools.partial(sweep_y_two_kernel, shape=shape, occ=occ, groups=groups),
        out_shape=[canvas, canvas],
        in_specs=[whole(SMEM)] + [whole(VMEM)] * 9,
        out_specs=[whole(HBM), whole(VMEM)],
        scratch_shapes=scratch
        + [
            VMEM(grid.shape, f32),
            pltpu.SemaphoreType.DMA((shape.slabs,)),
        ],
        input_output_aliases={9: 1},
        compiler_params=params(),
        name="sweep_y_two",
    )(own, field, one, one_prim, *sums, blank)
    return (
        out.reshape(NF, groups, rows, SUB, LANES)
        .transpose(1, 3, 0, 2, 4)
        .reshape(slots, NF, cells)
    )


def solution(mesh):
    placed = (
        P(AXES, None, None),
        P(None, AXES, None),
        P(None, AXES, None),
        P(),
    )
    return jax.shard_map(
        shards,
        mesh=mesh,
        in_specs=placed,
        out_specs=P(AXES, None, None),
        check_vma=False,
    )
```

```python
import functools

import jax
import jax.numpy as jnp
from jax import lax
from jax.experimental import pallas as pl
from jax.experimental.pallas import tpu as pltpu
from jax.sharding import PartitionSpec as P

gamma_ratio = 1.4
time_step = 0.05
LANES = 128
SUB = 8
NF = 5
FIELDS = range(NF)
AXES = ("gx", "gy", "gz")

VMEM = pltpu.VMEM
SMEM = pltpu.SMEM
HBM = pltpu.HBM
f32 = jnp.float32


def whole(space):
    return pl.BlockSpec(memory_space=space)


def params():
    return pltpu.CompilerParams(vmem_limit_bytes=16 * 1024 * 1024)


def cost(flops, moved):
    return pl.CostEstimate(flops=flops, bytes_accessed=moved, transcendentals=0)


def split_units(units, shares):
    ends = [units * sum(shares[: i + 1]) // sum(shares) for i in range(len(shares))]
    return list(zip([0] + ends[:-1], ends))


def from_state(state, tag, unit, slots, rows):
    slab, field = unit // NF, unit % NF
    groups = slots // SUB
    base = (tag // SUB) * (rows * SUB) + lax.rem(tag, SUB)
    start = base + (field * groups * rows + slab * SUB) * SUB
    return state[pl.ds(start, SUB, stride=SUB), :]


def pick(tag, unit, state, arrived, slots, rows, moves):
    value = from_state(state, jnp.minimum(tag, slots - 1), unit, slots, rows)
    for level, held in enumerate(arrived):
        base = slots + level * moves
        index = jnp.clip(tag - base, 0, moves - 1)
        for (begin, end), ref in held:
            if begin <= unit < end:
                at = (unit - begin) * SUB
                value = jnp.where(tag >= base, ref[index, at : at + SUB, :], value)
    return value


def first_kernel(send_hbm, state_hbm, out, send, held, sems, *, piece, slots, rows, moves):
    span = SUB * SUB
    groups = slots // SUB
    copies = [pltpu.make_async_copy(send_hbm, send, sems.at[0])]
    for unit in range(*piece):
        slab, field = unit // NF, unit % NF
        for g in range(groups):
            at = ((field * groups + g) * rows + slab * SUB) * SUB
            to = ((unit - piece[0]) * groups + g) * span
            copies.append(
                pltpu.make_async_copy(
                    state_hbm.at[pl.ds(at, span), :],
                    held.at[pl.ds(to, span), :],
                    sems.at[len(copies)],
                )
            )
    for c in copies:
        c.start()
    for c in copies:
        c.wait()
    for k in range(moves):
        slot = jnp.minimum(send[0, 0, k], slots - 1)
        base = (slot // SUB) * span + lax.rem(slot, SUB)
        for i in range(piece[1] - piece[0]):
            out[k, i * SUB : (i + 1) * SUB, :] = held[
                pl.ds(base + i * groups * span, SUB, stride=SUB), :
            ]


def rest_kernel(send, recv, own, state, tags, token, *refs, pieces, slots, rows, moves, occ):
    outs, where = refs[:-1], refs[-1]
    token[...] = jnp.zeros_like(token)
    for slot in range(slots):
        where[slot] = slot
    for level in range(3):
        if level:
            for k in range(moves):
                slot = jnp.minimum(send[level, 0, k], slots - 1)
                tags[(level - 1) * moves + k] = where[slot]
        for k in range(moves):
            where[recv[level, 0, k]] = slots + level * moves + k
    for b in range(occ):
        tags[2 * moves + b] = where[own[b]]
    for k in range(moves):
        slot = jnp.minimum(send[0, 0, k], slots - 1)
        for (begin, end), out in zip(pieces, outs):
            for unit in range(begin, end):
                at = (unit - begin) * SUB
                out[k, at : at + SUB, :] = from_state(state, slot, unit, slots, rows)


def group_levels(refs, held):
    levels = [[], [], []]
    for ref, (level, piece) in zip(refs, held):
        levels[level].append((piece, ref))
    return levels


def pick_kernel(tags, state, *refs, plan, held, passed, slots, rows, moves):
    given = len(held)
    arrived = group_levels(refs[:given], held)
    outs = refs[given + passed :]
    for (level, (begin, end)), out in zip(plan, outs):
        for k in range(moves):
            tag = tags[(level - 1) * moves + k]
            for unit in range(begin, end):
                at = (unit - begin) * SUB
                out[k, at : at + SUB, :] = pick(
                    tag, unit, state, arrived[:level], slots, rows, moves
                )


def primitives(cons):
    density = cons[0]
    inverse = 1.0 / density
    vel = [cons[1] * inverse, cons[2] * inverse, cons[3] * inverse]
    kinetic = cons[1] * vel[0] + cons[2] * vel[1] + cons[3] * vel[2]
    pressure = (gamma_ratio - 1.0) * (cons[4] - 0.5 * kinetic)
    return [density, vel[0], vel[1], vel[2], pressure]


def half_minmod(lower, upper):
    both = jnp.maximum(0.0, jnp.minimum(lower, upper)) + jnp.minimum(
        0.0, jnp.maximum(lower, upper)
    )
    return 0.5 * both


def half_slopes(before, here, after):
    return [half_minmod(h - b, a - h) for b, h, a in zip(before, here, after)]


def plus(a, b):
    return [x + y for x, y in zip(a, b)]


def minus(a, b):
    return [x - y for x, y in zip(a, b)]


def side_terms(prim, normal):
    density, vel, pressure = prim[0], prim[1:4], prim[4]
    along = vel[normal]
    mom = [density * v for v in vel]
    kinetic = mom[0] * vel[0] + mom[1] * vel[1] + mom[2] * vel[2]
    energy = pressure * (1.0 / (gamma_ratio - 1.0)) + 0.5 * kinetic
    flux = [m * along for m in mom]
    flux[normal] = flux[normal] + pressure
    scaled = gamma_ratio * pressure
    speed = jnp.abs(along) + scaled * lax.rsqrt(scaled * density)
    return [density] + mom + [energy], [mom[normal]] + flux + [(energy + pressure) * along], speed


def twice_flux(left, right, normal):
    left_cons, left_flux, left_speed = side_terms(left, normal)
    right_cons, right_flux, right_speed = side_terms(right, normal)
    speed = jnp.maximum(left_speed, right_speed)
    return [
        (fl + fr) - speed * (ur - ul)
        for fl, fr, ul, ur in zip(left_flux, right_flux, left_cons, right_cons)
    ]


def lane_of():
    return lax.broadcasted_iota(jnp.int32, (SUB, LANES), 1)


def sub_of():
    return lax.broadcasted_iota(jnp.int32, (SUB, LANES), 0)


def lane_roll(value, amount):
    amount = amount % LANES
    return value if amount == 0 else pltpu.roll(value, amount, 1)


class Shape:
    def __init__(self, rows, edge):
        self.rows, self.edge = rows, edge
        self.halves = rows // edge
        self.width = 2 * edge
        self.fit = LANES // self.width
        self.slabs = rows // SUB
        self.pad = 2 * self.halves

    def at(self, f, row):
        start = (f * self.rows + row) * SUB
        return pl.ds(start if isinstance(start, int) else pl.multiple_of(start, SUB), SUB)

    def across(self, f, slab, sub):
        return pl.ds((f * self.rows + slab * SUB) * SUB + sub, SUB, stride=SUB)

    def grid(self):
        return jax.ShapeDtypeStruct((NF * self.rows * SUB, LANES), f32)

    def faces(self):
        x = jax.ShapeDtypeStruct((2, NF, self.pad, SUB, LANES), f32)
        y = jax.ShapeDtypeStruct((NF, self.edge // self.fit, SUB, LANES), f32)
        z = jax.ShapeDtypeStruct((NF, self.rows, LANES), f32)
        return [x, y, y, z, z]


def in_turn(count, *phases):
    for step in range(count + len(phases) - 1):
        for late, phase in enumerate(phases):
            if 0 <= step - late < count:
                phase(step - late)


def send_slab(shape, prim, y_lo, y_hi, z_lo, z_hi, slab):
    lane = lane_of()
    halves = shape.halves
    for f in FIELDS:
        lo = hi = None
        for k in range(shape.fit):
            row = slab * SUB + k * halves
            below = lane_roll(prim[shape.at(f, row), :], shape.width * k)
            above = lane_roll(prim[shape.at(f, row + halves - 1), :], shape.width * (k + 1))
            if lo is None:
                lo, hi = below, above
            else:
                mine = lane >= shape.width * k
                lo = jnp.where(mine, below, lo)
                hi = jnp.where(mine, above, hi)
        y_lo[f, slab] = lo
        y_hi[f, slab] = hi
        to = pl.ds(slab * SUB, SUB) if isinstance(slab, int) else pl.ds(
            pl.multiple_of(slab * SUB, SUB), SUB
        )
        z_lo[f, to, :] = prim[shape.across(f, slab, 0), :]
        z_hi[f, to, :] = prim[shape.across(f, slab, SUB - 1), :]


def send_x(shape, prim, faces, low=True, high=True):
    for f in FIELDS:
        for i in range(shape.pad):
            if high:
                faces[0, f, i] = prim[shape.at(f, shape.rows - shape.pad + i), :]
            if low:
                faces[1, f, i] = prim[shape.at(f, i), :]


def assemble_kernel(tags, state, *refs, held, slabs, slots, moves, occ, shape, first):
    given = len(held)
    arrived = group_levels(refs[:given], held)
    outs = refs[given + (0 if first else 7) :]
    field, prim, y_lo, y_hi, z_lo, z_hi, x_faces = outs[:7]
    blocks = outs[-1]
    units = NF * shape.slabs
    for b in range(occ):
        tag = tags[2 * moves + b]
        for unit in range(slabs[0] * NF, slabs[1] * NF):
            at = (b * units + unit) * SUB
            blocks[at : at + SUB, :] = pick(tag, unit, state, arrived, slots, shape.rows, moves)
    for slab in range(*slabs):
        for i in range(SUB):
            row = slab * SUB + i
            cons = [
                blocks[pl.ds((slab * NF + f) * SUB + i, occ, stride=units * SUB), :] for f in FIELDS
            ]
            for f, (c, w) in enumerate(zip(cons, primitives(cons))):
                field[shape.at(f, row), :] = c
                prim[shape.at(f, row), :] = w
        send_slab(shape, prim, y_lo, y_hi, z_lo, z_hi, slab)
    if first:
        canvas = outs[7]

        def clear(i, carry):
            for c in range(canvas.shape[0]):
                canvas[c, pl.ds(pl.multiple_of(i * SUB, SUB), SUB), :] = jnp.zeros((SUB, LANES), f32)
            return carry

        lax.fori_loop(0, canvas.shape[1] // SUB, clear, 0)
    send_x(shape, prim, x_faces, low=first, high=not first)


def sweep_z_kernel(prim, z_lo, z_hi, z_prev, z_next, total, flux_z, right_z, left, right, flux, *, shape):
    edge, rows = shape.edge, shape.rows

    def ghost(a):
        at = pl.ds(a * SUB, SUB)
        low = [z_lo[f, at, :] for f in FIELDS]
        high = [z_hi[f, at, :] for f in FIELDS]
        prev = [z_prev[f, at, :] for f in FIELDS]
        after = [z_next[f, at, :] for f in FIELDS]
        below = [lane_roll(v, -(edge - 1)) for v in prev]
        before = [lane_roll(v, -(edge - 2)) for v in prev]
        second = [lane_roll(v, -1) for v in low]
        lefts = plus(below, half_slopes(before, below, low))
        rights = minus(low, half_slopes(below, low, second))
        fluxes = twice_flux(lefts, rights, 2)
        last = [lane_roll(v, -(edge - 1)) for v in high]
        beyond = [lane_roll(v, -1) for v in after]
        over = minus(after, half_slopes(last, after, beyond))
        for f in FIELDS:
            flux_z[f, at, :] = lane_roll(fluxes[f], edge - 1)
            right_z[f, at, :] = over[f]

    lane = lane_of()
    z_of = lax.rem(lane, edge)
    sub = sub_of()
    first_z, last_z = z_of == 0, z_of == edge - 1
    first_sub, last_sub = sub == 0, sub == SUB - 1
    higher = lane - z_of + lax.rem(z_of + 1, edge)
    lower = lane - z_of + lax.rem(z_of + edge - 1, edge)

    def insert(ref, f, row):
        return jnp.broadcast_to(ref[f, pl.ds(row, 1), :], (SUB, LANES))

    def up(value, f, row, ghosts):
        across = jnp.where(last_sub, insert(ghosts, f, row), pltpu.roll(value, SUB - 1, 0))
        return jnp.take_along_axis(jnp.where(first_z, across, value), higher, axis=1)

    def down(value, f, row, ghosts):
        across = jnp.where(first_sub, insert(ghosts, f, row), pltpu.roll(value, 1, 0))
        return jnp.take_along_axis(jnp.where(last_z, across, value), lower, axis=1)

    def slopes(slab):
        ghost(slab)
        for row in range(slab * SUB, (slab + 1) * SUB):
            for f in FIELDS:
                at = shape.at(f, row)
                mine = prim[at, :]
                shift = half_minmod(mine - down(mine, f, row, z_prev), up(mine, f, row, z_next) - mine)
                left[at, :] = mine + shift
                right[at, :] = mine - shift

    def fluxes(slab):
        for row in range(slab * SUB, (slab + 1) * SUB):
            lefts = [left[shape.at(f, row), :] for f in FIELDS]
            rights = [up(right[shape.at(f, row), :], f, row, right_z) for f in FIELDS]
            for f, value in enumerate(twice_flux(lefts, rights, 2)):
                flux[shape.at(f, row), :] = value

    def differences(slab):
        for row in range(slab * SUB, (slab + 1) * SUB):
            for f in FIELDS:
                at = shape.at(f, row)
                mine = flux[at, :]
                total[at, :] = mine - down(mine, f, row, flux_z)

    in_turn(shape.slabs, slopes, fluxes, differences)


def sweep_x_kernel(prim, x_faces, sofar, total, wide, *, shape):
    rows, halves, pad = shape.rows, shape.halves, shape.pad
    for f in FIELDS:
        for i in range(pad):
            wide[f, i] = x_faces[0, f, i]
            wide[f, pad + rows + i] = x_faces[1, f, i]

        def copy(r, carry, f=f):
            wide[f, pad + r] = prim[shape.at(f, r), :]
            return carry

        lax.fori_loop(0, rows, copy, 0, unroll=8)

    for h in range(halves):
        cells = [[wide[f, i * halves + h] for f in FIELDS] for i in range(4)]
        left = plus(cells[1], half_slopes(*cells[0:3]))
        shift = half_slopes(*cells[1:4])
        flux = twice_flux(left, minus(cells[2], shift), 0)
        keep = plus(cells[2], shift)

        def body(x, carry, h=h):
            below, left = carry
            here, one, two = (
                [wide[f, pad + (x + i) * halves + h] for f in FIELDS] for i in range(3)
            )
            shift = half_slopes(here, one, two)
            flux = twice_flux(left, minus(one, shift), 0)
            row = x * halves + h
            for f in FIELDS:
                at = shape.at(f, row)
                total[at, :] = sofar[at, :] + (flux[f] - below[f])
            return flux, plus(one, shift)

        lax.fori_loop(0, shape.edge, body, (flux, keep), unroll=4)


def sweep_y(prim, y_lo, y_hi, y_prev, y_next, sofar, ghost_prim, ghost_flux, left, right, flux, turned,
            shape, finish, after_slab):
    edge, halves, fit, width = shape.edge, shape.halves, shape.fit, shape.width
    lane = lane_of()
    upper = lax.rem(lane, width) >= edge

    def prepare(q):
        low = [y_lo[f, q] for f in FIELDS]
        high = [y_hi[f, q] for f in FIELDS]
        below = [y_prev[f, q] for f in FIELDS]
        after = [y_next[f, q] for f in FIELDS]
        before = [lane_roll(v, edge) for v in below]
        first = [lane_roll(v, edge) for v in low]
        lefts = plus(below, half_slopes(before, below, first))
        rights = minus(first, half_slopes(below, first, low))
        fluxes = twice_flux(lefts, rights, 1)
        last = [lane_roll(v, -edge) for v in high]
        beyond = [lane_roll(v, -edge) for v in after]
        over = minus(after, half_slopes(last, after, beyond))
        for f in FIELDS:
            ghost_prim[f, q] = jnp.where(upper, below[f], after[f])
            ghost_flux[f, q] = jnp.where(upper, fluxes[f], over[f])

    top_lanes = lane >= LANES - edge
    low_lanes = lane < edge

    def up(values, insert):
        rolled = [lane_roll(v, -edge) for v in values]
        follow = rolled[1:] + [insert]
        return [jnp.where(top_lanes, n, r) for r, n in zip(rolled, follow)]

    def down(values, insert):
        rolled = [lane_roll(v, edge) for v in values]
        lead = [insert] + rolled[:-1]
        return [jnp.where(low_lanes, n, r) for r, n in zip(rolled, lead)]

    def each(q):
        for k in range(fit):
            yield -(width * k + edge), (q * fit + k) * halves

    def slopes(q):
        prepare(q)
        for turn, base in each(q):
            for f in FIELDS:
                mine = [prim[shape.at(f, base + h), :] for h in range(halves)]
                ghost = lane_roll(ghost_prim[f, q], turn)
                over, under = up(mine, ghost), down(mine, ghost)
                for h in range(halves):
                    shift = half_minmod(mine[h] - under[h], over[h] - mine[h])
                    left[shape.at(f, base + h), :] = mine[h] + shift
                    right[shape.at(f, base + h), :] = mine[h] - shift

    def fluxes(q):
        for turn, base in each(q):
            rights = []
            for f in FIELDS:
                mine = [right[shape.at(f, base + h), :] for h in range(halves)]
                ghost = lane_roll(ghost_flux[f, q], turn)
                turned[shape.at(f, base), :] = ghost
                rights.append(up(mine, ghost))
            for h in range(halves):
                lefts = [left[shape.at(f, base + h), :] for f in FIELDS]
                result = twice_flux(lefts, [rights[f][h] for f in FIELDS], 1)
                for f in FIELDS:
                    flux[shape.at(f, base + h), :] = result[f]

    def differences(q):
        for turn, base in each(q):
            total = [[None] * NF for _ in range(halves)]
            for f in FIELDS:
                mine = [flux[shape.at(f, base + h), :] for h in range(halves)]
                under = down(mine, turned[shape.at(f, base), :])
                for h in range(halves):
                    total[h][f] = sofar[shape.at(f, base + h), :] + (mine[h] - under[h])
            for h in range(halves):
                finish(base + h, total[h])

    in_turn(edge // fit, slopes, fluxes, differences, after_slab)


def sweep_y_one_kernel(field, prim, y_lo, y_hi, y_prev, y_next, sofar, *refs, shape):
    one, one_prim, x_faces, out_y_lo, out_y_hi, z_lo, z_hi = refs[:7]

    def finish(row, total):
        cons = [field[shape.at(f, row), :] - (0.5 * time_step) * total[f] for f in FIELDS]
        for f, (c, w) in enumerate(zip(cons, primitives(cons))):
            one[shape.at(f, row), :] = c
            one_prim[shape.at(f, row), :] = w

    def after_slab(q):
        send_slab(shape, one_prim, out_y_lo, out_y_hi, z_lo, z_hi, q)

    sweep_y(prim, y_lo, y_hi, y_prev, y_next, sofar, *refs[7:], shape, finish, after_slab)
    send_x(shape, one_prim, x_faces)


def sweep_y_two_kernel(own, field, one, prim, y_lo, y_hi, y_prev, y_next, sofar, zeros, out,
                       canvas, *refs, shape, occ, groups):
    scratch, (result, sems) = refs[:6], refs[6:]
    rows = shape.rows
    span = SUB * SUB

    def finish(row, total):
        for f in FIELDS:
            at = shape.at(f, row)
            advanced = one[at, :] - (0.5 * time_step) * total[f]
            result[at, :] = 0.5 * field[at, :] + 0.5 * advanced

    def copy(part):
        begin = part * span if isinstance(part, int) else pl.multiple_of(part * span, span)
        at = pl.ds(begin, span)
        return pltpu.make_async_copy(canvas.at[:, at, :], out.at[:, at, :], sems.at[part])

    def after_slab(q):
        for b in range(occ):
            slot = own[b]
            to = pl.ds(q * span + lax.rem(slot, SUB), SUB, stride=SUB)
            for f in FIELDS:
                canvas[f * groups + slot // SUB, to, :] = result[shape.across(f, q, b), :]
        copy(q).start()

    sweep_y(prim, y_lo, y_hi, y_prev, y_next, sofar, *scratch, shape, finish, after_slab)
    for part in range(shape.slabs):
        copy(part).wait()


def shards(state, send_slots, recv_slots, owner_slot):
    slots, _, cells = state.shape
    moves = send_slots.shape[2]
    size_x, size_y, size_z = (lax.axis_size(axis) for axis in AXES)
    occ = owner_slot.shape[0] // (size_x * size_y * size_z)
    edge = round(cells ** (1 / 3))
    rows = cells // LANES
    groups = slots // SUB
    shape = Shape(rows, edge)
    units = NF * shape.slabs
    pieces = split_units(units, (3, 5, 4, 3, 3, 2))
    firsts = split_units(units, (3, 5, 7, 5))

    bit_z = size_z.bit_length() - 2
    bit_y = bit_z + size_y.bit_length() - 1
    bit_x = bit_y + size_x.bit_length() - 1
    pair_bits = (bit_x, bit_y, bit_z)

    def swapped(value, level):
        mask = 2 ** pair_bits[level]
        pairs = [(source, source ^ mask) for source in range(lax.axis_size(AXES))]
        return lax.ppermute(value, AXES, pairs)

    rows_of_state = (
        state.reshape(groups, SUB, NF, rows, LANES)
        .transpose(2, 0, 3, 1, 4)
        .reshape(NF * groups * rows * SUB, LANES)
    )
    state_there = pltpu.with_memory_space_constraint(rows_of_state, HBM)
    send_there = pltpu.with_memory_space_constraint(send_slots, HBM)
    device = lax.axis_index(AXES)
    own = lax.dynamic_slice(owner_slot, (device * occ,), (occ,))
    sizes = dict(slots=slots, moves=moves)

    def message(piece):
        begin, end = piece
        return jax.ShapeDtypeStruct((moves, (end - begin) * SUB, LANES), f32)

    head = firsts[0]
    sent = [None] * len(firsts)
    sent[0] = pl.pallas_call(
        functools.partial(first_kernel, piece=head, rows=rows, **sizes),
        out_shape=message(head),
        in_specs=[whole(HBM)] * 2,
        out_specs=whole(VMEM),
        scratch_shapes=[
            SMEM(send_slots.shape, jnp.int32),
            VMEM(((head[1] - head[0]) * groups * SUB * SUB, LANES), f32),
            pltpu.SemaphoreType.DMA((1 + (head[1] - head[0]) * groups,)),
        ],
        compiler_params=params(),
        name="pack_first",
    )(send_there, state_there)
    tags, token, *sent[1:] = pl.pallas_call(
        functools.partial(rest_kernel, pieces=firsts[1:], rows=rows, occ=occ, **sizes),
        out_shape=[
            jax.ShapeDtypeStruct((2 * moves + occ,), jnp.int32),
            jax.ShapeDtypeStruct((SUB, LANES), f32),
        ]
        + [message(piece) for piece in firsts[1:]],
        in_specs=[whole(SMEM)] * 3 + [whole(VMEM)],
        out_specs=[whole(SMEM)] + [whole(VMEM)] * len(firsts),
        scratch_shapes=[SMEM((slots + SUB,), jnp.int32)],
        compiler_params=params(),
        name="pack_rest",
    )(send_slots, recv_slots, own, rows_of_state)

    cuts = (firsts, pieces, pieces)
    got = [[None] * len(cut) for cut in cuts]

    def holding(levels, begin, end):
        found = [
            ((level, piece), got[level][p])
            for level in levels
            for p, piece in enumerate(cuts[level])
            if piece[0] < end and piece[1] > begin
        ]
        return found

    def make(wanted, through):
        found = {}
        for level, p in wanted:
            for key, value in holding(range(level), *pieces[p]):
                found[key] = value
        plan = tuple((level, pieces[p]) for level, p in wanted)
        given, passed, made = len(found), len(through), len(wanted)
        outs = pl.pallas_call(
            functools.partial(
                pick_kernel, plan=plan, held=tuple(found), passed=passed, rows=rows, **sizes
            ),
            out_shape=[message(piece) for _, piece in plan]
            + [jax.ShapeDtypeStruct(t.shape, f32) for t in through],
            in_specs=[whole(SMEM)] + [whole(VMEM)] * (1 + given) + [whole(pl.ANY)] * passed,
            out_specs=[whole(VMEM)] * made + [whole(pl.ANY)] * passed,
            input_output_aliases={2 + given + i: made + i for i in range(passed)},
            compiler_params=params(),
            cost_estimate=cost(10**9, 10**9),
            name="pick_" + "_".join("%d%d" % w for w in wanted),
        )(tags, rows_of_state, *found.values(), *through)
        return outs[:made], outs[made:]

    steps = [
        ([(1, 0)], [2], []),
        ([(1, 1)], [3], []),
        ([(1, 2), (2, 0)], [], []),
        ([(1, 3), (2, 1)], [], []),
        ([(1, 4), (2, 2)], [], [0]),
        ([(1, 5), (2, 3)], [], [1]),
        ([(2, 4)], [], [2]),
        ([(2, 5)], [], [3]),
    ]
    got[0][0] = swapped(sent[0], 0)
    got[0][1] = swapped(sent[1], 0)
    for wanted, leaving, awaited in steps:
        through = [token] + [sent[p] for p in leaving] + [got[2][p] for p in awaited]
        made, (token, *passed) = make(wanted, through)
        for p, value in zip(leaving, passed):
            got[0][p] = swapped(value, 0)
        for (level, p), value in reversed(list(zip(wanted, made))):
            got[level][p] = swapped(value, level)
        for p, value in zip(awaited, passed[len(leaving) :]):
            got[2][p] = value

    grid = shape.grid()
    face_x, face_y, _, face_z, _ = shape.faces()
    part = [grid, grid, face_y, face_y, face_z, face_z, face_x]
    canvas = jax.ShapeDtypeStruct((NF * groups, rows * SUB, LANES), f32)
    full = pieces[-2][0] // NF

    def assemble(slabs, before):
        first = not before
        found = dict(holding(range(3), slabs[0] * NF, slabs[1] * NF))
        shapes = part + [canvas] * first
        fixed = 2 + len(found)
        return pl.pallas_call(
            functools.partial(
                assemble_kernel, held=tuple(found), slabs=slabs, occ=occ, shape=shape,
                first=first, **sizes,
            ),
            out_shape=shapes,
            in_specs=[whole(SMEM)] + [whole(VMEM)] * (1 + len(found) + len(before)),
            out_specs=[whole(VMEM)] * len(shapes),
            scratch_shapes=[VMEM((occ * NF * rows, LANES), f32)],
            input_output_aliases={fixed + i: i for i in range(len(before))},
            compiler_params=params(),
            name="assemble_%d" % slabs[0],
        )(tags, rows_of_state, *found.values(), *before)

    *made, blank = assemble((0, full), [])
    *made, x_faces = assemble((full, shape.slabs), made)
    made = made[:2] + [x_faces] + made[2:]

    def ring(value, axis, step):
        size = lax.axis_size(axis)
        return lax.ppermute(value, axis, [(i, (i + step) % size) for i in range(size)])

    def flux_sums(prim, x_faces, y_lo, y_hi, z_lo, z_hi):
        if size_x == 2:
            x_faces = ring(x_faces, "gx", 1)
        else:
            x_faces = jnp.stack([ring(x_faces[0], "gx", 1), ring(x_faces[1], "gx", -1)])
        y_prev, y_next = ring(y_hi, "gy", 1), ring(y_lo, "gy", -1)
        z_prev, z_next = ring(z_hi, "gz", 1), ring(z_lo, "gz", -1)
        ghost = VMEM((NF, rows, LANES), f32)
        work = [VMEM(grid.shape, f32)] * 3
        total = pl.pallas_call(
            functools.partial(sweep_z_kernel, shape=shape),
            out_shape=grid,
            in_specs=[whole(VMEM)] * 5,
            out_specs=whole(VMEM),
            scratch_shapes=[ghost] * 2 + work,
            compiler_params=params(),
            name="sweep_z",
        )(prim, z_lo, z_hi, z_prev, z_next)
        total = pl.pallas_call(
            functools.partial(sweep_x_kernel, shape=shape),
            out_shape=grid,
            in_specs=[whole(VMEM)] * 3,
            out_specs=whole(VMEM),
            scratch_shapes=[VMEM((NF, rows + 2 * shape.pad, SUB, LANES), f32)],
            input_output_aliases={2: 0},
            compiler_params=params(),
            name="sweep_x",
        )(prim, x_faces, total)
        return y_lo, y_hi, y_prev, y_next, total

    produced = [grid, grid] + shape.faces()
    scratch = [VMEM(face_y.shape, f32)] * 2 + [VMEM(grid.shape, f32)] * 4
    field, prim = made[0], made[1]
    sums = flux_sums(prim, *made[2:])
    made = pl.pallas_call(
        functools.partial(sweep_y_one_kernel, shape=shape),
        out_shape=produced,
        in_specs=[whole(VMEM)] * 7,
        out_specs=[whole(VMEM)] * len(produced),
        scratch_shapes=scratch,
        compiler_params=params(),
        name="sweep_y_one",
    )(field, prim, *sums)
    one, one_prim = made[0], made[1]
    sums = flux_sums(one_prim, *made[2:])
    out, _ = pl.pallas_call(
        functools.partial(sweep_y_two_kernel, shape=shape, occ=occ, groups=groups),
        out_shape=[canvas, canvas],
        in_specs=[whole(SMEM)] + [whole(VMEM)] * 9,
        out_specs=[whole(HBM), whole(VMEM)],
        scratch_shapes=scratch
        + [
            VMEM(grid.shape, f32),
            pltpu.SemaphoreType.DMA((shape.slabs,)),
        ],
        input_output_aliases={9: 1},
        compiler_params=params(),
        name="sweep_y_two",
    )(own, field, one, one_prim, *sums, blank)
    return (
        out.reshape(NF, groups, rows, SUB, LANES)
        .transpose(1, 3, 0, 2, 4)
        .reshape(slots, NF, cells)
    )


def solution(mesh):
    placed = (
        P(AXES, None, None),
        P(None, AXES, None),
        P(None, AXES, None),
        P(),
    )
    return jax.shard_map(
        shards,
        mesh=mesh,
        in_specs=placed,
        out_specs=P(AXES, None, None),
        check_vma=False,
    )
```

```python
import functools

import jax
import jax.numpy as jnp
from jax import lax
from jax.experimental import pallas as pl
from jax.experimental.pallas import tpu as pltpu
from jax.sharding import PartitionSpec as P

gamma_ratio = 1.4
time_step = 0.05
LANES = 128
SUB = 8
NF = 5
FIELDS = range(NF)
AXES = ("gx", "gy", "gz")

VMEM = pltpu.VMEM
SMEM = pltpu.SMEM
HBM = pltpu.HBM
f32 = jnp.float32


def whole(space):
    return pl.BlockSpec(memory_space=space)


def params():
    return pltpu.CompilerParams(vmem_limit_bytes=16 * 1024 * 1024)


def cost(flops, moved):
    return pl.CostEstimate(flops=flops, bytes_accessed=moved, transcendentals=0)


def split_units(units, shares):
    ends = [units * sum(shares[: i + 1]) // sum(shares) for i in range(len(shares))]
    return list(zip([0] + ends[:-1], ends))


def from_state(state, tag, unit, slots, rows):
    slab, field = unit // NF, unit % NF
    groups = slots // SUB
    base = (tag // SUB) * (rows * SUB) + lax.rem(tag, SUB)
    start = base + (field * groups * rows + slab * SUB) * SUB
    return state[pl.ds(start, SUB, stride=SUB), :]


def pick(tag, unit, state, arrived, slots, rows, moves):
    value = from_state(state, jnp.minimum(tag, slots - 1), unit, slots, rows)
    for level, held in enumerate(arrived):
        base = slots + level * moves
        index = jnp.clip(tag - base, 0, moves - 1)
        for (begin, end), ref in held:
            if begin <= unit < end:
                at = (unit - begin) * SUB
                value = jnp.where(tag >= base, ref[index, at : at + SUB, :], value)
    return value


def first_kernel(send_hbm, state_hbm, out, send, held, sems, *, piece, slots, rows, moves):
    span = SUB * SUB
    groups = slots // SUB
    copies = [pltpu.make_async_copy(send_hbm, send, sems.at[0])]
    for unit in range(*piece):
        slab, field = unit // NF, unit % NF
        for g in range(groups):
            at = ((field * groups + g) * rows + slab * SUB) * SUB
            to = ((unit - piece[0]) * groups + g) * span
            copies.append(
                pltpu.make_async_copy(
                    state_hbm.at[pl.ds(at, span), :],
                    held.at[pl.ds(to, span), :],
                    sems.at[len(copies)],
                )
            )
    for c in copies:
        c.start()
    for c in copies:
        c.wait()
    for k in range(moves):
        slot = jnp.minimum(send[0, 0, k], slots - 1)
        base = (slot // SUB) * span + lax.rem(slot, SUB)
        for i in range(piece[1] - piece[0]):
            out[k, i * SUB : (i + 1) * SUB, :] = held[
                pl.ds(base + i * groups * span, SUB, stride=SUB), :
            ]


def rest_kernel(send, recv, own, state, tags, token, *refs, pieces, slots, rows, moves, occ):
    outs, where = refs[:-1], refs[-1]
    token[...] = jnp.zeros_like(token)
    for slot in range(slots):
        where[slot] = slot
    for level in range(3):
        if level:
            for k in range(moves):
                slot = jnp.minimum(send[level, 0, k], slots - 1)
                tags[(level - 1) * moves + k] = where[slot]
        for k in range(moves):
            where[recv[level, 0, k]] = slots + level * moves + k
    for b in range(occ):
        tags[2 * moves + b] = where[own[b]]
    for k in range(moves):
        slot = jnp.minimum(send[0, 0, k], slots - 1)
        for (begin, end), out in zip(pieces, outs):
            for unit in range(begin, end):
                at = (unit - begin) * SUB
                out[k, at : at + SUB, :] = from_state(state, slot, unit, slots, rows)


def group_levels(refs, held):
    levels = [[], [], []]
    for ref, (level, piece) in zip(refs, held):
        levels[level].append((piece, ref))
    return levels


def pick_kernel(tags, state, *refs, plan, held, passed, slots, rows, moves):
    given = len(held)
    arrived = group_levels(refs[:given], held)
    outs = refs[given + passed :]
    for (level, (begin, end)), out in zip(plan, outs):
        for k in range(moves):
            tag = tags[(level - 1) * moves + k]
            for unit in range(begin, end):
                at = (unit - begin) * SUB
                out[k, at : at + SUB, :] = pick(
                    tag, unit, state, arrived[:level], slots, rows, moves
                )


def primitives(cons):
    density = cons[0]
    inverse = 1.0 / density
    vel = [cons[1] * inverse, cons[2] * inverse, cons[3] * inverse]
    kinetic = cons[1] * vel[0] + cons[2] * vel[1] + cons[3] * vel[2]
    pressure = (gamma_ratio - 1.0) * (cons[4] - 0.5 * kinetic)
    return [density, vel[0], vel[1], vel[2], pressure]


def half_minmod(lower, upper):
    both = jnp.maximum(0.0, jnp.minimum(lower, upper)) + jnp.minimum(
        0.0, jnp.maximum(lower, upper)
    )
    return 0.5 * both


def half_slopes(before, here, after):
    return [half_minmod(h - b, a - h) for b, h, a in zip(before, here, after)]


def plus(a, b):
    return [x + y for x, y in zip(a, b)]


def minus(a, b):
    return [x - y for x, y in zip(a, b)]


def side_terms(prim, normal):
    density, vel, pressure = prim[0], prim[1:4], prim[4]
    along = vel[normal]
    mom = [density * v for v in vel]
    kinetic = mom[0] * vel[0] + mom[1] * vel[1] + mom[2] * vel[2]
    energy = pressure * (1.0 / (gamma_ratio - 1.0)) + 0.5 * kinetic
    flux = [m * along for m in mom]
    flux[normal] = flux[normal] + pressure
    scaled = gamma_ratio * pressure
    speed = jnp.abs(along) + scaled * lax.rsqrt(scaled * density)
    return [density] + mom + [energy], [mom[normal]] + flux + [(energy + pressure) * along], speed


def twice_flux(left, right, normal):
    left_cons, left_flux, left_speed = side_terms(left, normal)
    right_cons, right_flux, right_speed = side_terms(right, normal)
    speed = jnp.maximum(left_speed, right_speed)
    return [
        (fl + fr) - speed * (ur - ul)
        for fl, fr, ul, ur in zip(left_flux, right_flux, left_cons, right_cons)
    ]


def lane_of():
    return lax.broadcasted_iota(jnp.int32, (SUB, LANES), 1)


def sub_of():
    return lax.broadcasted_iota(jnp.int32, (SUB, LANES), 0)


def lane_roll(value, amount):
    amount = amount % LANES
    return value if amount == 0 else pltpu.roll(value, amount, 1)


class Shape:
    def __init__(self, rows, edge):
        self.rows, self.edge = rows, edge
        self.halves = rows // edge
        self.width = 2 * edge
        self.fit = LANES // self.width
        self.slabs = rows // SUB
        self.pad = 2 * self.halves

    def at(self, f, row):
        start = (f * self.rows + row) * SUB
        return pl.ds(start if isinstance(start, int) else pl.multiple_of(start, SUB), SUB)

    def across(self, f, slab, sub):
        return pl.ds((f * self.rows + slab * SUB) * SUB + sub, SUB, stride=SUB)

    def grid(self):
        return jax.ShapeDtypeStruct((NF * self.rows * SUB, LANES), f32)

    def faces(self):
        x = jax.ShapeDtypeStruct((2, NF, self.pad, SUB, LANES), f32)
        y = jax.ShapeDtypeStruct((NF, self.edge // self.fit, SUB, LANES), f32)
        z = jax.ShapeDtypeStruct((NF, SUB, LANES), f32)
        return [x, y, y, z, z]


def in_turn(count, *phases):
    for step in range(count + len(phases) - 1):
        for late, phase in enumerate(phases):
            if 0 <= step - late < count:
                phase(step - late)


def send_slab(shape, prim, y_lo, y_hi, z_lo, z_hi, slab):
    lane = lane_of()
    halves = shape.halves
    for f in FIELDS:
        lo = hi = None
        for k in range(shape.fit):
            row = slab * SUB + k * halves
            below = lane_roll(prim[shape.at(f, row), :], shape.width * k)
            above = lane_roll(prim[shape.at(f, row + halves - 1), :], shape.width * (k + 1))
            if lo is None:
                lo, hi = below, above
            else:
                mine = lane >= shape.width * k
                lo = jnp.where(mine, below, lo)
                hi = jnp.where(mine, above, hi)
        y_lo[f, slab] = lo
        y_hi[f, slab] = hi
        below = lane_roll(prim[shape.across(f, slab, 0), :], 2 * slab)
        above = lane_roll(prim[shape.across(f, slab, SUB - 1), :], 2 * slab + 2 - shape.edge)
        if slab:
            mine = lax.rem(lane, shape.edge) >= 2 * slab
            below = jnp.where(mine, below, z_lo[f])
            above = jnp.where(mine, above, z_hi[f])
        z_lo[f] = below
        z_hi[f] = above


def send_x(shape, prim, faces, low=True, high=True):
    for f in FIELDS:
        for i in range(shape.pad):
            if high:
                faces[0, f, i] = prim[shape.at(f, shape.rows - shape.pad + i), :]
            if low:
                faces[1, f, i] = prim[shape.at(f, i), :]


def assemble_kernel(tags, state, *refs, held, slabs, slots, moves, occ, shape, first):
    given = len(held)
    arrived = group_levels(refs[:given], held)
    outs = refs[given + (0 if first else 7) :]
    field, prim, y_lo, y_hi, z_lo, z_hi, x_faces = outs[:7]
    blocks = outs[-1]
    units = NF * shape.slabs
    for b in range(occ):
        tag = tags[2 * moves + b]
        for unit in range(slabs[0] * NF, slabs[1] * NF):
            at = (b * units + unit) * SUB
            blocks[at : at + SUB, :] = pick(tag, unit, state, arrived, slots, shape.rows, moves)
    for slab in range(*slabs):
        for i in range(SUB):
            row = slab * SUB + i
            cons = [
                blocks[pl.ds((slab * NF + f) * SUB + i, occ, stride=units * SUB), :] for f in FIELDS
            ]
            for f, (c, w) in enumerate(zip(cons, primitives(cons))):
                field[shape.at(f, row), :] = c
                prim[shape.at(f, row), :] = w
        send_slab(shape, prim, y_lo, y_hi, z_lo, z_hi, slab)
    if first:
        canvas = outs[7]

        def clear(i, carry):
            for c in range(canvas.shape[0]):
                canvas[c, pl.ds(pl.multiple_of(i * SUB, SUB), SUB), :] = jnp.zeros((SUB, LANES), f32)
            return carry

        lax.fori_loop(0, canvas.shape[1] // SUB, clear, 0)
    send_x(shape, prim, x_faces, low=first, high=not first)


def sweep_z_kernel(prim, z_prev, z_next, total, prev_z, next_z, flux_z, right_z, left, right, flux, *, shape):
    edge, rows = shape.edge, shape.rows

    def ghost(a):
        at = pl.ds(a * SUB, SUB)
        low = [prim[shape.across(f, a, 0), :] for f in FIELDS]
        high = [prim[shape.across(f, a, SUB - 1), :] for f in FIELDS]
        prev = [lane_roll(z_prev[f], edge - 2 - 2 * a) for f in FIELDS]
        after = [lane_roll(z_next[f], -2 * a) for f in FIELDS]
        for f in FIELDS:
            prev_z[f, at, :] = prev[f]
            next_z[f, at, :] = after[f]
        below = [lane_roll(v, -(edge - 1)) for v in prev]
        before = [lane_roll(v, -(edge - 2)) for v in prev]
        second = [lane_roll(v, -1) for v in low]
        lefts = plus(below, half_slopes(before, below, low))
        rights = minus(low, half_slopes(below, low, second))
        fluxes = twice_flux(lefts, rights, 2)
        last = [lane_roll(v, -(edge - 1)) for v in high]
        beyond = [lane_roll(v, -1) for v in after]
        over = minus(after, half_slopes(last, after, beyond))
        for f in FIELDS:
            flux_z[f, at, :] = lane_roll(fluxes[f], edge - 1)
            right_z[f, at, :] = over[f]

    lane = lane_of()
    z_of = lax.rem(lane, edge)
    sub = sub_of()
    first_z, last_z = z_of == 0, z_of == edge - 1
    first_sub, last_sub = sub == 0, sub == SUB - 1
    higher = lane - z_of + lax.rem(z_of + 1, edge)
    lower = lane - z_of + lax.rem(z_of + edge - 1, edge)

    def insert(ref, f, row):
        return jnp.broadcast_to(ref[f, pl.ds(row, 1), :], (SUB, LANES))

    def up(value, f, row, ghosts):
        across = jnp.where(last_sub, insert(ghosts, f, row), pltpu.roll(value, SUB - 1, 0))
        return jnp.take_along_axis(jnp.where(first_z, across, value), higher, axis=1)

    def down(value, f, row, ghosts):
        across = jnp.where(first_sub, insert(ghosts, f, row), pltpu.roll(value, 1, 0))
        return jnp.take_along_axis(jnp.where(last_z, across, value), lower, axis=1)

    def slopes(slab):
        ghost(slab)
        for row in range(slab * SUB, (slab + 1) * SUB):
            for f in FIELDS:
                at = shape.at(f, row)
                mine = prim[at, :]
                shift = half_minmod(mine - down(mine, f, row, prev_z), up(mine, f, row, next_z) - mine)
                left[at, :] = mine + shift
                right[at, :] = mine - shift

    def fluxes(slab):
        for row in range(slab * SUB, (slab + 1) * SUB):
            lefts = [left[shape.at(f, row), :] for f in FIELDS]
            rights = [up(right[shape.at(f, row), :], f, row, right_z) for f in FIELDS]
            for f, value in enumerate(twice_flux(lefts, rights, 2)):
                flux[shape.at(f, row), :] = value

    def differences(slab):
        for row in range(slab * SUB, (slab + 1) * SUB):
            for f in FIELDS:
                at = shape.at(f, row)
                mine = flux[at, :]
                total[at, :] = mine - down(mine, f, row, flux_z)

    in_turn(shape.slabs, slopes, fluxes, differences)


def sweep_x_kernel(prim, x_faces, sofar, total, *, shape):
    halves, edge = shape.halves, shape.edge

    def cells(x, h):
        if x < 0:
            return [x_faces[0, f, (x + 2) * halves + h] for f in FIELDS]
        if x >= edge:
            return [x_faces[1, f, (x - edge) * halves + h] for f in FIELDS]
        return [prim[shape.at(f, x * halves + h), :] for f in FIELDS]

    for h in range(halves):
        left = below = None
        ahead = [cells(x, h) for x in (-2, -1, 0)]
        for x in range(-1, edge + 1):
            shift = half_slopes(*ahead)
            if left is not None:
                flux = twice_flux(left, minus(ahead[1], shift), 0)
                if below is not None:
                    for f in FIELDS:
                        at = shape.at(f, (x - 1) * halves + h)
                        total[at, :] = sofar[at, :] + (flux[f] - below[f])
                below = flux
            left = plus(ahead[1], shift)
            if x < edge:
                ahead = ahead[1:] + [cells(x + 2, h)]


def sweep_y(prim, y_lo, y_hi, y_prev, y_next, sofar, ghost_prim, ghost_flux, left, right, flux, turned,
            shape, finish, after_slab):
    edge, halves, fit, width = shape.edge, shape.halves, shape.fit, shape.width
    lane = lane_of()
    upper = lax.rem(lane, width) >= edge

    def prepare(q):
        low = [y_lo[f, q] for f in FIELDS]
        high = [y_hi[f, q] for f in FIELDS]
        below = [y_prev[f, q] for f in FIELDS]
        after = [y_next[f, q] for f in FIELDS]
        before = [lane_roll(v, edge) for v in below]
        first = [lane_roll(v, edge) for v in low]
        lefts = plus(below, half_slopes(before, below, first))
        rights = minus(first, half_slopes(below, first, low))
        fluxes = twice_flux(lefts, rights, 1)
        last = [lane_roll(v, -edge) for v in high]
        beyond = [lane_roll(v, -edge) for v in after]
        over = minus(after, half_slopes(last, after, beyond))
        for f in FIELDS:
            ghost_prim[f, q] = jnp.where(upper, below[f], after[f])
            ghost_flux[f, q] = jnp.where(upper, fluxes[f], over[f])

    top_lanes = lane >= LANES - edge
    low_lanes = lane < edge

    def up(values, insert):
        rolled = [lane_roll(v, -edge) for v in values]
        follow = rolled[1:] + [insert]
        return [jnp.where(top_lanes, n, r) for r, n in zip(rolled, follow)]

    def down(values, insert):
        rolled = [lane_roll(v, edge) for v in values]
        lead = [insert] + rolled[:-1]
        return [jnp.where(low_lanes, n, r) for r, n in zip(rolled, lead)]

    def each(q):
        for k in range(fit):
            yield -(width * k + edge), (q * fit + k) * halves

    def slopes(q):
        prepare(q)
        for turn, base in each(q):
            for f in FIELDS:
                mine = [prim[shape.at(f, base + h), :] for h in range(halves)]
                ghost = lane_roll(ghost_prim[f, q], turn)
                over, under = up(mine, ghost), down(mine, ghost)
                for h in range(halves):
                    shift = half_minmod(mine[h] - under[h], over[h] - mine[h])
                    left[shape.at(f, base + h), :] = mine[h] + shift
                    right[shape.at(f, base + h), :] = mine[h] - shift

    def fluxes(q):
        for turn, base in each(q):
            rights = []
            for f in FIELDS:
                mine = [right[shape.at(f, base + h), :] for h in range(halves)]
                ghost = lane_roll(ghost_flux[f, q], turn)
                turned[shape.at(f, base), :] = ghost
                rights.append(up(mine, ghost))
            for h in range(halves):
                lefts = [left[shape.at(f, base + h), :] for f in FIELDS]
                result = twice_flux(lefts, [rights[f][h] for f in FIELDS], 1)
                for f in FIELDS:
                    flux[shape.at(f, base + h), :] = result[f]

    def differences(q):
        for turn, base in each(q):
            total = [[None] * NF for _ in range(halves)]
            for f in FIELDS:
                mine = [flux[shape.at(f, base + h), :] for h in range(halves)]
                under = down(mine, turned[shape.at(f, base), :])
                for h in range(halves):
                    total[h][f] = sofar[shape.at(f, base + h), :] + (mine[h] - under[h])
            for h in range(halves):
                finish(base + h, total[h])

    in_turn(edge // fit, slopes, fluxes, differences, after_slab)


def sweep_y_one_kernel(field, prim, y_lo, y_hi, y_prev, y_next, sofar, *refs, shape):
    one, one_prim, x_faces, out_y_lo, out_y_hi, z_lo, z_hi = refs[:7]

    def finish(row, total):
        cons = [field[shape.at(f, row), :] - (0.5 * time_step) * total[f] for f in FIELDS]
        for f, (c, w) in enumerate(zip(cons, primitives(cons))):
            one[shape.at(f, row), :] = c
            one_prim[shape.at(f, row), :] = w

    def after_slab(q):
        send_slab(shape, one_prim, out_y_lo, out_y_hi, z_lo, z_hi, q)

    sweep_y(prim, y_lo, y_hi, y_prev, y_next, sofar, *refs[7:], shape, finish, after_slab)
    send_x(shape, one_prim, x_faces)


def sweep_y_two_kernel(own, field, one, prim, y_lo, y_hi, y_prev, y_next, sofar, zeros, out,
                       canvas, *refs, shape, occ, groups):
    scratch, (result, sems) = refs[:6], refs[6:]
    rows = shape.rows
    span = SUB * SUB

    def finish(row, total):
        for f in FIELDS:
            at = shape.at(f, row)
            advanced = one[at, :] - (0.5 * time_step) * total[f]
            result[at, :] = 0.5 * field[at, :] + 0.5 * advanced

    def copy(part):
        begin = part * span if isinstance(part, int) else pl.multiple_of(part * span, span)
        at = pl.ds(begin, span)
        return pltpu.make_async_copy(canvas.at[:, at, :], out.at[:, at, :], sems.at[part])

    def after_slab(q):
        for b in range(occ):
            slot = own[b]
            to = pl.ds(q * span + lax.rem(slot, SUB), SUB, stride=SUB)
            for f in FIELDS:
                canvas[f * groups + slot // SUB, to, :] = result[shape.across(f, q, b), :]
        copy(q).start()

    sweep_y(prim, y_lo, y_hi, y_prev, y_next, sofar, *scratch, shape, finish, after_slab)
    for part in range(shape.slabs):
        copy(part).wait()


def shards(state, send_slots, recv_slots, owner_slot):
    slots, _, cells = state.shape
    moves = send_slots.shape[2]
    size_x, size_y, size_z = (lax.axis_size(axis) for axis in AXES)
    occ = owner_slot.shape[0] // (size_x * size_y * size_z)
    edge = round(cells ** (1 / 3))
    rows = cells // LANES
    groups = slots // SUB
    shape = Shape(rows, edge)
    units = NF * shape.slabs
    pieces = split_units(units, (3, 5, 7, 5))
    firsts = split_units(units, (3, 5, 7, 5))

    bit_z = size_z.bit_length() - 2
    bit_y = bit_z + size_y.bit_length() - 1
    bit_x = bit_y + size_x.bit_length() - 1
    pair_bits = (bit_x, bit_y, bit_z)

    def swapped(value, level):
        mask = 2 ** pair_bits[level]
        pairs = [(source, source ^ mask) for source in range(lax.axis_size(AXES))]
        return lax.ppermute(value, AXES, pairs)

    rows_of_state = (
        state.reshape(groups, SUB, NF, rows, LANES)
        .transpose(2, 0, 3, 1, 4)
        .reshape(NF * groups * rows * SUB, LANES)
    )
    state_there = pltpu.with_memory_space_constraint(rows_of_state, HBM)
    send_there = pltpu.with_memory_space_constraint(send_slots, HBM)
    device = lax.axis_index(AXES)
    own = lax.dynamic_slice(owner_slot, (device * occ,), (occ,))
    sizes = dict(slots=slots, moves=moves)

    def message(piece):
        begin, end = piece
        return jax.ShapeDtypeStruct((moves, (end - begin) * SUB, LANES), f32)

    head = firsts[0]
    sent = [None] * len(firsts)
    sent[0] = pl.pallas_call(
        functools.partial(first_kernel, piece=head, rows=rows, **sizes),
        out_shape=message(head),
        in_specs=[whole(HBM)] * 2,
        out_specs=whole(VMEM),
        scratch_shapes=[
            SMEM(send_slots.shape, jnp.int32),
            VMEM(((head[1] - head[0]) * groups * SUB * SUB, LANES), f32),
            pltpu.SemaphoreType.DMA((1 + (head[1] - head[0]) * groups,)),
        ],
        compiler_params=params(),
        name="pack_first",
    )(send_there, state_there)
    tags, token, *sent[1:] = pl.pallas_call(
        functools.partial(rest_kernel, pieces=firsts[1:], rows=rows, occ=occ, **sizes),
        out_shape=[
            jax.ShapeDtypeStruct((2 * moves + occ,), jnp.int32),
            jax.ShapeDtypeStruct((SUB, LANES), f32),
        ]
        + [message(piece) for piece in firsts[1:]],
        in_specs=[whole(SMEM)] * 3 + [whole(VMEM)],
        out_specs=[whole(SMEM)] + [whole(VMEM)] * len(firsts),
        scratch_shapes=[SMEM((slots + SUB,), jnp.int32)],
        compiler_params=params(),
        name="pack_rest",
    )(send_slots, recv_slots, own, rows_of_state)

    cuts = (firsts, pieces, pieces)
    got = [[None] * len(cut) for cut in cuts]

    def holding(levels, begin, end):
        found = [
            ((level, piece), got[level][p])
            for level in levels
            for p, piece in enumerate(cuts[level])
            if piece[0] < end and piece[1] > begin
        ]
        return found

    def make(wanted, through):
        found = {}
        for level, p in wanted:
            for key, value in holding(range(level), *pieces[p]):
                found[key] = value
        plan = tuple((level, pieces[p]) for level, p in wanted)
        given, passed, made = len(found), len(through), len(wanted)
        outs = pl.pallas_call(
            functools.partial(
                pick_kernel, plan=plan, held=tuple(found), passed=passed, rows=rows, **sizes
            ),
            out_shape=[message(piece) for _, piece in plan]
            + [jax.ShapeDtypeStruct(t.shape, f32) for t in through],
            in_specs=[whole(SMEM)] + [whole(VMEM)] * (1 + given) + [whole(pl.ANY)] * passed,
            out_specs=[whole(VMEM)] * made + [whole(pl.ANY)] * passed,
            input_output_aliases={2 + given + i: made + i for i in range(passed)},
            compiler_params=params(),
            cost_estimate=cost(10**9, 10**9),
            name="pick_" + "_".join("%d%d" % w for w in wanted),
        )(tags, rows_of_state, *found.values(), *through)
        return outs[:made], outs[made:]

    steps = [
        ([(1, 0)], [2], []),
        ([(1, 1)], [3], []),
        ([(1, 2), (2, 0)], [], []),
        ([(1, 3), (2, 1)], [], []),
        ([(2, 2)], [], [0]),
        ([(2, 3)], [], [1]),
    ]
    got[0][0] = swapped(sent[0], 0)
    got[0][1] = swapped(sent[1], 0)
    for wanted, leaving, awaited in steps:
        through = [token] + [sent[p] for p in leaving] + [got[2][p] for p in awaited]
        made, (token, *passed) = make(wanted, through)
        for p, value in zip(leaving, passed):
            got[0][p] = swapped(value, 0)
        for (level, p), value in reversed(list(zip(wanted, made))):
            got[level][p] = swapped(value, level)
        for p, value in zip(awaited, passed[len(leaving) :]):
            got[2][p] = value

    grid = shape.grid()
    face_x, face_y, _, face_z, _ = shape.faces()
    part = [grid, grid, face_y, face_y, face_z, face_z, face_x]
    canvas = jax.ShapeDtypeStruct((NF * groups, rows * SUB, LANES), f32)
    full = pieces[-1][0] // NF

    def assemble(slabs, before):
        first = not before
        found = dict(holding(range(3), slabs[0] * NF, slabs[1] * NF))
        shapes = part + [canvas] * first
        fixed = 2 + len(found)
        return pl.pallas_call(
            functools.partial(
                assemble_kernel, held=tuple(found), slabs=slabs, occ=occ, shape=shape,
                first=first, **sizes,
            ),
            out_shape=shapes,
            in_specs=[whole(SMEM)] + [whole(VMEM)] * (1 + len(found) + len(before)),
            out_specs=[whole(VMEM)] * len(shapes),
            scratch_shapes=[VMEM((occ * NF * rows, LANES), f32)],
            input_output_aliases={fixed + i: i for i in range(len(before))},
            compiler_params=params(),
            name="assemble_%d" % slabs[0],
        )(tags, rows_of_state, *found.values(), *before)

    *made, blank = assemble((0, full), [])
    *made, x_faces = assemble((full, shape.slabs), made)
    made = made[:2] + [x_faces] + made[2:]

    def ring(value, axis, step):
        size = lax.axis_size(axis)
        return lax.ppermute(value, axis, [(i, (i + step) % size) for i in range(size)])

    def flux_sums(prim, x_faces, y_lo, y_hi, z_lo, z_hi):
        if size_x == 2:
            x_faces = ring(x_faces, "gx", 1)
        else:
            x_faces = jnp.stack([ring(x_faces[0], "gx", 1), ring(x_faces[1], "gx", -1)])
        y_prev, y_next = ring(y_hi, "gy", 1), ring(y_lo, "gy", -1)
        z_prev, z_next = ring(z_hi, "gz", 1), ring(z_lo, "gz", -1)
        ghost = VMEM((NF, rows, LANES), f32)
        work = [VMEM(grid.shape, f32)] * 3
        total = pl.pallas_call(
            functools.partial(sweep_z_kernel, shape=shape),
            out_shape=grid,
            in_specs=[whole(VMEM)] * 3,
            out_specs=whole(VMEM),
            scratch_shapes=[ghost] * 4 + work,
            compiler_params=params(),
            cost_estimate=cost(1, 1),
            name="sweep_z",
        )(prim, z_prev, z_next)
        total = pl.pallas_call(
            functools.partial(sweep_x_kernel, shape=shape),
            out_shape=grid,
            in_specs=[whole(VMEM)] * 3,
            out_specs=whole(VMEM),
            input_output_aliases={2: 0},
            compiler_params=params(),
            cost_estimate=cost(1, 1),
            name="sweep_x",
        )(prim, x_faces, total)
        return y_lo, y_hi, y_prev, y_next, total

    produced = [grid, grid] + shape.faces()
    scratch = [VMEM(face_y.shape, f32)] * 2 + [VMEM(grid.shape, f32)] * 4
    field, prim = made[0], made[1]
    sums = flux_sums(prim, *made[2:])
    made = pl.pallas_call(
        functools.partial(sweep_y_one_kernel, shape=shape),
        out_shape=produced,
        in_specs=[whole(VMEM)] * 7,
        out_specs=[whole(VMEM)] * len(produced),
        scratch_shapes=scratch,
        compiler_params=params(),
        name="sweep_y_one",
    )(field, prim, *sums)
    one, one_prim = made[0], made[1]
    sums = flux_sums(one_prim, *made[2:])
    out, _ = pl.pallas_call(
        functools.partial(sweep_y_two_kernel, shape=shape, occ=occ, groups=groups),
        out_shape=[canvas, canvas],
        in_specs=[whole(SMEM)] + [whole(VMEM)] * 9,
        out_specs=[whole(HBM), whole(VMEM)],
        scratch_shapes=scratch
        + [
            VMEM(grid.shape, f32),
            pltpu.SemaphoreType.DMA((shape.slabs,)),
        ],
        input_output_aliases={9: 1},
        compiler_params=params(),
        name="sweep_y_two",
    )(own, field, one, one_prim, *sums, blank)
    return (
        out.reshape(NF, groups, rows, SUB, LANES)
        .transpose(1, 3, 0, 2, 4)
        .reshape(slots, NF, cells)
    )


def solution(mesh):
    placed = (
        P(AXES, None, None),
        P(None, AXES, None),
        P(None, AXES, None),
        P(),
    )
    return jax.shard_map(
        shards,
        mesh=mesh,
        in_specs=placed,
        out_specs=P(AXES, None, None),
        check_vma=False,
    )
```

```python
import functools

import jax
import jax.numpy as jnp
from jax import lax
from jax.experimental import pallas as pl
from jax.experimental.pallas import tpu as pltpu
from jax.sharding import PartitionSpec as P

gamma_ratio = 1.4
time_step = 0.05
LANES = 128
SUB = 8
NF = 5
FIELDS = range(NF)
AXES = ("gx", "gy", "gz")

VMEM = pltpu.VMEM
SMEM = pltpu.SMEM
HBM = pltpu.HBM
f32 = jnp.float32


def whole(space):
    return pl.BlockSpec(memory_space=space)


def params():
    return pltpu.CompilerParams(vmem_limit_bytes=16 * 1024 * 1024)


def cost(flops, moved):
    return pl.CostEstimate(flops=flops, bytes_accessed=moved, transcendentals=0)


def split_units(units, shares):
    ends = [units * sum(shares[: i + 1]) // sum(shares) for i in range(len(shares))]
    return list(zip([0] + ends[:-1], ends))


def from_state(state, tag, unit, slots, rows):
    slab, field = unit // NF, unit % NF
    groups = slots // SUB
    base = (tag // SUB) * (rows * SUB) + lax.rem(tag, SUB)
    start = base + (field * groups * rows + slab * SUB) * SUB
    return state[pl.ds(start, SUB, stride=SUB), :]


def pick(tag, unit, state, arrived, slots, rows, moves):
    value = from_state(state, jnp.minimum(tag, slots - 1), unit, slots, rows)
    for level, held in enumerate(arrived):
        base = slots + level * moves
        index = jnp.clip(tag - base, 0, moves - 1)
        for (begin, end), ref in held:
            if begin <= unit < end:
                at = (unit - begin) * SUB
                value = jnp.where(tag >= base, ref[index, at : at + SUB, :], value)
    return value


def first_kernel(send_hbm, state_hbm, out, send, held, sems, *, piece, slots, rows, moves):
    span = SUB * SUB
    groups = slots // SUB
    copies = [pltpu.make_async_copy(send_hbm, send, sems.at[0])]
    for unit in range(*piece):
        slab, field = unit // NF, unit % NF
        for g in range(groups):
            at = ((field * groups + g) * rows + slab * SUB) * SUB
            to = ((unit - piece[0]) * groups + g) * span
            copies.append(
                pltpu.make_async_copy(
                    state_hbm.at[pl.ds(at, span), :],
                    held.at[pl.ds(to, span), :],
                    sems.at[len(copies)],
                )
            )
    for c in copies:
        c.start()
    for c in copies:
        c.wait()
    for k in range(moves):
        slot = jnp.minimum(send[0, 0, k], slots - 1)
        base = (slot // SUB) * span + lax.rem(slot, SUB)
        for i in range(piece[1] - piece[0]):
            out[k, i * SUB : (i + 1) * SUB, :] = held[
                pl.ds(base + i * groups * span, SUB, stride=SUB), :
            ]


def rest_kernel(send, recv, own, state, tags, token, *refs, pieces, slots, rows, moves, occ):
    outs, where = refs[:-1], refs[-1]
    token[...] = jnp.zeros_like(token)
    for slot in range(slots):
        where[slot] = slot
    for level in range(3):
        if level:
            for k in range(moves):
                slot = jnp.minimum(send[level, 0, k], slots - 1)
                tags[(level - 1) * moves + k] = where[slot]
        for k in range(moves):
            where[recv[level, 0, k]] = slots + level * moves + k
    for b in range(occ):
        tags[2 * moves + b] = where[own[b]]
    for k in range(moves):
        slot = jnp.minimum(send[0, 0, k], slots - 1)
        for (begin, end), out in zip(pieces, outs):
            for unit in range(begin, end):
                at = (unit - begin) * SUB
                out[k, at : at + SUB, :] = from_state(state, slot, unit, slots, rows)


def group_levels(refs, held):
    levels = [[], [], []]
    for ref, (level, piece) in zip(refs, held):
        levels[level].append((piece, ref))
    return levels


def pick_kernel(tags, state, *refs, plan, held, passed, slots, rows, moves):
    given = len(held)
    arrived = group_levels(refs[:given], held)
    outs = refs[given + passed :]
    for (level, (begin, end)), out in zip(plan, outs):
        for k in range(moves):
            tag = tags[(level - 1) * moves + k]
            for unit in range(begin, end):
                at = (unit - begin) * SUB
                out[k, at : at + SUB, :] = pick(
                    tag, unit, state, arrived[:level], slots, rows, moves
                )


def primitives(cons):
    density = cons[0]
    inverse = 1.0 / density
    vel = [cons[1] * inverse, cons[2] * inverse, cons[3] * inverse]
    kinetic = cons[1] * vel[0] + cons[2] * vel[1] + cons[3] * vel[2]
    pressure = (gamma_ratio - 1.0) * (cons[4] - 0.5 * kinetic)
    return [density, vel[0], vel[1], vel[2], pressure]


def half_minmod(lower, upper):
    both = jnp.maximum(0.0, jnp.minimum(lower, upper)) + jnp.minimum(
        0.0, jnp.maximum(lower, upper)
    )
    return 0.5 * both


def half_slopes(before, here, after):
    return [half_minmod(h - b, a - h) for b, h, a in zip(before, here, after)]


def plus(a, b):
    return [x + y for x, y in zip(a, b)]


def minus(a, b):
    return [x - y for x, y in zip(a, b)]


def side_terms(prim, normal):
    density, vel, pressure = prim[0], prim[1:4], prim[4]
    along = vel[normal]
    mom = [density * v for v in vel]
    kinetic = mom[0] * vel[0] + mom[1] * vel[1] + mom[2] * vel[2]
    energy = pressure * (1.0 / (gamma_ratio - 1.0)) + 0.5 * kinetic
    flux = [m * along for m in mom]
    flux[normal] = flux[normal] + pressure
    scaled = gamma_ratio * pressure
    speed = jnp.abs(along) + scaled * lax.rsqrt(scaled * density)
    return [density] + mom + [energy], [mom[normal]] + flux + [(energy + pressure) * along], speed


def twice_flux(left, right, normal):
    left_cons, left_flux, left_speed = side_terms(left, normal)
    right_cons, right_flux, right_speed = side_terms(right, normal)
    speed = jnp.maximum(left_speed, right_speed)
    return [
        (fl + fr) - speed * (ur - ul)
        for fl, fr, ul, ur in zip(left_flux, right_flux, left_cons, right_cons)
    ]


def lane_of():
    return lax.broadcasted_iota(jnp.int32, (SUB, LANES), 1)


def sub_of():
    return lax.broadcasted_iota(jnp.int32, (SUB, LANES), 0)


def lane_roll(value, amount):
    amount = amount % LANES
    return value if amount == 0 else pltpu.roll(value, amount, 1)


class Shape:
    def __init__(self, rows, edge):
        self.rows, self.edge = rows, edge
        self.halves = rows // edge
        self.width = 2 * edge
        self.fit = LANES // self.width
        self.slabs = rows // SUB
        self.pad = 2 * self.halves

    def at(self, f, row):
        start = (f * self.rows + row) * SUB
        return pl.ds(start if isinstance(start, int) else pl.multiple_of(start, SUB), SUB)

    def across(self, f, slab, sub):
        return pl.ds((f * self.rows + slab * SUB) * SUB + sub, SUB, stride=SUB)

    def grid(self):
        return jax.ShapeDtypeStruct((NF * self.rows * SUB, LANES), f32)

    def faces(self):
        x = jax.ShapeDtypeStruct((2, NF, self.pad, SUB, LANES), f32)
        y = jax.ShapeDtypeStruct((NF, self.edge // self.fit, SUB, LANES), f32)
        z = jax.ShapeDtypeStruct((NF, self.rows, LANES), f32)
        return [x, y, y, z, z]


def in_turn(count, *phases):
    for step in range(count + len(phases) - 1):
        for late, phase in enumerate(phases):
            if 0 <= step - late < count:
                phase(step - late)


def send_slab(shape, prim, y_lo, y_hi, z_lo, z_hi, slab):
    lane = lane_of()
    halves = shape.halves
    for f in FIELDS:
        lo = hi = None
        for k in range(shape.fit):
            row = slab * SUB + k * halves
            below = lane_roll(prim[shape.at(f, row), :], shape.width * k)
            above = lane_roll(prim[shape.at(f, row + halves - 1), :], shape.width * (k + 1))
            if lo is None:
                lo, hi = below, above
            else:
                mine = lane >= shape.width * k
                lo = jnp.where(mine, below, lo)
                hi = jnp.where(mine, above, hi)
        y_lo[f, slab] = lo
        y_hi[f, slab] = hi
        to = pl.ds(slab * SUB, SUB) if isinstance(slab, int) else pl.ds(
            pl.multiple_of(slab * SUB, SUB), SUB
        )
        z_lo[f, to, :] = prim[shape.across(f, slab, 0), :]
        z_hi[f, to, :] = prim[shape.across(f, slab, SUB - 1), :]


def send_x(shape, prim, faces, low=True, high=True):
    for f in FIELDS:
        for i in range(shape.pad):
            if high:
                faces[0, f, i] = prim[shape.at(f, shape.rows - shape.pad + i), :]
            if low:
                faces[1, f, i] = prim[shape.at(f, i), :]


def assemble_kernel(tags, state, *refs, held, slabs, slots, moves, occ, shape, first):
    given = len(held)
    arrived = group_levels(refs[:given], held)
    outs = refs[given + (0 if first else 7) :]
    field, prim, y_lo, y_hi, z_lo, z_hi, x_faces = outs[:7]
    blocks = outs[-1]
    units = NF * shape.slabs
    for b in range(occ):
        tag = tags[2 * moves + b]
        for unit in range(slabs[0] * NF, slabs[1] * NF):
            at = (b * units + unit) * SUB
            blocks[at : at + SUB, :] = pick(tag, unit, state, arrived, slots, shape.rows, moves)
    for slab in range(*slabs):
        for i in range(SUB):
            row = slab * SUB + i
            cons = [
                blocks[pl.ds((slab * NF + f) * SUB + i, occ, stride=units * SUB), :] for f in FIELDS
            ]
            for f, (c, w) in enumerate(zip(cons, primitives(cons))):
                field[shape.at(f, row), :] = c
                prim[shape.at(f, row), :] = w
        send_slab(shape, prim, y_lo, y_hi, z_lo, z_hi, slab)
    if first:
        canvas = outs[7]

        def clear(i, carry):
            for c in range(canvas.shape[0]):
                canvas[c, pl.ds(pl.multiple_of(i * SUB, SUB), SUB), :] = jnp.zeros((SUB, LANES), f32)
            return carry

        lax.fori_loop(0, canvas.shape[1] // SUB, clear, 0)
    send_x(shape, prim, x_faces, low=first, high=not first)


def sweep_z_kernel(prim, z_lo, z_hi, z_prev, z_next, total, flux_z, right_z, left, right, flux, *, shape):
    edge, rows = shape.edge, shape.rows

    def ghost(a):
        at = pl.ds(a * SUB, SUB)
        low = [z_lo[f, at, :] for f in FIELDS]
        high = [z_hi[f, at, :] for f in FIELDS]
        prev = [z_prev[f, at, :] for f in FIELDS]
        after = [z_next[f, at, :] for f in FIELDS]
        below = [lane_roll(v, -(edge - 1)) for v in prev]
        before = [lane_roll(v, -(edge - 2)) for v in prev]
        second = [lane_roll(v, -1) for v in low]
        lefts = plus(below, half_slopes(before, below, low))
        rights = minus(low, half_slopes(below, low, second))
        fluxes = twice_flux(lefts, rights, 2)
        last = [lane_roll(v, -(edge - 1)) for v in high]
        beyond = [lane_roll(v, -1) for v in after]
        over = minus(after, half_slopes(last, after, beyond))
        for f in FIELDS:
            flux_z[f, at, :] = lane_roll(fluxes[f], edge - 1)
            right_z[f, at, :] = over[f]

    lane = lane_of()
    z_of = lax.rem(lane, edge)
    sub = sub_of()
    first_z, last_z = z_of == 0, z_of == edge - 1
    first_sub, last_sub = sub == 0, sub == SUB - 1
    higher = lane - z_of + lax.rem(z_of + 1, edge)
    lower = lane - z_of + lax.rem(z_of + edge - 1, edge)

    def insert(ref, f, row):
        return jnp.broadcast_to(ref[f, pl.ds(row, 1), :], (SUB, LANES))

    def up(value, f, row, ghosts):
        across = jnp.where(last_sub, insert(ghosts, f, row), pltpu.roll(value, SUB - 1, 0))
        return jnp.take_along_axis(jnp.where(first_z, across, value), higher, axis=1)

    def down(value, f, row, ghosts):
        across = jnp.where(first_sub, insert(ghosts, f, row), pltpu.roll(value, 1, 0))
        return jnp.take_along_axis(jnp.where(last_z, across, value), lower, axis=1)

    def slopes(slab):
        ghost(slab)
        for row in range(slab * SUB, (slab + 1) * SUB):
            for f in FIELDS:
                at = shape.at(f, row)
                mine = prim[at, :]
                shift = half_minmod(mine - down(mine, f, row, z_prev), up(mine, f, row, z_next) - mine)
                left[at, :] = mine + shift
                right[at, :] = mine - shift

    def fluxes(slab):
        for row in range(slab * SUB, (slab + 1) * SUB):
            lefts = [left[shape.at(f, row), :] for f in FIELDS]
            rights = [up(right[shape.at(f, row), :], f, row, right_z) for f in FIELDS]
            for f, value in enumerate(twice_flux(lefts, rights, 2)):
                flux[shape.at(f, row), :] = value

    def differences(slab):
        for row in range(slab * SUB, (slab + 1) * SUB):
            for f in FIELDS:
                at = shape.at(f, row)
                mine = flux[at, :]
                total[at, :] = mine - down(mine, f, row, flux_z)

    in_turn(shape.slabs, slopes, fluxes, differences)


def sweep_x_kernel(prim, x_faces, sofar, total, *, shape):
    halves, edge = shape.halves, shape.edge

    def cells(x, h):
        if x < 0:
            return [x_faces[0, f, (x + 2) * halves + h] for f in FIELDS]
        if x >= edge:
            return [x_faces[1, f, (x - edge) * halves + h] for f in FIELDS]
        return [prim[shape.at(f, x * halves + h), :] for f in FIELDS]

    for h in range(halves):
        left = below = None
        ahead = [cells(x, h) for x in (-2, -1, 0)]
        for x in range(-1, edge + 1):
            shift = half_slopes(*ahead)
            if left is not None:
                flux = twice_flux(left, minus(ahead[1], shift), 0)
                if below is not None:
                    for f in FIELDS:
                        at = shape.at(f, (x - 1) * halves + h)
                        total[at, :] = sofar[at, :] + (flux[f] - below[f])
                below = flux
            left = plus(ahead[1], shift)
            if x < edge:
                ahead = ahead[1:] + [cells(x + 2, h)]


def sweep_y(prim, y_lo, y_hi, y_prev, y_next, sofar, ghost_prim, ghost_flux, left, right, flux, turned,
            shape, finish, after_slab):
    edge, halves, fit, width = shape.edge, shape.halves, shape.fit, shape.width
    lane = lane_of()
    upper = lax.rem(lane, width) >= edge

    def prepare(q):
        low = [y_lo[f, q] for f in FIELDS]
        high = [y_hi[f, q] for f in FIELDS]
        below = [y_prev[f, q] for f in FIELDS]
        after = [y_next[f, q] for f in FIELDS]
        before = [lane_roll(v, edge) for v in below]
        first = [lane_roll(v, edge) for v in low]
        lefts = plus(below, half_slopes(before, below, first))
        rights = minus(first, half_slopes(below, first, low))
        fluxes = twice_flux(lefts, rights, 1)
        last = [lane_roll(v, -edge) for v in high]
        beyond = [lane_roll(v, -edge) for v in after]
        over = minus(after, half_slopes(last, after, beyond))
        for f in FIELDS:
            ghost_prim[f, q] = jnp.where(upper, below[f], after[f])
            ghost_flux[f, q] = jnp.where(upper, fluxes[f], over[f])

    top_lanes = lane >= LANES - edge
    low_lanes = lane < edge

    def up(values, insert):
        rolled = [lane_roll(v, -edge) for v in values]
        follow = rolled[1:] + [insert]
        return [jnp.where(top_lanes, n, r) for r, n in zip(rolled, follow)]

    def down(values, insert):
        rolled = [lane_roll(v, edge) for v in values]
        lead = [insert] + rolled[:-1]
        return [jnp.where(low_lanes, n, r) for r, n in zip(rolled, lead)]

    def each(q):
        for k in range(fit):
            yield -(width * k + edge), (q * fit + k) * halves

    def slopes(q):
        prepare(q)
        for turn, base in each(q):
            for f in FIELDS:
                mine = [prim[shape.at(f, base + h), :] for h in range(halves)]
                ghost = lane_roll(ghost_prim[f, q], turn)
                over, under = up(mine, ghost), down(mine, ghost)
                for h in range(halves):
                    shift = half_minmod(mine[h] - under[h], over[h] - mine[h])
                    left[shape.at(f, base + h), :] = mine[h] + shift
                    right[shape.at(f, base + h), :] = mine[h] - shift

    def fluxes(q):
        for turn, base in each(q):
            rights = []
            for f in FIELDS:
                mine = [right[shape.at(f, base + h), :] for h in range(halves)]
                ghost = lane_roll(ghost_flux[f, q], turn)
                turned[shape.at(f, base), :] = ghost
                rights.append(up(mine, ghost))
            for h in range(halves):
                lefts = [left[shape.at(f, base + h), :] for f in FIELDS]
                result = twice_flux(lefts, [rights[f][h] for f in FIELDS], 1)
                for f in FIELDS:
                    flux[shape.at(f, base + h), :] = result[f]

    def differences(q):
        for turn, base in each(q):
            total = [[None] * NF for _ in range(halves)]
            for f in FIELDS:
                mine = [flux[shape.at(f, base + h), :] for h in range(halves)]
                under = down(mine, turned[shape.at(f, base), :])
                for h in range(halves):
                    total[h][f] = sofar[shape.at(f, base + h), :] + (mine[h] - under[h])
            for h in range(halves):
                finish(base + h, total[h])

    in_turn(edge // fit, slopes, fluxes, differences, after_slab)


def sweep_y_one_kernel(field, prim, y_lo, y_hi, y_prev, y_next, sofar, *refs, shape):
    one, one_prim, x_faces, out_y_lo, out_y_hi, z_lo, z_hi = refs[:7]

    def finish(row, total):
        cons = [field[shape.at(f, row), :] - (0.5 * time_step) * total[f] for f in FIELDS]
        for f, (c, w) in enumerate(zip(cons, primitives(cons))):
            one[shape.at(f, row), :] = c
            one_prim[shape.at(f, row), :] = w

    def after_slab(q):
        send_slab(shape, one_prim, out_y_lo, out_y_hi, z_lo, z_hi, q)

    sweep_y(prim, y_lo, y_hi, y_prev, y_next, sofar, *refs[7:], shape, finish, after_slab)
    send_x(shape, one_prim, x_faces)


def sweep_y_two_kernel(own, field, one, prim, y_lo, y_hi, y_prev, y_next, sofar, zeros, out,
                       canvas, *refs, shape, occ, groups):
    scratch, (result, sems) = refs[:6], refs[6:]
    rows = shape.rows
    span = SUB * SUB

    def finish(row, total):
        for f in FIELDS:
            at = shape.at(f, row)
            advanced = one[at, :] - (0.5 * time_step) * total[f]
            result[at, :] = 0.5 * field[at, :] + 0.5 * advanced

    def copy(part):
        begin = part * span if isinstance(part, int) else pl.multiple_of(part * span, span)
        at = pl.ds(begin, span)
        return pltpu.make_async_copy(canvas.at[:, at, :], out.at[:, at, :], sems.at[part])

    def after_slab(q):
        for b in range(occ):
            slot = own[b]
            to = pl.ds(q * span + lax.rem(slot, SUB), SUB, stride=SUB)
            for f in FIELDS:
                canvas[f * groups + slot // SUB, to, :] = result[shape.across(f, q, b), :]
        copy(q).start()

    sweep_y(prim, y_lo, y_hi, y_prev, y_next, sofar, *scratch, shape, finish, after_slab)
    for part in range(shape.slabs):
        copy(part).wait()


def shards(state, send_slots, recv_slots, owner_slot):
    slots, _, cells = state.shape
    moves = send_slots.shape[2]
    size_x, size_y, size_z = (lax.axis_size(axis) for axis in AXES)
    occ = owner_slot.shape[0] // (size_x * size_y * size_z)
    edge = round(cells ** (1 / 3))
    rows = cells // LANES
    groups = slots // SUB
    shape = Shape(rows, edge)
    units = NF * shape.slabs
    pieces = split_units(units, (3, 5, 5, 4, 3))
    firsts = split_units(units, (3, 5, 7, 5))

    bit_z = size_z.bit_length() - 2
    bit_y = bit_z + size_y.bit_length() - 1
    bit_x = bit_y + size_x.bit_length() - 1
    pair_bits = (bit_x, bit_y, bit_z)

    def swapped(value, level):
        mask = 2 ** pair_bits[level]
        pairs = [(source, source ^ mask) for source in range(lax.axis_size(AXES))]
        return lax.ppermute(value, AXES, pairs)

    rows_of_state = (
        state.reshape(groups, SUB, NF, rows, LANES)
        .transpose(2, 0, 3, 1, 4)
        .reshape(NF * groups * rows * SUB, LANES)
    )
    state_there = pltpu.with_memory_space_constraint(rows_of_state, HBM)
    send_there = pltpu.with_memory_space_constraint(send_slots, HBM)
    device = lax.axis_index(AXES)
    own = lax.dynamic_slice(owner_slot, (device * occ,), (occ,))
    sizes = dict(slots=slots, moves=moves)

    def message(piece):
        begin, end = piece
        return jax.ShapeDtypeStruct((moves, (end - begin) * SUB, LANES), f32)

    head = firsts[0]
    sent = [None] * len(firsts)
    sent[0] = pl.pallas_call(
        functools.partial(first_kernel, piece=head, rows=rows, **sizes),
        out_shape=message(head),
        in_specs=[whole(HBM)] * 2,
        out_specs=whole(VMEM),
        scratch_shapes=[
            SMEM(send_slots.shape, jnp.int32),
            VMEM(((head[1] - head[0]) * groups * SUB * SUB, LANES), f32),
            pltpu.SemaphoreType.DMA((1 + (head[1] - head[0]) * groups,)),
        ],
        compiler_params=params(),
        name="pack_first",
    )(send_there, state_there)
    tags, token, *sent[1:] = pl.pallas_call(
        functools.partial(rest_kernel, pieces=firsts[1:], rows=rows, occ=occ, **sizes),
        out_shape=[
            jax.ShapeDtypeStruct((2 * moves + occ,), jnp.int32),
            jax.ShapeDtypeStruct((SUB, LANES), f32),
        ]
        + [message(piece) for piece in firsts[1:]],
        in_specs=[whole(SMEM)] * 3 + [whole(VMEM)],
        out_specs=[whole(SMEM)] + [whole(VMEM)] * len(firsts),
        scratch_shapes=[SMEM((slots + SUB,), jnp.int32)],
        compiler_params=params(),
        name="pack_rest",
    )(send_slots, recv_slots, own, rows_of_state)

    cuts = (firsts, pieces, pieces)
    got = [[None] * len(cut) for cut in cuts]

    def holding(levels, begin, end):
        found = [
            ((level, piece), got[level][p])
            for level in levels
            for p, piece in enumerate(cuts[level])
            if piece[0] < end and piece[1] > begin
        ]
        return found

    def make(wanted, through):
        found = {}
        for level, p in wanted:
            for key, value in holding(range(level), *pieces[p]):
                found[key] = value
        plan = tuple((level, pieces[p]) for level, p in wanted)
        given, passed, made = len(found), len(through), len(wanted)
        outs = pl.pallas_call(
            functools.partial(
                pick_kernel, plan=plan, held=tuple(found), passed=passed, rows=rows, **sizes
            ),
            out_shape=[message(piece) for _, piece in plan]
            + [jax.ShapeDtypeStruct(t.shape, f32) for t in through],
            in_specs=[whole(SMEM)] + [whole(VMEM)] * (1 + given) + [whole(pl.ANY)] * passed,
            out_specs=[whole(VMEM)] * made + [whole(pl.ANY)] * passed,
            input_output_aliases={2 + given + i: made + i for i in range(passed)},
            compiler_params=params(),
            cost_estimate=cost(10**9, 10**9),
            name="pick_" + "_".join("%d%d" % w for w in wanted),
        )(tags, rows_of_state, *found.values(), *through)
        return outs[:made], outs[made:]

    steps = [
        ([(1, 0)], [2], []),
        ([(1, 1)], [3], []),
        ([(1, 2), (2, 0)], [], []),
        ([(1, 3), (2, 1)], [], []),
        ([(1, 4), (2, 2)], [], [0]),
        ([(2, 3)], [], [1]),
        ([(2, 4)], [], [2]),
    ]
    got[0][0] = swapped(sent[0], 0)
    got[0][1] = swapped(sent[1], 0)
    for wanted, leaving, awaited in steps:
        through = [token] + [sent[p] for p in leaving] + [got[2][p] for p in awaited]
        made, (token, *passed) = make(wanted, through)
        for p, value in zip(leaving, passed):
            got[0][p] = swapped(value, 0)
        for (level, p), value in reversed(list(zip(wanted, made))):
            got[level][p] = swapped(value, level)
        for p, value in zip(awaited, passed[len(leaving) :]):
            got[2][p] = value

    grid = shape.grid()
    face_x, face_y, _, face_z, _ = shape.faces()
    part = [grid, grid, face_y, face_y, face_z, face_z, face_x]
    canvas = jax.ShapeDtypeStruct((NF * groups, rows * SUB, LANES), f32)
    full = pieces[-1][0] // NF

    def assemble(slabs, before):
        first = not before
        found = dict(holding(range(3), slabs[0] * NF, slabs[1] * NF))
        shapes = part + [canvas] * first
        fixed = 2 + len(found)
        return pl.pallas_call(
            functools.partial(
                assemble_kernel, held=tuple(found), slabs=slabs, occ=occ, shape=shape,
                first=first, **sizes,
            ),
            out_shape=shapes,
            in_specs=[whole(SMEM)] + [whole(VMEM)] * (1 + len(found) + len(before)),
            out_specs=[whole(VMEM)] * len(shapes),
            scratch_shapes=[VMEM((occ * NF * rows, LANES), f32)],
            input_output_aliases={fixed + i: i for i in range(len(before))},
            compiler_params=params(),
            name="assemble_%d" % slabs[0],
        )(tags, rows_of_state, *found.values(), *before)

    *made, blank = assemble((0, full), [])
    *made, x_faces = assemble((full, shape.slabs), made)
    made = made[:2] + [x_faces] + made[2:]

    def ring(value, axis, step):
        size = lax.axis_size(axis)
        return lax.ppermute(value, axis, [(i, (i + step) % size) for i in range(size)])

    def flux_sums(prim, x_faces, y_lo, y_hi, z_lo, z_hi):
        if size_x == 2:
            x_faces = ring(x_faces, "gx", 1)
        else:
            x_faces = jnp.stack([ring(x_faces[0], "gx", 1), ring(x_faces[1], "gx", -1)])
        y_prev, y_next = ring(y_hi, "gy", 1), ring(y_lo, "gy", -1)
        z_prev, z_next = ring(z_hi, "gz", 1), ring(z_lo, "gz", -1)
        ghost = VMEM((NF, rows, LANES), f32)
        work = [VMEM(grid.shape, f32)] * 3
        total = pl.pallas_call(
            functools.partial(sweep_z_kernel, shape=shape),
            out_shape=grid,
            in_specs=[whole(VMEM)] * 5,
            out_specs=whole(VMEM),
            scratch_shapes=[ghost] * 2 + work,
            compiler_params=params(),
            name="sweep_z",
        )(prim, z_lo, z_hi, z_prev, z_next)
        total = pl.pallas_call(
            functools.partial(sweep_x_kernel, shape=shape),
            out_shape=grid,
            in_specs=[whole(VMEM)] * 3,
            out_specs=whole(VMEM),
            input_output_aliases={2: 0},
            compiler_params=params(),
            name="sweep_x",
        )(prim, x_faces, total)
        return y_lo, y_hi, y_prev, y_next, total

    produced = [grid, grid] + shape.faces()
    scratch = [VMEM(face_y.shape, f32)] * 2 + [VMEM(grid.shape, f32)] * 4
    field, prim = made[0], made[1]
    sums = flux_sums(prim, *made[2:])
    made = pl.pallas_call(
        functools.partial(sweep_y_one_kernel, shape=shape),
        out_shape=produced,
        in_specs=[whole(VMEM)] * 7,
        out_specs=[whole(VMEM)] * len(produced),
        scratch_shapes=scratch,
        compiler_params=params(),
        name="sweep_y_one",
    )(field, prim, *sums)
    one, one_prim = made[0], made[1]
    sums = flux_sums(one_prim, *made[2:])
    out, _ = pl.pallas_call(
        functools.partial(sweep_y_two_kernel, shape=shape, occ=occ, groups=groups),
        out_shape=[canvas, canvas],
        in_specs=[whole(SMEM)] + [whole(VMEM)] * 9,
        out_specs=[whole(HBM), whole(VMEM)],
        scratch_shapes=scratch
        + [
            VMEM(grid.shape, f32),
            pltpu.SemaphoreType.DMA((shape.slabs,)),
        ],
        input_output_aliases={9: 1},
        compiler_params=params(),
        name="sweep_y_two",
    )(own, field, one, one_prim, *sums, blank)
    return (
        out.reshape(NF, groups, rows, SUB, LANES)
        .transpose(1, 3, 0, 2, 4)
        .reshape(slots, NF, cells)
    )


def solution(mesh):
    placed = (
        P(AXES, None, None),
        P(None, AXES, None),
        P(None, AXES, None),
        P(),
    )
    return jax.shard_map(
        shards,
        mesh=mesh,
        in_specs=placed,
        out_specs=P(AXES, None, None),
        check_vma=False,
    )
```

```python
import functools

import jax
import jax.numpy as jnp
from jax import lax
from jax.experimental import pallas as pl
from jax.experimental.pallas import tpu as pltpu
from jax.sharding import PartitionSpec as P

gamma_ratio = 1.4
time_step = 0.05
LANES = 128
SUB = 8
NF = 5
FIELDS = range(NF)
AXES = ("gx", "gy", "gz")

VMEM = pltpu.VMEM
SMEM = pltpu.SMEM
HBM = pltpu.HBM
f32 = jnp.float32


def whole(space):
    return pl.BlockSpec(memory_space=space)


def params():
    return pltpu.CompilerParams(vmem_limit_bytes=16 * 1024 * 1024)


def cost(flops, moved):
    return pl.CostEstimate(flops=flops, bytes_accessed=moved, transcendentals=0)


def split_units(units, shares):
    ends = [units * sum(shares[: i + 1]) // sum(shares) for i in range(len(shares))]
    return list(zip([0] + ends[:-1], ends))


def from_state(state, tag, unit, slots, rows):
    slab, field = unit // NF, unit % NF
    groups = slots // SUB
    base = (tag // SUB) * (rows * SUB) + lax.rem(tag, SUB)
    start = base + (field * groups * rows + slab * SUB) * SUB
    return state[pl.ds(start, SUB, stride=SUB), :]


def pick(tag, unit, state, arrived, slots, rows, moves):
    value = from_state(state, jnp.minimum(tag, slots - 1), unit, slots, rows)
    for level, held in enumerate(arrived):
        base = slots + level * moves
        index = jnp.clip(tag - base, 0, moves - 1)
        for (begin, end), ref in held:
            if begin <= unit < end:
                at = (unit - begin) * SUB
                value = jnp.where(tag >= base, ref[index, at : at + SUB, :], value)
    return value


def first_kernel(send_hbm, state_hbm, out, send, held, sems, *, piece, slots, rows, moves):
    span = SUB * SUB
    groups = slots // SUB
    copies = [pltpu.make_async_copy(send_hbm, send, sems.at[0])]
    for unit in range(*piece):
        slab, field = unit // NF, unit % NF
        for g in range(groups):
            at = ((field * groups + g) * rows + slab * SUB) * SUB
            to = ((unit - piece[0]) * groups + g) * span
            copies.append(
                pltpu.make_async_copy(
                    state_hbm.at[pl.ds(at, span), :],
                    held.at[pl.ds(to, span), :],
                    sems.at[len(copies)],
                )
            )
    for c in copies:
        c.start()
    for c in copies:
        c.wait()
    for k in range(moves):
        slot = jnp.minimum(send[0, 0, k], slots - 1)
        base = (slot // SUB) * span + lax.rem(slot, SUB)
        for i in range(piece[1] - piece[0]):
            out[k, i * SUB : (i + 1) * SUB, :] = held[
                pl.ds(base + i * groups * span, SUB, stride=SUB), :
            ]


def rest_kernel(send, recv, own, state, tags, token, *refs, pieces, slots, rows, moves, occ):
    outs, where = refs[:-1], refs[-1]
    token[...] = jnp.zeros_like(token)
    for slot in range(slots):
        where[slot] = slot
    for level in range(3):
        if level:
            for k in range(moves):
                slot = jnp.minimum(send[level, 0, k], slots - 1)
                tags[(level - 1) * moves + k] = where[slot]
        for k in range(moves):
            where[recv[level, 0, k]] = slots + level * moves + k
    for b in range(occ):
        tags[2 * moves + b] = where[own[b]]
    for k in range(moves):
        slot = jnp.minimum(send[0, 0, k], slots - 1)
        for (begin, end), out in zip(pieces, outs):
            for unit in range(begin, end):
                at = (unit - begin) * SUB
                out[k, at : at + SUB, :] = from_state(state, slot, unit, slots, rows)


def group_levels(refs, held):
    levels = [[], [], []]
    for ref, (level, piece) in zip(refs, held):
        levels[level].append((piece, ref))
    return levels


def pick_kernel(tags, state, *refs, plan, held, passed, slots, rows, moves):
    given = len(held)
    arrived = group_levels(refs[:given], held)
    outs = refs[given + passed :]
    for (level, (begin, end)), out in zip(plan, outs):
        for k in range(moves):
            tag = tags[(level - 1) * moves + k]
            for unit in range(begin, end):
                at = (unit - begin) * SUB
                out[k, at : at + SUB, :] = pick(
                    tag, unit, state, arrived[:level], slots, rows, moves
                )


def primitives(cons):
    density = cons[0]
    inverse = 1.0 / density
    vel = [cons[1] * inverse, cons[2] * inverse, cons[3] * inverse]
    kinetic = cons[1] * vel[0] + cons[2] * vel[1] + cons[3] * vel[2]
    pressure = (gamma_ratio - 1.0) * (cons[4] - 0.5 * kinetic)
    return [density, vel[0], vel[1], vel[2], pressure]


def half_minmod(lower, upper):
    both = jnp.maximum(0.0, jnp.minimum(lower, upper)) + jnp.minimum(
        0.0, jnp.maximum(lower, upper)
    )
    return 0.5 * both


def half_slopes(before, here, after):
    return [half_minmod(h - b, a - h) for b, h, a in zip(before, here, after)]


def plus(a, b):
    return [x + y for x, y in zip(a, b)]


def minus(a, b):
    return [x - y for x, y in zip(a, b)]


def side_terms(prim, normal):
    density, vel, pressure = prim[0], prim[1:4], prim[4]
    along = vel[normal]
    mom = [density * v for v in vel]
    kinetic = mom[0] * vel[0] + mom[1] * vel[1] + mom[2] * vel[2]
    energy = pressure * (1.0 / (gamma_ratio - 1.0)) + 0.5 * kinetic
    flux = [m * along for m in mom]
    flux[normal] = flux[normal] + pressure
    scaled = gamma_ratio * pressure
    speed = jnp.abs(along) + scaled * lax.rsqrt(scaled * density)
    return [density] + mom + [energy], [mom[normal]] + flux + [(energy + pressure) * along], speed


def twice_flux(left, right, normal):
    left_cons, left_flux, left_speed = side_terms(left, normal)
    right_cons, right_flux, right_speed = side_terms(right, normal)
    speed = jnp.maximum(left_speed, right_speed)
    return [
        (fl + fr) - speed * (ur - ul)
        for fl, fr, ul, ur in zip(left_flux, right_flux, left_cons, right_cons)
    ]


def lane_of():
    return lax.broadcasted_iota(jnp.int32, (SUB, LANES), 1)


def sub_of():
    return lax.broadcasted_iota(jnp.int32, (SUB, LANES), 0)


def lane_roll(value, amount):
    amount = amount % LANES
    return value if amount == 0 else pltpu.roll(value, amount, 1)


class Shape:
    def __init__(self, rows, edge):
        self.rows, self.edge = rows, edge
        self.halves = rows // edge
        self.width = 2 * edge
        self.fit = LANES // self.width
        self.slabs = rows // SUB
        self.pad = 2 * self.halves

    def at(self, f, row):
        start = (f * self.rows + row) * SUB
        return pl.ds(start if isinstance(start, int) else pl.multiple_of(start, SUB), SUB)

    def across(self, f, slab, sub):
        return pl.ds((f * self.rows + slab * SUB) * SUB + sub, SUB, stride=SUB)

    def grid(self):
        return jax.ShapeDtypeStruct((NF * self.rows * SUB, LANES), f32)

    def faces(self):
        x = jax.ShapeDtypeStruct((2, NF, self.pad, SUB, LANES), f32)
        y = jax.ShapeDtypeStruct((NF, self.edge // self.fit, SUB, LANES), f32)
        z = jax.ShapeDtypeStruct((NF, self.rows, LANES), f32)
        return [x, y, y, z, z]


def in_turn(count, *phases):
    for step in range(count + len(phases) - 1):
        for late, phase in enumerate(phases):
            if 0 <= step - late < count:
                phase(step - late)


def odd_y():
    return lax.rem(lax.axis_index("gy"), 2) == 1


def send_slab(shape, prim, y_one, y_two, z_lo, z_hi, slab):
    lane = lane_of()
    halves = shape.halves
    odd = odd_y()
    for f in FIELDS:
        lo = hi = None
        for k in range(shape.fit):
            row = slab * SUB + k * halves
            below = lane_roll(prim[shape.at(f, row), :], shape.width * k)
            above = lane_roll(prim[shape.at(f, row + halves - 1), :], shape.width * (k + 1))
            if lo is None:
                lo, hi = below, above
            else:
                mine = lane >= shape.width * k
                lo = jnp.where(mine, below, lo)
                hi = jnp.where(mine, above, hi)
        y_one[f, slab] = jnp.where(odd, lo, hi)
        y_two[f, slab] = jnp.where(odd, hi, lo)
        to = pl.ds(slab * SUB, SUB) if isinstance(slab, int) else pl.ds(
            pl.multiple_of(slab * SUB, SUB), SUB
        )
        z_lo[f, to, :] = prim[shape.across(f, slab, 0), :]
        z_hi[f, to, :] = prim[shape.across(f, slab, SUB - 1), :]


def send_x(shape, prim, faces, low=True, high=True):
    for f in FIELDS:
        for i in range(shape.pad):
            if high:
                faces[0, f, i] = prim[shape.at(f, shape.rows - shape.pad + i), :]
            if low:
                faces[1, f, i] = prim[shape.at(f, i), :]


def assemble_kernel(tags, state, *refs, held, slabs, slots, moves, occ, shape, first):
    given = len(held)
    arrived = group_levels(refs[:given], held)
    outs = refs[given + (0 if first else 7) :]
    field, prim, y_one, y_two, z_lo, z_hi, x_faces = outs[:7]
    blocks = outs[-1]
    units = NF * shape.slabs
    for b in range(occ):
        tag = tags[2 * moves + b]
        for unit in range(slabs[0] * NF, slabs[1] * NF):
            at = (b * units + unit) * SUB
            blocks[at : at + SUB, :] = pick(tag, unit, state, arrived, slots, shape.rows, moves)
    for slab in range(*slabs):
        for i in range(SUB):
            row = slab * SUB + i
            cons = [
                blocks[pl.ds((slab * NF + f) * SUB + i, occ, stride=units * SUB), :] for f in FIELDS
            ]
            for f, (c, w) in enumerate(zip(cons, primitives(cons))):
                field[shape.at(f, row), :] = c
                prim[shape.at(f, row), :] = w
        send_slab(shape, prim, y_one, y_two, z_lo, z_hi, slab)
    if first:
        canvas = outs[7]

        def clear(i, carry):
            for c in range(canvas.shape[0]):
                canvas[c, pl.ds(pl.multiple_of(i * SUB, SUB), SUB), :] = jnp.zeros((SUB, LANES), f32)
            return carry

        lax.fori_loop(0, canvas.shape[1] // SUB, clear, 0)
    send_x(shape, prim, x_faces, low=first, high=not first)


def sweep_z_kernel(prim, z_lo, z_hi, z_prev, z_next, total, flux_z, right_z, left, right, flux, *, shape):
    edge, rows = shape.edge, shape.rows

    def ghost(a):
        at = pl.ds(a * SUB, SUB)
        low = [z_lo[f, at, :] for f in FIELDS]
        high = [z_hi[f, at, :] for f in FIELDS]
        prev = [z_prev[f, at, :] for f in FIELDS]
        after = [z_next[f, at, :] for f in FIELDS]
        below = [lane_roll(v, -(edge - 1)) for v in prev]
        before = [lane_roll(v, -(edge - 2)) for v in prev]
        second = [lane_roll(v, -1) for v in low]
        lefts = plus(below, half_slopes(before, below, low))
        rights = minus(low, half_slopes(below, low, second))
        fluxes = twice_flux(lefts, rights, 2)
        last = [lane_roll(v, -(edge - 1)) for v in high]
        beyond = [lane_roll(v, -1) for v in after]
        over = minus(after, half_slopes(last, after, beyond))
        for f in FIELDS:
            flux_z[f, at, :] = lane_roll(fluxes[f], edge - 1)
            right_z[f, at, :] = over[f]

    lane = lane_of()
    z_of = lax.rem(lane, edge)
    sub = sub_of()
    first_z, last_z = z_of == 0, z_of == edge - 1
    first_sub, last_sub = sub == 0, sub == SUB - 1
    higher = lane - z_of + lax.rem(z_of + 1, edge)
    lower = lane - z_of + lax.rem(z_of + edge - 1, edge)

    def insert(ref, f, row):
        return jnp.broadcast_to(ref[f, pl.ds(row, 1), :], (SUB, LANES))

    def up(value, f, row, ghosts):
        across = jnp.where(last_sub, insert(ghosts, f, row), pltpu.roll(value, SUB - 1, 0))
        return jnp.take_along_axis(jnp.where(first_z, across, value), higher, axis=1)

    def down(value, f, row, ghosts):
        across = jnp.where(first_sub, insert(ghosts, f, row), pltpu.roll(value, 1, 0))
        return jnp.take_along_axis(jnp.where(last_z, across, value), lower, axis=1)

    def slopes(slab):
        ghost(slab)
        for row in range(slab * SUB, (slab + 1) * SUB):
            for f in FIELDS:
                at = shape.at(f, row)
                mine = prim[at, :]
                shift = half_minmod(mine - down(mine, f, row, z_prev), up(mine, f, row, z_next) - mine)
                left[at, :] = mine + shift
                right[at, :] = mine - shift

    def fluxes(slab):
        for row in range(slab * SUB, (slab + 1) * SUB):
            lefts = [left[shape.at(f, row), :] for f in FIELDS]
            rights = [up(right[shape.at(f, row), :], f, row, right_z) for f in FIELDS]
            for f, value in enumerate(twice_flux(lefts, rights, 2)):
                flux[shape.at(f, row), :] = value

    def differences(slab):
        for row in range(slab * SUB, (slab + 1) * SUB):
            for f in FIELDS:
                at = shape.at(f, row)
                mine = flux[at, :]
                total[at, :] = mine - down(mine, f, row, flux_z)

    in_turn(shape.slabs, slopes, fluxes, differences)


def sweep_x_kernel(prim, x_faces, sofar, total, *, shape):
    halves, edge = shape.halves, shape.edge

    def cells(x, h):
        if x < 0:
            return [x_faces[0, f, (x + 2) * halves + h] for f in FIELDS]
        if x >= edge:
            return [x_faces[1, f, (x - edge) * halves + h] for f in FIELDS]
        return [prim[shape.at(f, x * halves + h), :] for f in FIELDS]

    for h in range(halves):
        left = below = None
        ahead = [cells(x, h) for x in (-2, -1, 0)]
        for x in range(-1, edge + 1):
            shift = half_slopes(*ahead)
            if left is not None:
                flux = twice_flux(left, minus(ahead[1], shift), 0)
                if below is not None:
                    for f in FIELDS:
                        at = shape.at(f, (x - 1) * halves + h)
                        total[at, :] = sofar[at, :] + (flux[f] - below[f])
                below = flux
            left = plus(ahead[1], shift)
            if x < edge:
                ahead = ahead[1:] + [cells(x + 2, h)]


def sweep_y(prim, y_one, y_two, got_one, got_two, sofar, ghost_prim, ghost_flux, left, right, flux, turned,
            shape, finish, after_slab):
    edge, halves, fit, width = shape.edge, shape.halves, shape.fit, shape.width
    lane = lane_of()
    upper = lax.rem(lane, width) >= edge
    odd = odd_y()

    def prepare(q):
        low = [jnp.where(odd, y_one[f, q], y_two[f, q]) for f in FIELDS]
        high = [jnp.where(odd, y_two[f, q], y_one[f, q]) for f in FIELDS]
        below = [jnp.where(odd, got_one[f, q], got_two[f, q]) for f in FIELDS]
        after = [jnp.where(odd, got_two[f, q], got_one[f, q]) for f in FIELDS]
        before = [lane_roll(v, edge) for v in below]
        first = [lane_roll(v, edge) for v in low]
        lefts = plus(below, half_slopes(before, below, first))
        rights = minus(first, half_slopes(below, first, low))
        fluxes = twice_flux(lefts, rights, 1)
        last = [lane_roll(v, -edge) for v in high]
        beyond = [lane_roll(v, -edge) for v in after]
        over = minus(after, half_slopes(last, after, beyond))
        for f in FIELDS:
            ghost_prim[f, q] = jnp.where(upper, below[f], after[f])
            ghost_flux[f, q] = jnp.where(upper, fluxes[f], over[f])

    top_lanes = lane >= LANES - edge
    low_lanes = lane < edge

    def up(values, insert):
        rolled = [lane_roll(v, -edge) for v in values]
        follow = rolled[1:] + [insert]
        return [jnp.where(top_lanes, n, r) for r, n in zip(rolled, follow)]

    def down(values, insert):
        rolled = [lane_roll(v, edge) for v in values]
        lead = [insert] + rolled[:-1]
        return [jnp.where(low_lanes, n, r) for r, n in zip(rolled, lead)]

    def each(q):
        for k in range(fit):
            yield -(width * k + edge), (q * fit + k) * halves

    def slopes(q):
        prepare(q)
        for turn, base in each(q):
            for f in FIELDS:
                mine = [prim[shape.at(f, base + h), :] for h in range(halves)]
                ghost = lane_roll(ghost_prim[f, q], turn)
                over, under = up(mine, ghost), down(mine, ghost)
                for h in range(halves):
                    shift = half_minmod(mine[h] - under[h], over[h] - mine[h])
                    left[shape.at(f, base + h), :] = mine[h] + shift
                    right[shape.at(f, base + h), :] = mine[h] - shift

    def fluxes(q):
        for turn, base in each(q):
            rights = []
            for f in FIELDS:
                mine = [right[shape.at(f, base + h), :] for h in range(halves)]
                ghost = lane_roll(ghost_flux[f, q], turn)
                turned[shape.at(f, base), :] = ghost
                rights.append(up(mine, ghost))
            for h in range(halves):
                lefts = [left[shape.at(f, base + h), :] for f in FIELDS]
                result = twice_flux(lefts, [rights[f][h] for f in FIELDS], 1)
                for f in FIELDS:
                    flux[shape.at(f, base + h), :] = result[f]

    def differences(q):
        for turn, base in each(q):
            total = [[None] * NF for _ in range(halves)]
            for f in FIELDS:
                mine = [flux[shape.at(f, base + h), :] for h in range(halves)]
                under = down(mine, turned[shape.at(f, base), :])
                for h in range(halves):
                    total[h][f] = sofar[shape.at(f, base + h), :] + (mine[h] - under[h])
            for h in range(halves):
                finish(base + h, total[h])

    in_turn(edge // fit, slopes, fluxes, differences, after_slab)


def sweep_y_one_kernel(field, prim, y_one, y_two, got_one, got_two, sofar, *refs, shape):
    one, one_prim, x_faces, out_y_one, out_y_two, z_lo, z_hi = refs[:7]

    def finish(row, total):
        cons = [field[shape.at(f, row), :] - (0.5 * time_step) * total[f] for f in FIELDS]
        for f, (c, w) in enumerate(zip(cons, primitives(cons))):
            one[shape.at(f, row), :] = c
            one_prim[shape.at(f, row), :] = w

    def after_slab(q):
        send_slab(shape, one_prim, out_y_one, out_y_two, z_lo, z_hi, q)

    sweep_y(prim, y_one, y_two, got_one, got_two, sofar, *refs[7:], shape, finish, after_slab)
    send_x(shape, one_prim, x_faces)


def sweep_y_two_kernel(own_there, field, one, prim, y_one, y_two, got_one, got_two, sofar, zeros, out,
                       canvas, *refs, shape, occ, groups):
    scratch, (result, sems, own, own_sem) = refs[:6], refs[6:]
    slots = pltpu.make_async_copy(own_there, own, own_sem)
    slots.start()
    rows = shape.rows
    span = SUB * SUB

    def finish(row, total):
        for f in FIELDS:
            at = shape.at(f, row)
            advanced = one[at, :] - (0.5 * time_step) * total[f]
            result[at, :] = 0.5 * field[at, :] + 0.5 * advanced

    def copy(part):
        begin = part * span if isinstance(part, int) else pl.multiple_of(part * span, span)
        at = pl.ds(begin, span)
        return pltpu.make_async_copy(canvas.at[:, at, :], out.at[:, at, :], sems.at[part])

    def after_slab(q):
        if q == 0:
            slots.wait()
        for b in range(occ):
            slot = own[b]
            to = pl.ds(q * span + lax.rem(slot, SUB), SUB, stride=SUB)
            for f in FIELDS:
                canvas[f * groups + slot // SUB, to, :] = result[shape.across(f, q, b), :]
        copy(q).start()

    sweep_y(prim, y_one, y_two, got_one, got_two, sofar, *scratch, shape, finish, after_slab)
    for part in range(shape.slabs):
        copy(part).wait()


def shards(state, send_slots, recv_slots, owner_slot):
    slots, _, cells = state.shape
    moves = send_slots.shape[2]
    size_x, size_y, size_z = (lax.axis_size(axis) for axis in AXES)
    occ = owner_slot.shape[0] // (size_x * size_y * size_z)
    edge = round(cells ** (1 / 3))
    rows = cells // LANES
    groups = slots // SUB
    shape = Shape(rows, edge)
    units = NF * shape.slabs
    cuts = [split_units(units, shares) for shares in ((3, 5, 7, 5), (3, 5, 5, 4, 3), (8, 5, 4, 3))]
    firsts, final = cuts[0], cuts[2]

    bit_z = size_z.bit_length() - 2
    bit_y = bit_z + size_y.bit_length() - 1
    bit_x = bit_y + size_x.bit_length() - 1
    pair_bits = (bit_x, bit_y, bit_z)

    def swapped(value, level):
        mask = 2 ** pair_bits[level]
        pairs = [(source, source ^ mask) for source in range(lax.axis_size(AXES))]
        return lax.ppermute(value, AXES, pairs)

    rows_of_state = (
        state.reshape(groups, SUB, NF, rows, LANES)
        .transpose(2, 0, 3, 1, 4)
        .reshape(NF * groups * rows * SUB, LANES)
    )
    state_there = pltpu.with_memory_space_constraint(rows_of_state, HBM)
    send_there = pltpu.with_memory_space_constraint(send_slots, HBM)
    device = lax.axis_index(AXES)
    own = lax.dynamic_slice(owner_slot, (device * occ,), (occ,))
    sizes = dict(slots=slots, moves=moves)

    def message(piece):
        begin, end = piece
        return jax.ShapeDtypeStruct((moves, (end - begin) * SUB, LANES), f32)

    head = firsts[0]
    sent = [None] * len(firsts)
    sent[0] = pl.pallas_call(
        functools.partial(first_kernel, piece=head, rows=rows, **sizes),
        out_shape=message(head),
        in_specs=[whole(HBM)] * 2,
        out_specs=whole(VMEM),
        scratch_shapes=[
            SMEM(send_slots.shape, jnp.int32),
            VMEM(((head[1] - head[0]) * groups * SUB * SUB, LANES), f32),
            pltpu.SemaphoreType.DMA((1 + (head[1] - head[0]) * groups,)),
        ],
        compiler_params=params(),
        name="pack_first",
    )(send_there, state_there)
    tags, token, *sent[1:] = pl.pallas_call(
        functools.partial(rest_kernel, pieces=firsts[1:], rows=rows, occ=occ, **sizes),
        out_shape=[
            jax.ShapeDtypeStruct((2 * moves + occ,), jnp.int32),
            jax.ShapeDtypeStruct((SUB, LANES), f32),
        ]
        + [message(piece) for piece in firsts[1:]],
        in_specs=[whole(SMEM)] * 3 + [whole(VMEM)],
        out_specs=[whole(SMEM)] + [whole(VMEM)] * len(firsts),
        scratch_shapes=[SMEM((slots + SUB,), jnp.int32)],
        compiler_params=params(),
        name="pack_rest",
    )(send_slots, recv_slots, own, rows_of_state)

    got = [[None] * len(cut) for cut in cuts]

    def holding(levels, begin, end):
        found = [
            ((level, piece), got[level][p])
            for level in levels
            for p, piece in enumerate(cuts[level])
            if piece[0] < end and piece[1] > begin
        ]
        return found

    def make(wanted, through):
        found = {}
        for level, p in wanted:
            for key, value in holding(range(level), *cuts[level][p]):
                found[key] = value
        plan = tuple((level, cuts[level][p]) for level, p in wanted)
        given, passed, made = len(found), len(through), len(wanted)
        outs = pl.pallas_call(
            functools.partial(
                pick_kernel, plan=plan, held=tuple(found), passed=passed, rows=rows, **sizes
            ),
            out_shape=[message(piece) for _, piece in plan]
            + [jax.ShapeDtypeStruct(t.shape, f32) for t in through],
            in_specs=[whole(SMEM)] + [whole(VMEM)] * (1 + given) + [whole(pl.ANY)] * passed,
            out_specs=[whole(VMEM)] * made + [whole(pl.ANY)] * passed,
            input_output_aliases={2 + given + i: made + i for i in range(passed)},
            compiler_params=params(),
            cost_estimate=cost(10**9, 10**9),
            name="pick_" + "_".join("%d%d" % w for w in wanted),
        )(tags, rows_of_state, *found.values(), *through)
        return outs[:made], outs[made:]

    steps = [
        ([(1, 0)], [2], []),
        ([(1, 1)], [3], []),
        ([(1, 2)], [], [(1, 0)]),
        ([(1, 3), (2, 0)], [], []),
        ([(1, 4), (2, 1)], [], []),
        ([(2, 2)], [], [(2, 0)]),
        ([(2, 3)], [], [(2, 1)]),
    ]
    got[0][0] = swapped(sent[0], 0)
    got[0][1] = swapped(sent[1], 0)
    for wanted, leaving, awaited in steps:
        through = [token] + [sent[p] for p in leaving] + [got[level][p] for level, p in awaited]
        made, (token, *passed) = make(wanted, through)
        for p, value in zip(leaving, passed):
            got[0][p] = swapped(value, 0)
        for (level, p), value in reversed(list(zip(wanted, made))):
            got[level][p] = swapped(value, level)
        for (level, p), value in zip(awaited, passed[len(leaving) :]):
            got[level][p] = value

    grid = shape.grid()
    face_x, face_y, _, face_z, _ = shape.faces()
    part = [grid, grid, face_y, face_y, face_z, face_z, face_x]
    canvas = jax.ShapeDtypeStruct((NF * groups, rows * SUB, LANES), f32)
    full = final[-1][0] // NF

    def assemble(slabs, before):
        first = not before
        found = dict(holding(range(3), slabs[0] * NF, slabs[1] * NF))
        shapes = part + [canvas] * first
        fixed = 2 + len(found)
        return pl.pallas_call(
            functools.partial(
                assemble_kernel, held=tuple(found), slabs=slabs, occ=occ, shape=shape,
                first=first, **sizes,
            ),
            out_shape=shapes,
            in_specs=[whole(SMEM)] + [whole(VMEM)] * (1 + len(found) + len(before)),
            out_specs=[whole(VMEM)] * len(shapes),
            scratch_shapes=[VMEM((occ * NF * rows, LANES), f32)],
            input_output_aliases={fixed + i: i for i in range(len(before))},
            compiler_params=params(),
            name="assemble_%d" % slabs[0],
        )(tags, rows_of_state, *found.values(), *before)

    *made, blank = assemble((0, full), [])
    *made, x_faces = assemble((full, shape.slabs), made)
    made = made[:2] + [x_faces] + made[2:]

    def ring(value, axis, step):
        size = lax.axis_size(axis)
        return lax.ppermute(value, axis, [(i, (i + step) % size) for i in range(size)])

    def beside(value, axis, shift):
        size = lax.axis_size(axis)
        pairs = [(i, ((i + shift) ^ 1) - shift) for i in range(size)]
        return lax.ppermute(value, axis, [(i, j % size) for i, j in pairs])

    def flux_sums(prim, x_faces, y_one, y_two, z_lo, z_hi):
        if size_x == 2:
            x_faces = ring(x_faces, "gx", 1)
        else:
            x_faces = jnp.stack([ring(x_faces[0], "gx", 1), ring(x_faces[1], "gx", -1)])
        got_one, got_two = beside(y_one, "gy", 0), beside(y_two, "gy", 1)
        z_prev, z_next = ring(z_hi, "gz", 1), ring(z_lo, "gz", -1)
        ghost = VMEM((NF, rows, LANES), f32)
        work = [VMEM(grid.shape, f32)] * 3
        total = pl.pallas_call(
            functools.partial(sweep_z_kernel, shape=shape),
            out_shape=grid,
            in_specs=[whole(VMEM)] * 5,
            out_specs=whole(VMEM),
            scratch_shapes=[ghost] * 2 + work,
            compiler_params=params(),
            name="sweep_z",
        )(prim, z_lo, z_hi, z_prev, z_next)
        total = pl.pallas_call(
            functools.partial(sweep_x_kernel, shape=shape),
            out_shape=grid,
            in_specs=[whole(VMEM)] * 3,
            out_specs=whole(VMEM),
            input_output_aliases={2: 0},
            compiler_params=params(),
            name="sweep_x",
        )(prim, x_faces, total)
        return y_one, y_two, got_one, got_two, total

    produced = [grid, grid] + shape.faces()
    scratch = [VMEM(face_y.shape, f32)] * 2 + [VMEM(grid.shape, f32)] * 4
    field, prim = made[0], made[1]
    sums = flux_sums(prim, *made[2:])
    made = pl.pallas_call(
        functools.partial(sweep_y_one_kernel, shape=shape),
        out_shape=produced,
        in_specs=[whole(VMEM)] * 7,
        out_specs=[whole(VMEM)] * len(produced),
        scratch_shapes=scratch,
        compiler_params=params(),
        name="sweep_y_one",
    )(field, prim, *sums)
    one, one_prim = made[0], made[1]
    sums = flux_sums(one_prim, *made[2:])
    out, _ = pl.pallas_call(
        functools.partial(sweep_y_two_kernel, shape=shape, occ=occ, groups=groups),
        out_shape=[canvas, canvas],
        in_specs=[whole(HBM)] + [whole(VMEM)] * 9,
        out_specs=[whole(HBM), whole(VMEM)],
        scratch_shapes=scratch
        + [
            VMEM(grid.shape, f32),
            pltpu.SemaphoreType.DMA((shape.slabs,)),
            SMEM((occ,), jnp.int32),
            pltpu.SemaphoreType.DMA,
        ],
        input_output_aliases={9: 1},
        compiler_params=params(),
        name="sweep_y_two",
    )(pltpu.with_memory_space_constraint(own, HBM), field, one, one_prim, *sums, blank)
    return (
        out.reshape(NF, groups, rows, SUB, LANES)
        .transpose(1, 3, 0, 2, 4)
        .reshape(slots, NF, cells)
    )


def solution(mesh):
    placed = (
        P(AXES, None, None),
        P(None, AXES, None),
        P(None, AXES, None),
        P(),
    )
    return jax.shard_map(
        shards,
        mesh=mesh,
        in_specs=placed,
        out_specs=P(AXES, None, None),
        check_vma=False,
    )
```

```python
import functools

import jax
import jax.numpy as jnp
from jax import lax
from jax.experimental import pallas as pl
from jax.experimental.pallas import tpu as pltpu
from jax.sharding import PartitionSpec as P

gamma_ratio = 1.4
time_step = 0.05
LANES = 128
SUB = 8
NF = 5
FIELDS = range(NF)
AXES = ("gx", "gy", "gz")

VMEM = pltpu.VMEM
SMEM = pltpu.SMEM
HBM = pltpu.HBM
f32 = jnp.float32


def whole(space):
    return pl.BlockSpec(memory_space=space)


def params():
    return pltpu.CompilerParams(vmem_limit_bytes=16 * 1024 * 1024)


def cost(flops, moved):
    return pl.CostEstimate(flops=flops, bytes_accessed=moved, transcendentals=0)


def split_units(units, shares):
    ends = [units * sum(shares[: i + 1]) // sum(shares) for i in range(len(shares))]
    return list(zip([0] + ends[:-1], ends))


def from_state(state, tag, unit, slots, rows):
    slab, field = unit // NF, unit % NF
    groups = slots // SUB
    base = (tag // SUB) * (rows * SUB) + lax.rem(tag, SUB)
    start = base + (field * groups * rows + slab * SUB) * SUB
    return state[pl.ds(start, SUB, stride=SUB), :]


def pick(tag, unit, state, arrived, slots, rows, moves):
    value = from_state(state, jnp.minimum(tag, slots - 1), unit, slots, rows)
    for level, held in enumerate(arrived):
        base = slots + level * moves
        index = jnp.clip(tag - base, 0, moves - 1)
        for (begin, end), ref in held:
            if begin <= unit < end:
                at = (unit - begin) * SUB
                value = jnp.where(tag >= base, ref[index, at : at + SUB, :], value)
    return value


def first_kernel(send_hbm, state_hbm, out, send, held, sems, *, piece, slots, rows, moves):
    span = SUB * SUB
    groups = slots // SUB
    copies = [pltpu.make_async_copy(send_hbm, send, sems.at[0])]
    for unit in range(*piece):
        slab, field = unit // NF, unit % NF
        for g in range(groups):
            at = ((field * groups + g) * rows + slab * SUB) * SUB
            to = ((unit - piece[0]) * groups + g) * span
            copies.append(
                pltpu.make_async_copy(
                    state_hbm.at[pl.ds(at, span), :],
                    held.at[pl.ds(to, span), :],
                    sems.at[len(copies)],
                )
            )
    for c in copies:
        c.start()
    for c in copies:
        c.wait()
    for k in range(moves):
        slot = jnp.minimum(send[0, 0, k], slots - 1)
        base = (slot // SUB) * span + lax.rem(slot, SUB)
        for i in range(piece[1] - piece[0]):
            out[k, i * SUB : (i + 1) * SUB, :] = held[
                pl.ds(base + i * groups * span, SUB, stride=SUB), :
            ]


def rest_kernel(send, recv, own, state, tags, token, *refs, pieces, slots, rows, moves, occ):
    outs, where = refs[:-1], refs[-1]
    token[...] = jnp.zeros_like(token)
    for slot in range(slots):
        where[slot] = slot
    for level in range(3):
        if level:
            for k in range(moves):
                slot = jnp.minimum(send[level, 0, k], slots - 1)
                tags[(level - 1) * moves + k] = where[slot]
        for k in range(moves):
            where[recv[level, 0, k]] = slots + level * moves + k
    for b in range(occ):
        tags[2 * moves + b] = where[own[b]]
    for k in range(moves):
        slot = jnp.minimum(send[0, 0, k], slots - 1)
        for (begin, end), out in zip(pieces, outs):
            for unit in range(begin, end):
                at = (unit - begin) * SUB
                out[k, at : at + SUB, :] = from_state(state, slot, unit, slots, rows)


def group_levels(refs, held):
    levels = [[], [], []]
    for ref, (level, piece) in zip(refs, held):
        levels[level].append((piece, ref))
    return levels


def pick_kernel(tags, state, *refs, plan, held, passed, slots, rows, moves):
    given = len(held)
    arrived = group_levels(refs[:given], held)
    outs = refs[given + passed :]
    for (level, (begin, end)), out in zip(plan, outs):
        for k in range(moves):
            tag = tags[(level - 1) * moves + k]
            for unit in range(begin, end):
                at = (unit - begin) * SUB
                out[k, at : at + SUB, :] = pick(
                    tag, unit, state, arrived[:level], slots, rows, moves
                )


def primitives(cons):
    density = cons[0]
    inverse = 1.0 / density
    vel = [cons[1] * inverse, cons[2] * inverse, cons[3] * inverse]
    kinetic = cons[1] * vel[0] + cons[2] * vel[1] + cons[3] * vel[2]
    pressure = (gamma_ratio - 1.0) * (cons[4] - 0.5 * kinetic)
    return [density, vel[0], vel[1], vel[2], pressure]


def half_minmod(lower, upper):
    both = jnp.maximum(0.0, jnp.minimum(lower, upper)) + jnp.minimum(
        0.0, jnp.maximum(lower, upper)
    )
    return 0.5 * both


def half_slopes(before, here, after):
    return [half_minmod(h - b, a - h) for b, h, a in zip(before, here, after)]


def plus(a, b):
    return [x + y for x, y in zip(a, b)]


def minus(a, b):
    return [x - y for x, y in zip(a, b)]


def side_terms(prim, normal):
    density, vel, pressure = prim[0], prim[1:4], prim[4]
    along = vel[normal]
    mom = [density * v for v in vel]
    kinetic = mom[0] * vel[0] + mom[1] * vel[1] + mom[2] * vel[2]
    energy = pressure * (1.0 / (gamma_ratio - 1.0)) + 0.5 * kinetic
    flux = [m * along for m in mom]
    flux[normal] = flux[normal] + pressure
    scaled = gamma_ratio * pressure
    speed = jnp.abs(along) + scaled * lax.rsqrt(scaled * density)
    return [density] + mom + [energy], [mom[normal]] + flux + [(energy + pressure) * along], speed


def twice_flux(left, right, normal):
    left_cons, left_flux, left_speed = side_terms(left, normal)
    right_cons, right_flux, right_speed = side_terms(right, normal)
    speed = jnp.maximum(left_speed, right_speed)
    return [
        (fl + fr) - speed * (ur - ul)
        for fl, fr, ul, ur in zip(left_flux, right_flux, left_cons, right_cons)
    ]


def lane_of():
    return lax.broadcasted_iota(jnp.int32, (SUB, LANES), 1)


def sub_of():
    return lax.broadcasted_iota(jnp.int32, (SUB, LANES), 0)


def lane_roll(value, amount):
    amount = amount % LANES
    return value if amount == 0 else pltpu.roll(value, amount, 1)


class Shape:
    def __init__(self, rows, edge):
        self.rows, self.edge = rows, edge
        self.halves = rows // edge
        self.width = 2 * edge
        self.fit = LANES // self.width
        self.slabs = rows // SUB
        self.pad = 2 * self.halves

    def at(self, f, row):
        start = (f * self.rows + row) * SUB
        return pl.ds(start if isinstance(start, int) else pl.multiple_of(start, SUB), SUB)

    def across(self, f, slab, sub):
        return pl.ds((f * self.rows + slab * SUB) * SUB + sub, SUB, stride=SUB)

    def grid(self):
        return jax.ShapeDtypeStruct((NF * self.rows * SUB, LANES), f32)

    def faces(self):
        x = jax.ShapeDtypeStruct((2, NF, self.pad, SUB, LANES), f32)
        y = jax.ShapeDtypeStruct((NF, self.edge // self.fit, SUB, LANES), f32)
        z = jax.ShapeDtypeStruct((NF, self.rows, LANES), f32)
        return [x, y, y, z, z]


def in_turn(count, *phases):
    for step in range(count + len(phases) - 1):
        for late, phase in enumerate(phases):
            if 0 <= step - late < count:
                phase(step - late)


def odd_y():
    return lax.rem(lax.axis_index("gy"), 2) == 1


def send_slab(shape, prim, y_one, y_two, z_lo, z_hi, slab):
    lane = lane_of()
    halves = shape.halves
    odd = odd_y()
    for f in FIELDS:
        lo = hi = None
        for k in range(shape.fit):
            row = slab * SUB + k * halves
            below = lane_roll(prim[shape.at(f, row), :], shape.width * k)
            above = lane_roll(prim[shape.at(f, row + halves - 1), :], shape.width * (k + 1))
            if lo is None:
                lo, hi = below, above
            else:
                mine = lane >= shape.width * k
                lo = jnp.where(mine, below, lo)
                hi = jnp.where(mine, above, hi)
        y_one[f, slab] = jnp.where(odd, hi, lo)
        y_two[f, slab] = jnp.where(odd, lo, hi)
        to = pl.ds(slab * SUB, SUB) if isinstance(slab, int) else pl.ds(
            pl.multiple_of(slab * SUB, SUB), SUB
        )
        z_lo[f, to, :] = prim[shape.across(f, slab, 0), :]
        z_hi[f, to, :] = prim[shape.across(f, slab, SUB - 1), :]


def send_x(shape, prim, faces, low=True, high=True):
    for f in FIELDS:
        for i in range(shape.pad):
            if high:
                faces[0, f, i] = prim[shape.at(f, shape.rows - shape.pad + i), :]
            if low:
                faces[1, f, i] = prim[shape.at(f, i), :]


def assemble_kernel(tags, state, *refs, held, slabs, slots, moves, occ, shape, first):
    given = len(held)
    arrived = group_levels(refs[:given], held)
    outs = refs[given + (0 if first else 7) :]
    field, prim, y_one, y_two, z_lo, z_hi, x_faces = outs[:7]
    blocks = outs[-1]
    units = NF * shape.slabs
    for b in range(occ):
        tag = tags[2 * moves + b]
        for unit in range(slabs[0] * NF, slabs[1] * NF):
            at = (b * units + unit) * SUB
            blocks[at : at + SUB, :] = pick(tag, unit, state, arrived, slots, shape.rows, moves)
    for slab in range(*slabs):
        for i in range(SUB):
            row = slab * SUB + i
            cons = [
                blocks[pl.ds((slab * NF + f) * SUB + i, occ, stride=units * SUB), :] for f in FIELDS
            ]
            for f, (c, w) in enumerate(zip(cons, primitives(cons))):
                field[shape.at(f, row), :] = c
                prim[shape.at(f, row), :] = w
        send_slab(shape, prim, y_one, y_two, z_lo, z_hi, slab)
    if first:
        canvas = outs[7]

        def clear(i, carry):
            for c in range(canvas.shape[0]):
                canvas[c, pl.ds(pl.multiple_of(i * SUB, SUB), SUB), :] = jnp.zeros((SUB, LANES), f32)
            return carry

        lax.fori_loop(0, canvas.shape[1] // SUB, clear, 0)
    send_x(shape, prim, x_faces, low=first, high=not first)


def sweep_z_kernel(prim, z_lo, z_hi, z_prev, z_next, total, flux_z, right_z, left, right, flux, *, shape):
    edge, rows = shape.edge, shape.rows

    def ghost(a):
        at = pl.ds(a * SUB, SUB)
        low = [z_lo[f, at, :] for f in FIELDS]
        high = [z_hi[f, at, :] for f in FIELDS]
        prev = [z_prev[f, at, :] for f in FIELDS]
        after = [z_next[f, at, :] for f in FIELDS]
        below = [lane_roll(v, -(edge - 1)) for v in prev]
        before = [lane_roll(v, -(edge - 2)) for v in prev]
        second = [lane_roll(v, -1) for v in low]
        lefts = plus(below, half_slopes(before, below, low))
        rights = minus(low, half_slopes(below, low, second))
        fluxes = twice_flux(lefts, rights, 2)
        last = [lane_roll(v, -(edge - 1)) for v in high]
        beyond = [lane_roll(v, -1) for v in after]
        over = minus(after, half_slopes(last, after, beyond))
        for f in FIELDS:
            flux_z[f, at, :] = lane_roll(fluxes[f], edge - 1)
            right_z[f, at, :] = over[f]

    lane = lane_of()
    z_of = lax.rem(lane, edge)
    sub = sub_of()
    first_z, last_z = z_of == 0, z_of == edge - 1
    first_sub, last_sub = sub == 0, sub == SUB - 1
    higher = lane - z_of + lax.rem(z_of + 1, edge)
    lower = lane - z_of + lax.rem(z_of + edge - 1, edge)

    def insert(ref, f, row):
        return jnp.broadcast_to(ref[f, pl.ds(row, 1), :], (SUB, LANES))

    def up(value, f, row, ghosts):
        across = jnp.where(last_sub, insert(ghosts, f, row), pltpu.roll(value, SUB - 1, 0))
        return jnp.take_along_axis(jnp.where(first_z, across, value), higher, axis=1)

    def down(value, f, row, ghosts):
        across = jnp.where(first_sub, insert(ghosts, f, row), pltpu.roll(value, 1, 0))
        return jnp.take_along_axis(jnp.where(last_z, across, value), lower, axis=1)

    def slopes(slab):
        ghost(slab)
        for row in range(slab * SUB, (slab + 1) * SUB):
            for f in FIELDS:
                at = shape.at(f, row)
                mine = prim[at, :]
                shift = half_minmod(mine - down(mine, f, row, z_prev), up(mine, f, row, z_next) - mine)
                left[at, :] = mine + shift
                right[at, :] = mine - shift

    def fluxes(slab):
        for row in range(slab * SUB, (slab + 1) * SUB):
            lefts = [left[shape.at(f, row), :] for f in FIELDS]
            rights = [up(right[shape.at(f, row), :], f, row, right_z) for f in FIELDS]
            for f, value in enumerate(twice_flux(lefts, rights, 2)):
                flux[shape.at(f, row), :] = value

    def differences(slab):
        for row in range(slab * SUB, (slab + 1) * SUB):
            for f in FIELDS:
                at = shape.at(f, row)
                mine = flux[at, :]
                total[at, :] = mine - down(mine, f, row, flux_z)

    in_turn(shape.slabs, slopes, fluxes, differences)


def sweep_x_kernel(prim, x_faces, sofar, total, *, shape):
    halves, edge = shape.halves, shape.edge

    def cells(x, h):
        if x < 0:
            return [x_faces[0, f, (x + 2) * halves + h] for f in FIELDS]
        if x >= edge:
            return [x_faces[1, f, (x - edge) * halves + h] for f in FIELDS]
        return [prim[shape.at(f, x * halves + h), :] for f in FIELDS]

    for h in range(halves):
        left = below = None
        ahead = [cells(x, h) for x in (-2, -1, 0)]
        for x in range(-1, edge + 1):
            shift = half_slopes(*ahead)
            if left is not None:
                flux = twice_flux(left, minus(ahead[1], shift), 0)
                if below is not None:
                    for f in FIELDS:
                        at = shape.at(f, (x - 1) * halves + h)
                        total[at, :] = sofar[at, :] + (flux[f] - below[f])
                below = flux
            left = plus(ahead[1], shift)
            if x < edge:
                ahead = ahead[1:] + [cells(x + 2, h)]


def sweep_y(prim, y_one, y_two, got_one, got_two, sofar, ghost_prim, ghost_flux, left, right, flux, turned,
            shape, finish, after_slab):
    edge, halves, fit, width = shape.edge, shape.halves, shape.fit, shape.width
    lane = lane_of()
    upper = lax.rem(lane, width) >= edge
    odd = odd_y()

    def prepare(q):
        low = [jnp.where(odd, y_two[f, q], y_one[f, q]) for f in FIELDS]
        high = [jnp.where(odd, y_one[f, q], y_two[f, q]) for f in FIELDS]
        below = [jnp.where(odd, got_two[f, q], got_one[f, q]) for f in FIELDS]
        after = [jnp.where(odd, got_one[f, q], got_two[f, q]) for f in FIELDS]
        before = [lane_roll(v, edge) for v in below]
        first = [lane_roll(v, edge) for v in low]
        lefts = plus(below, half_slopes(before, below, first))
        rights = minus(first, half_slopes(below, first, low))
        fluxes = twice_flux(lefts, rights, 1)
        last = [lane_roll(v, -edge) for v in high]
        beyond = [lane_roll(v, -edge) for v in after]
        over = minus(after, half_slopes(last, after, beyond))
        for f in FIELDS:
            ghost_prim[f, q] = jnp.where(upper, below[f], after[f])
            ghost_flux[f, q] = jnp.where(upper, fluxes[f], over[f])

    top_lanes = lane >= LANES - edge
    low_lanes = lane < edge

    def up(values, insert):
        rolled = [lane_roll(v, -edge) for v in values]
        follow = rolled[1:] + [insert]
        return [jnp.where(top_lanes, n, r) for r, n in zip(rolled, follow)]

    def down(values, insert):
        rolled = [lane_roll(v, edge) for v in values]
        lead = [insert] + rolled[:-1]
        return [jnp.where(low_lanes, n, r) for r, n in zip(rolled, lead)]

    def each(q):
        for k in range(fit):
            yield -(width * k + edge), (q * fit + k) * halves

    def slopes(q):
        prepare(q)
        for turn, base in each(q):
            for f in FIELDS:
                mine = [prim[shape.at(f, base + h), :] for h in range(halves)]
                ghost = lane_roll(ghost_prim[f, q], turn)
                over, under = up(mine, ghost), down(mine, ghost)
                for h in range(halves):
                    shift = half_minmod(mine[h] - under[h], over[h] - mine[h])
                    left[shape.at(f, base + h), :] = mine[h] + shift
                    right[shape.at(f, base + h), :] = mine[h] - shift

    def fluxes(q):
        for turn, base in each(q):
            rights = []
            for f in FIELDS:
                mine = [right[shape.at(f, base + h), :] for h in range(halves)]
                ghost = lane_roll(ghost_flux[f, q], turn)
                turned[shape.at(f, base), :] = ghost
                rights.append(up(mine, ghost))
            for h in range(halves):
                lefts = [left[shape.at(f, base + h), :] for f in FIELDS]
                result = twice_flux(lefts, [rights[f][h] for f in FIELDS], 1)
                for f in FIELDS:
                    flux[shape.at(f, base + h), :] = result[f]

    def differences(q):
        for turn, base in each(q):
            total = [[None] * NF for _ in range(halves)]
            for f in FIELDS:
                mine = [flux[shape.at(f, base + h), :] for h in range(halves)]
                under = down(mine, turned[shape.at(f, base), :])
                for h in range(halves):
                    total[h][f] = sofar[shape.at(f, base + h), :] + (mine[h] - under[h])
            for h in range(halves):
                finish(base + h, total[h])

    in_turn(edge // fit, slopes, fluxes, differences, after_slab)


def sweep_y_one_kernel(field, prim, y_one, y_two, got_one, got_two, sofar, *refs, shape):
    one, one_prim, x_faces, out_y_one, out_y_two, z_lo, z_hi = refs[:7]

    def finish(row, total):
        cons = [field[shape.at(f, row), :] - (0.5 * time_step) * total[f] for f in FIELDS]
        for f, (c, w) in enumerate(zip(cons, primitives(cons))):
            one[shape.at(f, row), :] = c
            one_prim[shape.at(f, row), :] = w

    def after_slab(q):
        send_slab(shape, one_prim, out_y_one, out_y_two, z_lo, z_hi, q)

    sweep_y(prim, y_one, y_two, got_one, got_two, sofar, *refs[7:], shape, finish, after_slab)
    send_x(shape, one_prim, x_faces)


def sweep_y_two_kernel(own_there, field, one, prim, y_one, y_two, got_one, got_two, sofar, zeros, out,
                       canvas, *refs, shape, occ, groups):
    scratch, (result, sems, own, own_sem) = refs[:6], refs[6:]
    slots = pltpu.make_async_copy(own_there, own, own_sem)
    slots.start()
    rows = shape.rows
    span = SUB * SUB

    def finish(row, total):
        for f in FIELDS:
            at = shape.at(f, row)
            advanced = one[at, :] - (0.5 * time_step) * total[f]
            result[at, :] = 0.5 * field[at, :] + 0.5 * advanced

    def copy(part):
        begin = part * span if isinstance(part, int) else pl.multiple_of(part * span, span)
        at = pl.ds(begin, span)
        return pltpu.make_async_copy(canvas.at[:, at, :], out.at[:, at, :], sems.at[part])

    def after_slab(q):
        if q == 0:
            slots.wait()
        for b in range(occ):
            slot = own[b]
            to = pl.ds(q * span + lax.rem(slot, SUB), SUB, stride=SUB)
            for f in FIELDS:
                canvas[f * groups + slot // SUB, to, :] = result[shape.across(f, q, b), :]
        copy(q).start()

    sweep_y(prim, y_one, y_two, got_one, got_two, sofar, *scratch, shape, finish, after_slab)
    for part in range(shape.slabs):
        copy(part).wait()


def shards(state, send_slots, recv_slots, owner_slot):
    slots, _, cells = state.shape
    moves = send_slots.shape[2]
    size_x, size_y, size_z = (lax.axis_size(axis) for axis in AXES)
    occ = owner_slot.shape[0] // (size_x * size_y * size_z)
    edge = round(cells ** (1 / 3))
    rows = cells // LANES
    groups = slots // SUB
    shape = Shape(rows, edge)
    units = NF * shape.slabs
    cuts = [split_units(units, shares) for shares in ((3, 5, 7, 5), (3, 5, 5, 4, 3), (8, 5, 4, 3))]
    firsts, final = cuts[0], cuts[2]

    bit_z = size_z.bit_length() - 2
    bit_y = bit_z + size_y.bit_length() - 1
    bit_x = bit_y + size_x.bit_length() - 1
    pair_bits = (bit_x, bit_y, bit_z)

    def swapped(value, level):
        mask = 2 ** pair_bits[level]
        pairs = [(source, source ^ mask) for source in range(lax.axis_size(AXES))]
        return lax.ppermute(value, AXES, pairs)

    rows_of_state = (
        state.reshape(groups, SUB, NF, rows, LANES)
        .transpose(2, 0, 3, 1, 4)
        .reshape(NF * groups * rows * SUB, LANES)
    )
    state_there = pltpu.with_memory_space_constraint(rows_of_state, HBM)
    send_there = pltpu.with_memory_space_constraint(send_slots, HBM)
    device = lax.axis_index(AXES)
    own = lax.dynamic_slice(owner_slot, (device * occ,), (occ,))
    sizes = dict(slots=slots, moves=moves)

    def message(piece):
        begin, end = piece
        return jax.ShapeDtypeStruct((moves, (end - begin) * SUB, LANES), f32)

    head = firsts[0]
    sent = [None] * len(firsts)
    sent[0] = pl.pallas_call(
        functools.partial(first_kernel, piece=head, rows=rows, **sizes),
        out_shape=message(head),
        in_specs=[whole(HBM)] * 2,
        out_specs=whole(VMEM),
        scratch_shapes=[
            SMEM(send_slots.shape, jnp.int32),
            VMEM(((head[1] - head[0]) * groups * SUB * SUB, LANES), f32),
            pltpu.SemaphoreType.DMA((1 + (head[1] - head[0]) * groups,)),
        ],
        compiler_params=params(),
        name="pack_first",
    )(send_there, state_there)
    tags, token, *sent[1:] = pl.pallas_call(
        functools.partial(rest_kernel, pieces=firsts[1:], rows=rows, occ=occ, **sizes),
        out_shape=[
            jax.ShapeDtypeStruct((2 * moves + occ,), jnp.int32),
            jax.ShapeDtypeStruct((SUB, LANES), f32),
        ]
        + [message(piece) for piece in firsts[1:]],
        in_specs=[whole(SMEM)] * 3 + [whole(VMEM)],
        out_specs=[whole(SMEM)] + [whole(VMEM)] * len(firsts),
        scratch_shapes=[SMEM((slots + SUB,), jnp.int32)],
        compiler_params=params(),
        name="pack_rest",
    )(send_slots, recv_slots, own, rows_of_state)

    got = [[None] * len(cut) for cut in cuts]

    def holding(levels, begin, end):
        found = [
            ((level, piece), got[level][p])
            for level in levels
            for p, piece in enumerate(cuts[level])
            if piece[0] < end and piece[1] > begin
        ]
        return found

    def make(wanted, through):
        found = {}
        for level, p in wanted:
            for key, value in holding(range(level), *cuts[level][p]):
                found[key] = value
        plan = tuple((level, cuts[level][p]) for level, p in wanted)
        given, passed, made = len(found), len(through), len(wanted)
        outs = pl.pallas_call(
            functools.partial(
                pick_kernel, plan=plan, held=tuple(found), passed=passed, rows=rows, **sizes
            ),
            out_shape=[message(piece) for _, piece in plan]
            + [jax.ShapeDtypeStruct(t.shape, f32) for t in through],
            in_specs=[whole(SMEM)] + [whole(VMEM)] * (1 + given) + [whole(pl.ANY)] * passed,
            out_specs=[whole(VMEM)] * made + [whole(pl.ANY)] * passed,
            input_output_aliases={2 + given + i: made + i for i in range(passed)},
            compiler_params=params(),
            cost_estimate=cost(10**9, 10**9),
            name="pick_" + "_".join("%d%d" % w for w in wanted),
        )(tags, rows_of_state, *found.values(), *through)
        return outs[:made], outs[made:]

    steps = [
        ([(1, 0)], [2], []),
        ([(1, 1)], [3], []),
        ([(1, 2)], [], [(1, 0)]),
        ([(1, 3), (2, 0)], [], []),
        ([(1, 4), (2, 1)], [], []),
        ([(2, 2)], [], [(2, 0)]),
        ([(2, 3)], [], [(2, 1)]),
    ]
    got[0][0] = swapped(sent[0], 0)
    got[0][1] = swapped(sent[1], 0)
    for wanted, leaving, awaited in steps:
        through = [token] + [sent[p] for p in leaving] + [got[level][p] for level, p in awaited]
        made, (token, *passed) = make(wanted, through)
        for p, value in zip(leaving, passed):
            got[0][p] = swapped(value, 0)
        for (level, p), value in reversed(list(zip(wanted, made))):
            got[level][p] = swapped(value, level)
        for (level, p), value in zip(awaited, passed[len(leaving) :]):
            got[level][p] = value

    grid = shape.grid()
    face_x, face_y, _, face_z, _ = shape.faces()
    part = [grid, grid, face_y, face_y, face_z, face_z, face_x]
    canvas = jax.ShapeDtypeStruct((NF * groups, rows * SUB, LANES), f32)
    full = final[-1][0] // NF

    def assemble(slabs, before):
        first = not before
        found = dict(holding(range(3), slabs[0] * NF, slabs[1] * NF))
        shapes = part + [canvas] * first
        fixed = 2 + len(found)
        return pl.pallas_call(
            functools.partial(
                assemble_kernel, held=tuple(found), slabs=slabs, occ=occ, shape=shape,
                first=first, **sizes,
            ),
            out_shape=shapes,
            in_specs=[whole(SMEM)] + [whole(VMEM)] * (1 + len(found) + len(before)),
            out_specs=[whole(VMEM)] * len(shapes),
            scratch_shapes=[VMEM((occ * NF * rows, LANES), f32)],
            input_output_aliases={fixed + i: i for i in range(len(before))},
            compiler_params=params(),
            name="assemble_%d" % slabs[0],
        )(tags, rows_of_state, *found.values(), *before)

    *made, blank = assemble((0, full), [])
    *made, x_faces = assemble((full, shape.slabs), made)
    made = made[:2] + [x_faces] + made[2:]

    def ring(value, axis, step):
        size = lax.axis_size(axis)
        return lax.ppermute(value, axis, [(i, (i + step) % size) for i in range(size)])

    def beside(value, axis, shift):
        size = lax.axis_size(axis)
        pairs = [(i, ((i + shift) ^ 1) - shift) for i in range(size)]
        return lax.ppermute(value, axis, [(i, j % size) for i, j in pairs])

    def flux_sums(prim, x_faces, y_one, y_two, z_lo, z_hi):
        if size_x == 2:
            x_faces = ring(x_faces, "gx", 1)
        else:
            x_faces = jnp.stack([ring(x_faces[0], "gx", 1), ring(x_faces[1], "gx", -1)])
        got_one, got_two = beside(y_one, "gy", 1), beside(y_two, "gy", 0)
        z_prev, z_next = ring(z_hi, "gz", 1), ring(z_lo, "gz", -1)
        ghost = VMEM((NF, rows, LANES), f32)
        work = [VMEM(grid.shape, f32)] * 3
        total = pl.pallas_call(
            functools.partial(sweep_z_kernel, shape=shape),
            out_shape=grid,
            in_specs=[whole(VMEM)] * 5,
            out_specs=whole(VMEM),
            scratch_shapes=[ghost] * 2 + work,
            compiler_params=params(),
            name="sweep_z",
        )(prim, z_lo, z_hi, z_prev, z_next)
        total = pl.pallas_call(
            functools.partial(sweep_x_kernel, shape=shape),
            out_shape=grid,
            in_specs=[whole(VMEM)] * 3,
            out_specs=whole(VMEM),
            input_output_aliases={2: 0},
            compiler_params=params(),
            name="sweep_x",
        )(prim, x_faces, total)
        return y_one, y_two, got_one, got_two, total

    produced = [grid, grid] + shape.faces()
    scratch = [VMEM(face_y.shape, f32)] * 2 + [VMEM(grid.shape, f32)] * 4
    field, prim = made[0], made[1]
    sums = flux_sums(prim, *made[2:])
    made = pl.pallas_call(
        functools.partial(sweep_y_one_kernel, shape=shape),
        out_shape=produced,
        in_specs=[whole(VMEM)] * 7,
        out_specs=[whole(VMEM)] * len(produced),
        scratch_shapes=scratch,
        compiler_params=params(),
        name="sweep_y_one",
    )(field, prim, *sums)
    one, one_prim = made[0], made[1]
    sums = flux_sums(one_prim, *made[2:])
    out, _ = pl.pallas_call(
        functools.partial(sweep_y_two_kernel, shape=shape, occ=occ, groups=groups),
        out_shape=[canvas, canvas],
        in_specs=[whole(HBM)] + [whole(VMEM)] * 9,
        out_specs=[whole(HBM), whole(VMEM)],
        scratch_shapes=scratch
        + [
            VMEM(grid.shape, f32),
            pltpu.SemaphoreType.DMA((shape.slabs,)),
            SMEM((occ,), jnp.int32),
            pltpu.SemaphoreType.DMA,
        ],
        input_output_aliases={9: 1},
        compiler_params=params(),
        name="sweep_y_two",
    )(pltpu.with_memory_space_constraint(own, HBM), field, one, one_prim, *sums, blank)
    return (
        out.reshape(NF, groups, rows, SUB, LANES)
        .transpose(1, 3, 0, 2, 4)
        .reshape(slots, NF, cells)
    )


def solution(mesh):
    placed = (
        P(AXES, None, None),
        P(None, AXES, None),
        P(None, AXES, None),
        P(),
    )
    return jax.shard_map(
        shards,
        mesh=mesh,
        in_specs=placed,
        out_specs=P(AXES, None, None),
        check_vma=False,
    )
```

```python
import functools

import jax
import jax.numpy as jnp
from jax import lax
from jax.experimental import pallas as pl
from jax.experimental.pallas import tpu as pltpu
from jax.sharding import PartitionSpec as P

gamma_ratio = 1.4
time_step = 0.05
LANES = 128
SUB = 8
NF = 5
FIELDS = range(NF)
AXES = ("gx", "gy", "gz")

VMEM = pltpu.VMEM
SMEM = pltpu.SMEM
HBM = pltpu.HBM
f32 = jnp.float32


def whole(space):
    return pl.BlockSpec(memory_space=space)


def params():
    return pltpu.CompilerParams(vmem_limit_bytes=16 * 1024 * 1024)


def cost(flops, moved):
    return pl.CostEstimate(flops=flops, bytes_accessed=moved, transcendentals=0)


def split_units(units, shares):
    ends = [units * sum(shares[: i + 1]) // sum(shares) for i in range(len(shares))]
    return list(zip([0] + ends[:-1], ends))


def from_state(state, tag, unit, slots, rows):
    slab, field = unit // NF, unit % NF
    groups = slots // SUB
    base = (tag // SUB) * (rows * SUB) + lax.rem(tag, SUB)
    start = base + (field * groups * rows + slab * SUB) * SUB
    return state[pl.ds(start, SUB, stride=SUB), :]


def pick(tag, unit, state, arrived, slots, rows, moves):
    value = from_state(state, jnp.minimum(tag, slots - 1), unit, slots, rows)
    for level, held in enumerate(arrived):
        base = slots + level * moves
        index = jnp.clip(tag - base, 0, moves - 1)
        for (begin, end), ref in held:
            if begin <= unit < end:
                at = (unit - begin) * SUB
                value = jnp.where(tag >= base, ref[index, at : at + SUB, :], value)
    return value


def first_kernel(send_hbm, state_hbm, out, send, held, sems, *, piece, slots, rows, moves):
    span = SUB * SUB
    groups = slots // SUB
    copies = [pltpu.make_async_copy(send_hbm, send, sems.at[0])]
    for unit in range(*piece):
        slab, field = unit // NF, unit % NF
        for g in range(groups):
            at = ((field * groups + g) * rows + slab * SUB) * SUB
            to = ((unit - piece[0]) * groups + g) * span
            copies.append(
                pltpu.make_async_copy(
                    state_hbm.at[pl.ds(at, span), :],
                    held.at[pl.ds(to, span), :],
                    sems.at[len(copies)],
                )
            )
    for c in copies:
        c.start()
    for c in copies:
        c.wait()
    for k in range(moves):
        slot = jnp.minimum(send[0, 0, k], slots - 1)
        base = (slot // SUB) * span + lax.rem(slot, SUB)
        for i in range(piece[1] - piece[0]):
            out[k, i * SUB : (i + 1) * SUB, :] = held[
                pl.ds(base + i * groups * span, SUB, stride=SUB), :
            ]


def rest_kernel(send, recv, own, state, tags, token, *refs, pieces, slots, rows, moves, occ):
    outs, where = refs[:-1], refs[-1]
    token[...] = jnp.zeros_like(token)
    for slot in range(slots):
        where[slot] = slot
    for level in range(3):
        if level:
            for k in range(moves):
                slot = jnp.minimum(send[level, 0, k], slots - 1)
                tags[(level - 1) * moves + k] = where[slot]
        for k in range(moves):
            where[recv[level, 0, k]] = slots + level * moves + k
    for b in range(occ):
        tags[2 * moves + b] = where[own[b]]
    for k in range(moves):
        slot = jnp.minimum(send[0, 0, k], slots - 1)
        for (begin, end), out in zip(pieces, outs):
            for unit in range(begin, end):
                at = (unit - begin) * SUB
                out[k, at : at + SUB, :] = from_state(state, slot, unit, slots, rows)


def group_levels(refs, held):
    levels = [[], [], []]
    for ref, (level, piece) in zip(refs, held):
        levels[level].append((piece, ref))
    return levels


def pick_kernel(tags, state, *refs, plan, held, passed, slots, rows, moves):
    given = len(held)
    arrived = group_levels(refs[:given], held)
    outs = refs[given + passed :]
    for (level, (begin, end)), out in zip(plan, outs):
        for k in range(moves):
            tag = tags[(level - 1) * moves + k]
            for unit in range(begin, end):
                at = (unit - begin) * SUB
                out[k, at : at + SUB, :] = pick(
                    tag, unit, state, arrived[:level], slots, rows, moves
                )


def primitives(cons):
    density = cons[0]
    inverse = 1.0 / density
    vel = [cons[1] * inverse, cons[2] * inverse, cons[3] * inverse]
    kinetic = cons[1] * vel[0] + cons[2] * vel[1] + cons[3] * vel[2]
    pressure = (gamma_ratio - 1.0) * (cons[4] - 0.5 * kinetic)
    return [density, vel[0], vel[1], vel[2], pressure]


def half_minmod(lower, upper):
    both = jnp.maximum(0.0, jnp.minimum(lower, upper)) + jnp.minimum(
        0.0, jnp.maximum(lower, upper)
    )
    return 0.5 * both


def half_slopes(before, here, after):
    return [half_minmod(h - b, a - h) for b, h, a in zip(before, here, after)]


def plus(a, b):
    return [x + y for x, y in zip(a, b)]


def minus(a, b):
    return [x - y for x, y in zip(a, b)]


def side_terms(prim, normal):
    density, vel, pressure = prim[0], prim[1:4], prim[4]
    along = vel[normal]
    mom = [density * v for v in vel]
    kinetic = mom[0] * vel[0] + mom[1] * vel[1] + mom[2] * vel[2]
    energy = pressure * (1.0 / (gamma_ratio - 1.0)) + 0.5 * kinetic
    flux = [m * along for m in mom]
    flux[normal] = flux[normal] + pressure
    scaled = gamma_ratio * pressure
    speed = jnp.abs(along) + scaled * lax.rsqrt(scaled * density)
    return [density] + mom + [energy], [mom[normal]] + flux + [(energy + pressure) * along], speed


def twice_flux(left, right, normal):
    left_cons, left_flux, left_speed = side_terms(left, normal)
    right_cons, right_flux, right_speed = side_terms(right, normal)
    speed = jnp.maximum(left_speed, right_speed)
    return [
        (fl + fr) - speed * (ur - ul)
        for fl, fr, ul, ur in zip(left_flux, right_flux, left_cons, right_cons)
    ]


def lane_of():
    return lax.broadcasted_iota(jnp.int32, (SUB, LANES), 1)


def sub_of():
    return lax.broadcasted_iota(jnp.int32, (SUB, LANES), 0)


def lane_roll(value, amount):
    amount = amount % LANES
    return value if amount == 0 else pltpu.roll(value, amount, 1)


class Shape:
    def __init__(self, rows, edge):
        self.rows, self.edge = rows, edge
        self.halves = rows // edge
        self.width = 2 * edge
        self.fit = LANES // self.width
        self.slabs = rows // SUB
        self.pad = 2 * self.halves

    def at(self, f, row):
        start = (f * self.rows + row) * SUB
        return pl.ds(start if isinstance(start, int) else pl.multiple_of(start, SUB), SUB)

    def across(self, f, slab, sub):
        return pl.ds((f * self.rows + slab * SUB) * SUB + sub, SUB, stride=SUB)

    def grid(self):
        return jax.ShapeDtypeStruct((NF * self.rows * SUB, LANES), f32)

    def faces(self):
        x = jax.ShapeDtypeStruct((2, NF, self.pad, SUB, LANES), f32)
        y = jax.ShapeDtypeStruct((NF, self.edge // self.fit, SUB, LANES), f32)
        z = jax.ShapeDtypeStruct((NF, self.rows, LANES), f32)
        return [x, y, y, z, z]


def in_turn(count, *phases):
    for step in range(count + len(phases) - 1):
        for late, phase in enumerate(phases):
            if 0 <= step - late < count:
                phase(step - late)


def odd_y():
    return lax.rem(lax.axis_index("gy"), 2) == 1


def send_slab(shape, prim, y_one, y_two, z_lo, z_hi, slab):
    lane = lane_of()
    halves = shape.halves
    odd = odd_y()
    for f in FIELDS:
        lo = hi = None
        for k in range(shape.fit):
            row = slab * SUB + k * halves
            below = lane_roll(prim[shape.at(f, row), :], shape.width * k)
            above = lane_roll(prim[shape.at(f, row + halves - 1), :], shape.width * (k + 1))
            if lo is None:
                lo, hi = below, above
            else:
                mine = lane >= shape.width * k
                lo = jnp.where(mine, below, lo)
                hi = jnp.where(mine, above, hi)
        y_one[f, slab] = jnp.where(odd, hi, lo)
        y_two[f, slab] = jnp.where(odd, lo, hi)
        to = pl.ds(slab * SUB, SUB) if isinstance(slab, int) else pl.ds(
            pl.multiple_of(slab * SUB, SUB), SUB
        )
        z_lo[f, to, :] = prim[shape.across(f, slab, 0), :]
        z_hi[f, to, :] = prim[shape.across(f, slab, SUB - 1), :]


def send_x(shape, prim, faces, low=True, high=True):
    for f in FIELDS:
        for i in range(shape.pad):
            if high:
                faces[0, f, i] = prim[shape.at(f, shape.rows - shape.pad + i), :]
            if low:
                faces[1, f, i] = prim[shape.at(f, i), :]


def assemble_kernel(tags, state, *refs, held, slabs, slots, moves, occ, shape, first):
    given = len(held)
    arrived = group_levels(refs[:given], held)
    outs = refs[given + (0 if first else 7) :]
    field, prim, y_one, y_two, z_lo, z_hi, x_faces = outs[:7]
    blocks = outs[-1]
    units = NF * shape.slabs
    for b in range(occ):
        tag = tags[2 * moves + b]
        for unit in range(slabs[0] * NF, slabs[1] * NF):
            at = (b * units + unit) * SUB
            blocks[at : at + SUB, :] = pick(tag, unit, state, arrived, slots, shape.rows, moves)
    for slab in range(*slabs):
        for i in range(SUB):
            row = slab * SUB + i
            cons = [
                blocks[pl.ds((slab * NF + f) * SUB + i, occ, stride=units * SUB), :] for f in FIELDS
            ]
            for f, (c, w) in enumerate(zip(cons, primitives(cons))):
                field[shape.at(f, row), :] = c
                prim[shape.at(f, row), :] = w
        send_slab(shape, prim, y_one, y_two, z_lo, z_hi, slab)
    if first:
        canvas = outs[7]

        def clear(i, carry):
            for c in range(canvas.shape[0]):
                canvas[c, pl.ds(pl.multiple_of(i * SUB, SUB), SUB), :] = jnp.zeros((SUB, LANES), f32)
            return carry

        lax.fori_loop(0, canvas.shape[1] // SUB, clear, 0)
    send_x(shape, prim, x_faces, low=first, high=not first)


def sweep_z_kernel(prim, z_lo, z_hi, z_prev, z_next, total, flux_z, right_z, left, right, flux, *, shape):
    edge, rows = shape.edge, shape.rows

    def ghost(a):
        at = pl.ds(a * SUB, SUB)
        low = [z_lo[f, at, :] for f in FIELDS]
        high = [z_hi[f, at, :] for f in FIELDS]
        prev = [z_prev[f, at, :] for f in FIELDS]
        after = [z_next[f, at, :] for f in FIELDS]
        below = [lane_roll(v, -(edge - 1)) for v in prev]
        before = [lane_roll(v, -(edge - 2)) for v in prev]
        second = [lane_roll(v, -1) for v in low]
        lefts = plus(below, half_slopes(before, below, low))
        rights = minus(low, half_slopes(below, low, second))
        fluxes = twice_flux(lefts, rights, 2)
        last = [lane_roll(v, -(edge - 1)) for v in high]
        beyond = [lane_roll(v, -1) for v in after]
        over = minus(after, half_slopes(last, after, beyond))
        for f in FIELDS:
            flux_z[f, at, :] = lane_roll(fluxes[f], edge - 1)
            right_z[f, at, :] = over[f]

    lane = lane_of()
    z_of = lax.rem(lane, edge)
    sub = sub_of()
    first_z, last_z = z_of == 0, z_of == edge - 1
    first_sub, last_sub = sub == 0, sub == SUB - 1
    higher = lane - z_of + lax.rem(z_of + 1, edge)
    lower = lane - z_of + lax.rem(z_of + edge - 1, edge)

    def insert(ref, f, row):
        return jnp.broadcast_to(ref[f, pl.ds(row, 1), :], (SUB, LANES))

    def up(value, f, row, ghosts):
        across = jnp.where(last_sub, insert(ghosts, f, row), pltpu.roll(value, SUB - 1, 0))
        return jnp.take_along_axis(jnp.where(first_z, across, value), higher, axis=1)

    def down(value, f, row, ghosts):
        across = jnp.where(first_sub, insert(ghosts, f, row), pltpu.roll(value, 1, 0))
        return jnp.take_along_axis(jnp.where(last_z, across, value), lower, axis=1)

    def slopes(slab):
        ghost(slab)
        for row in range(slab * SUB, (slab + 1) * SUB):
            for f in FIELDS:
                at = shape.at(f, row)
                mine = prim[at, :]
                shift = half_minmod(mine - down(mine, f, row, z_prev), up(mine, f, row, z_next) - mine)
                left[at, :] = mine + shift
                right[at, :] = mine - shift

    def fluxes(slab):
        for row in range(slab * SUB, (slab + 1) * SUB):
            lefts = [left[shape.at(f, row), :] for f in FIELDS]
            rights = [up(right[shape.at(f, row), :], f, row, right_z) for f in FIELDS]
            for f, value in enumerate(twice_flux(lefts, rights, 2)):
                flux[shape.at(f, row), :] = value

    def differences(slab):
        for row in range(slab * SUB, (slab + 1) * SUB):
            for f in FIELDS:
                at = shape.at(f, row)
                mine = flux[at, :]
                total[at, :] = mine - down(mine, f, row, flux_z)

    in_turn(shape.slabs, slopes, fluxes, differences)


def sweep_x_kernel(prim, x_faces, sofar, total, *, shape):
    halves, edge = shape.halves, shape.edge

    def cells(x, h):
        if x < 0:
            return [x_faces[0, f, (x + 2) * halves + h] for f in FIELDS]
        if x >= edge:
            return [x_faces[1, f, (x - edge) * halves + h] for f in FIELDS]
        return [prim[shape.at(f, x * halves + h), :] for f in FIELDS]

    for h in range(halves):
        left = below = None
        ahead = [cells(x, h) for x in (-2, -1, 0)]
        for x in range(-1, edge + 1):
            shift = half_slopes(*ahead)
            if left is not None:
                flux = twice_flux(left, minus(ahead[1], shift), 0)
                if below is not None:
                    for f in FIELDS:
                        at = shape.at(f, (x - 1) * halves + h)
                        total[at, :] = sofar[at, :] + (flux[f] - below[f])
                below = flux
            left = plus(ahead[1], shift)
            if x < edge:
                ahead = ahead[1:] + [cells(x + 2, h)]


def sweep_y(prim, y_one, y_two, got_one, got_two, sofar, ghost_prim, ghost_flux, left, right, flux, turned,
            shape, finish, after_slab):
    edge, halves, fit, width = shape.edge, shape.halves, shape.fit, shape.width
    lane = lane_of()
    upper = lax.rem(lane, width) >= edge
    odd = odd_y()

    def prepare(q):
        low = [jnp.where(odd, y_two[f, q], y_one[f, q]) for f in FIELDS]
        high = [jnp.where(odd, y_one[f, q], y_two[f, q]) for f in FIELDS]
        below = [jnp.where(odd, got_two[f, q], got_one[f, q]) for f in FIELDS]
        after = [jnp.where(odd, got_one[f, q], got_two[f, q]) for f in FIELDS]
        before = [lane_roll(v, edge) for v in below]
        first = [lane_roll(v, edge) for v in low]
        lefts = plus(below, half_slopes(before, below, first))
        rights = minus(first, half_slopes(below, first, low))
        fluxes = twice_flux(lefts, rights, 1)
        last = [lane_roll(v, -edge) for v in high]
        beyond = [lane_roll(v, -edge) for v in after]
        over = minus(after, half_slopes(last, after, beyond))
        for f in FIELDS:
            ghost_prim[f, q] = jnp.where(upper, below[f], after[f])
            ghost_flux[f, q] = jnp.where(upper, fluxes[f], over[f])

    top_lanes = lane >= LANES - edge
    low_lanes = lane < edge

    def up(values, insert):
        rolled = [lane_roll(v, -edge) for v in values]
        follow = rolled[1:] + [insert]
        return [jnp.where(top_lanes, n, r) for r, n in zip(rolled, follow)]

    def down(values, insert):
        rolled = [lane_roll(v, edge) for v in values]
        lead = [insert] + rolled[:-1]
        return [jnp.where(low_lanes, n, r) for r, n in zip(rolled, lead)]

    def each(q):
        for k in range(fit):
            yield -(width * k + edge), (q * fit + k) * halves

    def slopes(q):
        prepare(q)
        for turn, base in each(q):
            for f in FIELDS:
                mine = [prim[shape.at(f, base + h), :] for h in range(halves)]
                ghost = lane_roll(ghost_prim[f, q], turn)
                over, under = up(mine, ghost), down(mine, ghost)
                for h in range(halves):
                    shift = half_minmod(mine[h] - under[h], over[h] - mine[h])
                    left[shape.at(f, base + h), :] = mine[h] + shift
                    right[shape.at(f, base + h), :] = mine[h] - shift

    def fluxes(q):
        for turn, base in each(q):
            rights = []
            for f in FIELDS:
                mine = [right[shape.at(f, base + h), :] for h in range(halves)]
                ghost = lane_roll(ghost_flux[f, q], turn)
                turned[shape.at(f, base), :] = ghost
                rights.append(up(mine, ghost))
            for h in range(halves):
                lefts = [left[shape.at(f, base + h), :] for f in FIELDS]
                result = twice_flux(lefts, [rights[f][h] for f in FIELDS], 1)
                for f in FIELDS:
                    flux[shape.at(f, base + h), :] = result[f]

    def differences(q):
        for turn, base in each(q):
            total = [[None] * NF for _ in range(halves)]
            for f in FIELDS:
                mine = [flux[shape.at(f, base + h), :] for h in range(halves)]
                under = down(mine, turned[shape.at(f, base), :])
                for h in range(halves):
                    total[h][f] = sofar[shape.at(f, base + h), :] + (mine[h] - under[h])
            for h in range(halves):
                finish(base + h, total[h])

    in_turn(edge // fit, slopes, fluxes, differences, after_slab)


def sweep_y_one_kernel(field, prim, y_one, y_two, got_one, got_two, sofar, *refs, shape):
    one, one_prim, x_faces, out_y_one, out_y_two, z_lo, z_hi = refs[:7]

    def finish(row, total):
        cons = [field[shape.at(f, row), :] - (0.5 * time_step) * total[f] for f in FIELDS]
        for f, (c, w) in enumerate(zip(cons, primitives(cons))):
            one[shape.at(f, row), :] = c
            one_prim[shape.at(f, row), :] = w

    def after_slab(q):
        send_slab(shape, one_prim, out_y_one, out_y_two, z_lo, z_hi, q)

    sweep_y(prim, y_one, y_two, got_one, got_two, sofar, *refs[7:], shape, finish, after_slab)
    send_x(shape, one_prim, x_faces)


def sweep_y_two_kernel(own_there, field, one, prim, y_one, y_two, got_one, got_two, sofar, zeros, out,
                       canvas, *refs, shape, occ, groups):
    scratch, (result, sems, own, own_sem) = refs[:6], refs[6:]
    slots = pltpu.make_async_copy(own_there, own, own_sem)
    slots.start()
    rows = shape.rows
    span = SUB * SUB

    def finish(row, total):
        for f in FIELDS:
            at = shape.at(f, row)
            advanced = one[at, :] - (0.5 * time_step) * total[f]
            result[at, :] = 0.5 * field[at, :] + 0.5 * advanced

    def copy(part):
        begin = part * span if isinstance(part, int) else pl.multiple_of(part * span, span)
        at = pl.ds(begin, span)
        return [
            pltpu.make_async_copy(canvas.at[of, at, :], out.at[of, at, :], sems.at[part, f])
            for f, of in enumerate(pl.ds(f * groups, groups) for f in FIELDS)
        ]

    def after_slab(q):
        if q == 0:
            slots.wait()
        for b in range(occ):
            slot = own[b]
            to = pl.ds(q * span + lax.rem(slot, SUB), SUB, stride=SUB)
            for f in FIELDS:
                canvas[f * groups + slot // SUB, to, :] = result[shape.across(f, q, b), :]
        for c in copy(q):
            c.start()

    sweep_y(prim, y_one, y_two, got_one, got_two, sofar, *scratch, shape, finish, after_slab)
    for part in range(shape.slabs):
        for c in copy(part):
            c.wait()


def shards(state, send_slots, recv_slots, owner_slot):
    slots, _, cells = state.shape
    moves = send_slots.shape[2]
    size_x, size_y, size_z = (lax.axis_size(axis) for axis in AXES)
    occ = owner_slot.shape[0] // (size_x * size_y * size_z)
    edge = round(cells ** (1 / 3))
    rows = cells // LANES
    groups = slots // SUB
    shape = Shape(rows, edge)
    units = NF * shape.slabs
    cuts = [split_units(units, shares) for shares in ((3, 5, 7, 5), (3, 4, 5, 5, 3), (3, 4, 5, 5, 3))]
    firsts, final = cuts[0], cuts[2]

    bit_z = size_z.bit_length() - 2
    bit_y = bit_z + size_y.bit_length() - 1
    bit_x = bit_y + size_x.bit_length() - 1
    pair_bits = (bit_x, bit_y, bit_z)

    def swapped(value, level):
        mask = 2 ** pair_bits[level]
        pairs = [(source, source ^ mask) for source in range(lax.axis_size(AXES))]
        return lax.ppermute(value, AXES, pairs)

    rows_of_state = (
        state.reshape(groups, SUB, NF, rows, LANES)
        .transpose(2, 0, 3, 1, 4)
        .reshape(NF * groups * rows * SUB, LANES)
    )
    state_there = pltpu.with_memory_space_constraint(rows_of_state, HBM)
    send_there = pltpu.with_memory_space_constraint(send_slots, HBM)
    device = lax.axis_index(AXES)
    own = lax.dynamic_slice(owner_slot, (device * occ,), (occ,))
    sizes = dict(slots=slots, moves=moves)

    def message(piece):
        begin, end = piece
        return jax.ShapeDtypeStruct((moves, (end - begin) * SUB, LANES), f32)

    head = firsts[0]
    sent = [None] * len(firsts)
    sent[0] = pl.pallas_call(
        functools.partial(first_kernel, piece=head, rows=rows, **sizes),
        out_shape=message(head),
        in_specs=[whole(HBM)] * 2,
        out_specs=whole(VMEM),
        scratch_shapes=[
            SMEM(send_slots.shape, jnp.int32),
            VMEM(((head[1] - head[0]) * groups * SUB * SUB, LANES), f32),
            pltpu.SemaphoreType.DMA((1 + (head[1] - head[0]) * groups,)),
        ],
        compiler_params=params(),
        name="pack_first",
    )(send_there, state_there)
    tags, token, *sent[1:] = pl.pallas_call(
        functools.partial(rest_kernel, pieces=firsts[1:], rows=rows, occ=occ, **sizes),
        out_shape=[
            jax.ShapeDtypeStruct((2 * moves + occ,), jnp.int32),
            jax.ShapeDtypeStruct((SUB, LANES), f32),
        ]
        + [message(piece) for piece in firsts[1:]],
        in_specs=[whole(SMEM)] * 3 + [whole(VMEM)],
        out_specs=[whole(SMEM)] + [whole(VMEM)] * len(firsts),
        scratch_shapes=[SMEM((slots + SUB,), jnp.int32)],
        compiler_params=params(),
        name="pack_rest",
    )(send_slots, recv_slots, own, rows_of_state)

    got = [[None] * len(cut) for cut in cuts]

    def holding(levels, begin, end):
        found = [
            ((level, piece), got[level][p])
            for level in levels
            for p, piece in enumerate(cuts[level])
            if piece[0] < end and piece[1] > begin
        ]
        return found

    def make(wanted, through):
        found = {}
        for level, p in wanted:
            for key, value in holding(range(level), *cuts[level][p]):
                found[key] = value
        plan = tuple((level, cuts[level][p]) for level, p in wanted)
        given, passed, made = len(found), len(through), len(wanted)
        outs = pl.pallas_call(
            functools.partial(
                pick_kernel, plan=plan, held=tuple(found), passed=passed, rows=rows, **sizes
            ),
            out_shape=[message(piece) for _, piece in plan]
            + [jax.ShapeDtypeStruct(t.shape, f32) for t in through],
            in_specs=[whole(SMEM)] + [whole(VMEM)] * (1 + given) + [whole(pl.ANY)] * passed,
            out_specs=[whole(VMEM)] * made + [whole(pl.ANY)] * passed,
            input_output_aliases={2 + given + i: made + i for i in range(passed)},
            compiler_params=params(),
            cost_estimate=cost(10**9, 10**9),
            name="pick_" + "_".join("%d%d" % w for w in wanted),
        )(tags, rows_of_state, *found.values(), *through)
        return outs[:made], outs[made:]

    steps = [
        ([(1, 0)], [2], []),
        ([(1, 1)], [3], []),
        ([(1, 2), (2, 0)], [], []),
        ([(1, 3), (2, 1)], [], []),
        ([(1, 4), (2, 2)], [], [(2, 0)]),
        ([(2, 3)], [], [(2, 1)]),
        ([(2, 4)], [], [(2, 2)]),
    ]
    got[0][0] = swapped(sent[0], 0)
    got[0][1] = swapped(sent[1], 0)
    for wanted, leaving, awaited in steps:
        through = [token] + [sent[p] for p in leaving] + [got[level][p] for level, p in awaited]
        made, (token, *passed) = make(wanted, through)
        for p, value in zip(leaving, passed):
            got[0][p] = swapped(value, 0)
        for (level, p), value in reversed(list(zip(wanted, made))):
            got[level][p] = swapped(value, level)
        for (level, p), value in zip(awaited, passed[len(leaving) :]):
            got[level][p] = value

    grid = shape.grid()
    face_x, face_y, _, face_z, _ = shape.faces()
    part = [grid, grid, face_y, face_y, face_z, face_z, face_x]
    canvas = jax.ShapeDtypeStruct((NF * groups, rows * SUB, LANES), f32)
    full = final[-1][0] // NF

    def assemble(slabs, before):
        first = not before
        found = dict(holding(range(3), slabs[0] * NF, slabs[1] * NF))
        shapes = part + [canvas] * first
        fixed = 2 + len(found)
        return pl.pallas_call(
            functools.partial(
                assemble_kernel, held=tuple(found), slabs=slabs, occ=occ, shape=shape,
                first=first, **sizes,
            ),
            out_shape=shapes,
            in_specs=[whole(SMEM)] + [whole(VMEM)] * (1 + len(found) + len(before)),
            out_specs=[whole(VMEM)] * len(shapes),
            scratch_shapes=[VMEM((occ * NF * rows, LANES), f32)],
            input_output_aliases={fixed + i: i for i in range(len(before))},
            compiler_params=params(),
            name="assemble_%d" % slabs[0],
        )(tags, rows_of_state, *found.values(), *before)

    *made, blank = assemble((0, full), [])
    *made, x_faces = assemble((full, shape.slabs), made)
    made = made[:2] + [x_faces] + made[2:]

    def ring(value, axis, step):
        size = lax.axis_size(axis)
        return lax.ppermute(value, axis, [(i, (i + step) % size) for i in range(size)])

    def beside(value, axis, shift):
        size = lax.axis_size(axis)
        pairs = [(i, ((i + shift) ^ 1) - shift) for i in range(size)]
        return lax.ppermute(value, axis, [(i, j % size) for i, j in pairs])

    def flux_sums(prim, x_faces, y_one, y_two, z_lo, z_hi):
        if size_x == 2:
            x_faces = ring(x_faces, "gx", 1)
        else:
            x_faces = jnp.stack([ring(x_faces[0], "gx", 1), ring(x_faces[1], "gx", -1)])
        got_one, got_two = beside(y_one, "gy", 1), beside(y_two, "gy", 0)
        z_prev, z_next = ring(z_hi, "gz", 1), ring(z_lo, "gz", -1)
        ghost = VMEM((NF, rows, LANES), f32)
        work = [VMEM(grid.shape, f32)] * 3
        total = pl.pallas_call(
            functools.partial(sweep_z_kernel, shape=shape),
            out_shape=grid,
            in_specs=[whole(VMEM)] * 5,
            out_specs=whole(VMEM),
            scratch_shapes=[ghost] * 2 + work,
            compiler_params=params(),
            name="sweep_z",
        )(prim, z_lo, z_hi, z_prev, z_next)
        total = pl.pallas_call(
            functools.partial(sweep_x_kernel, shape=shape),
            out_shape=grid,
            in_specs=[whole(VMEM)] * 3,
            out_specs=whole(VMEM),
            input_output_aliases={2: 0},
            compiler_params=params(),
            name="sweep_x",
        )(prim, x_faces, total)
        return y_one, y_two, got_one, got_two, total

    produced = [grid, grid] + shape.faces()
    scratch = [VMEM(face_y.shape, f32)] * 2 + [VMEM(grid.shape, f32)] * 4
    field, prim = made[0], made[1]
    sums = flux_sums(prim, *made[2:])
    made = pl.pallas_call(
        functools.partial(sweep_y_one_kernel, shape=shape),
        out_shape=produced,
        in_specs=[whole(VMEM)] * 7,
        out_specs=[whole(VMEM)] * len(produced),
        scratch_shapes=scratch,
        compiler_params=params(),
        name="sweep_y_one",
    )(field, prim, *sums)
    one, one_prim = made[0], made[1]
    sums = flux_sums(one_prim, *made[2:])
    out, _ = pl.pallas_call(
        functools.partial(sweep_y_two_kernel, shape=shape, occ=occ, groups=groups),
        out_shape=[canvas, canvas],
        in_specs=[whole(HBM)] + [whole(VMEM)] * 9,
        out_specs=[whole(HBM), whole(VMEM)],
        scratch_shapes=scratch
        + [
            VMEM(grid.shape, f32),
            pltpu.SemaphoreType.DMA((shape.slabs, NF)),
            SMEM((occ,), jnp.int32),
            pltpu.SemaphoreType.DMA,
        ],
        input_output_aliases={9: 1},
        compiler_params=params(),
        name="sweep_y_two",
    )(pltpu.with_memory_space_constraint(own, HBM), field, one, one_prim, *sums, blank)
    return (
        out.reshape(NF, groups, rows, SUB, LANES)
        .transpose(1, 3, 0, 2, 4)
        .reshape(slots, NF, cells)
    )


def solution(mesh):
    placed = (
        P(AXES, None, None),
        P(None, AXES, None),
        P(None, AXES, None),
        P(),
    )
    return jax.shard_map(
        shards,
        mesh=mesh,
        in_specs=placed,
        out_specs=P(AXES, None, None),
        check_vma=False,
    )
```

```python
import functools

import jax
import jax.numpy as jnp
from jax import lax
from jax.experimental import pallas as pl
from jax.experimental.pallas import tpu as pltpu
from jax.sharding import PartitionSpec as P

gamma_ratio = 1.4
time_step = 0.05
LANES = 128
SUB = 8
NF = 5
FIELDS = range(NF)
AXES = ("gx", "gy", "gz")

VMEM = pltpu.VMEM
SMEM = pltpu.SMEM
HBM = pltpu.HBM
f32 = jnp.float32


def whole(space):
    return pl.BlockSpec(memory_space=space)


def params():
    return pltpu.CompilerParams(vmem_limit_bytes=16 * 1024 * 1024)


def cost(flops, moved):
    return pl.CostEstimate(flops=flops, bytes_accessed=moved, transcendentals=0)


def split_units(units, shares):
    ends = [units * sum(shares[: i + 1]) // sum(shares) for i in range(len(shares))]
    return list(zip([0] + ends[:-1], ends))


def from_state(state, tag, unit, slots, rows):
    slab, field = unit // NF, unit % NF
    groups = slots // SUB
    base = (tag // SUB) * (rows * SUB) + lax.rem(tag, SUB)
    start = base + (field * groups * rows + slab * SUB) * SUB
    return state[pl.ds(start, SUB, stride=SUB), :]


def pick(tag, unit, state, arrived, slots, rows, moves):
    value = from_state(state, jnp.minimum(tag, slots - 1), unit, slots, rows)
    for level, held in enumerate(arrived):
        base = slots + level * moves
        index = jnp.clip(tag - base, 0, moves - 1)
        for (begin, end), ref in held:
            if begin <= unit < end:
                at = (unit - begin) * SUB
                value = jnp.where(tag >= base, ref[index, at : at + SUB, :], value)
    return value


def first_kernel(send_hbm, state_hbm, out, send, held, sems, *, piece, slots, rows, moves):
    span = SUB * SUB
    groups = slots // SUB
    copies = [pltpu.make_async_copy(send_hbm, send, sems.at[0])]
    for unit in range(*piece):
        slab, field = unit // NF, unit % NF
        for g in range(groups):
            at = ((field * groups + g) * rows + slab * SUB) * SUB
            to = ((unit - piece[0]) * groups + g) * span
            copies.append(
                pltpu.make_async_copy(
                    state_hbm.at[pl.ds(at, span), :],
                    held.at[pl.ds(to, span), :],
                    sems.at[len(copies)],
                )
            )
    for c in copies:
        c.start()
    for c in copies:
        c.wait()
    for k in range(moves):
        slot = jnp.minimum(send[0, 0, k], slots - 1)
        base = (slot // SUB) * span + lax.rem(slot, SUB)
        for i in range(piece[1] - piece[0]):
            out[k, i * SUB : (i + 1) * SUB, :] = held[
                pl.ds(base + i * groups * span, SUB, stride=SUB), :
            ]


def rest_kernel(send, recv, own, state, tags, token, *refs, pieces, slots, rows, moves, occ):
    outs, where = refs[:-1], refs[-1]
    token[...] = jnp.zeros_like(token)
    for slot in range(slots):
        where[slot] = slot
    for level in range(3):
        if level:
            for k in range(moves):
                slot = jnp.minimum(send[level, 0, k], slots - 1)
                tags[(level - 1) * moves + k] = where[slot]
        for k in range(moves):
            where[recv[level, 0, k]] = slots + level * moves + k
    for b in range(occ):
        tags[2 * moves + b] = where[own[b]]
    for k in range(moves):
        slot = jnp.minimum(send[0, 0, k], slots - 1)
        for (begin, end), out in zip(pieces, outs):
            for unit in range(begin, end):
                at = (unit - begin) * SUB
                out[k, at : at + SUB, :] = from_state(state, slot, unit, slots, rows)


def group_levels(refs, held):
    levels = [[], [], []]
    for ref, (level, piece) in zip(refs, held):
        levels[level].append((piece, ref))
    return levels


def pick_kernel(tags, state, *refs, plan, held, passed, slots, rows, moves):
    given = len(held)
    arrived = group_levels(refs[:given], held)
    outs = refs[given + passed :]
    for (level, (begin, end)), out in zip(plan, outs):
        for k in range(moves):
            tag = tags[(level - 1) * moves + k]
            for unit in range(begin, end):
                at = (unit - begin) * SUB
                out[k, at : at + SUB, :] = pick(
                    tag, unit, state, arrived[:level], slots, rows, moves
                )


def primitives(cons):
    density = cons[0]
    inverse = 1.0 / density
    vel = [cons[1] * inverse, cons[2] * inverse, cons[3] * inverse]
    kinetic = cons[1] * vel[0] + cons[2] * vel[1] + cons[3] * vel[2]
    pressure = (gamma_ratio - 1.0) * (cons[4] - 0.5 * kinetic)
    return [density, vel[0], vel[1], vel[2], pressure]


def half_minmod(lower, upper):
    both = jnp.maximum(0.0, jnp.minimum(lower, upper)) + jnp.minimum(
        0.0, jnp.maximum(lower, upper)
    )
    return 0.5 * both


def half_slopes(before, here, after):
    return [half_minmod(h - b, a - h) for b, h, a in zip(before, here, after)]


def plus(a, b):
    return [x + y for x, y in zip(a, b)]


def minus(a, b):
    return [x - y for x, y in zip(a, b)]


def side_terms(prim, normal):
    density, vel, pressure = prim[0], prim[1:4], prim[4]
    along = vel[normal]
    mom = [density * v for v in vel]
    kinetic = mom[0] * vel[0] + mom[1] * vel[1] + mom[2] * vel[2]
    energy = pressure * (1.0 / (gamma_ratio - 1.0)) + 0.5 * kinetic
    flux = [m * along for m in mom]
    flux[normal] = flux[normal] + pressure
    scaled = gamma_ratio * pressure
    speed = jnp.abs(along) + scaled * lax.rsqrt(scaled * density)
    return [density] + mom + [energy], [mom[normal]] + flux + [(energy + pressure) * along], speed


def twice_flux(left, right, normal):
    left_cons, left_flux, left_speed = side_terms(left, normal)
    right_cons, right_flux, right_speed = side_terms(right, normal)
    speed = jnp.maximum(left_speed, right_speed)
    return [
        (fl + fr) - speed * (ur - ul)
        for fl, fr, ul, ur in zip(left_flux, right_flux, left_cons, right_cons)
    ]


def lane_of():
    return lax.broadcasted_iota(jnp.int32, (SUB, LANES), 1)


def sub_of():
    return lax.broadcasted_iota(jnp.int32, (SUB, LANES), 0)


def lane_roll(value, amount):
    amount = amount % LANES
    return value if amount == 0 else pltpu.roll(value, amount, 1)


class Shape:
    def __init__(self, rows, edge):
        self.rows, self.edge = rows, edge
        self.halves = rows // edge
        self.width = 2 * edge
        self.fit = LANES // self.width
        self.slabs = rows // SUB
        self.pad = 2 * self.halves

    def at(self, f, row):
        start = (f * self.rows + row) * SUB
        return pl.ds(start if isinstance(start, int) else pl.multiple_of(start, SUB), SUB)

    def across(self, f, slab, sub):
        return pl.ds((f * self.rows + slab * SUB) * SUB + sub, SUB, stride=SUB)

    def grid(self):
        return jax.ShapeDtypeStruct((NF * self.rows * SUB, LANES), f32)

    def faces(self):
        x = jax.ShapeDtypeStruct((2, NF, self.pad, SUB, LANES), f32)
        y = jax.ShapeDtypeStruct((NF, self.edge // self.fit, SUB, LANES), f32)
        z = jax.ShapeDtypeStruct((NF, self.rows, LANES), f32)
        return [x, y, y, z, z]


def in_turn(count, *phases):
    for step in range(count + len(phases) - 1):
        for late, phase in enumerate(phases):
            if 0 <= step - late < count:
                phase(step - late)


def odd_y():
    return lax.rem(lax.axis_index("gy"), 2) == 1


def send_slab(shape, prim, y_one, y_two, z_lo, z_hi, slab):
    lane = lane_of()
    halves = shape.halves
    odd = odd_y()
    for f in FIELDS:
        lo = hi = None
        for k in range(shape.fit):
            row = slab * SUB + k * halves
            below = lane_roll(prim[shape.at(f, row), :], shape.width * k)
            above = lane_roll(prim[shape.at(f, row + halves - 1), :], shape.width * (k + 1))
            if lo is None:
                lo, hi = below, above
            else:
                mine = lane >= shape.width * k
                lo = jnp.where(mine, below, lo)
                hi = jnp.where(mine, above, hi)
        y_one[f, slab] = jnp.where(odd, hi, lo)
        y_two[f, slab] = jnp.where(odd, lo, hi)
        to = pl.ds(slab * SUB, SUB) if isinstance(slab, int) else pl.ds(
            pl.multiple_of(slab * SUB, SUB), SUB
        )
        z_lo[f, to, :] = prim[shape.across(f, slab, 0), :]
        z_hi[f, to, :] = prim[shape.across(f, slab, SUB - 1), :]


def send_x(shape, prim, faces, low=True, high=True):
    for f in FIELDS:
        for i in range(shape.pad):
            if high:
                faces[0, f, i] = prim[shape.at(f, shape.rows - shape.pad + i), :]
            if low:
                faces[1, f, i] = prim[shape.at(f, i), :]


def assemble_kernel(tags, state, *refs, held, slabs, slots, moves, occ, shape, first):
    given = len(held)
    arrived = group_levels(refs[:given], held)
    outs = refs[given + (0 if first else 7) :]
    field, prim, y_one, y_two, z_lo, z_hi, x_faces = outs[:7]
    blocks = outs[-1]
    units = NF * shape.slabs
    for b in range(occ):
        tag = tags[2 * moves + b]
        for unit in range(slabs[0] * NF, slabs[1] * NF):
            at = (b * units + unit) * SUB
            blocks[at : at + SUB, :] = pick(tag, unit, state, arrived, slots, shape.rows, moves)
    for slab in range(*slabs):
        for i in range(SUB):
            row = slab * SUB + i
            cons = [
                blocks[pl.ds((slab * NF + f) * SUB + i, occ, stride=units * SUB), :] for f in FIELDS
            ]
            for f, (c, w) in enumerate(zip(cons, primitives(cons))):
                field[shape.at(f, row), :] = c
                prim[shape.at(f, row), :] = w
        send_slab(shape, prim, y_one, y_two, z_lo, z_hi, slab)
    if first:
        canvas = outs[7]

        def clear(i, carry):
            for c in range(canvas.shape[0]):
                canvas[c, pl.ds(pl.multiple_of(i * SUB, SUB), SUB), :] = jnp.zeros((SUB, LANES), f32)
            return carry

        lax.fori_loop(0, canvas.shape[1] // SUB, clear, 0)
    send_x(shape, prim, x_faces, low=first, high=not first)


def sweep_z_kernel(prim, z_lo, z_hi, z_prev, z_next, total, flux_z, right_z, left, right, flux, *, shape):
    edge, rows = shape.edge, shape.rows

    def ghost(a):
        at = pl.ds(a * SUB, SUB)
        low = [z_lo[f, at, :] for f in FIELDS]
        high = [z_hi[f, at, :] for f in FIELDS]
        prev = [z_prev[f, at, :] for f in FIELDS]
        after = [z_next[f, at, :] for f in FIELDS]
        below = [lane_roll(v, -(edge - 1)) for v in prev]
        before = [lane_roll(v, -(edge - 2)) for v in prev]
        second = [lane_roll(v, -1) for v in low]
        lefts = plus(below, half_slopes(before, below, low))
        rights = minus(low, half_slopes(below, low, second))
        fluxes = twice_flux(lefts, rights, 2)
        last = [lane_roll(v, -(edge - 1)) for v in high]
        beyond = [lane_roll(v, -1) for v in after]
        over = minus(after, half_slopes(last, after, beyond))
        for f in FIELDS:
            flux_z[f, at, :] = lane_roll(fluxes[f], edge - 1)
            right_z[f, at, :] = over[f]

    lane = lane_of()
    z_of = lax.rem(lane, edge)
    sub = sub_of()
    first_z, last_z = z_of == 0, z_of == edge - 1
    first_sub, last_sub = sub == 0, sub == SUB - 1
    higher = lane - z_of + lax.rem(z_of + 1, edge)
    lower = lane - z_of + lax.rem(z_of + edge - 1, edge)

    def insert(ref, f, row):
        return jnp.broadcast_to(ref[f, pl.ds(row, 1), :], (SUB, LANES))

    def up(value, f, row, ghosts):
        across = jnp.where(last_sub, insert(ghosts, f, row), pltpu.roll(value, SUB - 1, 0))
        return jnp.take_along_axis(jnp.where(first_z, across, value), higher, axis=1)

    def down(value, f, row, ghosts):
        across = jnp.where(first_sub, insert(ghosts, f, row), pltpu.roll(value, 1, 0))
        return jnp.take_along_axis(jnp.where(last_z, across, value), lower, axis=1)

    def slopes(slab):
        ghost(slab)
        for row in range(slab * SUB, (slab + 1) * SUB):
            for f in FIELDS:
                at = shape.at(f, row)
                mine = prim[at, :]
                shift = half_minmod(mine - down(mine, f, row, z_prev), up(mine, f, row, z_next) - mine)
                left[at, :] = mine + shift
                right[at, :] = mine - shift

    def fluxes(slab):
        for row in range(slab * SUB, (slab + 1) * SUB):
            lefts = [left[shape.at(f, row), :] for f in FIELDS]
            rights = [up(right[shape.at(f, row), :], f, row, right_z) for f in FIELDS]
            for f, value in enumerate(twice_flux(lefts, rights, 2)):
                flux[shape.at(f, row), :] = value

    def differences(slab):
        for row in range(slab * SUB, (slab + 1) * SUB):
            for f in FIELDS:
                at = shape.at(f, row)
                mine = flux[at, :]
                total[at, :] = mine - down(mine, f, row, flux_z)

    in_turn(shape.slabs, slopes, fluxes, differences)


def sweep_x_kernel(prim, x_faces, sofar, total, *, shape):
    halves, edge = shape.halves, shape.edge

    def cells(x, h):
        if x < 0:
            return [x_faces[0, f, (x + 2) * halves + h] for f in FIELDS]
        if x >= edge:
            return [x_faces[1, f, (x - edge) * halves + h] for f in FIELDS]
        return [prim[shape.at(f, x * halves + h), :] for f in FIELDS]

    for h in range(halves):
        left = below = None
        ahead = [cells(x, h) for x in (-2, -1, 0)]
        for x in range(-1, edge + 1):
            shift = half_slopes(*ahead)
            if left is not None:
                flux = twice_flux(left, minus(ahead[1], shift), 0)
                if below is not None:
                    for f in FIELDS:
                        at = shape.at(f, (x - 1) * halves + h)
                        total[at, :] = sofar[at, :] + (flux[f] - below[f])
                below = flux
            left = plus(ahead[1], shift)
            if x < edge:
                ahead = ahead[1:] + [cells(x + 2, h)]


def sweep_y(prim, y_one, y_two, got_one, got_two, sofar, ghost_prim, ghost_flux, left, right, flux, turned,
            shape, finish, after_slab):
    edge, halves, fit, width = shape.edge, shape.halves, shape.fit, shape.width
    lane = lane_of()
    upper = lax.rem(lane, width) >= edge
    odd = odd_y()

    def prepare(q):
        low = [jnp.where(odd, y_two[f, q], y_one[f, q]) for f in FIELDS]
        high = [jnp.where(odd, y_one[f, q], y_two[f, q]) for f in FIELDS]
        below = [jnp.where(odd, got_two[f, q], got_one[f, q]) for f in FIELDS]
        after = [jnp.where(odd, got_one[f, q], got_two[f, q]) for f in FIELDS]
        before = [lane_roll(v, edge) for v in below]
        first = [lane_roll(v, edge) for v in low]
        lefts = plus(below, half_slopes(before, below, first))
        rights = minus(first, half_slopes(below, first, low))
        fluxes = twice_flux(lefts, rights, 1)
        last = [lane_roll(v, -edge) for v in high]
        beyond = [lane_roll(v, -edge) for v in after]
        over = minus(after, half_slopes(last, after, beyond))
        for f in FIELDS:
            ghost_prim[f, q] = jnp.where(upper, below[f], after[f])
            ghost_flux[f, q] = jnp.where(upper, fluxes[f], over[f])

    top_lanes = lane >= LANES - edge
    low_lanes = lane < edge

    def up(values, insert):
        rolled = [lane_roll(v, -edge) for v in values]
        follow = rolled[1:] + [insert]
        return [jnp.where(top_lanes, n, r) for r, n in zip(rolled, follow)]

    def down(values, insert):
        rolled = [lane_roll(v, edge) for v in values]
        lead = [insert] + rolled[:-1]
        return [jnp.where(low_lanes, n, r) for r, n in zip(rolled, lead)]

    def each(q):
        for k in range(fit):
            yield -(width * k + edge), (q * fit + k) * halves

    def slopes(q):
        prepare(q)
        for turn, base in each(q):
            for f in FIELDS:
                mine = [prim[shape.at(f, base + h), :] for h in range(halves)]
                ghost = lane_roll(ghost_prim[f, q], turn)
                over, under = up(mine, ghost), down(mine, ghost)
                for h in range(halves):
                    shift = half_minmod(mine[h] - under[h], over[h] - mine[h])
                    left[shape.at(f, base + h), :] = mine[h] + shift
                    right[shape.at(f, base + h), :] = mine[h] - shift

    def fluxes(q):
        for turn, base in each(q):
            rights = []
            for f in FIELDS:
                mine = [right[shape.at(f, base + h), :] for h in range(halves)]
                ghost = lane_roll(ghost_flux[f, q], turn)
                turned[shape.at(f, base), :] = ghost
                rights.append(up(mine, ghost))
            for h in range(halves):
                lefts = [left[shape.at(f, base + h), :] for f in FIELDS]
                result = twice_flux(lefts, [rights[f][h] for f in FIELDS], 1)
                for f in FIELDS:
                    flux[shape.at(f, base + h), :] = result[f]

    def differences(q):
        for turn, base in each(q):
            total = [[None] * NF for _ in range(halves)]
            for f in FIELDS:
                mine = [flux[shape.at(f, base + h), :] for h in range(halves)]
                under = down(mine, turned[shape.at(f, base), :])
                for h in range(halves):
                    total[h][f] = sofar[shape.at(f, base + h), :] + (mine[h] - under[h])
            for h in range(halves):
                finish(base + h, total[h])

    in_turn(edge // fit, slopes, fluxes, differences, after_slab)


def sweep_y_one_kernel(field, prim, y_one, y_two, got_one, got_two, sofar, *refs, shape):
    one, one_prim, x_faces, out_y_one, out_y_two, z_lo, z_hi = refs[:7]

    def finish(row, total):
        cons = [field[shape.at(f, row), :] - (0.5 * time_step) * total[f] for f in FIELDS]
        for f, (c, w) in enumerate(zip(cons, primitives(cons))):
            one[shape.at(f, row), :] = c
            one_prim[shape.at(f, row), :] = w

    def after_slab(q):
        send_slab(shape, one_prim, out_y_one, out_y_two, z_lo, z_hi, q)

    sweep_y(prim, y_one, y_two, got_one, got_two, sofar, *refs[7:], shape, finish, after_slab)
    send_x(shape, one_prim, x_faces)


def sweep_y_two_kernel(own_there, field, one, prim, y_one, y_two, got_one, got_two, sofar, zeros, out,
                       canvas, *refs, shape, occ, groups):
    scratch, (result, sems, own, own_sem) = refs[:6], refs[6:]
    slots = pltpu.make_async_copy(own_there, own, own_sem)
    slots.start()
    rows = shape.rows
    span = SUB * SUB

    def finish(row, total):
        for f in FIELDS:
            at = shape.at(f, row)
            advanced = one[at, :] - (0.5 * time_step) * total[f]
            result[at, :] = 0.5 * field[at, :] + 0.5 * advanced

    def copy(part):
        begin = part * span if isinstance(part, int) else pl.multiple_of(part * span, span)
        at = pl.ds(begin, span)
        return [
            pltpu.make_async_copy(canvas.at[of, at, :], out.at[of, at, :], sems.at[part, f])
            for f, of in enumerate(pl.ds(f * groups, groups) for f in FIELDS)
        ]

    def after_slab(q):
        if q == 0:
            slots.wait()
        for b in range(occ):
            slot = own[b]
            to = pl.ds(q * span + lax.rem(slot, SUB), SUB, stride=SUB)
            for f in FIELDS:
                canvas[f * groups + slot // SUB, to, :] = result[shape.across(f, q, b), :]
        for c in copy(q):
            c.start()

    sweep_y(prim, y_one, y_two, got_one, got_two, sofar, *scratch, shape, finish, after_slab)
    for part in range(shape.slabs):
        for c in copy(part):
            c.wait()


def shards(state, send_slots, recv_slots, owner_slot):
    slots, _, cells = state.shape
    moves = send_slots.shape[2]
    size_x, size_y, size_z = (lax.axis_size(axis) for axis in AXES)
    occ = owner_slot.shape[0] // (size_x * size_y * size_z)
    edge = round(cells ** (1 / 3))
    rows = cells // LANES
    groups = slots // SUB
    shape = Shape(rows, edge)
    units = NF * shape.slabs
    cuts = [split_units(units, shares) for shares in ((3, 5, 7, 5), (3, 4, 6, 4, 3), (3, 4, 6, 4, 3))]
    firsts, final = cuts[0], cuts[2]

    bit_z = size_z.bit_length() - 2
    bit_y = bit_z + size_y.bit_length() - 1
    bit_x = bit_y + size_x.bit_length() - 1
    pair_bits = (bit_x, bit_y, bit_z)

    def swapped(value, level):
        mask = 2 ** pair_bits[level]
        pairs = [(source, source ^ mask) for source in range(lax.axis_size(AXES))]
        return lax.ppermute(value, AXES, pairs)

    rows_of_state = (
        state.reshape(groups, SUB, NF, rows, LANES)
        .transpose(2, 0, 3, 1, 4)
        .reshape(NF * groups * rows * SUB, LANES)
    )
    state_there = pltpu.with_memory_space_constraint(rows_of_state, HBM)
    send_there = pltpu.with_memory_space_constraint(send_slots, HBM)
    device = lax.axis_index(AXES)
    own = lax.dynamic_slice(owner_slot, (device * occ,), (occ,))
    sizes = dict(slots=slots, moves=moves)

    def message(piece):
        begin, end = piece
        return jax.ShapeDtypeStruct((moves, (end - begin) * SUB, LANES), f32)

    head = firsts[0]
    sent = [None] * len(firsts)
    sent[0] = pl.pallas_call(
        functools.partial(first_kernel, piece=head, rows=rows, **sizes),
        out_shape=message(head),
        in_specs=[whole(HBM)] * 2,
        out_specs=whole(VMEM),
        scratch_shapes=[
            SMEM(send_slots.shape, jnp.int32),
            VMEM(((head[1] - head[0]) * groups * SUB * SUB, LANES), f32),
            pltpu.SemaphoreType.DMA((1 + (head[1] - head[0]) * groups,)),
        ],
        compiler_params=params(),
        name="pack_first",
    )(send_there, state_there)
    tags, token, *sent[1:] = pl.pallas_call(
        functools.partial(rest_kernel, pieces=firsts[1:], rows=rows, occ=occ, **sizes),
        out_shape=[
            jax.ShapeDtypeStruct((2 * moves + occ,), jnp.int32),
            jax.ShapeDtypeStruct((SUB, LANES), f32),
        ]
        + [message(piece) for piece in firsts[1:]],
        in_specs=[whole(SMEM)] * 3 + [whole(VMEM)],
        out_specs=[whole(SMEM)] + [whole(VMEM)] * len(firsts),
        scratch_shapes=[SMEM((slots + SUB,), jnp.int32)],
        compiler_params=params(),
        name="pack_rest",
    )(send_slots, recv_slots, own, rows_of_state)

    got = [[None] * len(cut) for cut in cuts]

    def holding(levels, begin, end):
        found = [
            ((level, piece), got[level][p])
            for level in levels
            for p, piece in enumerate(cuts[level])
            if piece[0] < end and piece[1] > begin
        ]
        return found

    def make(wanted, through):
        found = {}
        for level, p in wanted:
            for key, value in holding(range(level), *cuts[level][p]):
                found[key] = value
        plan = tuple((level, cuts[level][p]) for level, p in wanted)
        given, passed, made = len(found), len(through), len(wanted)
        outs = pl.pallas_call(
            functools.partial(
                pick_kernel, plan=plan, held=tuple(found), passed=passed, rows=rows, **sizes
            ),
            out_shape=[message(piece) for _, piece in plan]
            + [jax.ShapeDtypeStruct(t.shape, f32) for t in through],
            in_specs=[whole(SMEM)] + [whole(VMEM)] * (1 + given) + [whole(pl.ANY)] * passed,
            out_specs=[whole(VMEM)] * made + [whole(pl.ANY)] * passed,
            input_output_aliases={2 + given + i: made + i for i in range(passed)},
            compiler_params=params(),
            cost_estimate=cost(10**9, 10**9),
            name="pick_" + "_".join("%d%d" % w for w in wanted),
        )(tags, rows_of_state, *found.values(), *through)
        return outs[:made], outs[made:]

    steps = [
        ([(1, 0)], [2], []),
        ([(1, 1)], [3], []),
        ([(1, 2), (2, 0)], [], []),
        ([(1, 3), (2, 1)], [], []),
        ([(1, 4), (2, 2)], [], [(2, 0)]),
        ([(2, 3)], [], [(2, 1)]),
        ([(2, 4)], [], [(2, 2)]),
    ]
    got[0][0] = swapped(sent[0], 0)
    got[0][1] = swapped(sent[1], 0)
    for wanted, leaving, awaited in steps:
        through = [token] + [sent[p] for p in leaving] + [got[level][p] for level, p in awaited]
        made, (token, *passed) = make(wanted, through)
        for p, value in zip(leaving, passed):
            got[0][p] = swapped(value, 0)
        for (level, p), value in reversed(list(zip(wanted, made))):
            got[level][p] = swapped(value, level)
        for (level, p), value in zip(awaited, passed[len(leaving) :]):
            got[level][p] = value

    grid = shape.grid()
    face_x, face_y, _, face_z, _ = shape.faces()
    part = [grid, grid, face_y, face_y, face_z, face_z, face_x]
    canvas = jax.ShapeDtypeStruct((NF * groups, rows * SUB, LANES), f32)
    full = final[-1][0] // NF

    def assemble(slabs, before):
        first = not before
        found = dict(holding(range(3), slabs[0] * NF, slabs[1] * NF))
        shapes = part + [canvas] * first
        fixed = 2 + len(found)
        return pl.pallas_call(
            functools.partial(
                assemble_kernel, held=tuple(found), slabs=slabs, occ=occ, shape=shape,
                first=first, **sizes,
            ),
            out_shape=shapes,
            in_specs=[whole(SMEM)] + [whole(VMEM)] * (1 + len(found) + len(before)),
            out_specs=[whole(VMEM)] * len(shapes),
            scratch_shapes=[VMEM((occ * NF * rows, LANES), f32)],
            input_output_aliases={fixed + i: i for i in range(len(before))},
            compiler_params=params(),
            name="assemble_%d" % slabs[0],
        )(tags, rows_of_state, *found.values(), *before)

    *made, blank = assemble((0, full), [])
    *made, x_faces = assemble((full, shape.slabs), made)
    made = made[:2] + [x_faces] + made[2:]

    def ring(value, axis, step):
        size = lax.axis_size(axis)
        return lax.ppermute(value, axis, [(i, (i + step) % size) for i in range(size)])

    def beside(value, axis, shift):
        size = lax.axis_size(axis)
        pairs = [(i, ((i + shift) ^ 1) - shift) for i in range(size)]
        return lax.ppermute(value, axis, [(i, j % size) for i, j in pairs])

    def flux_sums(prim, x_faces, y_one, y_two, z_lo, z_hi):
        if size_x == 2:
            x_faces = ring(x_faces, "gx", 1)
        else:
            x_faces = jnp.stack([ring(x_faces[0], "gx", 1), ring(x_faces[1], "gx", -1)])
        got_one, got_two = beside(y_one, "gy", 1), beside(y_two, "gy", 0)
        z_prev, z_next = ring(z_hi, "gz", 1), ring(z_lo, "gz", -1)
        ghost = VMEM((NF, rows, LANES), f32)
        work = [VMEM(grid.shape, f32)] * 3
        total = pl.pallas_call(
            functools.partial(sweep_z_kernel, shape=shape),
            out_shape=grid,
            in_specs=[whole(VMEM)] * 5,
            out_specs=whole(VMEM),
            scratch_shapes=[ghost] * 2 + work,
            compiler_params=params(),
            name="sweep_z",
        )(prim, z_lo, z_hi, z_prev, z_next)
        total = pl.pallas_call(
            functools.partial(sweep_x_kernel, shape=shape),
            out_shape=grid,
            in_specs=[whole(VMEM)] * 3,
            out_specs=whole(VMEM),
            input_output_aliases={2: 0},
            compiler_params=params(),
            name="sweep_x",
        )(prim, x_faces, total)
        return y_one, y_two, got_one, got_two, total

    produced = [grid, grid] + shape.faces()
    scratch = [VMEM(face_y.shape, f32)] * 2 + [VMEM(grid.shape, f32)] * 4
    field, prim = made[0], made[1]
    sums = flux_sums(prim, *made[2:])
    made = pl.pallas_call(
        functools.partial(sweep_y_one_kernel, shape=shape),
        out_shape=produced,
        in_specs=[whole(VMEM)] * 7,
        out_specs=[whole(VMEM)] * len(produced),
        scratch_shapes=scratch,
        compiler_params=params(),
        name="sweep_y_one",
    )(field, prim, *sums)
    one, one_prim = made[0], made[1]
    sums = flux_sums(one_prim, *made[2:])
    out, _ = pl.pallas_call(
        functools.partial(sweep_y_two_kernel, shape=shape, occ=occ, groups=groups),
        out_shape=[canvas, canvas],
        in_specs=[whole(HBM)] + [whole(VMEM)] * 9,
        out_specs=[whole(HBM), whole(VMEM)],
        scratch_shapes=scratch
        + [
            VMEM(grid.shape, f32),
            pltpu.SemaphoreType.DMA((shape.slabs, NF)),
            SMEM((occ,), jnp.int32),
            pltpu.SemaphoreType.DMA,
        ],
        input_output_aliases={9: 1},
        compiler_params=params(),
        name="sweep_y_two",
    )(pltpu.with_memory_space_constraint(own, HBM), field, one, one_prim, *sums, blank)
    return (
        out.reshape(NF, groups, rows, SUB, LANES)
        .transpose(1, 3, 0, 2, 4)
        .reshape(slots, NF, cells)
    )


def solution(mesh):
    placed = (
        P(AXES, None, None),
        P(None, AXES, None),
        P(None, AXES, None),
        P(),
    )
    return jax.shard_map(
        shards,
        mesh=mesh,
        in_specs=placed,
        out_specs=P(AXES, None, None),
        check_vma=False,
    )
```

```python
import functools

import jax
import jax.numpy as jnp
from jax import lax
from jax.experimental import pallas as pl
from jax.experimental.pallas import tpu as pltpu
from jax.sharding import PartitionSpec as P

gamma_ratio = 1.4
time_step = 0.05
LANES = 128
SUB = 8
NF = 5
FIELDS = range(NF)
AXES = ("gx", "gy", "gz")

VMEM = pltpu.VMEM
SMEM = pltpu.SMEM
HBM = pltpu.HBM
f32 = jnp.float32


def whole(space):
    return pl.BlockSpec(memory_space=space)


def params():
    return pltpu.CompilerParams(vmem_limit_bytes=16 * 1024 * 1024)


def cost(flops, moved):
    return pl.CostEstimate(flops=flops, bytes_accessed=moved, transcendentals=0)


def split_units(units, shares):
    ends = [units * sum(shares[: i + 1]) // sum(shares) for i in range(len(shares))]
    return list(zip([0] + ends[:-1], ends))


def from_state(state, tag, unit, slots, rows):
    slab, field = unit // NF, unit % NF
    groups = slots // SUB
    base = (tag // SUB) * (rows * SUB) + lax.rem(tag, SUB)
    start = base + (field * groups * rows + slab * SUB) * SUB
    return state[pl.ds(start, SUB, stride=SUB), :]


def pick(tag, unit, state, arrived, slots, rows, moves):
    value = from_state(state, jnp.minimum(tag, slots - 1), unit, slots, rows)
    for level, held in enumerate(arrived):
        base = slots + level * moves
        index = jnp.clip(tag - base, 0, moves - 1)
        for (begin, end), ref in held:
            if begin <= unit < end:
                at = (unit - begin) * SUB
                value = jnp.where(tag >= base, ref[index, at : at + SUB, :], value)
    return value


def first_kernel(send_hbm, state_hbm, out, send, held, sems, *, piece, slots, rows, moves):
    span = SUB * SUB
    groups = slots // SUB
    copies = [pltpu.make_async_copy(send_hbm, send, sems.at[0])]
    for unit in range(*piece):
        slab, field = unit // NF, unit % NF
        for g in range(groups):
            at = ((field * groups + g) * rows + slab * SUB) * SUB
            to = ((unit - piece[0]) * groups + g) * span
            copies.append(
                pltpu.make_async_copy(
                    state_hbm.at[pl.ds(at, span), :],
                    held.at[pl.ds(to, span), :],
                    sems.at[len(copies)],
                )
            )
    for c in copies:
        c.start()
    for c in copies:
        c.wait()
    for k in range(moves):
        slot = jnp.minimum(send[0, 0, k], slots - 1)
        base = (slot // SUB) * span + lax.rem(slot, SUB)
        for i in range(piece[1] - piece[0]):
            out[k, i * SUB : (i + 1) * SUB, :] = held[
                pl.ds(base + i * groups * span, SUB, stride=SUB), :
            ]


def rest_kernel(send, recv, own, state, tags, token, *refs, pieces, slots, rows, moves, occ):
    outs, where = refs[:-1], refs[-1]
    token[...] = jnp.zeros_like(token)
    for slot in range(slots):
        where[slot] = slot
    for level in range(3):
        if level:
            for k in range(moves):
                slot = jnp.minimum(send[level, 0, k], slots - 1)
                tags[(level - 1) * moves + k] = where[slot]
        for k in range(moves):
            where[recv[level, 0, k]] = slots + level * moves + k
    for b in range(occ):
        tags[2 * moves + b] = where[own[b]]
    for k in range(moves):
        slot = jnp.minimum(send[0, 0, k], slots - 1)
        for (begin, end), out in zip(pieces, outs):
            for unit in range(begin, end):
                at = (unit - begin) * SUB
                out[k, at : at + SUB, :] = from_state(state, slot, unit, slots, rows)


def group_levels(refs, held):
    levels = [[], [], []]
    for ref, (level, piece) in zip(refs, held):
        levels[level].append((piece, ref))
    return levels


def pick_kernel(tags, state, *refs, plan, held, passed, slots, rows, moves):
    given = len(held)
    arrived = group_levels(refs[:given], held)
    outs = refs[given + passed :]
    for (level, (begin, end)), out in zip(plan, outs):
        for k in range(moves):
            tag = tags[(level - 1) * moves + k]
            for unit in range(begin, end):
                at = (unit - begin) * SUB
                out[k, at : at + SUB, :] = pick(
                    tag, unit, state, arrived[:level], slots, rows, moves
                )


def primitives(cons):
    density = cons[0]
    inverse = 1.0 / density
    vel = [cons[1] * inverse, cons[2] * inverse, cons[3] * inverse]
    kinetic = cons[1] * vel[0] + cons[2] * vel[1] + cons[3] * vel[2]
    pressure = (gamma_ratio - 1.0) * (cons[4] - 0.5 * kinetic)
    return [density, vel[0], vel[1], vel[2], pressure]


def half_minmod(lower, upper):
    both = jnp.maximum(0.0, jnp.minimum(lower, upper)) + jnp.minimum(
        0.0, jnp.maximum(lower, upper)
    )
    return 0.5 * both


def half_slopes(before, here, after):
    return [half_minmod(h - b, a - h) for b, h, a in zip(before, here, after)]


def plus(a, b):
    return [x + y for x, y in zip(a, b)]


def minus(a, b):
    return [x - y for x, y in zip(a, b)]


def side_terms(prim, normal):
    density, vel, pressure = prim[0], prim[1:4], prim[4]
    along = vel[normal]
    mom = [density * v for v in vel]
    kinetic = mom[0] * vel[0] + mom[1] * vel[1] + mom[2] * vel[2]
    energy = pressure * (1.0 / (gamma_ratio - 1.0)) + 0.5 * kinetic
    flux = [m * along for m in mom]
    flux[normal] = flux[normal] + pressure
    scaled = gamma_ratio * pressure
    speed = jnp.abs(along) + scaled * lax.rsqrt(scaled * density)
    return [density] + mom + [energy], [mom[normal]] + flux + [(energy + pressure) * along], speed


def twice_flux(left, right, normal):
    left_cons, left_flux, left_speed = side_terms(left, normal)
    right_cons, right_flux, right_speed = side_terms(right, normal)
    speed = jnp.maximum(left_speed, right_speed)
    return [
        (fl + fr) - speed * (ur - ul)
        for fl, fr, ul, ur in zip(left_flux, right_flux, left_cons, right_cons)
    ]


def lane_of():
    return lax.broadcasted_iota(jnp.int32, (SUB, LANES), 1)


def sub_of():
    return lax.broadcasted_iota(jnp.int32, (SUB, LANES), 0)


def lane_roll(value, amount):
    amount = amount % LANES
    return value if amount == 0 else pltpu.roll(value, amount, 1)


class Shape:
    def __init__(self, rows, edge):
        self.rows, self.edge = rows, edge
        self.halves = rows // edge
        self.width = 2 * edge
        self.fit = LANES // self.width
        self.slabs = rows // SUB
        self.pad = 2 * self.halves

    def at(self, f, row):
        start = (f * self.rows + row) * SUB
        return pl.ds(start if isinstance(start, int) else pl.multiple_of(start, SUB), SUB)

    def across(self, f, slab, sub):
        return pl.ds((f * self.rows + slab * SUB) * SUB + sub, SUB, stride=SUB)

    def grid(self):
        return jax.ShapeDtypeStruct((NF * self.rows * SUB, LANES), f32)

    def faces(self):
        x = jax.ShapeDtypeStruct((2, NF, self.pad, SUB, LANES), f32)
        y = jax.ShapeDtypeStruct((NF, self.edge // self.fit, SUB, LANES), f32)
        z = jax.ShapeDtypeStruct((NF, self.rows, LANES), f32)
        return [x, y, y, z, z]


def in_turn(count, *phases):
    for step in range(count + len(phases) - 1):
        for late, phase in enumerate(phases):
            if 0 <= step - late < count:
                phase(step - late)


def odd_y():
    return lax.rem(lax.axis_index("gy"), 2) == 1


def send_slab(shape, prim, y_one, y_two, z_lo, z_hi, slab):
    lane = lane_of()
    halves = shape.halves
    odd = odd_y()
    for f in FIELDS:
        lo = hi = None
        for k in range(shape.fit):
            row = slab * SUB + k * halves
            below = lane_roll(prim[shape.at(f, row), :], shape.width * k)
            above = lane_roll(prim[shape.at(f, row + halves - 1), :], shape.width * (k + 1))
            if lo is None:
                lo, hi = below, above
            else:
                mine = lane >= shape.width * k
                lo = jnp.where(mine, below, lo)
                hi = jnp.where(mine, above, hi)
        y_one[f, slab] = jnp.where(odd, hi, lo)
        y_two[f, slab] = jnp.where(odd, lo, hi)
        to = pl.ds(slab * SUB, SUB) if isinstance(slab, int) else pl.ds(
            pl.multiple_of(slab * SUB, SUB), SUB
        )
        z_lo[f, to, :] = prim[shape.across(f, slab, 0), :]
        z_hi[f, to, :] = prim[shape.across(f, slab, SUB - 1), :]


def send_x(shape, prim, faces, low=True, high=True):
    for f in FIELDS:
        for i in range(shape.pad):
            if high:
                faces[0, f, i] = prim[shape.at(f, shape.rows - shape.pad + i), :]
            if low:
                faces[1, f, i] = prim[shape.at(f, i), :]


def assemble_kernel(tags, state, *refs, held, slabs, slots, moves, occ, shape, first):
    given = len(held)
    arrived = group_levels(refs[:given], held)
    outs = refs[given + (0 if first else 7) :]
    field, prim, y_one, y_two, z_lo, z_hi, x_faces = outs[:7]
    blocks = outs[-1]
    units = NF * shape.slabs
    for b in range(occ):
        tag = tags[2 * moves + b]
        for unit in range(slabs[0] * NF, slabs[1] * NF):
            at = (b * units + unit) * SUB
            blocks[at : at + SUB, :] = pick(tag, unit, state, arrived, slots, shape.rows, moves)
    for slab in range(*slabs):
        for i in range(SUB):
            row = slab * SUB + i
            cons = [
                blocks[pl.ds((slab * NF + f) * SUB + i, occ, stride=units * SUB), :] for f in FIELDS
            ]
            for f, (c, w) in enumerate(zip(cons, primitives(cons))):
                field[shape.at(f, row), :] = c
                prim[shape.at(f, row), :] = w
        send_slab(shape, prim, y_one, y_two, z_lo, z_hi, slab)
    if first:
        canvas = outs[7]

        def clear(i, carry):
            for c in range(canvas.shape[0]):
                canvas[c, pl.ds(pl.multiple_of(i * SUB, SUB), SUB), :] = jnp.zeros((SUB, LANES), f32)
            return carry

        lax.fori_loop(0, canvas.shape[1] // SUB, clear, 0)
    send_x(shape, prim, x_faces, low=first, high=not first)


def sweep_z_kernel(prim, z_lo, z_hi, z_prev, z_next, total, flux_z, right_z, left, right, flux, *, shape):
    edge, rows = shape.edge, shape.rows

    def ghost(a):
        at = pl.ds(a * SUB, SUB)
        low = [z_lo[f, at, :] for f in FIELDS]
        high = [z_hi[f, at, :] for f in FIELDS]
        prev = [z_prev[f, at, :] for f in FIELDS]
        after = [z_next[f, at, :] for f in FIELDS]
        below = [lane_roll(v, -(edge - 1)) for v in prev]
        before = [lane_roll(v, -(edge - 2)) for v in prev]
        second = [lane_roll(v, -1) for v in low]
        lefts = plus(below, half_slopes(before, below, low))
        rights = minus(low, half_slopes(below, low, second))
        fluxes = twice_flux(lefts, rights, 2)
        last = [lane_roll(v, -(edge - 1)) for v in high]
        beyond = [lane_roll(v, -1) for v in after]
        over = minus(after, half_slopes(last, after, beyond))
        for f in FIELDS:
            flux_z[f, at, :] = lane_roll(fluxes[f], edge - 1)
            right_z[f, at, :] = over[f]

    lane = lane_of()
    z_of = lax.rem(lane, edge)
    sub = sub_of()
    first_z, last_z = z_of == 0, z_of == edge - 1
    first_sub, last_sub = sub == 0, sub == SUB - 1
    higher = lane - z_of + lax.rem(z_of + 1, edge)
    lower = lane - z_of + lax.rem(z_of + edge - 1, edge)

    def insert(ref, f, row):
        return jnp.broadcast_to(ref[f, pl.ds(row, 1), :], (SUB, LANES))

    def up(value, f, row, ghosts):
        across = jnp.where(last_sub, insert(ghosts, f, row), pltpu.roll(value, SUB - 1, 0))
        return jnp.take_along_axis(jnp.where(first_z, across, value), higher, axis=1)

    def down(value, f, row, ghosts):
        across = jnp.where(first_sub, insert(ghosts, f, row), pltpu.roll(value, 1, 0))
        return jnp.take_along_axis(jnp.where(last_z, across, value), lower, axis=1)

    def slopes(slab):
        ghost(slab)
        for row in range(slab * SUB, (slab + 1) * SUB):
            for f in FIELDS:
                at = shape.at(f, row)
                mine = prim[at, :]
                shift = half_minmod(mine - down(mine, f, row, z_prev), up(mine, f, row, z_next) - mine)
                left[at, :] = mine + shift
                right[at, :] = mine - shift

    def fluxes(slab):
        for row in range(slab * SUB, (slab + 1) * SUB):
            lefts = [left[shape.at(f, row), :] for f in FIELDS]
            rights = [up(right[shape.at(f, row), :], f, row, right_z) for f in FIELDS]
            for f, value in enumerate(twice_flux(lefts, rights, 2)):
                flux[shape.at(f, row), :] = value

    def differences(slab):
        for row in range(slab * SUB, (slab + 1) * SUB):
            for f in FIELDS:
                at = shape.at(f, row)
                mine = flux[at, :]
                total[at, :] = mine - down(mine, f, row, flux_z)

    in_turn(shape.slabs, slopes, fluxes, differences)


def sweep_x_kernel(prim, x_faces, sofar, total, *, shape):
    halves, edge = shape.halves, shape.edge

    def cells(x, h):
        if x < 0:
            return [x_faces[0, f, (x + 2) * halves + h] for f in FIELDS]
        if x >= edge:
            return [x_faces[1, f, (x - edge) * halves + h] for f in FIELDS]
        return [prim[shape.at(f, x * halves + h), :] for f in FIELDS]

    for h in range(halves):
        left = below = None
        ahead = [cells(x, h) for x in (-2, -1, 0)]
        for x in range(-1, edge + 1):
            shift = half_slopes(*ahead)
            if left is not None:
                flux = twice_flux(left, minus(ahead[1], shift), 0)
                if below is not None:
                    for f in FIELDS:
                        at = shape.at(f, (x - 1) * halves + h)
                        total[at, :] = sofar[at, :] + (flux[f] - below[f])
                below = flux
            left = plus(ahead[1], shift)
            if x < edge:
                ahead = ahead[1:] + [cells(x + 2, h)]


def sweep_y(prim, y_one, y_two, got_one, got_two, sofar, ghost_prim, ghost_flux, left, right, flux, turned,
            shape, finish, after_slab):
    edge, halves, fit, width = shape.edge, shape.halves, shape.fit, shape.width
    lane = lane_of()
    upper = lax.rem(lane, width) >= edge
    odd = odd_y()

    def prepare(q):
        low = [jnp.where(odd, y_two[f, q], y_one[f, q]) for f in FIELDS]
        high = [jnp.where(odd, y_one[f, q], y_two[f, q]) for f in FIELDS]
        below = [jnp.where(odd, got_two[f, q], got_one[f, q]) for f in FIELDS]
        after = [jnp.where(odd, got_one[f, q], got_two[f, q]) for f in FIELDS]
        before = [lane_roll(v, edge) for v in below]
        first = [lane_roll(v, edge) for v in low]
        lefts = plus(below, half_slopes(before, below, first))
        rights = minus(first, half_slopes(below, first, low))
        fluxes = twice_flux(lefts, rights, 1)
        last = [lane_roll(v, -edge) for v in high]
        beyond = [lane_roll(v, -edge) for v in after]
        over = minus(after, half_slopes(last, after, beyond))
        for f in FIELDS:
            ghost_prim[f, q] = jnp.where(upper, below[f], after[f])
            ghost_flux[f, q] = jnp.where(upper, fluxes[f], over[f])

    top_lanes = lane >= LANES - edge
    low_lanes = lane < edge

    def up(values, insert):
        rolled = [lane_roll(v, -edge) for v in values]
        follow = rolled[1:] + [insert]
        return [jnp.where(top_lanes, n, r) for r, n in zip(rolled, follow)]

    def down(values, insert):
        rolled = [lane_roll(v, edge) for v in values]
        lead = [insert] + rolled[:-1]
        return [jnp.where(low_lanes, n, r) for r, n in zip(rolled, lead)]

    def each(q):
        for k in range(fit):
            yield -(width * k + edge), (q * fit + k) * halves

    def slopes(q):
        prepare(q)
        for turn, base in each(q):
            for f in FIELDS:
                mine = [prim[shape.at(f, base + h), :] for h in range(halves)]
                ghost = lane_roll(ghost_prim[f, q], turn)
                over, under = up(mine, ghost), down(mine, ghost)
                for h in range(halves):
                    shift = half_minmod(mine[h] - under[h], over[h] - mine[h])
                    left[shape.at(f, base + h), :] = mine[h] + shift
                    right[shape.at(f, base + h), :] = mine[h] - shift

    def fluxes(q):
        for turn, base in each(q):
            rights = []
            for f in FIELDS:
                mine = [right[shape.at(f, base + h), :] for h in range(halves)]
                ghost = lane_roll(ghost_flux[f, q], turn)
                turned[shape.at(f, base), :] = ghost
                rights.append(up(mine, ghost))
            for h in range(halves):
                lefts = [left[shape.at(f, base + h), :] for f in FIELDS]
                result = twice_flux(lefts, [rights[f][h] for f in FIELDS], 1)
                for f in FIELDS:
                    flux[shape.at(f, base + h), :] = result[f]

    def differences(q):
        for turn, base in each(q):
            total = [[None] * NF for _ in range(halves)]
            for f in FIELDS:
                mine = [flux[shape.at(f, base + h), :] for h in range(halves)]
                under = down(mine, turned[shape.at(f, base), :])
                for h in range(halves):
                    total[h][f] = sofar[shape.at(f, base + h), :] + (mine[h] - under[h])
            for h in range(halves):
                finish(base + h, total[h])

    in_turn(edge // fit, slopes, fluxes, differences, after_slab)


def sweep_y_one_kernel(field, prim, y_one, y_two, got_one, got_two, sofar, *refs, shape):
    one, one_prim, x_faces, out_y_one, out_y_two, z_lo, z_hi = refs[:7]

    def finish(row, total):
        cons = [field[shape.at(f, row), :] - (0.5 * time_step) * total[f] for f in FIELDS]
        for f, (c, w) in enumerate(zip(cons, primitives(cons))):
            one[shape.at(f, row), :] = c
            one_prim[shape.at(f, row), :] = w

    def after_slab(q):
        send_slab(shape, one_prim, out_y_one, out_y_two, z_lo, z_hi, q)

    sweep_y(prim, y_one, y_two, got_one, got_two, sofar, *refs[7:], shape, finish, after_slab)
    send_x(shape, one_prim, x_faces)


def sweep_y_two_kernel(own_there, field, one, prim, y_one, y_two, got_one, got_two, sofar, zeros, out,
                       canvas, *refs, shape, occ, groups):
    scratch, (result, sems, own, own_sem) = refs[:6], refs[6:]
    slots = pltpu.make_async_copy(own_there, own, own_sem)
    slots.start()
    rows = shape.rows
    span = SUB * SUB

    def finish(row, total):
        for f in FIELDS:
            at = shape.at(f, row)
            advanced = one[at, :] - (0.5 * time_step) * total[f]
            result[at, :] = 0.5 * field[at, :] + 0.5 * advanced

    def copy(part):
        begin = part * span if isinstance(part, int) else pl.multiple_of(part * span, span)
        at = pl.ds(begin, span)
        return [
            pltpu.make_async_copy(canvas.at[of, at, :], out.at[of, at, :], sems.at[part, f])
            for f, of in enumerate(pl.ds(f * groups, groups) for f in FIELDS)
        ]

    def after_slab(q):
        if q == 0:
            slots.wait()
        for b in range(occ):
            slot = own[b]
            to = pl.ds(q * span + lax.rem(slot, SUB), SUB, stride=SUB)
            for f in FIELDS:
                canvas[f * groups + slot // SUB, to, :] = result[shape.across(f, q, b), :]
        for c in copy(q):
            c.start()

    sweep_y(prim, y_one, y_two, got_one, got_two, sofar, *scratch, shape, finish, after_slab)
    for part in range(shape.slabs):
        for c in copy(part):
            c.wait()


def shards(state, send_slots, recv_slots, owner_slot):
    slots, _, cells = state.shape
    moves = send_slots.shape[2]
    size_x, size_y, size_z = (lax.axis_size(axis) for axis in AXES)
    occ = owner_slot.shape[0] // (size_x * size_y * size_z)
    edge = round(cells ** (1 / 3))
    rows = cells // LANES
    groups = slots // SUB
    shape = Shape(rows, edge)
    units = NF * shape.slabs
    cuts = [split_units(units, shares) for shares in ((3, 5, 7, 5), (2, 4, 5, 5, 4), (2, 4, 5, 5, 4))]
    firsts, final = cuts[0], cuts[2]

    bit_z = size_z.bit_length() - 2
    bit_y = bit_z + size_y.bit_length() - 1
    bit_x = bit_y + size_x.bit_length() - 1
    pair_bits = (bit_x, bit_y, bit_z)

    def swapped(value, level):
        mask = 2 ** pair_bits[level]
        pairs = [(source, source ^ mask) for source in range(lax.axis_size(AXES))]
        return lax.ppermute(value, AXES, pairs)

    rows_of_state = (
        state.reshape(groups, SUB, NF, rows, LANES)
        .transpose(2, 0, 3, 1, 4)
        .reshape(NF * groups * rows * SUB, LANES)
    )
    state_there = pltpu.with_memory_space_constraint(rows_of_state, HBM)
    send_there = pltpu.with_memory_space_constraint(send_slots, HBM)
    device = lax.axis_index(AXES)
    own = lax.dynamic_slice(owner_slot, (device * occ,), (occ,))
    sizes = dict(slots=slots, moves=moves)

    def message(piece):
        begin, end = piece
        return jax.ShapeDtypeStruct((moves, (end - begin) * SUB, LANES), f32)

    head = firsts[0]
    sent = [None] * len(firsts)
    sent[0] = pl.pallas_call(
        functools.partial(first_kernel, piece=head, rows=rows, **sizes),
        out_shape=message(head),
        in_specs=[whole(HBM)] * 2,
        out_specs=whole(VMEM),
        scratch_shapes=[
            SMEM(send_slots.shape, jnp.int32),
            VMEM(((head[1] - head[0]) * groups * SUB * SUB, LANES), f32),
            pltpu.SemaphoreType.DMA((1 + (head[1] - head[0]) * groups,)),
        ],
        compiler_params=params(),
        name="pack_first",
    )(send_there, state_there)
    tags, token, *sent[1:] = pl.pallas_call(
        functools.partial(rest_kernel, pieces=firsts[1:], rows=rows, occ=occ, **sizes),
        out_shape=[
            jax.ShapeDtypeStruct((2 * moves + occ,), jnp.int32),
            jax.ShapeDtypeStruct((SUB, LANES), f32),
        ]
        + [message(piece) for piece in firsts[1:]],
        in_specs=[whole(SMEM)] * 3 + [whole(VMEM)],
        out_specs=[whole(SMEM)] + [whole(VMEM)] * len(firsts),
        scratch_shapes=[SMEM((slots + SUB,), jnp.int32)],
        compiler_params=params(),
        name="pack_rest",
    )(send_slots, recv_slots, own, rows_of_state)

    got = [[None] * len(cut) for cut in cuts]

    def holding(levels, begin, end):
        found = [
            ((level, piece), got[level][p])
            for level in levels
            for p, piece in enumerate(cuts[level])
            if piece[0] < end and piece[1] > begin
        ]
        return found

    def make(wanted, through):
        found = {}
        for level, p in wanted:
            for key, value in holding(range(level), *cuts[level][p]):
                found[key] = value
        plan = tuple((level, cuts[level][p]) for level, p in wanted)
        given, passed, made = len(found), len(through), len(wanted)
        outs = pl.pallas_call(
            functools.partial(
                pick_kernel, plan=plan, held=tuple(found), passed=passed, rows=rows, **sizes
            ),
            out_shape=[message(piece) for _, piece in plan]
            + [jax.ShapeDtypeStruct(t.shape, f32) for t in through],
            in_specs=[whole(SMEM)] + [whole(VMEM)] * (1 + given) + [whole(pl.ANY)] * passed,
            out_specs=[whole(VMEM)] * made + [whole(pl.ANY)] * passed,
            input_output_aliases={2 + given + i: made + i for i in range(passed)},
            compiler_params=params(),
            cost_estimate=cost(10**9, 10**9),
            name="pick_" + "_".join("%d%d" % w for w in wanted),
        )(tags, rows_of_state, *found.values(), *through)
        return outs[:made], outs[made:]

    steps = [
        ([(1, 0)], [2], []),
        ([(1, 1)], [3], []),
        ([(1, 2), (2, 0)], [], []),
        ([(1, 3), (2, 1)], [], []),
        ([(1, 4), (2, 2)], [], [(2, 0)]),
        ([(2, 3)], [], [(2, 1)]),
        ([(2, 4)], [], [(2, 2)]),
    ]
    got[0][0] = swapped(sent[0], 0)
    got[0][1] = swapped(sent[1], 0)
    for wanted, leaving, awaited in steps:
        through = [token] + [sent[p] for p in leaving] + [got[level][p] for level, p in awaited]
        made, (token, *passed) = make(wanted, through)
        for p, value in zip(leaving, passed):
            got[0][p] = swapped(value, 0)
        for (level, p), value in reversed(list(zip(wanted, made))):
            got[level][p] = swapped(value, level)
        for (level, p), value in zip(awaited, passed[len(leaving) :]):
            got[level][p] = value

    grid = shape.grid()
    face_x, face_y, _, face_z, _ = shape.faces()
    part = [grid, grid, face_y, face_y, face_z, face_z, face_x]
    canvas = jax.ShapeDtypeStruct((NF * groups, rows * SUB, LANES), f32)
    full = final[-1][0] // NF

    def assemble(slabs, before):
        first = not before
        found = dict(holding(range(3), slabs[0] * NF, slabs[1] * NF))
        shapes = part + [canvas] * first
        fixed = 2 + len(found)
        return pl.pallas_call(
            functools.partial(
                assemble_kernel, held=tuple(found), slabs=slabs, occ=occ, shape=shape,
                first=first, **sizes,
            ),
            out_shape=shapes,
            in_specs=[whole(SMEM)] + [whole(VMEM)] * (1 + len(found) + len(before)),
            out_specs=[whole(VMEM)] * len(shapes),
            scratch_shapes=[VMEM((occ * NF * rows, LANES), f32)],
            input_output_aliases={fixed + i: i for i in range(len(before))},
            compiler_params=params(),
            name="assemble_%d" % slabs[0],
        )(tags, rows_of_state, *found.values(), *before)

    *made, blank = assemble((0, full), [])
    *made, x_faces = assemble((full, shape.slabs), made)
    made = made[:2] + [x_faces] + made[2:]

    def ring(value, axis, step):
        size = lax.axis_size(axis)
        return lax.ppermute(value, axis, [(i, (i + step) % size) for i in range(size)])

    def beside(value, axis, shift):
        size = lax.axis_size(axis)
        pairs = [(i, ((i + shift) ^ 1) - shift) for i in range(size)]
        return lax.ppermute(value, axis, [(i, j % size) for i, j in pairs])

    def flux_sums(prim, x_faces, y_one, y_two, z_lo, z_hi):
        if size_x == 2:
            x_faces = ring(x_faces, "gx", 1)
        else:
            x_faces = jnp.stack([ring(x_faces[0], "gx", 1), ring(x_faces[1], "gx", -1)])
        got_one, got_two = beside(y_one, "gy", 1), beside(y_two, "gy", 0)
        z_prev, z_next = ring(z_hi, "gz", 1), ring(z_lo, "gz", -1)
        ghost = VMEM((NF, rows, LANES), f32)
        work = [VMEM(grid.shape, f32)] * 3
        total = pl.pallas_call(
            functools.partial(sweep_z_kernel, shape=shape),
            out_shape=grid,
            in_specs=[whole(VMEM)] * 5,
            out_specs=whole(VMEM),
            scratch_shapes=[ghost] * 2 + work,
            compiler_params=params(),
            name="sweep_z",
        )(prim, z_lo, z_hi, z_prev, z_next)
        total = pl.pallas_call(
            functools.partial(sweep_x_kernel, shape=shape),
            out_shape=grid,
            in_specs=[whole(VMEM)] * 3,
            out_specs=whole(VMEM),
            input_output_aliases={2: 0},
            compiler_params=params(),
            name="sweep_x",
        )(prim, x_faces, total)
        return y_one, y_two, got_one, got_two, total

    produced = [grid, grid] + shape.faces()
    scratch = [VMEM(face_y.shape, f32)] * 2 + [VMEM(grid.shape, f32)] * 4
    field, prim = made[0], made[1]
    sums = flux_sums(prim, *made[2:])
    made = pl.pallas_call(
        functools.partial(sweep_y_one_kernel, shape=shape),
        out_shape=produced,
        in_specs=[whole(VMEM)] * 7,
        out_specs=[whole(VMEM)] * len(produced),
        scratch_shapes=scratch,
        compiler_params=params(),
        name="sweep_y_one",
    )(field, prim, *sums)
    one, one_prim = made[0], made[1]
    sums = flux_sums(one_prim, *made[2:])
    out, _ = pl.pallas_call(
        functools.partial(sweep_y_two_kernel, shape=shape, occ=occ, groups=groups),
        out_shape=[canvas, canvas],
        in_specs=[whole(HBM)] + [whole(VMEM)] * 9,
        out_specs=[whole(HBM), whole(VMEM)],
        scratch_shapes=scratch
        + [
            VMEM(grid.shape, f32),
            pltpu.SemaphoreType.DMA((shape.slabs, NF)),
            SMEM((occ,), jnp.int32),
            pltpu.SemaphoreType.DMA,
        ],
        input_output_aliases={9: 1},
        compiler_params=params(),
        name="sweep_y_two",
    )(pltpu.with_memory_space_constraint(own, HBM), field, one, one_prim, *sums, blank)
    return (
        out.reshape(NF, groups, rows, SUB, LANES)
        .transpose(1, 3, 0, 2, 4)
        .reshape(slots, NF, cells)
    )


def solution(mesh):
    placed = (
        P(AXES, None, None),
        P(None, AXES, None),
        P(None, AXES, None),
        P(),
    )
    return jax.shard_map(
        shards,
        mesh=mesh,
        in_specs=placed,
        out_specs=P(AXES, None, None),
        check_vma=False,
    )
```

```python
import functools

import jax
import jax.numpy as jnp
from jax import lax
from jax.experimental import pallas as pl
from jax.experimental.pallas import tpu as pltpu
from jax.sharding import PartitionSpec as P

gamma_ratio = 1.4
time_step = 0.05
LANES = 128
SUB = 8
NF = 5
FIELDS = range(NF)
AXES = ("gx", "gy", "gz")

VMEM = pltpu.VMEM
SMEM = pltpu.SMEM
HBM = pltpu.HBM
f32 = jnp.float32


def whole(space):
    return pl.BlockSpec(memory_space=space)


def params():
    return pltpu.CompilerParams(vmem_limit_bytes=16 * 1024 * 1024)


def cost(flops, moved):
    return pl.CostEstimate(flops=flops, bytes_accessed=moved, transcendentals=0)


def split_units(units, shares):
    ends = [units * sum(shares[: i + 1]) // sum(shares) for i in range(len(shares))]
    return list(zip([0] + ends[:-1], ends))


def from_state(state, tag, unit, slots, rows):
    slab, field = unit // NF, unit % NF
    groups = slots // SUB
    base = (tag // SUB) * (rows * SUB) + lax.rem(tag, SUB)
    start = base + (field * groups * rows + slab * SUB) * SUB
    return state[pl.ds(start, SUB, stride=SUB), :]


def pick(tag, unit, state, arrived, slots, rows, moves):
    value = from_state(state, jnp.minimum(tag, slots - 1), unit, slots, rows)
    for level, held in enumerate(arrived):
        base = slots + level * moves
        index = jnp.clip(tag - base, 0, moves - 1)
        for (begin, end), ref in held:
            if begin <= unit < end:
                at = (unit - begin) * SUB
                value = jnp.where(tag >= base, ref[index, at : at + SUB, :], value)
    return value


def first_kernel(send_hbm, state_hbm, out, send, held, sems, *, piece, slots, rows, moves):
    span = SUB * SUB
    groups = slots // SUB
    copies = [pltpu.make_async_copy(send_hbm, send, sems.at[0])]
    for unit in range(*piece):
        slab, field = unit // NF, unit % NF
        for g in range(groups):
            at = ((field * groups + g) * rows + slab * SUB) * SUB
            to = ((unit - piece[0]) * groups + g) * span
            copies.append(
                pltpu.make_async_copy(
                    state_hbm.at[pl.ds(at, span), :],
                    held.at[pl.ds(to, span), :],
                    sems.at[len(copies)],
                )
            )
    for c in copies:
        c.start()
    for c in copies:
        c.wait()
    for k in range(moves):
        slot = jnp.minimum(send[0, 0, k], slots - 1)
        base = (slot // SUB) * span + lax.rem(slot, SUB)
        for i in range(piece[1] - piece[0]):
            out[k, i * SUB : (i + 1) * SUB, :] = held[
                pl.ds(base + i * groups * span, SUB, stride=SUB), :
            ]


def rest_kernel(send, recv, own, state, tags, token, *refs, pieces, slots, rows, moves, occ):
    outs, where = refs[:-1], refs[-1]
    token[...] = jnp.zeros_like(token)
    for slot in range(slots):
        where[slot] = slot
    for level in range(3):
        if level:
            for k in range(moves):
                slot = jnp.minimum(send[level, 0, k], slots - 1)
                tags[(level - 1) * moves + k] = where[slot]
        for k in range(moves):
            where[recv[level, 0, k]] = slots + level * moves + k
    for b in range(occ):
        tags[2 * moves + b] = where[own[b]]
    for k in range(moves):
        slot = jnp.minimum(send[0, 0, k], slots - 1)
        for (begin, end), out in zip(pieces, outs):
            for unit in range(begin, end):
                at = (unit - begin) * SUB
                out[k, at : at + SUB, :] = from_state(state, slot, unit, slots, rows)


def group_levels(refs, held):
    levels = [[], [], []]
    for ref, (level, piece) in zip(refs, held):
        levels[level].append((piece, ref))
    return levels


def pick_kernel(tags, state, *refs, plan, held, passed, slots, rows, moves):
    given = len(held)
    arrived = group_levels(refs[:given], held)
    outs = refs[given + passed :]
    for (level, (begin, end)), out in zip(plan, outs):
        for k in range(moves):
            tag = tags[(level - 1) * moves + k]
            for unit in range(begin, end):
                at = (unit - begin) * SUB
                out[k, at : at + SUB, :] = pick(
                    tag, unit, state, arrived[:level], slots, rows, moves
                )


def primitives(cons):
    density = cons[0]
    inverse = 1.0 / density
    vel = [cons[1] * inverse, cons[2] * inverse, cons[3] * inverse]
    kinetic = cons[1] * vel[0] + cons[2] * vel[1] + cons[3] * vel[2]
    pressure = (gamma_ratio - 1.0) * (cons[4] - 0.5 * kinetic)
    return [density, vel[0], vel[1], vel[2], pressure]


def half_minmod(lower, upper):
    both = jnp.maximum(0.0, jnp.minimum(lower, upper)) + jnp.minimum(
        0.0, jnp.maximum(lower, upper)
    )
    return 0.5 * both


def half_slopes(before, here, after):
    return [half_minmod(h - b, a - h) for b, h, a in zip(before, here, after)]


def plus(a, b):
    return [x + y for x, y in zip(a, b)]


def minus(a, b):
    return [x - y for x, y in zip(a, b)]


def side_terms(prim, normal):
    density, vel, pressure = prim[0], prim[1:4], prim[4]
    along = vel[normal]
    mom = [density * v for v in vel]
    kinetic = mom[0] * vel[0] + mom[1] * vel[1] + mom[2] * vel[2]
    energy = pressure * (1.0 / (gamma_ratio - 1.0)) + 0.5 * kinetic
    flux = [m * along for m in mom]
    flux[normal] = flux[normal] + pressure
    scaled = gamma_ratio * pressure
    speed = jnp.abs(along) + scaled * lax.rsqrt(scaled * density)
    return [density] + mom + [energy], [mom[normal]] + flux + [(energy + pressure) * along], speed


def twice_flux(left, right, normal):
    left_cons, left_flux, left_speed = side_terms(left, normal)
    right_cons, right_flux, right_speed = side_terms(right, normal)
    speed = jnp.maximum(left_speed, right_speed)
    return [
        (fl + fr) - speed * (ur - ul)
        for fl, fr, ul, ur in zip(left_flux, right_flux, left_cons, right_cons)
    ]


def lane_of():
    return lax.broadcasted_iota(jnp.int32, (SUB, LANES), 1)


def sub_of():
    return lax.broadcasted_iota(jnp.int32, (SUB, LANES), 0)


def lane_roll(value, amount):
    amount = amount % LANES
    return value if amount == 0 else pltpu.roll(value, amount, 1)


class Shape:
    def __init__(self, rows, edge):
        self.rows, self.edge = rows, edge
        self.halves = rows // edge
        self.width = 2 * edge
        self.fit = LANES // self.width
        self.slabs = rows // SUB
        self.pad = 2 * self.halves

    def at(self, f, row):
        start = (f * self.rows + row) * SUB
        return pl.ds(start if isinstance(start, int) else pl.multiple_of(start, SUB), SUB)

    def across(self, f, slab, sub):
        return pl.ds((f * self.rows + slab * SUB) * SUB + sub, SUB, stride=SUB)

    def grid(self):
        return jax.ShapeDtypeStruct((NF * self.rows * SUB, LANES), f32)

    def faces(self):
        x = jax.ShapeDtypeStruct((2, NF, self.pad, SUB, LANES), f32)
        y = jax.ShapeDtypeStruct((NF, self.edge // self.fit, SUB, LANES), f32)
        z = jax.ShapeDtypeStruct((NF, SUB, LANES), f32)
        return [x, y, y, z, z]


def in_turn(count, *phases):
    for step in range(count + len(phases) - 1):
        for late, phase in enumerate(phases):
            if 0 <= step - late < count:
                phase(step - late)


def odd_y():
    return lax.rem(lax.axis_index("gy"), 2) == 1


def send_slab(shape, prim, y_one, y_two, z_lo, z_hi, slab):
    lane = lane_of()
    halves = shape.halves
    odd = odd_y()
    for f in FIELDS:
        lo = hi = None
        for k in range(shape.fit):
            row = slab * SUB + k * halves
            below = lane_roll(prim[shape.at(f, row), :], shape.width * k)
            above = lane_roll(prim[shape.at(f, row + halves - 1), :], shape.width * (k + 1))
            if lo is None:
                lo, hi = below, above
            else:
                mine = lane >= shape.width * k
                lo = jnp.where(mine, below, lo)
                hi = jnp.where(mine, above, hi)
        y_one[f, slab] = jnp.where(odd, hi, lo)
        y_two[f, slab] = jnp.where(odd, lo, hi)
        below = lane_roll(prim[shape.across(f, slab, 0), :], 2 * slab)
        above = lane_roll(prim[shape.across(f, slab, SUB - 1), :], 2 * slab + 2 - shape.edge)
        if slab:
            mine = lax.rem(lane, shape.edge) >= 2 * slab
            below = jnp.where(mine, below, z_lo[f])
            above = jnp.where(mine, above, z_hi[f])
        z_lo[f] = below
        z_hi[f] = above


def send_x(shape, prim, faces, low=True, high=True):
    for f in FIELDS:
        for i in range(shape.pad):
            if high:
                faces[0, f, i] = prim[shape.at(f, shape.rows - shape.pad + i), :]
            if low:
                faces[1, f, i] = prim[shape.at(f, i), :]


def assemble_kernel(tags, state, *refs, held, slabs, slots, moves, occ, shape, first):
    given = len(held)
    arrived = group_levels(refs[:given], held)
    outs = refs[given + (0 if first else 7) :]
    field, prim, y_one, y_two, z_lo, z_hi, x_faces = outs[:7]
    blocks = outs[-1]
    units = NF * shape.slabs
    for b in range(occ):
        tag = tags[2 * moves + b]
        for unit in range(slabs[0] * NF, slabs[1] * NF):
            at = (b * units + unit) * SUB
            blocks[at : at + SUB, :] = pick(tag, unit, state, arrived, slots, shape.rows, moves)
    for slab in range(*slabs):
        for i in range(SUB):
            row = slab * SUB + i
            cons = [
                blocks[pl.ds((slab * NF + f) * SUB + i, occ, stride=units * SUB), :] for f in FIELDS
            ]
            for f, (c, w) in enumerate(zip(cons, primitives(cons))):
                field[shape.at(f, row), :] = c
                prim[shape.at(f, row), :] = w
        send_slab(shape, prim, y_one, y_two, z_lo, z_hi, slab)
    if first:
        canvas = outs[7]

        def clear(i, carry):
            for c in range(canvas.shape[0]):
                canvas[c, pl.ds(pl.multiple_of(i * SUB, SUB), SUB), :] = jnp.zeros((SUB, LANES), f32)
            return carry

        lax.fori_loop(0, canvas.shape[1] // SUB, clear, 0)
    send_x(shape, prim, x_faces, low=first, high=not first)


def sweep_z_kernel(prim, z_prev, z_next, sofar, total, prev_z, next_z, flux_z, right_z, left, right, flux, *, shape):
    edge, rows = shape.edge, shape.rows

    def ghost(a):
        at = pl.ds(a * SUB, SUB)
        low = [prim[shape.across(f, a, 0), :] for f in FIELDS]
        high = [prim[shape.across(f, a, SUB - 1), :] for f in FIELDS]
        prev = [lane_roll(z_prev[f], edge - 2 - 2 * a) for f in FIELDS]
        after = [lane_roll(z_next[f], -2 * a) for f in FIELDS]
        for f in FIELDS:
            prev_z[f, at, :] = prev[f]
            next_z[f, at, :] = after[f]
        below = [lane_roll(v, -(edge - 1)) for v in prev]
        before = [lane_roll(v, -(edge - 2)) for v in prev]
        second = [lane_roll(v, -1) for v in low]
        lefts = plus(below, half_slopes(before, below, low))
        rights = minus(low, half_slopes(below, low, second))
        fluxes = twice_flux(lefts, rights, 2)
        last = [lane_roll(v, -(edge - 1)) for v in high]
        beyond = [lane_roll(v, -1) for v in after]
        over = minus(after, half_slopes(last, after, beyond))
        for f in FIELDS:
            flux_z[f, at, :] = lane_roll(fluxes[f], edge - 1)
            right_z[f, at, :] = over[f]

    lane = lane_of()
    z_of = lax.rem(lane, edge)
    sub = sub_of()
    first_z, last_z = z_of == 0, z_of == edge - 1
    first_sub, last_sub = sub == 0, sub == SUB - 1
    higher = lane - z_of + lax.rem(z_of + 1, edge)
    lower = lane - z_of + lax.rem(z_of + edge - 1, edge)

    def insert(ref, f, row):
        return jnp.broadcast_to(ref[f, pl.ds(row, 1), :], (SUB, LANES))

    def up(value, f, row, ghosts):
        across = jnp.where(last_sub, insert(ghosts, f, row), pltpu.roll(value, SUB - 1, 0))
        return jnp.take_along_axis(jnp.where(first_z, across, value), higher, axis=1)

    def down(value, f, row, ghosts):
        across = jnp.where(first_sub, insert(ghosts, f, row), pltpu.roll(value, 1, 0))
        return jnp.take_along_axis(jnp.where(last_z, across, value), lower, axis=1)

    def slopes(slab):
        ghost(slab)
        for row in range(slab * SUB, (slab + 1) * SUB):
            for f in FIELDS:
                at = shape.at(f, row)
                mine = prim[at, :]
                shift = half_minmod(mine - down(mine, f, row, prev_z), up(mine, f, row, next_z) - mine)
                left[at, :] = mine + shift
                right[at, :] = mine - shift

    def fluxes(slab):
        for row in range(slab * SUB, (slab + 1) * SUB):
            lefts = [left[shape.at(f, row), :] for f in FIELDS]
            rights = [up(right[shape.at(f, row), :], f, row, right_z) for f in FIELDS]
            for f, value in enumerate(twice_flux(lefts, rights, 2)):
                flux[shape.at(f, row), :] = value

    def differences(slab):
        for row in range(slab * SUB, (slab + 1) * SUB):
            for f in FIELDS:
                at = shape.at(f, row)
                mine = flux[at, :]
                total[at, :] = sofar[at, :] + (mine - down(mine, f, row, flux_z))

    in_turn(shape.slabs, slopes, fluxes, differences)


def sweep_x_kernel(prim, x_faces, total, *, shape):
    halves, edge = shape.halves, shape.edge

    def cells(x, h):
        if x < 0:
            return [x_faces[0, f, (x + 2) * halves + h] for f in FIELDS]
        if x >= edge:
            return [x_faces[1, f, (x - edge) * halves + h] for f in FIELDS]
        return [prim[shape.at(f, x * halves + h), :] for f in FIELDS]

    for h in range(halves):
        left = below = None
        ahead = [cells(x, h) for x in (-2, -1, 0)]
        for x in range(-1, edge + 1):
            shift = half_slopes(*ahead)
            if left is not None:
                flux = twice_flux(left, minus(ahead[1], shift), 0)
                if below is not None:
                    for f in FIELDS:
                        at = shape.at(f, (x - 1) * halves + h)
                        total[at, :] = flux[f] - below[f]
                below = flux
            left = plus(ahead[1], shift)
            if x < edge:
                ahead = ahead[1:] + [cells(x + 2, h)]


def sweep_y(prim, y_one, y_two, got_one, got_two, sofar, ghost_prim, ghost_flux, left, right, flux, turned,
            shape, finish, after_slab):
    edge, halves, fit, width = shape.edge, shape.halves, shape.fit, shape.width
    lane = lane_of()
    upper = lax.rem(lane, width) >= edge
    odd = odd_y()

    def prepare(q):
        low = [jnp.where(odd, y_two[f, q], y_one[f, q]) for f in FIELDS]
        high = [jnp.where(odd, y_one[f, q], y_two[f, q]) for f in FIELDS]
        below = [jnp.where(odd, got_two[f, q], got_one[f, q]) for f in FIELDS]
        after = [jnp.where(odd, got_one[f, q], got_two[f, q]) for f in FIELDS]
        before = [lane_roll(v, edge) for v in below]
        first = [lane_roll(v, edge) for v in low]
        lefts = plus(below, half_slopes(before, below, first))
        rights = minus(first, half_slopes(below, first, low))
        fluxes = twice_flux(lefts, rights, 1)
        last = [lane_roll(v, -edge) for v in high]
        beyond = [lane_roll(v, -edge) for v in after]
        over = minus(after, half_slopes(last, after, beyond))
        for f in FIELDS:
            ghost_prim[f, q] = jnp.where(upper, below[f], after[f])
            ghost_flux[f, q] = jnp.where(upper, fluxes[f], over[f])

    top_lanes = lane >= LANES - edge
    low_lanes = lane < edge

    def up(values, insert):
        rolled = [lane_roll(v, -edge) for v in values]
        follow = rolled[1:] + [insert]
        return [jnp.where(top_lanes, n, r) for r, n in zip(rolled, follow)]

    def down(values, insert):
        rolled = [lane_roll(v, edge) for v in values]
        lead = [insert] + rolled[:-1]
        return [jnp.where(low_lanes, n, r) for r, n in zip(rolled, lead)]

    def each(q):
        for k in range(fit):
            yield -(width * k + edge), (q * fit + k) * halves

    def slopes(q):
        prepare(q)
        for turn, base in each(q):
            for f in FIELDS:
                mine = [prim[shape.at(f, base + h), :] for h in range(halves)]
                ghost = lane_roll(ghost_prim[f, q], turn)
                over, under = up(mine, ghost), down(mine, ghost)
                for h in range(halves):
                    shift = half_minmod(mine[h] - under[h], over[h] - mine[h])
                    left[shape.at(f, base + h), :] = mine[h] + shift
                    right[shape.at(f, base + h), :] = mine[h] - shift

    def fluxes(q):
        for turn, base in each(q):
            rights = []
            for f in FIELDS:
                mine = [right[shape.at(f, base + h), :] for h in range(halves)]
                ghost = lane_roll(ghost_flux[f, q], turn)
                turned[shape.at(f, base), :] = ghost
                rights.append(up(mine, ghost))
            for h in range(halves):
                lefts = [left[shape.at(f, base + h), :] for f in FIELDS]
                result = twice_flux(lefts, [rights[f][h] for f in FIELDS], 1)
                for f in FIELDS:
                    flux[shape.at(f, base + h), :] = result[f]

    def differences(q):
        for turn, base in each(q):
            total = [[None] * NF for _ in range(halves)]
            for f in FIELDS:
                mine = [flux[shape.at(f, base + h), :] for h in range(halves)]
                under = down(mine, turned[shape.at(f, base), :])
                for h in range(halves):
                    total[h][f] = sofar[shape.at(f, base + h), :] + (mine[h] - under[h])
            for h in range(halves):
                finish(base + h, total[h])

    in_turn(edge // fit, slopes, fluxes, differences, after_slab)


def sweep_y_one_kernel(field, prim, y_one, y_two, got_one, got_two, sofar, *refs, shape):
    one, one_prim, x_faces, out_y_one, out_y_two, z_lo, z_hi = refs[:7]

    def finish(row, total):
        cons = [field[shape.at(f, row), :] - (0.5 * time_step) * total[f] for f in FIELDS]
        for f, (c, w) in enumerate(zip(cons, primitives(cons))):
            one[shape.at(f, row), :] = c
            one_prim[shape.at(f, row), :] = w

    def after_slab(q):
        send_slab(shape, one_prim, out_y_one, out_y_two, z_lo, z_hi, q)

    sweep_y(prim, y_one, y_two, got_one, got_two, sofar, *refs[7:], shape, finish, after_slab)
    send_x(shape, one_prim, x_faces)


def sweep_y_two_kernel(own_there, field, one, prim, y_one, y_two, got_one, got_two, sofar, zeros, out,
                       canvas, *refs, shape, occ, groups):
    scratch, (result, sems, own, own_sem) = refs[:6], refs[6:]
    slots = pltpu.make_async_copy(own_there, own, own_sem)
    slots.start()
    rows = shape.rows
    span = SUB * SUB

    def finish(row, total):
        for f in FIELDS:
            at = shape.at(f, row)
            advanced = one[at, :] - (0.5 * time_step) * total[f]
            result[at, :] = 0.5 * field[at, :] + 0.5 * advanced

    def copy(part):
        begin = part * span if isinstance(part, int) else pl.multiple_of(part * span, span)
        at = pl.ds(begin, span)
        return [
            pltpu.make_async_copy(canvas.at[of, at, :], out.at[of, at, :], sems.at[part, f])
            for f, of in enumerate(pl.ds(f * groups, groups) for f in FIELDS)
        ]

    def after_slab(q):
        if q == 0:
            slots.wait()
        for b in range(occ):
            slot = own[b]
            to = pl.ds(q * span + lax.rem(slot, SUB), SUB, stride=SUB)
            for f in FIELDS:
                canvas[f * groups + slot // SUB, to, :] = result[shape.across(f, q, b), :]
        for c in copy(q):
            c.start()

    sweep_y(prim, y_one, y_two, got_one, got_two, sofar, *scratch, shape, finish, after_slab)
    for part in range(shape.slabs):
        for c in copy(part):
            c.wait()


def shards(state, send_slots, recv_slots, owner_slot):
    slots, _, cells = state.shape
    moves = send_slots.shape[2]
    size_x, size_y, size_z = (lax.axis_size(axis) for axis in AXES)
    occ = owner_slot.shape[0] // (size_x * size_y * size_z)
    edge = round(cells ** (1 / 3))
    rows = cells // LANES
    groups = slots // SUB
    shape = Shape(rows, edge)
    units = NF * shape.slabs
    cuts = [split_units(units, shares) for shares in ((3, 5, 7, 5), (3, 4, 5, 5, 3), (3, 4, 5, 5, 3))]
    firsts, final = cuts[0], cuts[2]

    bit_z = size_z.bit_length() - 2
    bit_y = bit_z + size_y.bit_length() - 1
    bit_x = bit_y + size_x.bit_length() - 1
    pair_bits = (bit_x, bit_y, bit_z)

    def swapped(value, level):
        mask = 2 ** pair_bits[level]
        pairs = [(source, source ^ mask) for source in range(lax.axis_size(AXES))]
        return lax.ppermute(value, AXES, pairs)

    rows_of_state = (
        state.reshape(groups, SUB, NF, rows, LANES)
        .transpose(2, 0, 3, 1, 4)
        .reshape(NF * groups * rows * SUB, LANES)
    )
    state_there = pltpu.with_memory_space_constraint(rows_of_state, HBM)
    send_there = pltpu.with_memory_space_constraint(send_slots, HBM)
    device = lax.axis_index(AXES)
    own = lax.dynamic_slice(owner_slot, (device * occ,), (occ,))
    sizes = dict(slots=slots, moves=moves)

    def message(piece):
        begin, end = piece
        return jax.ShapeDtypeStruct((moves, (end - begin) * SUB, LANES), f32)

    head = firsts[0]
    sent = [None] * len(firsts)
    sent[0] = pl.pallas_call(
        functools.partial(first_kernel, piece=head, rows=rows, **sizes),
        out_shape=message(head),
        in_specs=[whole(HBM)] * 2,
        out_specs=whole(VMEM),
        scratch_shapes=[
            SMEM(send_slots.shape, jnp.int32),
            VMEM(((head[1] - head[0]) * groups * SUB * SUB, LANES), f32),
            pltpu.SemaphoreType.DMA((1 + (head[1] - head[0]) * groups,)),
        ],
        compiler_params=params(),
        name="pack_first",
    )(send_there, state_there)
    tags, token, *sent[1:] = pl.pallas_call(
        functools.partial(rest_kernel, pieces=firsts[1:], rows=rows, occ=occ, **sizes),
        out_shape=[
            jax.ShapeDtypeStruct((2 * moves + occ,), jnp.int32),
            jax.ShapeDtypeStruct((SUB, LANES), f32),
        ]
        + [message(piece) for piece in firsts[1:]],
        in_specs=[whole(SMEM)] * 3 + [whole(VMEM)],
        out_specs=[whole(SMEM)] + [whole(VMEM)] * len(firsts),
        scratch_shapes=[SMEM((slots + SUB,), jnp.int32)],
        compiler_params=params(),
        name="pack_rest",
    )(send_slots, recv_slots, own, rows_of_state)

    got = [[None] * len(cut) for cut in cuts]

    def holding(levels, begin, end):
        found = [
            ((level, piece), got[level][p])
            for level in levels
            for p, piece in enumerate(cuts[level])
            if piece[0] < end and piece[1] > begin
        ]
        return found

    def make(wanted, through):
        found = {}
        for level, p in wanted:
            for key, value in holding(range(level), *cuts[level][p]):
                found[key] = value
        plan = tuple((level, cuts[level][p]) for level, p in wanted)
        given, passed, made = len(found), len(through), len(wanted)
        outs = pl.pallas_call(
            functools.partial(
                pick_kernel, plan=plan, held=tuple(found), passed=passed, rows=rows, **sizes
            ),
            out_shape=[message(piece) for _, piece in plan]
            + [jax.ShapeDtypeStruct(t.shape, f32) for t in through],
            in_specs=[whole(SMEM)] + [whole(VMEM)] * (1 + given) + [whole(pl.ANY)] * passed,
            out_specs=[whole(VMEM)] * made + [whole(pl.ANY)] * passed,
            input_output_aliases={2 + given + i: made + i for i in range(passed)},
            compiler_params=params(),
            cost_estimate=cost(10**9, 10**9),
            name="pick_" + "_".join("%d%d" % w for w in wanted),
        )(tags, rows_of_state, *found.values(), *through)
        return outs[:made], outs[made:]

    steps = [
        ([(1, 0)], [2], []),
        ([(1, 1)], [3], []),
        ([(1, 2), (2, 0)], [], []),
        ([(1, 3), (2, 1)], [], []),
        ([(1, 4), (2, 2)], [], [(2, 0)]),
        ([(2, 3)], [], [(2, 1)]),
        ([(2, 4)], [], [(2, 2)]),
    ]
    got[0][0] = swapped(sent[0], 0)
    got[0][1] = swapped(sent[1], 0)
    for wanted, leaving, awaited in steps:
        through = [token] + [sent[p] for p in leaving] + [got[level][p] for level, p in awaited]
        made, (token, *passed) = make(wanted, through)
        for p, value in zip(leaving, passed):
            got[0][p] = swapped(value, 0)
        for (level, p), value in reversed(list(zip(wanted, made))):
            got[level][p] = swapped(value, level)
        for (level, p), value in zip(awaited, passed[len(leaving) :]):
            got[level][p] = value

    grid = shape.grid()
    face_x, face_y, _, face_z, _ = shape.faces()
    part = [grid, grid, face_y, face_y, face_z, face_z, face_x]
    canvas = jax.ShapeDtypeStruct((NF * groups, rows * SUB, LANES), f32)
    full = final[-1][0] // NF

    def assemble(slabs, before):
        first = not before
        found = dict(holding(range(3), slabs[0] * NF, slabs[1] * NF))
        shapes = part + [canvas] * first
        fixed = 2 + len(found)
        return pl.pallas_call(
            functools.partial(
                assemble_kernel, held=tuple(found), slabs=slabs, occ=occ, shape=shape,
                first=first, **sizes,
            ),
            out_shape=shapes,
            in_specs=[whole(SMEM)] + [whole(VMEM)] * (1 + len(found) + len(before)),
            out_specs=[whole(VMEM)] * len(shapes),
            scratch_shapes=[VMEM((occ * NF * rows, LANES), f32)],
            input_output_aliases={fixed + i: i for i in range(len(before))},
            compiler_params=params(),
            name="assemble_%d" % slabs[0],
        )(tags, rows_of_state, *found.values(), *before)

    *made, blank = assemble((0, full), [])
    *made, x_faces = assemble((full, shape.slabs), made)
    made = made[:2] + [x_faces] + made[2:]

    def ring(value, axis, step):
        size = lax.axis_size(axis)
        return lax.ppermute(value, axis, [(i, (i + step) % size) for i in range(size)])

    def beside(value, axis, shift):
        size = lax.axis_size(axis)
        pairs = [(i, ((i + shift) ^ 1) - shift) for i in range(size)]
        return lax.ppermute(value, axis, [(i, j % size) for i, j in pairs])

    def flux_sums(prim, x_faces, y_one, y_two, z_lo, z_hi):
        if size_x == 2:
            x_faces = ring(x_faces, "gx", 1)
        else:
            x_faces = jnp.stack([ring(x_faces[0], "gx", 1), ring(x_faces[1], "gx", -1)])
        got_one, got_two = beside(y_one, "gy", 1), beside(y_two, "gy", 0)
        z_prev, z_next = ring(z_hi, "gz", 1), ring(z_lo, "gz", -1)
        ghost = VMEM((NF, rows, LANES), f32)
        work = [VMEM(grid.shape, f32)] * 3
        total = pl.pallas_call(
            functools.partial(sweep_x_kernel, shape=shape),
            out_shape=grid,
            in_specs=[whole(VMEM)] * 2,
            out_specs=whole(VMEM),
            compiler_params=params(),
            cost_estimate=cost(1, 1),
            name="sweep_x",
        )(prim, x_faces)
        total = pl.pallas_call(
            functools.partial(sweep_z_kernel, shape=shape),
            out_shape=grid,
            in_specs=[whole(VMEM)] * 4,
            out_specs=whole(VMEM),
            scratch_shapes=[ghost] * 4 + work,
            input_output_aliases={3: 0},
            compiler_params=params(),
            cost_estimate=cost(1, 1),
            name="sweep_z",
        )(prim, z_prev, z_next, total)
        return y_one, y_two, got_one, got_two, total

    produced = [grid, grid] + shape.faces()
    scratch = [VMEM(face_y.shape, f32)] * 2 + [VMEM(grid.shape, f32)] * 4
    field, prim = made[0], made[1]
    sums = flux_sums(prim, *made[2:])
    made = pl.pallas_call(
        functools.partial(sweep_y_one_kernel, shape=shape),
        out_shape=produced,
        in_specs=[whole(VMEM)] * 7,
        out_specs=[whole(VMEM)] * len(produced),
        scratch_shapes=scratch,
        compiler_params=params(),
        name="sweep_y_one",
    )(field, prim, *sums)
    one, one_prim = made[0], made[1]
    sums = flux_sums(one_prim, *made[2:])
    out, _ = pl.pallas_call(
        functools.partial(sweep_y_two_kernel, shape=shape, occ=occ, groups=groups),
        out_shape=[canvas, canvas],
        in_specs=[whole(HBM)] + [whole(VMEM)] * 9,
        out_specs=[whole(HBM), whole(VMEM)],
        scratch_shapes=scratch
        + [
            VMEM(grid.shape, f32),
            pltpu.SemaphoreType.DMA((shape.slabs, NF)),
            SMEM((occ,), jnp.int32),
            pltpu.SemaphoreType.DMA,
        ],
        input_output_aliases={9: 1},
        compiler_params=params(),
        name="sweep_y_two",
    )(pltpu.with_memory_space_constraint(own, HBM), field, one, one_prim, *sums, blank)
    return (
        out.reshape(NF, groups, rows, SUB, LANES)
        .transpose(1, 3, 0, 2, 4)
        .reshape(slots, NF, cells)
    )


def solution(mesh):
    placed = (
        P(AXES, None, None),
        P(None, AXES, None),
        P(None, AXES, None),
        P(),
    )
    return jax.shard_map(
        shards,
        mesh=mesh,
        in_specs=placed,
        out_specs=P(AXES, None, None),
        check_vma=False,
    )
```

```python
import functools

import jax
import jax.numpy as jnp
from jax import lax
from jax.experimental import pallas as pl
from jax.experimental.pallas import tpu as pltpu
from jax.sharding import PartitionSpec as P

gamma_ratio = 1.4
time_step = 0.05
LANES = 128
SUB = 8
NF = 5
FIELDS = range(NF)
AXES = ("gx", "gy", "gz")

VMEM = pltpu.VMEM
SMEM = pltpu.SMEM
HBM = pltpu.HBM
f32 = jnp.float32


def whole(space):
    return pl.BlockSpec(memory_space=space)


def params():
    return pltpu.CompilerParams(vmem_limit_bytes=16 * 1024 * 1024)


def cost(flops, moved):
    return pl.CostEstimate(flops=flops, bytes_accessed=moved, transcendentals=0)


def split_units(units, shares):
    ends = [units * sum(shares[: i + 1]) // sum(shares) for i in range(len(shares))]
    return list(zip([0] + ends[:-1], ends))


def from_state(state, tag, unit, slots, rows):
    slab, field = unit // NF, unit % NF
    groups = slots // SUB
    base = (tag // SUB) * (rows * SUB) + lax.rem(tag, SUB)
    start = base + (field * groups * rows + slab * SUB) * SUB
    return state[pl.ds(start, SUB, stride=SUB), :]


def pick(tag, unit, state, arrived, slots, rows, moves):
    value = from_state(state, jnp.minimum(tag, slots - 1), unit, slots, rows)
    for level, held in enumerate(arrived):
        base = slots + level * moves
        index = jnp.clip(tag - base, 0, moves - 1)
        for (begin, end), ref in held:
            if begin <= unit < end:
                at = (unit - begin) * SUB
                value = jnp.where(tag >= base, ref[index, at : at + SUB, :], value)
    return value


def first_kernel(send_hbm, state_hbm, out, send, held, sems, *, piece, slots, rows, moves):
    span = SUB * SUB
    groups = slots // SUB
    copies = [pltpu.make_async_copy(send_hbm, send, sems.at[0])]
    for unit in range(*piece):
        slab, field = unit // NF, unit % NF
        for g in range(groups):
            at = ((field * groups + g) * rows + slab * SUB) * SUB
            to = ((unit - piece[0]) * groups + g) * span
            copies.append(
                pltpu.make_async_copy(
                    state_hbm.at[pl.ds(at, span), :],
                    held.at[pl.ds(to, span), :],
                    sems.at[len(copies)],
                )
            )
    for c in copies:
        c.start()
    for c in copies:
        c.wait()
    for k in range(moves):
        slot = jnp.minimum(send[0, 0, k], slots - 1)
        base = (slot // SUB) * span + lax.rem(slot, SUB)
        for i in range(piece[1] - piece[0]):
            out[k, i * SUB : (i + 1) * SUB, :] = held[
                pl.ds(base + i * groups * span, SUB, stride=SUB), :
            ]


def rest_kernel(send, recv, own, state, tags, token, *refs, pieces, slots, rows, moves, occ):
    outs, where = refs[:-1], refs[-1]
    token[...] = jnp.zeros_like(token)
    for slot in range(slots):
        where[slot] = slot
    for level in range(3):
        if level:
            for k in range(moves):
                slot = jnp.minimum(send[level, 0, k], slots - 1)
                tags[(level - 1) * moves + k] = where[slot]
        for k in range(moves):
            where[recv[level, 0, k]] = slots + level * moves + k
    for b in range(occ):
        tags[2 * moves + b] = where[own[b]]
    for k in range(moves):
        slot = jnp.minimum(send[0, 0, k], slots - 1)
        for (begin, end), out in zip(pieces, outs):
            for unit in range(begin, end):
                at = (unit - begin) * SUB
                out[k, at : at + SUB, :] = from_state(state, slot, unit, slots, rows)


def group_levels(refs, held):
    levels = [[], [], []]
    for ref, (level, piece) in zip(refs, held):
        levels[level].append((piece, ref))
    return levels


def pick_kernel(tags, state, *refs, plan, held, passed, slots, rows, moves):
    given = len(held)
    arrived = group_levels(refs[:given], held)
    outs = refs[given + passed :]
    for (level, (begin, end)), out in zip(plan, outs):
        for k in range(moves):
            tag = tags[(level - 1) * moves + k]
            for unit in range(begin, end):
                at = (unit - begin) * SUB
                out[k, at : at + SUB, :] = pick(
                    tag, unit, state, arrived[:level], slots, rows, moves
                )


def primitives(cons):
    density = cons[0]
    inverse = 1.0 / density
    vel = [cons[1] * inverse, cons[2] * inverse, cons[3] * inverse]
    kinetic = cons[1] * vel[0] + cons[2] * vel[1] + cons[3] * vel[2]
    pressure = (gamma_ratio - 1.0) * (cons[4] - 0.5 * kinetic)
    return [density, vel[0], vel[1], vel[2], pressure]


def half_minmod(lower, upper):
    both = jnp.maximum(0.0, jnp.minimum(lower, upper)) + jnp.minimum(
        0.0, jnp.maximum(lower, upper)
    )
    return 0.5 * both


def half_slopes(before, here, after):
    return [half_minmod(h - b, a - h) for b, h, a in zip(before, here, after)]


def plus(a, b):
    return [x + y for x, y in zip(a, b)]


def minus(a, b):
    return [x - y for x, y in zip(a, b)]


def side_terms(prim, normal):
    density, vel, pressure = prim[0], prim[1:4], prim[4]
    along = vel[normal]
    mom = [density * v for v in vel]
    kinetic = mom[0] * vel[0] + mom[1] * vel[1] + mom[2] * vel[2]
    energy = pressure * (1.0 / (gamma_ratio - 1.0)) + 0.5 * kinetic
    flux = [m * along for m in mom]
    flux[normal] = flux[normal] + pressure
    scaled = gamma_ratio * pressure
    speed = jnp.abs(along) + scaled * lax.rsqrt(scaled * density)
    return [density] + mom + [energy], [mom[normal]] + flux + [(energy + pressure) * along], speed


def twice_flux(left, right, normal):
    left_cons, left_flux, left_speed = side_terms(left, normal)
    right_cons, right_flux, right_speed = side_terms(right, normal)
    speed = jnp.maximum(left_speed, right_speed)
    return [
        (fl + fr) - speed * (ur - ul)
        for fl, fr, ul, ur in zip(left_flux, right_flux, left_cons, right_cons)
    ]


def lane_of():
    return lax.broadcasted_iota(jnp.int32, (SUB, LANES), 1)


def sub_of():
    return lax.broadcasted_iota(jnp.int32, (SUB, LANES), 0)


def lane_roll(value, amount):
    amount = amount % LANES
    return value if amount == 0 else pltpu.roll(value, amount, 1)


class Shape:
    def __init__(self, rows, edge):
        self.rows, self.edge = rows, edge
        self.halves = rows // edge
        self.width = 2 * edge
        self.fit = LANES // self.width
        self.slabs = rows // SUB
        self.pad = 2 * self.halves

    def at(self, f, row):
        start = (f * self.rows + row) * SUB
        return pl.ds(start if isinstance(start, int) else pl.multiple_of(start, SUB), SUB)

    def across(self, f, slab, sub):
        return pl.ds((f * self.rows + slab * SUB) * SUB + sub, SUB, stride=SUB)

    def grid(self):
        return jax.ShapeDtypeStruct((NF * self.rows * SUB, LANES), f32)

    def faces(self):
        x = jax.ShapeDtypeStruct((2, NF, self.pad, SUB, LANES), f32)
        y = jax.ShapeDtypeStruct((NF, self.edge // self.fit, SUB, LANES), f32)
        z = jax.ShapeDtypeStruct((NF, SUB, LANES), f32)
        return [x, y, y, z, z]


def in_turn(count, *phases):
    for step in range(count + len(phases) - 1):
        for late, phase in enumerate(phases):
            if 0 <= step - late < count:
                phase(step - late)


def odd_y():
    return lax.rem(lax.axis_index("gy"), 2) == 1


def send_slab(shape, prim, y_one, y_two, z_lo, z_hi, slab):
    lane = lane_of()
    halves = shape.halves
    odd = odd_y()
    for f in FIELDS:
        lo = hi = None
        for k in range(shape.fit):
            row = slab * SUB + k * halves
            below = lane_roll(prim[shape.at(f, row), :], shape.width * k)
            above = lane_roll(prim[shape.at(f, row + halves - 1), :], shape.width * (k + 1))
            if lo is None:
                lo, hi = below, above
            else:
                mine = lane >= shape.width * k
                lo = jnp.where(mine, below, lo)
                hi = jnp.where(mine, above, hi)
        y_one[f, slab] = jnp.where(odd, hi, lo)
        y_two[f, slab] = jnp.where(odd, lo, hi)
        below = lane_roll(prim[shape.across(f, slab, 0), :], 2 * slab)
        above = lane_roll(prim[shape.across(f, slab, SUB - 1), :], 2 * slab + 2 - shape.edge)
        if slab:
            mine = lax.rem(lane, shape.edge) >= 2 * slab
            below = jnp.where(mine, below, z_lo[f])
            above = jnp.where(mine, above, z_hi[f])
        z_lo[f] = below
        z_hi[f] = above


def send_x(shape, prim, faces, low=True, high=True):
    for f in FIELDS:
        for i in range(shape.pad):
            if high:
                faces[0, f, i] = prim[shape.at(f, shape.rows - shape.pad + i), :]
            if low:
                faces[1, f, i] = prim[shape.at(f, i), :]


def assemble_kernel(tags, state, *refs, held, slabs, slots, moves, occ, shape, first):
    given = len(held)
    arrived = group_levels(refs[:given], held)
    outs = refs[given + (0 if first else 7) :]
    field, prim, y_one, y_two, z_lo, z_hi, x_faces = outs[:7]
    blocks = outs[-1]
    units = NF * shape.slabs
    for b in range(occ):
        tag = tags[2 * moves + b]
        for unit in range(slabs[0] * NF, slabs[1] * NF):
            at = (b * units + unit) * SUB
            blocks[at : at + SUB, :] = pick(tag, unit, state, arrived, slots, shape.rows, moves)
    for slab in range(*slabs):
        for i in range(SUB):
            row = slab * SUB + i
            cons = [
                blocks[pl.ds((slab * NF + f) * SUB + i, occ, stride=units * SUB), :] for f in FIELDS
            ]
            for f, (c, w) in enumerate(zip(cons, primitives(cons))):
                field[shape.at(f, row), :] = c
                prim[shape.at(f, row), :] = w
        send_slab(shape, prim, y_one, y_two, z_lo, z_hi, slab)
    if first:
        canvas = outs[7]

        def clear(i, carry):
            for c in range(canvas.shape[0]):
                canvas[c, pl.ds(pl.multiple_of(i * SUB, SUB), SUB), :] = jnp.zeros((SUB, LANES), f32)
            return carry

        lax.fori_loop(0, canvas.shape[1] // SUB, clear, 0)
    send_x(shape, prim, x_faces, low=first, high=not first)


def sweep_z_kernel(prim, z_prev, z_next, sofar, total, prev_z, next_z, flux_z, right_z, left, right, flux, *, shape):
    edge, rows = shape.edge, shape.rows

    def ghost(a):
        at = pl.ds(a * SUB, SUB)
        low = [prim[shape.across(f, a, 0), :] for f in FIELDS]
        high = [prim[shape.across(f, a, SUB - 1), :] for f in FIELDS]
        prev = [lane_roll(z_prev[f], edge - 2 - 2 * a) for f in FIELDS]
        after = [lane_roll(z_next[f], -2 * a) for f in FIELDS]
        for f in FIELDS:
            prev_z[f, at, :] = prev[f]
            next_z[f, at, :] = after[f]
        below = [lane_roll(v, -(edge - 1)) for v in prev]
        before = [lane_roll(v, -(edge - 2)) for v in prev]
        second = [lane_roll(v, -1) for v in low]
        lefts = plus(below, half_slopes(before, below, low))
        rights = minus(low, half_slopes(below, low, second))
        fluxes = twice_flux(lefts, rights, 2)
        last = [lane_roll(v, -(edge - 1)) for v in high]
        beyond = [lane_roll(v, -1) for v in after]
        over = minus(after, half_slopes(last, after, beyond))
        for f in FIELDS:
            flux_z[f, at, :] = lane_roll(fluxes[f], edge - 1)
            right_z[f, at, :] = over[f]

    lane = lane_of()
    z_of = lax.rem(lane, edge)
    sub = sub_of()
    first_z, last_z = z_of == 0, z_of == edge - 1
    first_sub, last_sub = sub == 0, sub == SUB - 1
    higher = lane - z_of + lax.rem(z_of + 1, edge)
    lower = lane - z_of + lax.rem(z_of + edge - 1, edge)

    def insert(ref, f, row):
        return jnp.broadcast_to(ref[f, pl.ds(row, 1), :], (SUB, LANES))

    def up(value, f, row, ghosts):
        across = jnp.where(last_sub, insert(ghosts, f, row), pltpu.roll(value, SUB - 1, 0))
        return jnp.take_along_axis(jnp.where(first_z, across, value), higher, axis=1)

    def down(value, f, row, ghosts):
        across = jnp.where(first_sub, insert(ghosts, f, row), pltpu.roll(value, 1, 0))
        return jnp.take_along_axis(jnp.where(last_z, across, value), lower, axis=1)

    def slopes(slab):
        ghost(slab)
        for row in range(slab * SUB, (slab + 1) * SUB):
            for f in FIELDS:
                at = shape.at(f, row)
                mine = prim[at, :]
                shift = half_minmod(mine - down(mine, f, row, prev_z), up(mine, f, row, next_z) - mine)
                left[at, :] = mine + shift
                right[at, :] = mine - shift

    def fluxes(slab):
        for row in range(slab * SUB, (slab + 1) * SUB):
            lefts = [left[shape.at(f, row), :] for f in FIELDS]
            rights = [up(right[shape.at(f, row), :], f, row, right_z) for f in FIELDS]
            for f, value in enumerate(twice_flux(lefts, rights, 2)):
                flux[shape.at(f, row), :] = value

    def differences(slab):
        for row in range(slab * SUB, (slab + 1) * SUB):
            for f in FIELDS:
                at = shape.at(f, row)
                mine = flux[at, :]
                total[at, :] = sofar[at, :] + (mine - down(mine, f, row, flux_z))

    in_turn(shape.slabs, slopes, fluxes, differences)


def sweep_x_kernel(prim, x_faces, total, *, shape):
    halves, edge = shape.halves, shape.edge

    def cells(x, h):
        if x < 0:
            return [x_faces[0, f, (x + 2) * halves + h] for f in FIELDS]
        if x >= edge:
            return [x_faces[1, f, (x - edge) * halves + h] for f in FIELDS]
        return [prim[shape.at(f, x * halves + h), :] for f in FIELDS]

    for h in range(halves):
        left = below = None
        ahead = [cells(x, h) for x in (-2, -1, 0)]
        for x in range(-1, edge + 1):
            shift = half_slopes(*ahead)
            if left is not None:
                flux = twice_flux(left, minus(ahead[1], shift), 0)
                if below is not None:
                    for f in FIELDS:
                        at = shape.at(f, (x - 1) * halves + h)
                        total[at, :] = flux[f] - below[f]
                below = flux
            left = plus(ahead[1], shift)
            if x < edge:
                ahead = ahead[1:] + [cells(x + 2, h)]


def sweep_y(prim, y_one, y_two, got_one, got_two, sofar, ghost_prim, ghost_flux, left, right, flux, turned,
            shape, finish, after_slab):
    edge, halves, fit, width = shape.edge, shape.halves, shape.fit, shape.width
    lane = lane_of()
    upper = lax.rem(lane, width) >= edge
    odd = odd_y()

    def prepare(q):
        low = [jnp.where(odd, y_two[f, q], y_one[f, q]) for f in FIELDS]
        high = [jnp.where(odd, y_one[f, q], y_two[f, q]) for f in FIELDS]
        below = [jnp.where(odd, got_two[f, q], got_one[f, q]) for f in FIELDS]
        after = [jnp.where(odd, got_one[f, q], got_two[f, q]) for f in FIELDS]
        before = [lane_roll(v, edge) for v in below]
        first = [lane_roll(v, edge) for v in low]
        lefts = plus(below, half_slopes(before, below, first))
        rights = minus(first, half_slopes(below, first, low))
        fluxes = twice_flux(lefts, rights, 1)
        last = [lane_roll(v, -edge) for v in high]
        beyond = [lane_roll(v, -edge) for v in after]
        over = minus(after, half_slopes(last, after, beyond))
        for f in FIELDS:
            ghost_prim[f, q] = jnp.where(upper, below[f], after[f])
            ghost_flux[f, q] = jnp.where(upper, fluxes[f], over[f])

    top_lanes = lane >= LANES - edge
    low_lanes = lane < edge

    def up(values, insert):
        rolled = [lane_roll(v, -edge) for v in values]
        follow = rolled[1:] + [insert]
        return [jnp.where(top_lanes, n, r) for r, n in zip(rolled, follow)]

    def down(values, insert):
        rolled = [lane_roll(v, edge) for v in values]
        lead = [insert] + rolled[:-1]
        return [jnp.where(low_lanes, n, r) for r, n in zip(rolled, lead)]

    def each(q):
        for k in range(fit):
            yield -(width * k + edge), (q * fit + k) * halves

    def slopes(q):
        prepare(q)
        for turn, base in each(q):
            for f in FIELDS:
                mine = [prim[shape.at(f, base + h), :] for h in range(halves)]
                ghost = lane_roll(ghost_prim[f, q], turn)
                over, under = up(mine, ghost), down(mine, ghost)
                for h in range(halves):
                    shift = half_minmod(mine[h] - under[h], over[h] - mine[h])
                    left[shape.at(f, base + h), :] = mine[h] + shift
                    right[shape.at(f, base + h), :] = mine[h] - shift

    def fluxes(q):
        for turn, base in each(q):
            rights = []
            for f in FIELDS:
                mine = [right[shape.at(f, base + h), :] for h in range(halves)]
                ghost = lane_roll(ghost_flux[f, q], turn)
                turned[shape.at(f, base), :] = ghost
                rights.append(up(mine, ghost))
            for h in range(halves):
                lefts = [left[shape.at(f, base + h), :] for f in FIELDS]
                result = twice_flux(lefts, [rights[f][h] for f in FIELDS], 1)
                for f in FIELDS:
                    flux[shape.at(f, base + h), :] = result[f]

    def differences(q):
        for turn, base in each(q):
            total = [[None] * NF for _ in range(halves)]
            for f in FIELDS:
                mine = [flux[shape.at(f, base + h), :] for h in range(halves)]
                under = down(mine, turned[shape.at(f, base), :])
                for h in range(halves):
                    total[h][f] = sofar[shape.at(f, base + h), :] + (mine[h] - under[h])
            for h in range(halves):
                finish(base + h, total[h])

    in_turn(edge // fit, slopes, fluxes, differences, after_slab)


def sweep_y_one_kernel(field, prim, y_one, y_two, got_one, got_two, sofar, *refs, shape):
    one, one_prim, x_faces, out_y_one, out_y_two, z_lo, z_hi = refs[:7]

    def finish(row, total):
        cons = [field[shape.at(f, row), :] - (0.5 * time_step) * total[f] for f in FIELDS]
        for f, (c, w) in enumerate(zip(cons, primitives(cons))):
            one[shape.at(f, row), :] = c
            one_prim[shape.at(f, row), :] = w

    def after_slab(q):
        send_slab(shape, one_prim, out_y_one, out_y_two, z_lo, z_hi, q)

    sweep_y(prim, y_one, y_two, got_one, got_two, sofar, *refs[7:], shape, finish, after_slab)
    send_x(shape, one_prim, x_faces)


def sweep_y_two_kernel(own_there, field, one, prim, y_one, y_two, got_one, got_two, sofar, zeros, out,
                       canvas, *refs, shape, occ, groups):
    scratch, (result, sems, own, own_sem) = refs[:6], refs[6:]
    slots = pltpu.make_async_copy(own_there, own, own_sem)
    slots.start()
    rows = shape.rows
    span = SUB * SUB

    def finish(row, total):
        for f in FIELDS:
            at = shape.at(f, row)
            advanced = one[at, :] - (0.5 * time_step) * total[f]
            result[at, :] = 0.5 * field[at, :] + 0.5 * advanced

    def copy(part):
        begin = part * span if isinstance(part, int) else pl.multiple_of(part * span, span)
        at = pl.ds(begin, span)
        return [
            pltpu.make_async_copy(canvas.at[of, at, :], out.at[of, at, :], sems.at[part, f])
            for f, of in enumerate(pl.ds(f * groups, groups) for f in FIELDS)
        ]

    def after_slab(q):
        if q == 0:
            slots.wait()
        for b in range(occ):
            slot = own[b]
            to = pl.ds(q * span + lax.rem(slot, SUB), SUB, stride=SUB)
            for f in FIELDS:
                canvas[f * groups + slot // SUB, to, :] = result[shape.across(f, q, b), :]
        for c in copy(q):
            c.start()

    sweep_y(prim, y_one, y_two, got_one, got_two, sofar, *scratch, shape, finish, after_slab)
    for part in range(shape.slabs):
        for c in copy(part):
            c.wait()


def shards(state, send_slots, recv_slots, owner_slot):
    slots, _, cells = state.shape
    moves = send_slots.shape[2]
    size_x, size_y, size_z = (lax.axis_size(axis) for axis in AXES)
    occ = owner_slot.shape[0] // (size_x * size_y * size_z)
    edge = round(cells ** (1 / 3))
    rows = cells // LANES
    groups = slots // SUB
    shape = Shape(rows, edge)
    units = NF * shape.slabs
    cuts = [split_units(units, shares) for shares in ((3, 5, 7, 5), (3, 4, 5, 4, 4), (3, 4, 5, 4, 4))]
    firsts, final = cuts[0], cuts[2]

    bit_z = size_z.bit_length() - 2
    bit_y = bit_z + size_y.bit_length() - 1
    bit_x = bit_y + size_x.bit_length() - 1
    pair_bits = (bit_x, bit_y, bit_z)

    def swapped(value, level):
        mask = 2 ** pair_bits[level]
        pairs = [(source, source ^ mask) for source in range(lax.axis_size(AXES))]
        return lax.ppermute(value, AXES, pairs)

    rows_of_state = (
        state.reshape(groups, SUB, NF, rows, LANES)
        .transpose(2, 0, 3, 1, 4)
        .reshape(NF * groups * rows * SUB, LANES)
    )
    state_there = pltpu.with_memory_space_constraint(rows_of_state, HBM)
    send_there = pltpu.with_memory_space_constraint(send_slots, HBM)
    device = lax.axis_index(AXES)
    own = lax.dynamic_slice(owner_slot, (device * occ,), (occ,))
    sizes = dict(slots=slots, moves=moves)

    def message(piece):
        begin, end = piece
        return jax.ShapeDtypeStruct((moves, (end - begin) * SUB, LANES), f32)

    head = firsts[0]
    sent = [None] * len(firsts)
    sent[0] = pl.pallas_call(
        functools.partial(first_kernel, piece=head, rows=rows, **sizes),
        out_shape=message(head),
        in_specs=[whole(HBM)] * 2,
        out_specs=whole(VMEM),
        scratch_shapes=[
            SMEM(send_slots.shape, jnp.int32),
            VMEM(((head[1] - head[0]) * groups * SUB * SUB, LANES), f32),
            pltpu.SemaphoreType.DMA((1 + (head[1] - head[0]) * groups,)),
        ],
        compiler_params=params(),
        name="pack_first",
    )(send_there, state_there)
    tags, token, *sent[1:] = pl.pallas_call(
        functools.partial(rest_kernel, pieces=firsts[1:], rows=rows, occ=occ, **sizes),
        out_shape=[
            jax.ShapeDtypeStruct((2 * moves + occ,), jnp.int32),
            jax.ShapeDtypeStruct((SUB, LANES), f32),
        ]
        + [message(piece) for piece in firsts[1:]],
        in_specs=[whole(SMEM)] * 3 + [whole(VMEM)],
        out_specs=[whole(SMEM)] + [whole(VMEM)] * len(firsts),
        scratch_shapes=[SMEM((slots + SUB,), jnp.int32)],
        compiler_params=params(),
        name="pack_rest",
    )(send_slots, recv_slots, own, rows_of_state)

    got = [[None] * len(cut) for cut in cuts]

    def holding(levels, begin, end):
        found = [
            ((level, piece), got[level][p])
            for level in levels
            for p, piece in enumerate(cuts[level])
            if piece[0] < end and piece[1] > begin
        ]
        return found

    def make(wanted, through):
        found = {}
        for level, p in wanted:
            for key, value in holding(range(level), *cuts[level][p]):
                found[key] = value
        plan = tuple((level, cuts[level][p]) for level, p in wanted)
        given, passed, made = len(found), len(through), len(wanted)
        outs = pl.pallas_call(
            functools.partial(
                pick_kernel, plan=plan, held=tuple(found), passed=passed, rows=rows, **sizes
            ),
            out_shape=[message(piece) for _, piece in plan]
            + [jax.ShapeDtypeStruct(t.shape, f32) for t in through],
            in_specs=[whole(SMEM)] + [whole(VMEM)] * (1 + given) + [whole(pl.ANY)] * passed,
            out_specs=[whole(VMEM)] * made + [whole(pl.ANY)] * passed,
            input_output_aliases={2 + given + i: made + i for i in range(passed)},
            compiler_params=params(),
            cost_estimate=cost(10**9, 10**9),
            name="pick_" + "_".join("%d%d" % w for w in wanted),
        )(tags, rows_of_state, *found.values(), *through)
        return outs[:made], outs[made:]

    steps = [
        ([(1, 0)], [2], []),
        ([(1, 1)], [3], []),
        ([(1, 2), (2, 0)], [], []),
        ([(1, 3), (2, 1)], [], []),
        ([(1, 4), (2, 2)], [], [(2, 0)]),
        ([(2, 3)], [], [(2, 1)]),
        ([(2, 4)], [], [(2, 2)]),
    ]
    got[0][0] = swapped(sent[0], 0)
    got[0][1] = swapped(sent[1], 0)
    for wanted, leaving, awaited in steps:
        through = [token] + [sent[p] for p in leaving] + [got[level][p] for level, p in awaited]
        made, (token, *passed) = make(wanted, through)
        for p, value in zip(leaving, passed):
            got[0][p] = swapped(value, 0)
        for (level, p), value in reversed(list(zip(wanted, made))):
            got[level][p] = swapped(value, level)
        for (level, p), value in zip(awaited, passed[len(leaving) :]):
            got[level][p] = value

    grid = shape.grid()
    face_x, face_y, _, face_z, _ = shape.faces()
    part = [grid, grid, face_y, face_y, face_z, face_z, face_x]
    canvas = jax.ShapeDtypeStruct((NF * groups, rows * SUB, LANES), f32)
    full = final[-1][0] // NF

    def assemble(slabs, before):
        first = not before
        found = dict(holding(range(3), slabs[0] * NF, slabs[1] * NF))
        shapes = part + [canvas] * first
        fixed = 2 + len(found)
        return pl.pallas_call(
            functools.partial(
                assemble_kernel, held=tuple(found), slabs=slabs, occ=occ, shape=shape,
                first=first, **sizes,
            ),
            out_shape=shapes,
            in_specs=[whole(SMEM)] + [whole(VMEM)] * (1 + len(found) + len(before)),
            out_specs=[whole(VMEM)] * len(shapes),
            scratch_shapes=[VMEM((occ * NF * rows, LANES), f32)],
            input_output_aliases={fixed + i: i for i in range(len(before))},
            compiler_params=params(),
            name="assemble_%d" % slabs[0],
        )(tags, rows_of_state, *found.values(), *before)

    *made, blank = assemble((0, full), [])
    *made, x_faces = assemble((full, shape.slabs), made)
    made = made[:2] + [x_faces] + made[2:]

    def ring(value, axis, step):
        size = lax.axis_size(axis)
        return lax.ppermute(value, axis, [(i, (i + step) % size) for i in range(size)])

    def beside(value, axis, shift):
        size = lax.axis_size(axis)
        pairs = [(i, ((i + shift) ^ 1) - shift) for i in range(size)]
        return lax.ppermute(value, axis, [(i, j % size) for i, j in pairs])

    def flux_sums(prim, x_faces, y_one, y_two, z_lo, z_hi):
        if size_x == 2:
            x_faces = ring(x_faces, "gx", 1)
        else:
            x_faces = jnp.stack([ring(x_faces[0], "gx", 1), ring(x_faces[1], "gx", -1)])
        got_one, got_two = beside(y_one, "gy", 1), beside(y_two, "gy", 0)
        z_prev, z_next = ring(z_hi, "gz", 1), ring(z_lo, "gz", -1)
        ghost = VMEM((NF, rows, LANES), f32)
        work = [VMEM(grid.shape, f32)] * 3
        total = pl.pallas_call(
            functools.partial(sweep_x_kernel, shape=shape),
            out_shape=grid,
            in_specs=[whole(VMEM)] * 2,
            out_specs=whole(VMEM),
            compiler_params=params(),
            cost_estimate=cost(1, 1),
            name="sweep_x",
        )(prim, x_faces)
        total = pl.pallas_call(
            functools.partial(sweep_z_kernel, shape=shape),
            out_shape=grid,
            in_specs=[whole(VMEM)] * 4,
            out_specs=whole(VMEM),
            scratch_shapes=[ghost] * 4 + work,
            input_output_aliases={3: 0},
            compiler_params=params(),
            cost_estimate=cost(1, 1),
            name="sweep_z",
        )(prim, z_prev, z_next, total)
        return y_one, y_two, got_one, got_two, total

    produced = [grid, grid] + shape.faces()
    scratch = [VMEM(face_y.shape, f32)] * 2 + [VMEM(grid.shape, f32)] * 4
    field, prim = made[0], made[1]
    sums = flux_sums(prim, *made[2:])
    made = pl.pallas_call(
        functools.partial(sweep_y_one_kernel, shape=shape),
        out_shape=produced,
        in_specs=[whole(VMEM)] * 7,
        out_specs=[whole(VMEM)] * len(produced),
        scratch_shapes=scratch,
        compiler_params=params(),
        name="sweep_y_one",
    )(field, prim, *sums)
    one, one_prim = made[0], made[1]
    sums = flux_sums(one_prim, *made[2:])
    out, _ = pl.pallas_call(
        functools.partial(sweep_y_two_kernel, shape=shape, occ=occ, groups=groups),
        out_shape=[canvas, canvas],
        in_specs=[whole(HBM)] + [whole(VMEM)] * 9,
        out_specs=[whole(HBM), whole(VMEM)],
        scratch_shapes=scratch
        + [
            VMEM(grid.shape, f32),
            pltpu.SemaphoreType.DMA((shape.slabs, NF)),
            SMEM((occ,), jnp.int32),
            pltpu.SemaphoreType.DMA,
        ],
        input_output_aliases={9: 1},
        compiler_params=params(),
        name="sweep_y_two",
    )(pltpu.with_memory_space_constraint(own, HBM), field, one, one_prim, *sums, blank)
    return (
        out.reshape(NF, groups, rows, SUB, LANES)
        .transpose(1, 3, 0, 2, 4)
        .reshape(slots, NF, cells)
    )


def solution(mesh):
    placed = (
        P(AXES, None, None),
        P(None, AXES, None),
        P(None, AXES, None),
        P(),
    )
    return jax.shard_map(
        shards,
        mesh=mesh,
        in_specs=placed,
        out_specs=P(AXES, None, None),
        check_vma=False,
    )
```
